32 devices in a mesh: pipe: 2 (over y), seq: 4 (over x, core), dp: 4 (over z).
Axes of the slice: x: 2, y: 2, z: 4, core: 2. Of those that a mesh axis runs over, the one named last changes fastest.
Arguments:
- incoming: bfloat16 [2, 3, 4, 512, 1536], P('pipe', None, 'dp', 'seq'), may hold values from -9 to 9, as said below
- contacts: int32 [4, 4, 512], P(None, 'dp', 'seq'), may hold values from 0 to 15
- keyframes: int32 [4, 4, 512], P(None, 'dp'), may hold values 0 or 1
- timesteps: int32 [4, 4], P(None, 'dp'), may hold values from 0 to 999
- w_query: bfloat16 [2, 1536, 1536], P('pipe', ('seq', 'dp')), may hold values from -1 to 1, as said below
- w_keyval: bfloat16 [2, 1536, 1536], P('pipe', ('seq', 'dp')), may hold values from -1 to 1, as said below
- norm_gain: float32 [2, 1536], P('pipe'), may hold values from 0.5 to 1.5
- time_freq: float32 [2, 1536], P('pipe'), may hold values from 0.0005 to 0.05
- contact_table: bfloat16 [2, 16, 1536], P('pipe'), may hold values from -3 to 3
- key_bias: float32 [2, 16], P('pipe'), may hold values from 0.5 to 4
- attn_gate: float32 [2, 1536], P('pipe'), may hold values from 1 to 4
- head_cotangent: bfloat16 [2, 3, 4, 512, 256], P('pipe', None, 'dp', 'seq'), may hold values from -6 to 6
Outputs:
- section_out: bfloat16 [2, 3, 4, 512, 1536], P('pipe', None, 'dp', 'seq')
- head_grad: float32 [2, 1536, 256], P('pipe', ('seq', 'dp'))
The draws below stay inside these ranges and needn't reach their ends.
Inputs may be any that keep to these rules, and one draw needn't show every extreme that they name: `contacts`: each frame's contact state, four limbs as bits. `incoming`: activations of order one. `w_query`: entries of about 1536 ** -0.5. `w_keyval`: entries of about 1536 ** -0.5.
All inputs are finite; a program needn't handle non-finite values. No bound on the sum of `keyframes` on one device may be relied on, other than what follows from the above.
Results may differ from the reference program's by a relative error of at most 0.014.
Values may be sent and summed in bfloat16 or wider, within the bound.
No kernel may reach another device: no remote copies, remote signals or barrier semaphores. Data moves between devices by JAX's collectives and lax.ppermute only.
A program may use at most 64 MiB of HBM per device.

```python
import math
import jax
import jax.numpy as jnp
from jax import lax

D = 1536
HEADS = 16
HEAD = 96
KVHEADS = 8
F = 256
CONTACTS = 16
TSTEPS = 1000
TURNS = 3
SECTIONS = 2
REPLICAS = 4
FRAMES = 512
BATCHES = 4


def draw_incoming(key, part):
    own_key = jax.random.fold_in(key, 11)
    normal_key = jax.random.fold_in(own_key, 0)
    shape = (SECTIONS, TURNS, REPLICAS, FRAMES, D)
    values = jax.random.truncated_normal(normal_key, -6.0, 6.0, shape, dtype=jnp.float32)
    return jnp.clip(values, -9.0, 9.0).astype(jnp.bfloat16)


def draw_w_query(key, part):
    own_key = jax.random.fold_in(key, 23)
    values = jax.random.truncated_normal(own_key, -6.0, 6.0, (SECTIONS, D, D), dtype=jnp.float32) * D ** (-0.5)
    return jnp.clip(values, -1.0, 1.0).astype(jnp.bfloat16)


def draw_w_keyval(key, part):
    own_key = jax.random.fold_in(key, 37)
    width = 2 * KVHEADS * HEAD
    values = jax.random.truncated_normal(own_key, -6.0, 6.0, (SECTIONS, D, width), dtype=jnp.float32) * D ** (-0.5)
    return jnp.clip(values, -1.0, 1.0).astype(jnp.bfloat16)


def touch_ends(entries, key, low, largest):
    index_at = [jax.random.randint(jax.random.fold_in(key, axis), (), 0, length) for axis, length in enumerate(entries.shape)]
    widest = entries.shape.index(max(entries.shape))
    next_to = index_at[:widest] + [(index_at[widest] + 1) % entries.shape[widest]] + index_at[widest + 1:]
    return entries.at[tuple(index_at)].set(low).at[tuple(next_to)].set(largest)


def block_levels(key, shape, pieces, low, high):
    def one(position, shards_of):
        heights = jax.random.uniform(jax.random.fold_in(jax.random.fold_in(key, 6), position), (shards_of,), jnp.float32, low / len(pieces), high / len(pieces))
        return jnp.repeat(jnp.exp(heights), shape[position] // shards_of).reshape((-1,) + (1,) * (len(shape) - position - 1))

    loudness = one(*pieces[0])
    for cut in pieces[1:]:
        loudness = loudness * one(*cut)
    return loudness


def normal_values(rng, shape, spread, reach, shards=(), kind=jnp.bfloat16):
    entries = spread * jax.random.normal(rng, shape, jnp.float32)
    if shards:
        entries = entries * block_levels(rng, shape, shards, -0.22, 0.18)
    return jnp.clip(entries, -reach, reach).astype(kind)


def setup_inputs(seed: int = 0) -> dict:
    key_of = jax.random.split(jax.random.key(seed), 13)
    return {
        "incoming": draw_incoming(jax.random.fold_in(key_of[12], 71), 0),
        "contacts": touch_ends(jax.random.randint(key_of[1], (BATCHES, REPLICAS, FRAMES), 0, CONTACTS), jax.random.fold_in(key_of[1], 1), 0, CONTACTS - 1).astype(jnp.int32),
        "keyframes": touch_ends((jax.random.randint(key_of[2], (BATCHES, REPLICAS, FRAMES), 0, 16) < 1).astype(jnp.int32), jax.random.fold_in(key_of[2], 1), 0, 1),
        "timesteps": touch_ends(jax.random.randint(key_of[3], (BATCHES, REPLICAS), 0, TSTEPS), jax.random.fold_in(key_of[3], 1), 0, TSTEPS - 1).astype(jnp.int32),
        "w_query": draw_w_query(jax.random.fold_in(key_of[12], 71), 0),
        "w_keyval": draw_w_keyval(jax.random.fold_in(key_of[12], 71), 0),
        "norm_gain": jnp.clip(1.0 + 0.1 * jax.random.normal(key_of[6], (SECTIONS, D), jnp.float32), 0.5, 1.5),
        "time_freq": jnp.clip(jnp.exp(math.log(0.05) - 4.6051702 * jax.random.uniform(key_of[7], (SECTIONS, D), jnp.float32) ** block_levels(key_of[7], (SECTIONS, D), ((0, 2),), -0.2, 0.2)), 0.0005, 0.05),
        "contact_table": normal_values(key_of[8], (SECTIONS, CONTACTS, D), 0.5, 3.0, ((0, 2),)),
        "key_bias": jnp.clip(0.5 + 3.5 * jax.random.uniform(key_of[9], (SECTIONS, HEADS), jnp.float32) ** block_levels(key_of[9], (SECTIONS, HEADS), ((0, 2),), -0.2, 0.2), 0.5, 4.0),
        "attn_gate": jnp.clip(jnp.exp(math.log(4.0) - 1.3862944 * jax.random.uniform(key_of[10], (SECTIONS, D), jnp.float32) ** block_levels(key_of[10], (SECTIONS, D), ((0, 2),), -0.2, 0.2)), 1.0, 4.0),
        "head_cotangent": normal_values(key_of[11], (SECTIONS, TURNS, REPLICAS, FRAMES, F), 1.0, 6.0, ((0, 2), (2, 4), (3, 4))),
    }


epsilon = 1e-06

def attend(queries, keyval, key_flags, bias_heads):
    queries_f = queries.reshape(FRAMES, HEADS, HEAD).astype(jnp.float32)
    keyval_f = keyval.reshape(FRAMES, KVHEADS, 2, HEAD).astype(jnp.float32)
    group_size = HEADS // KVHEADS
    key_rows = jnp.repeat(keyval_f[:, :, 0], group_size, axis=1)
    value_rows = jnp.repeat(keyval_f[:, :, 1], group_size, axis=1)
    scores = jnp.einsum('qhd,khd->hqk', queries_f, key_rows) * HEAD ** (-0.5)
    scores = scores + bias_heads[:, None, None] * key_flags.astype(jnp.float32)[None, None, :]
    row_max = lax.optimization_barrier(jnp.max(scores, axis=-1, keepdims=True))
    exponent = jnp.exp(scores - row_max)
    probabilities = (exponent / lax.optimization_barrier(jnp.sum(exponent, axis=-1, keepdims=True))).astype(jnp.bfloat16)
    attended = jnp.einsum('hqk,khd->qhd', probabilities.astype(jnp.float32), value_rows)
    return attended.astype(jnp.bfloat16).reshape(FRAMES, D)

def section_apply(current, contact_rows, key_flags, timestep, wquery, wkeyval, gain_row, freq_row, table, bias_heads, gate_row):
    onehot = (contact_rows[..., None] == jnp.arange(CONTACTS)[None, None, :]).astype(jnp.float32)
    embedded = jnp.einsum('rfc,cd->rfd', onehot, table.astype(jnp.float32))
    hidden = current.astype(jnp.float32) + embedded
    root_mean = jnp.sqrt(lax.optimization_barrier(jnp.mean(hidden * hidden, axis=-1, keepdims=True)) + epsilon)
    modulation = gain_row[None, :] * (1.0 + 0.5 * jnp.sin(timestep.astype(jnp.float32)[:, None] * freq_row[None, :]))
    normed = (hidden / root_mean * modulation[:, None, :]).astype(jnp.bfloat16)
    flat = normed.reshape(REPLICAS * FRAMES, D)
    queries = jnp.dot(flat, wquery, preferred_element_type=jnp.float32).astype(jnp.bfloat16)
    keyval = jnp.dot(flat, wkeyval, preferred_element_type=jnp.float32).astype(jnp.bfloat16)
    queries = queries.reshape(REPLICAS, FRAMES, D)
    keyval = keyval.reshape(REPLICAS, FRAMES, 2 * KVHEADS * HEAD)
    attended = lax.map(lambda items: attend(items[0], items[1], items[2], bias_heads), (queries, keyval, key_flags))
    return (hidden + gate_row[None, None, :] * attended.astype(jnp.float32)).astype(jnp.bfloat16)

def reference(incoming, contacts, keyframes, timesteps, w_query, w_keyval, norm_gain, time_freq, contact_table, key_bias, attn_gate, head_cotangent):
    factor = float(TURNS * REPLICAS * FRAMES) ** (-0.5)
    results = []
    grads = []
    previous = None
    for section_idx in range(SECTIONS):
        current_row = []
        for turn in range(TURNS):
            if section_idx == 0 or turn == 0:
                current = incoming[section_idx, turn]
            else:
                current = previous[turn - 1]
            batch_idx = turn - section_idx + SECTIONS - 1
            output = section_apply(current, contacts[batch_idx], keyframes[batch_idx], timesteps[batch_idx], w_query[section_idx], w_keyval[section_idx], norm_gain[section_idx], time_freq[section_idx], contact_table[section_idx], key_bias[section_idx], attn_gate[section_idx])
            current_row.append(output)
        stacked = jnp.stack(current_row)
        results.append(stacked)
        grad = jnp.dot(stacked.reshape(TURNS * REPLICAS * FRAMES, D).T, head_cotangent[section_idx].reshape(TURNS * REPLICAS * FRAMES, F), preferred_element_type=jnp.float32) * factor
        grads.append(grad)
        previous = current_row
    return (jnp.stack(results), jnp.stack(grads))
```

```python
import jax
import jax.numpy as jnp
from jax import lax
from jax.sharding import PartitionSpec as P

epsilon = 1e-06


def passed_along(value, axis, steps):
    count = lax.axis_size(axis)
    first, last = (max(0, -steps), min(count, count - steps))
    return lax.ppermute(value, axis, [(source, source + steps) for source in range(first, last)])


def ring(value, axis):
    count = lax.axis_size(axis)
    return lax.ppermute(value, axis, [(source, (source + 1) % count) for source in range(count)])


def body(
    incoming,
    contacts,
    keyframes,
    timesteps,
    w_query,
    w_keyval,
    norm_gain,
    time_freq,
    contact_table,
    key_bias,
    attn_gate,
    head_cotangent,
):
    section_idx = lax.axis_index("pipe")
    seq_idx = lax.axis_index("seq")
    rep_idx = lax.axis_index("dp")
    seq_count = lax.axis_size("seq")
    section_count = lax.axis_size("pipe")
    rep_count = lax.axis_size("dp")
    tok_rows = incoming.shape[3]
    width = incoming.shape[4]
    turns = incoming.shape[1]
    frames = tok_rows * seq_count
    heads_all = key_bias.shape[1]
    head_size = width // heads_all
    heads_local = heads_all // seq_count
    kv_width = w_keyval.shape[2]
    kv_local = kv_width // (2 * head_size * seq_count)
    group_size = heads_local // kv_local
    feat_count = head_cotangent.shape[4]
    score_scale = head_size ** (-0.5)
    q_cols = width // seq_count
    kv_cols = kv_width // seq_count
    w_rows = w_query.shape[1]

    w_parts = jnp.concatenate(
        [
            w_query[0].reshape(w_rows, seq_count, q_cols),
            w_keyval[0].reshape(w_rows, seq_count, kv_cols),
        ],
        axis=2,
    ).transpose(1, 0, 2)
    block = lax.all_to_all(w_parts, "seq", split_axis=0, concat_axis=0, tiled=True)
    weights = jnp.zeros((seq_count, rep_count, w_rows, q_cols + kv_cols), jnp.bfloat16)
    for hop in range(rep_count):
        owner = lax.rem(rep_idx + rep_count - hop, rep_count)
        weights = lax.dynamic_update_slice_in_dim(weights, block[:, None], owner, 1)
        if hop + 1 < rep_count:
            block = ring(block, "dp")
    weights = weights.reshape(width, q_cols + kv_cols)

    gain_row = norm_gain[0]
    freq_row = time_freq[0]
    table = contact_table[0]
    gate_local = lax.dynamic_slice_in_dim(attn_gate[0], seq_idx * q_cols, q_cols)
    table_local = lax.dynamic_slice_in_dim(table, seq_idx * q_cols, q_cols, 1)
    bias_local = lax.dynamic_slice_in_dim(key_bias[0], seq_idx * heads_local, heads_local)
    contact_all = lax.all_gather(contacts[:, 0, :], "seq", axis=1, tiled=True)
    key_all = keyframes[:, 0, :]
    step_all = timesteps[:, 0]
    labels = jnp.arange(table.shape[0], dtype=jnp.int32)
    cot_all = lax.all_gather(head_cotangent[0, :, 0], "seq", axis=1, tiled=True)

    lag = 2 if section_count == 2 else 1
    if lag == 2:
        steps = turns + 1
    else:
        steps = turns

    def turn_at(step):
        if lag == 1:
            return jnp.int32(step)
        return jnp.clip(step - section_idx, 0, turns - 1)

    outputs = []
    handed = {}
    for step in range(steps):
        turn = turn_at(step)
        fresh = lax.dynamic_index_in_dim(incoming[0, :, 0], turn, 0, keepdims=False)
        current = lax.all_gather(fresh, "seq", axis=0, tiled=True)
        if step in handed:
            current = jnp.where((section_idx == 0) | (turn == 0), current, handed[step])
        batch_idx = turn - section_idx + section_count - 1
        contact_rows = lax.dynamic_index_in_dim(contact_all, batch_idx, 0, keepdims=False)
        key_flags = lax.dynamic_index_in_dim(key_all, batch_idx, 0, keepdims=False).astype(
            jnp.float32
        )
        timestep = lax.dynamic_index_in_dim(step_all, batch_idx, 0, keepdims=False).astype(
            jnp.float32
        )
        onehot = (contact_rows[:, None] == labels[None, :]).astype(jnp.bfloat16)
        hidden = current.astype(jnp.float32) + jnp.dot(
            onehot, table, preferred_element_type=jnp.float32
        )
        root_mean = jnp.sqrt(jnp.mean(hidden * hidden, axis=-1, keepdims=True) + epsilon)
        modulation = gain_row * (1.0 + 0.5 * jnp.sin(timestep * freq_row))
        normed = (hidden / root_mean * modulation[None, :]).astype(jnp.bfloat16)
        projected = jnp.dot(normed, weights, preferred_element_type=jnp.float32).astype(
            jnp.bfloat16
        )
        query_heads = projected[:, :q_cols].reshape(frames, heads_local, head_size)
        keyval_heads = projected[:, q_cols:].reshape(frames, kv_local, 2, head_size)
        head_outputs = []
        for head in range(heads_local):
            key_rows = keyval_heads[:, head // group_size, 0]
            value_rows = keyval_heads[:, head // group_size, 1]
            scores = (
                lax.dot_general(
                    query_heads[:, head],
                    key_rows,
                    (((1,), (1,)), ((), ())),
                    preferred_element_type=jnp.float32,
                )
                * score_scale
            )
            scores = scores + bias_local[head] * key_flags[None, :]
            row_max = jnp.max(scores, axis=-1, keepdims=True)
            exponent = jnp.exp(scores - row_max)
            probabilities = (exponent / jnp.sum(exponent, axis=-1, keepdims=True)).astype(
                jnp.bfloat16
            )
            head_outputs.append(
                jnp.dot(probabilities, value_rows, preferred_element_type=jnp.float32).astype(
                    jnp.bfloat16
                )
            )
        attended = jnp.concatenate(head_outputs, axis=1)
        hidden_local = lax.dynamic_slice_in_dim(current, seq_idx * q_cols, q_cols, 1).astype(
            jnp.float32
        ) + jnp.dot(onehot, table_local, preferred_element_type=jnp.float32)
        output = (hidden_local + gate_local[None, :] * attended.astype(jnp.float32)).astype(
            jnp.bfloat16
        )
        outputs.append(output)
        if step + lag < steps:
            piece = passed_along(output, "pipe", 1)
            handed[step + lag] = lax.all_gather(piece, "seq", axis=1, tiled=True)

    factor = float(turns * rep_count * frames) ** (-0.5)
    total = None
    rows_out = []
    for turn in range(turns):
        if lag == 2:
            own = jnp.where(section_idx == 0, outputs[turn], outputs[turn + 1])
        else:
            own = outputs[turn]
        term = lax.dot_general(
            own, cot_all[turn], (((0,), (0,)), ((), ())), preferred_element_type=jnp.float32
        )
        total = term if total is None else total + term
        rows_out.append(lax.all_to_all(own, "seq", split_axis=0, concat_axis=1, tiled=True))
    section_out = jnp.stack(rows_out)[None, :, None]
    grad_parts = lax.all_to_all(
        (total * factor).astype(jnp.bfloat16).reshape(rep_count, q_cols // rep_count, feat_count),
        "dp",
        split_axis=0,
        concat_axis=0,
        tiled=True,
    )
    grad_rows = jnp.sum(grad_parts.astype(jnp.float32), axis=0)
    return (section_out, grad_rows[None])


def solution(mesh):
    in_specs = (
        P("pipe", None, "dp", "seq", None),
        P(None, "dp", "seq"),
        P(None, "dp", None),
        P(None, "dp"),
        P("pipe", ("seq", "dp"), None),
        P("pipe", ("seq", "dp"), None),
        P("pipe", None),
        P("pipe", None),
        P("pipe", None, None),
        P("pipe", None),
        P("pipe", None),
        P("pipe", None, "dp", "seq", None),
    )
    out_specs = (P("pipe", None, "dp", "seq", None), P("pipe", ("seq", "dp"), None))
    return jax.shard_map(body, mesh=mesh, in_specs=in_specs, out_specs=out_specs, check_vma=False)
```

```python
import functools
import math

import jax
import jax.numpy as jnp
from jax import lax
from jax.experimental import pallas as pl
from jax.experimental.pallas import tpu as pltpu
from jax.sharding import PartitionSpec as P

epsilon = 1e-06


def passed_along(value, axis, steps):
    count = lax.axis_size(axis)
    first, last = (max(0, -steps), min(count, count - steps))
    return lax.ppermute(value, axis, [(source, source + steps) for source in range(first, last)])


def ring(value, axis):
    count = lax.axis_size(axis)
    return lax.ppermute(value, axis, [(source, (source + 1) % count) for source in range(count)])


def swap(value, bit):
    count = lax.axis_size("seq")
    return lax.ppermute(value, "seq", [(source, source ^ bit) for source in range(count)])


def offsets_of(count):
    offsets = [0]
    bit = count // 2
    while bit:
        offsets = offsets + [offset ^ bit for offset in offsets]
        bit //= 2
    return offsets


def gathered_pieces(value):
    pieces = [value]
    bit = lax.axis_size("seq") // 2
    while bit:
        pieces = pieces + [swap(piece, bit) for piece in pieces]
        bit //= 2
    return pieces


def pack_kernel(offsets, meta, wq, wkv, *outs):
    q_cols = outs[0].shape[1] // 2
    for offset, out in zip(offsets, outs):
        start = pl.multiple_of((meta[0] ^ offset) * q_cols, 128)
        out[:, :q_cols] = wq[0, :, pl.ds(start, q_cols)]
        out[:, q_cols:] = wkv[0, :, pl.ds(start, q_cols)]


def step_kernel(cfg, *refs):
    step, has_relay, has_prev, last = cfg["step"], cfg["has_relay"], cfg["has_prev"], cfg["last"]
    pieces, hops, head = cfg["pieces"], cfg["hops"], cfg["head"]
    heads, group = cfg["heads"], cfg["group"]
    refs = list(refs)

    def take(count):
        taken, refs[:count] = refs[:count], []
        return taken

    meta, bias, table, mod, gate, flags = take(6)
    prev = take(1)[0] if has_prev else None
    inc = take(pieces)
    side = take(pieces)
    chunks = take(2 * hops)
    relay = take(pieces) if has_relay else None
    out, grad = take(2)
    xs, cot, ids, w, normed, proj, att, sem_x, sem_c, sem_w = take(10)
    offsets = offsets_of(pieces)
    rows, width = xs.shape[1], xs.shape[2]
    cols = out.shape[2]
    w_rows = chunks[0].shape[1]
    frames = pieces * rows
    seq, rep = meta[0], meta[1]
    turn = meta[8 + step]

    def fresh_copies():
        return [
            pltpu.make_async_copy(inc[i].at[turn], xs.at[seq ^ offsets[i]], sem_x.at[i])
            for i in range(pieces)
        ]

    def relay_copies():
        return [
            pltpu.make_async_copy(
                relay[i],
                xs.at[:, :, pl.ds(pl.multiple_of((seq ^ offsets[i]) * cols, 128), cols)],
                sem_x.at[i],
            )
            for i in range(pieces)
        ]

    def either(act):
        if has_relay:
            relayed = meta[16 + step]

            @pl.when(relayed == 0)
            def _():
                for copy in fresh_copies():
                    act(copy)

            @pl.when(relayed != 0)
            def _():
                for copy in relay_copies():
                    act(copy)
        else:
            for copy in fresh_copies():
                act(copy)

    turns_rows = cfg["turns"] * rows
    side_copies = []
    for i in range(pieces):
        side_copies.append(
            pltpu.make_async_copy(
                side[i].at[pl.ds(turns_rows, 16)], ids.at[seq ^ offsets[i]], sem_c.at[i]
            )
        )
    cot_copies = []
    for i in range(pieces):
        cot_copies.append(
            pltpu.make_async_copy(
                side[i].at[pl.ds(pl.multiple_of(turn * rows, 128), rows)],
                cot.at[seq ^ offsets[i]],
                sem_c.at[pieces + i],
            )
        )
    w_copies = []
    for half in range(2):
        for hop in range(hops):
            owner = lax.rem(rep + hops - hop, hops)
            for j in range(pieces // 2):
                offset = half * (pieces // 2) + j
                block = (seq ^ offset) * hops + owner
                w_copies.append(
                    pltpu.make_async_copy(
                        chunks[half * hops + hop].at[j],
                        w.at[pl.ds(pl.multiple_of(block * w_rows, 16), w_rows)],
                        sem_w.at[len(w_copies)],
                    )
                )
    either(lambda copy: copy.start())
    for copy in side_copies + w_copies + cot_copies:
        copy.start()
    for copy in side_copies:
        copy.wait()
    either(lambda copy: copy.wait())

    def onehot_of(block):
        state = ids[block, step : step + 1, :rows].astype(jnp.float32).astype(jnp.int32)
        labels = lax.broadcasted_iota(jnp.int32, (table.shape[0], rows), 0)
        return jnp.where(labels == state, 1.0, 0.0).T.astype(jnp.bfloat16)

    mod_row = mod[step]
    for block in range(pieces):
        hidden = xs[block].astype(jnp.float32) + jnp.dot(
            onehot_of(block), table[...], preferred_element_type=jnp.float32
        )
        square = jnp.sum(hidden * hidden, axis=1, keepdims=True) * (1.0 / width)
        scale = lax.rsqrt(square + epsilon)
        normed[block] = (hidden * scale * mod_row).astype(jnp.bfloat16)
    for copy in w_copies:
        copy.wait()
    for block in range(pieces):
        proj[pl.ds(block * rows, rows), : 2 * cols] = jnp.dot(
            normed[block], w[...], preferred_element_type=jnp.float32
        ).astype(jnp.bfloat16)
    score_scale = head ** (-0.5) * math.log2(math.e)
    lanes = lax.broadcasted_iota(jnp.int32, (frames, 128), 1)
    flag_row = flags[step] * math.log2(math.e)
    for kv in range(heads // group):
        base = cols + kv * 2 * head
        keys = proj[:, base : base + head]
        values = proj[:, base + head : base + head + 128].astype(jnp.float32)
        values = jnp.where(lanes < head, values, jnp.where(lanes == head, 1.0, 0.0)).astype(
            jnp.bfloat16
        )
        for h in range(kv * group, (kv + 1) * group):
            bias_row = flag_row * bias[h]
            for block in range(pieces):
                queries = proj[block * rows : (block + 1) * rows, h * head : (h + 1) * head]
                scores = lax.dot_general(
                    queries, keys, (((1,), (1,)), ((), ())), preferred_element_type=jnp.float32
                )
                scores = scores * score_scale + bias_row
                top = jnp.max(scores, axis=1, keepdims=True)
                weight = jnp.exp2(scores - top).astype(jnp.bfloat16)
                mixed = jnp.dot(weight, values, preferred_element_type=jnp.float32)
                att[block, :, h * head : (h + 1) * head] = (
                    mixed[:, :head] / mixed[:, head : head + 1]
                )
    start = pl.multiple_of(seq * cols, 128)
    for block in range(pieces):
        hidden = xs[block, :, pl.ds(start, cols)].astype(jnp.float32) + jnp.dot(
            onehot_of(block), table[:, pl.ds(start, cols)], preferred_element_type=jnp.float32
        )
        attended = att[block].astype(jnp.bfloat16).astype(jnp.float32)
        out[block] = (hidden + gate[...] * attended).astype(jnp.bfloat16)
    for copy in cot_copies:
        copy.wait()
    total = lax.dot_general(
        out[...].reshape(frames, cols),
        cot[...].reshape(frames, cot.shape[2]),
        (((0,), (0,)), ((), ())),
        preferred_element_type=jnp.float32,
    )
    total = total * meta[24 + step].astype(jnp.float32)
    if has_prev:
        total = total + prev[...]
    if last:
        factor = float(cfg["turns"] * hops * frames) ** (-0.5)
        grad[...] = (total * factor).astype(jnp.bfloat16)
    else:
        grad[...] = total


def finish_kernel(early, late, parts, section_out, grad):
    count, turns_early, _, cols = early.shape
    for source in range(count):
        lanes = pl.ds(source * cols, cols)
        for turn in range(turns_early):
            section_out[turn, :, lanes] = early[source, turn]
        section_out[turns_early, :, lanes] = late[source]
    total = parts[0].astype(jnp.float32)
    for source in range(1, parts.shape[0]):
        total = total + parts[source].astype(jnp.float32)
    grad[...] = total


VMEM_LIMIT = 40 * 1024 * 1024


def paired_body(
    incoming,
    contacts,
    keyframes,
    timesteps,
    w_query,
    w_keyval,
    norm_gain,
    time_freq,
    contact_table,
    key_bias,
    attn_gate,
    head_cotangent,
):
    section_idx = lax.axis_index("pipe")
    seq_idx = lax.axis_index("seq")
    rep_idx = lax.axis_index("dp")
    seq_count = lax.axis_size("seq")
    hops = lax.axis_size("dp")
    rows, width, turns = incoming.shape[3], incoming.shape[4], incoming.shape[1]
    frames = rows * seq_count
    heads_all = key_bias.shape[1]
    head = width // heads_all
    heads = heads_all // seq_count
    kv_heads = w_keyval.shape[2] // (2 * head * seq_count)
    feats = head_cotangent.shape[4]
    cols = width // seq_count
    w_rows = w_query.shape[1]
    steps = turns + 1
    contact_states = contact_table.shape[1]

    step_ids = jnp.arange(8, dtype=jnp.int32)
    turn_ids = jnp.clip(step_ids - section_idx, 0, turns - 1)
    batch_ids = (turn_ids - section_idx + 1)[:steps]
    meta = jnp.concatenate(
        [
            jnp.stack([seq_idx, rep_idx] + [jnp.int32(0)] * 6).astype(jnp.int32),
            turn_ids,
            jnp.where((section_idx > 0) & (turn_ids > 0), 1, 0).astype(jnp.int32),
            jnp.where((step_ids >= section_idx) & (step_ids < turns + section_idx), 1, 0).astype(
                jnp.int32
            ),
        ]
    )

    smem = pl.BlockSpec(memory_space=pltpu.SMEM)
    vmem = pl.BlockSpec(memory_space=pltpu.VMEM)
    anywhere = pl.BlockSpec(memory_space=pl.ANY)
    parts = pl.pallas_call(
        functools.partial(pack_kernel, range(seq_count)),
        out_shape=[jax.ShapeDtypeStruct((w_rows, 2 * cols), jnp.bfloat16)] * seq_count,
        in_specs=[smem, vmem, vmem],
        out_specs=[vmem] * seq_count,
        name="pack",
    )(meta, w_query, w_keyval)
    arrived = [parts[0]] + [
        lax.ppermute(parts[m], "seq", [(i, i ^ m) for i in range(seq_count)])
        for m in range(1, seq_count)
    ]
    half = seq_count // 2
    rings = [jnp.stack(arrived[:half]), jnp.stack(arrived[half:])]
    chunks = [[rings[0]], [rings[1]]]
    for hop in range(1, hops):
        for which in range(2):
            chunks[which].append(ring(chunks[which][-1], "dp"))

    contact_steps = jnp.take(contacts[:, 0, :], batch_ids, axis=0).astype(jnp.bfloat16)
    side = jnp.concatenate(
        [
            head_cotangent[0, :, 0].reshape(turns * rows, feats),
            jnp.pad(contact_steps, ((0, 16 - steps), (0, feats - rows))),
        ]
    )
    side_pieces = gathered_pieces(side)
    fresh_pieces = gathered_pieces(incoming[0, :, 0])

    flag_steps = jnp.take(keyframes[:, 0, :], batch_ids, axis=0).astype(jnp.float32)[:, None, :]
    time_steps = jnp.take(timesteps[:, 0], batch_ids, axis=0).astype(jnp.float32)
    mod_steps = (
        norm_gain[0][None] * (1.0 + 0.5 * jnp.sin(time_steps[:, None] * time_freq[0][None]))
    )[:, None, :]
    gate_local = lax.dynamic_slice_in_dim(attn_gate[0], seq_idx * cols, cols)[None]
    bias_local = lax.dynamic_slice_in_dim(key_bias[0], seq_idx * heads, heads)

    outputs = []
    relayed = {}
    grad = None
    for step in range(steps):
        last = step + 1 == steps
        cfg = {
            "step": step,
            "has_relay": step in relayed,
            "has_prev": grad is not None,
            "last": last,
            "pieces": seq_count,
            "hops": hops,
            "head": head,
            "heads": heads,
            "group": heads // kv_heads,
            "turns": turns,
        }
        operands = [meta, bias_local, contact_table[0], mod_steps, gate_local, flag_steps]
        specs = [smem, smem, vmem, vmem, vmem, vmem]
        if grad is not None:
            operands.append(grad)
            specs.append(vmem)
        loose = fresh_pieces + side_pieces + chunks[0] + chunks[1] + relayed.get(step, [])
        operands += loose
        specs += [anywhere] * len(loose)
        output, grad = pl.pallas_call(
            functools.partial(step_kernel, cfg),
            out_shape=[
                jax.ShapeDtypeStruct((seq_count, rows, cols), jnp.bfloat16),
                jax.ShapeDtypeStruct((cols, feats), jnp.bfloat16 if last else jnp.float32),
            ],
            in_specs=specs,
            out_specs=[vmem, vmem],
            scratch_shapes=[
                pltpu.VMEM((seq_count, rows, width), jnp.bfloat16),
                pltpu.VMEM((seq_count, rows, feats), jnp.bfloat16),
                pltpu.VMEM((seq_count, 16, feats), jnp.bfloat16),
                pltpu.VMEM((width, 2 * cols), jnp.bfloat16),
                pltpu.VMEM((seq_count, rows, width), jnp.bfloat16),
                pltpu.VMEM((frames, 2 * cols + 128), jnp.bfloat16),
                pltpu.VMEM((seq_count, rows, cols), jnp.float32),
                pltpu.SemaphoreType.DMA((seq_count,)),
                pltpu.SemaphoreType.DMA((2 * seq_count,)),
                pltpu.SemaphoreType.DMA((seq_count * hops,)),
            ],
            compiler_params=pltpu.CompilerParams(vmem_limit_bytes=VMEM_LIMIT),
            cost_estimate=pl.CostEstimate(
                flops=2 * frames * width * 2 * cols + 4 * heads * frames * frames * head,
                bytes_accessed=6 * frames * width,
                transcendentals=heads * frames * frames,
            ),
            name="step%d" % step,
        )(*operands)
        outputs.append(output)
        if step + 2 < steps:
            relayed[step + 2] = gathered_pieces(passed_along(output, "pipe", 1))

    first_section = section_idx == 0
    own = [jnp.where(first_section, outputs[t], outputs[t + 1]) for t in range(turns)]
    early = lax.all_to_all(
        jnp.stack(own[:-1], axis=1), "seq", split_axis=0, concat_axis=0, tiled=True
    )
    late = lax.all_to_all(own[-1], "seq", split_axis=0, concat_axis=0, tiled=True)
    grad_parts = lax.all_to_all(
        grad.reshape(hops, cols // hops, feats), "dp", split_axis=0, concat_axis=0, tiled=True
    )
    section_out, grad_rows = pl.pallas_call(
        finish_kernel,
        out_shape=[
            jax.ShapeDtypeStruct((turns, rows, width), jnp.bfloat16),
            jax.ShapeDtypeStruct((cols // hops, feats), jnp.float32),
        ],
        in_specs=[vmem] * 3,
        out_specs=[vmem] * 2,
        name="finish",
    )(early, late, grad_parts)
    return (section_out[None, :, None], grad_rows[None])


def body(incoming, contacts, keyframes, timesteps, w_query, *others):
    count = lax.axis_size("seq")
    cols = w_query.shape[2] // count
    paired = (
        lax.axis_size("pipe") == 2
        and count in (2, 4, 8)
        and cols % 128 == 0
        and w_query.shape[1] % 16 == 0
        and incoming.shape[3] == 128
        and incoming.shape[1] < 8
    )
    chosen = paired_body if paired else general_body
    return chosen(incoming, contacts, keyframes, timesteps, w_query, *others)


def general_body(
    incoming,
    contacts,
    keyframes,
    timesteps,
    w_query,
    w_keyval,
    norm_gain,
    time_freq,
    contact_table,
    key_bias,
    attn_gate,
    head_cotangent,
):
    section_idx = lax.axis_index("pipe")
    seq_idx = lax.axis_index("seq")
    rep_idx = lax.axis_index("dp")
    seq_count = lax.axis_size("seq")
    section_count = lax.axis_size("pipe")
    rep_count = lax.axis_size("dp")
    tok_rows = incoming.shape[3]
    width = incoming.shape[4]
    turns = incoming.shape[1]
    frames = tok_rows * seq_count
    heads_all = key_bias.shape[1]
    head_size = width // heads_all
    heads_local = heads_all // seq_count
    kv_width = w_keyval.shape[2]
    kv_local = kv_width // (2 * head_size * seq_count)
    group_size = heads_local // kv_local
    feat_count = head_cotangent.shape[4]
    score_scale = head_size ** (-0.5)
    q_cols = width // seq_count
    kv_cols = kv_width // seq_count
    w_rows = w_query.shape[1]

    w_parts = jnp.concatenate(
        [
            w_query[0].reshape(w_rows, seq_count, q_cols),
            w_keyval[0].reshape(w_rows, seq_count, kv_cols),
        ],
        axis=2,
    ).transpose(1, 0, 2)
    block = lax.all_to_all(w_parts, "seq", split_axis=0, concat_axis=0, tiled=True)
    weights = jnp.zeros((seq_count, rep_count, w_rows, q_cols + kv_cols), jnp.bfloat16)
    for hop in range(rep_count):
        owner = lax.rem(rep_idx + rep_count - hop, rep_count)
        weights = lax.dynamic_update_slice_in_dim(weights, block[:, None], owner, 1)
        if hop + 1 < rep_count:
            block = ring(block, "dp")
    weights = weights.reshape(width, q_cols + kv_cols)

    gain_row = norm_gain[0]
    freq_row = time_freq[0]
    table = contact_table[0]
    gate_local = lax.dynamic_slice_in_dim(attn_gate[0], seq_idx * q_cols, q_cols)
    table_local = lax.dynamic_slice_in_dim(table, seq_idx * q_cols, q_cols, 1)
    bias_local = lax.dynamic_slice_in_dim(key_bias[0], seq_idx * heads_local, heads_local)
    contact_all = lax.all_gather(contacts[:, 0, :], "seq", axis=1, tiled=True)
    key_all = keyframes[:, 0, :]
    step_all = timesteps[:, 0]
    labels = jnp.arange(table.shape[0], dtype=jnp.int32)
    cot_all = lax.all_gather(head_cotangent[0, :, 0], "seq", axis=1, tiled=True)

    lag = 2 if section_count == 2 else 1
    if lag == 2:
        steps = turns + 1
    else:
        steps = turns

    def turn_at(step):
        if lag == 1:
            return jnp.int32(step)
        return jnp.clip(step - section_idx, 0, turns - 1)

    outputs = []
    handed = {}
    for step in range(steps):
        turn = turn_at(step)
        fresh = lax.dynamic_index_in_dim(incoming[0, :, 0], turn, 0, keepdims=False)
        current = lax.all_gather(fresh, "seq", axis=0, tiled=True)
        if step in handed:
            current = jnp.where((section_idx == 0) | (turn == 0), current, handed[step])
        batch_idx = turn - section_idx + section_count - 1
        contact_rows = lax.dynamic_index_in_dim(contact_all, batch_idx, 0, keepdims=False)
        key_flags = lax.dynamic_index_in_dim(key_all, batch_idx, 0, keepdims=False).astype(
            jnp.float32
        )
        timestep = lax.dynamic_index_in_dim(step_all, batch_idx, 0, keepdims=False).astype(
            jnp.float32
        )
        onehot = (contact_rows[:, None] == labels[None, :]).astype(jnp.bfloat16)
        hidden = current.astype(jnp.float32) + jnp.dot(
            onehot, table, preferred_element_type=jnp.float32
        )
        root_mean = jnp.sqrt(jnp.mean(hidden * hidden, axis=-1, keepdims=True) + epsilon)
        modulation = gain_row * (1.0 + 0.5 * jnp.sin(timestep * freq_row))
        normed = (hidden / root_mean * modulation[None, :]).astype(jnp.bfloat16)
        projected = jnp.dot(normed, weights, preferred_element_type=jnp.float32).astype(
            jnp.bfloat16
        )
        query_heads = projected[:, :q_cols].reshape(frames, heads_local, head_size)
        keyval_heads = projected[:, q_cols:].reshape(frames, kv_local, 2, head_size)
        head_outputs = []
        for head in range(heads_local):
            key_rows = keyval_heads[:, head // group_size, 0]
            value_rows = keyval_heads[:, head // group_size, 1]
            scores = (
                lax.dot_general(
                    query_heads[:, head],
                    key_rows,
                    (((1,), (1,)), ((), ())),
                    preferred_element_type=jnp.float32,
                )
                * score_scale
            )
            scores = scores + bias_local[head] * key_flags[None, :]
            row_max = jnp.max(scores, axis=-1, keepdims=True)
            exponent = jnp.exp(scores - row_max)
            probabilities = (exponent / jnp.sum(exponent, axis=-1, keepdims=True)).astype(
                jnp.bfloat16
            )
            head_outputs.append(
                jnp.dot(probabilities, value_rows, preferred_element_type=jnp.float32).astype(
                    jnp.bfloat16
                )
            )
        attended = jnp.concatenate(head_outputs, axis=1)
        hidden_local = lax.dynamic_slice_in_dim(current, seq_idx * q_cols, q_cols, 1).astype(
            jnp.float32
        ) + jnp.dot(onehot, table_local, preferred_element_type=jnp.float32)
        output = (hidden_local + gate_local[None, :] * attended.astype(jnp.float32)).astype(
            jnp.bfloat16
        )
        outputs.append(output)
        if step + lag < steps:
            piece = passed_along(output, "pipe", 1)
            handed[step + lag] = lax.all_gather(piece, "seq", axis=1, tiled=True)

    factor = float(turns * rep_count * frames) ** (-0.5)
    total = None
    rows_out = []
    for turn in range(turns):
        if lag == 2:
            own = jnp.where(section_idx == 0, outputs[turn], outputs[turn + 1])
        else:
            own = outputs[turn]
        term = lax.dot_general(
            own, cot_all[turn], (((0,), (0,)), ((), ())), preferred_element_type=jnp.float32
        )
        total = term if total is None else total + term
        rows_out.append(lax.all_to_all(own, "seq", split_axis=0, concat_axis=1, tiled=True))
    section_out = jnp.stack(rows_out)[None, :, None]
    grad_parts = lax.all_to_all(
        (total * factor).astype(jnp.bfloat16).reshape(rep_count, q_cols // rep_count, feat_count),
        "dp",
        split_axis=0,
        concat_axis=0,
        tiled=True,
    )
    grad_rows = jnp.sum(grad_parts.astype(jnp.float32), axis=0)
    return (section_out, grad_rows[None])


def solution(mesh):
    in_specs = (
        P("pipe", None, "dp", "seq", None),
        P(None, "dp", "seq"),
        P(None, "dp", None),
        P(None, "dp"),
        P("pipe", ("seq", "dp"), None),
        P("pipe", ("seq", "dp"), None),
        P("pipe", None),
        P("pipe", None),
        P("pipe", None, None),
        P("pipe", None),
        P("pipe", None),
        P("pipe", None, "dp", "seq", None),
    )
    out_specs = (P("pipe", None, "dp", "seq", None), P("pipe", ("seq", "dp"), None))
    return jax.shard_map(body, mesh=mesh, in_specs=in_specs, out_specs=out_specs, check_vma=False)
```

```python
import functools
import math

import jax
import jax.numpy as jnp
from jax import lax
from jax.experimental import pallas as pl
from jax.experimental.pallas import tpu as pltpu
from jax.sharding import PartitionSpec as P

epsilon = 1e-06


def passed_along(value, axis, steps):
    count = lax.axis_size(axis)
    first, last = (max(0, -steps), min(count, count - steps))
    return lax.ppermute(value, axis, [(source, source + steps) for source in range(first, last)])


def ring(value, axis):
    count = lax.axis_size(axis)
    return lax.ppermute(value, axis, [(source, (source + 1) % count) for source in range(count)])


def swap(value, bit):
    count = lax.axis_size("seq")
    return lax.ppermute(value, "seq", [(source, source ^ bit) for source in range(count)])


def shifted(value, axis, shift):
    count = lax.axis_size(axis)
    return lax.ppermute(value, axis, [(source, (source + shift) % count) for source in range(count)])


def offsets_of(count):
    offsets = [0]
    bit = count // 2
    while bit:
        offsets = offsets + [offset ^ bit for offset in offsets]
        bit //= 2
    return offsets


def gathered_pieces(value):
    pieces = [value]
    bit = lax.axis_size("seq") // 2
    while bit:
        pieces = pieces + [swap(piece, bit) for piece in pieces]
        bit //= 2
    return pieces


def turn_and_batch(step, turns):
    section = lax.axis_index("pipe")
    turn = jnp.clip(step - section, 0, turns - 1)
    return turn, turn - section + 1


def pack_kernel(wq, wkv, *outs):
    cols = outs[0].shape[1] // 2
    seq = lax.axis_index("seq")
    for m, out in enumerate(outs):
        start = pl.multiple_of((seq ^ m) * cols, 128)
        out[:, :cols] = wq[0, :, pl.ds(start, cols)]
        out[:, cols:] = wkv[0, :, pl.ds(start, cols)]


def prep_kernel(turns, *refs):
    incoming, contacts, cotangent, first, second, states = refs[-6:]
    steps = turns + 1
    rows, feats = cotangent.shape[3:]
    base = (turns - 2) * rows
    for turn in range(turns):
        if turn < 2:
            first[turn] = incoming[0, turn, 0]
        else:
            second[(turn - 2) * rows : (turn - 1) * rows] = incoming[0, turn, 0]
        second[base : base + rows, turn * feats : (turn + 1) * feats] = cotangent[0, turn, 0]
    states[...] = jnp.zeros_like(states)
    for step in range(steps):
        _, batch = turn_and_batch(step, turns)
        states[step : step + 1, :rows] = contacts[batch].astype(jnp.float32)
    second[base + rows :, : states.shape[1]] = states[...].astype(jnp.bfloat16)


def step_kernel(cfg, *refs):
    step, has_relay, has_prev, last = cfg["step"], cfg["has_relay"], cfg["has_prev"], cfg["last"]
    pieces, hops, head, turns = cfg["pieces"], cfg["hops"], cfg["head"], cfg["turns"]
    heads, group, halves = cfg["heads"], cfg["group"], cfg["halves"]
    refs = list(refs)

    def take(count):
        taken, refs[:count] = refs[:count], []
        return taken

    bias, times, table, gain, freq, gate, flags = take(7)
    prev = take(1)[0] if has_prev else None
    first, second = take(pieces), take(pieces)
    chunks = take(pieces * hops)
    relay = take(pieces * halves) if has_relay else None
    before = take(halves) if last else None
    if last:
        take(pieces)
        late = take(pieces)
        own_grad = take(1)[0]
        grads = take(hops - 1)
    else:
        outs = take(halves)
        grad = take(1)[0]
    xs, cot, ids, w, scaled, proj, att, keep, total, sem_x, sem_c, sem_w, sem_k = take(13)
    offsets = offsets_of(pieces)
    rows, width = xs.shape[1], xs.shape[2]
    cols = att.shape[1]
    feats = cot.shape[2]
    w_rows = chunks[0].shape[0]
    frames = pieces * rows
    part = pieces // halves
    seq, rep, section = lax.axis_index("seq"), lax.axis_index("dp"), lax.axis_index("pipe")
    turn, batch = turn_and_batch(step, turns)
    base = (turns - 2) * rows

    def copy_of(source, target, sems, index):
        return pltpu.make_async_copy(source, target, sems.at[index])

    fresh = []
    for i in range(pieces):
        target = xs.at[seq ^ offsets[i]]
        if step < 2:
            source = first[i].at[jnp.minimum(turn, 1)]
        else:
            at = pl.multiple_of(jnp.clip(turn - 2, 0, turns - 3) * rows, 128)
            source = second[i].at[pl.ds(at, rows)]
        fresh.append(copy_of(source, target, sem_x, i * halves))
    arrived = []
    if has_relay:
        for i in range(pieces):
            lanes = pl.ds(pl.multiple_of((seq ^ offsets[i]) * cols, 128), cols)
            for k in range(halves):
                arrived.append(
                    copy_of(
                        relay[k * pieces + i],
                        xs.at[pl.ds(k * part, part), :, lanes],
                        sem_x,
                        i * halves + k,
                    )
                )

    def current(act):
        if has_relay:

            @pl.when(section == 0)
            def _():
                for copy in fresh:
                    act(copy)

            @pl.when(section != 0)
            def _():
                for copy in arrived:
                    act(copy)
        else:
            for copy in fresh:
                act(copy)

    state_copies, cot_copies, w_copies, keep_copies = [], [], [], []
    for i in range(pieces):
        state_copies.append(
            copy_of(
                second[i].at[pl.ds(base + rows, 16), pl.ds(0, 128)],
                ids.at[seq ^ offsets[i]],
                sem_c,
                i,
            )
        )
        cot_copies.append(
            copy_of(
                second[i].at[pl.ds(base, rows), pl.ds(pl.multiple_of(turn * feats, 128), feats)],
                cot.at[seq ^ offsets[i]],
                sem_c,
                pieces + i,
            )
        )
    for m in range(pieces):
        for hop in range(hops):
            block = (seq ^ m) * hops + lax.rem(rep + hops - hop, hops)
            w_copies.append(
                copy_of(
                    chunks[m * hops + hop],
                    w.at[pl.ds(pl.multiple_of(block * w_rows, 16), w_rows)],
                    sem_w,
                    m * hops + hop,
                )
            )
    if last:
        for k in range(halves):
            keep_copies.append(copy_of(before[k], keep.at[pl.ds(k * part, part)], sem_k, k))
    for copy in state_copies:
        copy.start()
    current(lambda copy: copy.start())
    for copy in w_copies + cot_copies + keep_copies:
        copy.start()
    for copy in state_copies:
        copy.wait()
    current(lambda copy: copy.wait())

    labels = lax.broadcasted_iota(jnp.int32, (table.shape[1], rows), 0)
    onehots = []
    for block in range(pieces):
        state = ids[block, step : step + 1, :].astype(jnp.float32).astype(jnp.int32)
        onehots.append(jnp.where(labels == state, 1.0, 0.0).T.astype(jnp.bfloat16))
    onehot = jnp.concatenate(onehots, axis=0)
    time = times[batch, 0].astype(jnp.float32)
    mod = gain[...] * (1.0 + 0.5 * jnp.sin(time * freq[...]))
    tile = 256
    square = jnp.zeros((frames, 128), jnp.float32)
    for at in range(0, width, tile):
        hidden = xs[:, :, at : at + tile].reshape(frames, tile).astype(jnp.float32) + jnp.dot(
            onehot, table[0, :, at : at + tile], preferred_element_type=jnp.float32
        )
        for lane in range(0, tile, 128):
            piece = hidden[:, lane : lane + 128]
            square = square + piece * piece
        scaled[:, at : at + tile] = (hidden * mod[:, at : at + tile]).astype(jnp.bfloat16)
    scale = lax.rsqrt(jnp.sum(square, axis=1, keepdims=True) * (1.0 / width) + epsilon)
    for copy in w_copies:
        copy.wait()
    for at in range(0, 2 * cols, tile):
        proj[:, at : at + tile] = (
            jnp.dot(scaled[...], w[:, at : at + tile], preferred_element_type=jnp.float32) * scale
        ).astype(jnp.bfloat16)
    score_scale = head ** (-0.5) * math.log2(math.e)
    lanes = lax.broadcasted_iota(jnp.int32, (frames, 128), 1)
    flag_row = flags[batch].astype(jnp.float32) * math.log2(math.e)
    for kv in range(heads // group):
        base = cols + kv * 2 * head
        keys = proj[:, base : base + head]
        values = proj[:, base + head : base + head + 128].astype(jnp.float32)
        values = jnp.where(lanes < head, values, jnp.where(lanes == head, 1.0, 0.0)).astype(
            jnp.bfloat16
        )
        for h in range(kv * group, (kv + 1) * group):
            queries = proj[:, h * head : (h + 1) * head]
            scores = lax.dot_general(
                queries, keys, (((1,), (1,)), ((), ())), preferred_element_type=jnp.float32
            )
            scores = scores * score_scale + flag_row * bias[0, seq * heads + h]
            top = jnp.max(scores, axis=1, keepdims=True)
            weight = jnp.exp2(scores - top).astype(jnp.bfloat16)
            mixed = jnp.dot(weight, values, preferred_element_type=jnp.float32)
            att[:, h * head : (h + 1) * head] = mixed[:, :head] / mixed[:, head : head + 1]
    own = pl.ds(pl.multiple_of(seq * cols, 128), cols)
    hidden = xs[:, :, own].reshape(frames, cols).astype(jnp.float32) + jnp.dot(
        onehot, table[0, :, own], preferred_element_type=jnp.float32
    )
    attended = att[...].astype(jnp.bfloat16).astype(jnp.float32)
    output = (hidden + gate[:, own] * attended).astype(jnp.bfloat16)
    for copy in cot_copies:
        copy.wait()
    share = lax.dot_general(
        output,
        cot[...].reshape(frames, feats),
        (((0,), (0,)), ((), ())),
        preferred_element_type=jnp.float32,
    )
    valid = jnp.logical_and(step >= section, step < turns + section)
    share = jnp.where(valid, share, 0.0)
    if has_prev:
        share = share + prev[...]
    blocks = output.reshape(pieces, rows, cols)
    if not last:
        for k in range(halves):
            outs[k][...] = blocks[k * part : (k + 1) * part]
        grad[...] = share
        return
    for copy in keep_copies:
        copy.wait()

    @pl.when(section != 0)
    def _():
        keep[...] = blocks

    for m in range(pieces):
        late[m][...] = keep[seq ^ m]
    total[...] = share * float(turns * hops * frames) ** (-0.5)
    g_rows = cols // hops
    own_grad[...] = total[pl.ds(pl.multiple_of(rep * g_rows, 8), g_rows)]
    for shift in range(1, hops):
        at = pl.multiple_of(lax.rem(rep + shift, hops) * g_rows, 8)
        grads[shift - 1][...] = total[pl.ds(at, g_rows)].astype(jnp.bfloat16)


def early_kernel(turns, pieces, halves, *refs):
    outs, sends = refs[: turns * halves], refs[turns * halves : turns * halves + pieces]
    keep, sems = refs[turns * halves + pieces :]
    section, seq = lax.axis_index("pipe"), lax.axis_index("seq")
    part = pieces // halves

    def copies(skew):
        return [
            pltpu.make_async_copy(
                outs[(turn + skew) * halves + k],
                keep.at[turn, pl.ds(k * part, part)],
                sems.at[turn * halves + k],
            )
            for turn in range(turns - 1)
            for k in range(halves)
        ]

    @pl.when(section == 0)
    def _():
        for copy in copies(0):
            copy.start()
        for copy in copies(0):
            copy.wait()

    @pl.when(section != 0)
    def _():
        for copy in copies(1):
            copy.start()
        for copy in copies(1):
            copy.wait()

    for m in range(pieces):
        for turn in range(turns - 1):
            sends[m][turn] = keep[turn, seq ^ m]


def finish_kernel(pieces, hops, *refs):
    early, late, refs = refs[:pieces], refs[pieces : 2 * pieces], refs[2 * pieces :]
    own_grad, parts, (section_out, grad) = refs[0], refs[1:hops], refs[hops:]
    seq = lax.axis_index("seq")
    turns_early, _, cols = early[0].shape
    for m in range(pieces):
        lanes = pl.ds(pl.multiple_of((seq ^ m) * cols, 128), cols)
        for turn in range(turns_early):
            section_out[turn, :, lanes] = early[m][turn]
        section_out[turns_early, :, lanes] = late[m][...]
    total = own_grad[...]
    for part in parts:
        total = total + part[...].astype(jnp.float32)
    grad[...] = total


VMEM_LIMIT = 40 * 1024 * 1024
HALVES = 2


def paired_body(
    incoming,
    contacts,
    keyframes,
    timesteps,
    w_query,
    w_keyval,
    norm_gain,
    time_freq,
    contact_table,
    key_bias,
    attn_gate,
    head_cotangent,
):
    seq_count = lax.axis_size("seq")
    hops = lax.axis_size("dp")
    rows, width, turns = incoming.shape[3], incoming.shape[4], incoming.shape[1]
    frames = rows * seq_count
    heads_all = key_bias.shape[1]
    head = width // heads_all
    heads = heads_all // seq_count
    kv_heads = w_keyval.shape[2] // (2 * head * seq_count)
    feats = head_cotangent.shape[4]
    cols = width // seq_count
    w_rows = w_query.shape[1]
    steps = turns + 1
    part = seq_count // HALVES
    kind = jnp.bfloat16
    smem = pl.BlockSpec(memory_space=pltpu.SMEM)
    vmem = pl.BlockSpec(memory_space=pltpu.VMEM)
    hbm = pl.BlockSpec(memory_space=pltpu.HBM)
    params = pltpu.CompilerParams(vmem_limit_bytes=VMEM_LIMIT)
    shape = jax.ShapeDtypeStruct

    packed = pl.pallas_call(
        pack_kernel,
        out_shape=[shape((w_rows, 2 * cols), kind)] * seq_count,
        in_specs=[vmem, vmem],
        out_specs=[vmem] * seq_count,
        name="pack",
    )(w_query, w_keyval)
    blocks = [packed[0]] + [swap(packed[m], m) for m in range(1, seq_count)]
    chunks = [[block] for block in blocks]
    for hop in range(1, hops):
        for m in range(seq_count):
            chunks[m].append(shifted(chunks[m][-1], "dp", 1))

    waits = blocks[seq_count // 2 :] + [ring[1] for ring in chunks[: seq_count // 2]]
    first, second = pl.pallas_call(
        functools.partial(prep_kernel, turns),
        out_shape=[
            shape((2, rows, width), kind),
            shape(((turns - 1) * rows + 16, width), kind),
        ],
        in_specs=[hbm] * len(waits) + [vmem] * 3,
        out_specs=[vmem] * 2,
        scratch_shapes=[pltpu.VMEM((16, 128), jnp.float32)],
        compiler_params=params,
        name="prep",
    )(*waits, incoming, contacts, head_cotangent)
    loose = gathered_pieces(first) + gathered_pieces(second)
    loose = loose + [chunk for ring in chunks for chunk in ring]

    outputs = []
    relayed = {}
    grad = None
    for step in range(steps):
        last = step + 1 == steps
        cfg = {
            "step": step,
            "has_relay": step in relayed,
            "has_prev": grad is not None,
            "last": last,
            "pieces": seq_count,
            "hops": hops,
            "head": head,
            "heads": heads,
            "group": heads // kv_heads,
            "turns": turns,
            "halves": HALVES,
        }
        operands = [key_bias, timesteps, contact_table, norm_gain, time_freq, attn_gate, keyframes]
        specs = [smem, smem] + [vmem] * 5
        if grad is not None:
            operands.append(grad)
            specs.append(vmem)
        pieces = loose + relayed.get(step, [])
        if last:
            early = pl.pallas_call(
                functools.partial(early_kernel, turns, seq_count, HALVES),
                out_shape=[shape((turns - 1, rows, cols), kind)] * seq_count,
                in_specs=[hbm] * (turns * HALVES),
                out_specs=[vmem] * seq_count,
                scratch_shapes=[
                    pltpu.VMEM((turns - 1, seq_count, rows, cols), kind),
                    pltpu.SemaphoreType.DMA(((turns - 1) * HALVES,)),
                ],
                compiler_params=params,
                name="early",
            )(*[half for output in outputs for half in output])
            pieces = pieces + list(outputs[-1]) + list(early)
        if last:
            out_shape = [shape((rows, cols), kind)] * seq_count
            out_shape += [shape((cols // hops, feats), jnp.float32)]
            out_shape += [shape((cols // hops, feats), kind)] * (hops - 1)
        else:
            out_shape = [shape((part, rows, cols), kind)] * HALVES
            out_shape += [shape((cols, feats), jnp.float32)]
        results = pl.pallas_call(
            functools.partial(step_kernel, cfg),
            out_shape=out_shape,
            in_specs=specs + [hbm] * len(pieces),
            out_specs=[vmem] * len(out_shape),
            scratch_shapes=[
                pltpu.VMEM((seq_count, rows, width), kind),
                pltpu.VMEM((seq_count, rows, feats), kind),
                pltpu.VMEM((seq_count, 16, 128), kind),
                pltpu.VMEM((width, 2 * cols), kind),
                pltpu.VMEM((frames, width), kind),
                pltpu.VMEM((frames, 2 * cols + 128), kind),
                pltpu.VMEM((frames, cols), jnp.float32),
                pltpu.VMEM((seq_count, rows, cols), kind),
                pltpu.VMEM((cols, feats), jnp.float32),
                pltpu.SemaphoreType.DMA((seq_count * HALVES,)),
                pltpu.SemaphoreType.DMA((2 * seq_count,)),
                pltpu.SemaphoreType.DMA((seq_count * hops,)),
                pltpu.SemaphoreType.DMA((HALVES,)),
            ],
            compiler_params=params,
            cost_estimate=pl.CostEstimate(
                flops=2 * frames * width * 2 * cols + 4 * heads * frames * frames * head,
                bytes_accessed=6 * frames * width,
                transcendentals=heads * frames * frames,
            ),
            name="step%d" % step,
        )(*operands, *pieces)
        results = list(results)
        if last:
            break
        outputs.append(results[:HALVES])
        grad = results[HALVES]
        if step + 2 < steps:
            relayed[step + 2] = [
                piece
                for half in outputs[-1]
                for piece in gathered_pieces(passed_along(half, "pipe", 1))
            ]

    early = [early[0]] + [swap(early[m], m) for m in range(1, seq_count)]
    late = results[:seq_count]
    late = [late[0]] + [swap(late[m], m) for m in range(1, seq_count)]
    grads = results[seq_count:]
    grads = [grads[0]] + [shifted(grads[k], "dp", k) for k in range(1, hops)]
    section_out, grad_rows = pl.pallas_call(
        functools.partial(finish_kernel, seq_count, hops),
        out_shape=[
            shape((turns, rows, width), kind),
            shape((cols // hops, feats), jnp.float32),
        ],
        in_specs=[vmem] * (2 * seq_count + hops),
        out_specs=[vmem] * 2,
        compiler_params=params,
        name="finish",
    )(*early, *late, *grads)
    return (section_out[None, :, None], grad_rows[None])


def body(incoming, contacts, keyframes, timesteps, w_query, *others):
    count = lax.axis_size("seq")
    cols = w_query.shape[2] // count
    paired = (
        lax.axis_size("pipe") == 2
        and count in (2, 4, 8)
        and cols % 128 == 0
        and w_query.shape[1] % 16 == 0
        and incoming.shape[3] == 128
        and incoming.shape[1] < 8
    )
    chosen = paired_body if paired else general_body
    return chosen(incoming, contacts, keyframes, timesteps, w_query, *others)


def general_body(
    incoming,
    contacts,
    keyframes,
    timesteps,
    w_query,
    w_keyval,
    norm_gain,
    time_freq,
    contact_table,
    key_bias,
    attn_gate,
    head_cotangent,
):
    section_idx = lax.axis_index("pipe")
    seq_idx = lax.axis_index("seq")
    rep_idx = lax.axis_index("dp")
    seq_count = lax.axis_size("seq")
    section_count = lax.axis_size("pipe")
    rep_count = lax.axis_size("dp")
    tok_rows = incoming.shape[3]
    width = incoming.shape[4]
    turns = incoming.shape[1]
    frames = tok_rows * seq_count
    heads_all = key_bias.shape[1]
    head_size = width // heads_all
    heads_local = heads_all // seq_count
    kv_width = w_keyval.shape[2]
    kv_local = kv_width // (2 * head_size * seq_count)
    group_size = heads_local // kv_local
    feat_count = head_cotangent.shape[4]
    score_scale = head_size ** (-0.5)
    q_cols = width // seq_count
    kv_cols = kv_width // seq_count
    w_rows = w_query.shape[1]

    w_parts = jnp.concatenate(
        [
            w_query[0].reshape(w_rows, seq_count, q_cols),
            w_keyval[0].reshape(w_rows, seq_count, kv_cols),
        ],
        axis=2,
    ).transpose(1, 0, 2)
    block = lax.all_to_all(w_parts, "seq", split_axis=0, concat_axis=0, tiled=True)
    weights = jnp.zeros((seq_count, rep_count, w_rows, q_cols + kv_cols), jnp.bfloat16)
    for hop in range(rep_count):
        owner = lax.rem(rep_idx + rep_count - hop, rep_count)
        weights = lax.dynamic_update_slice_in_dim(weights, block[:, None], owner, 1)
        if hop + 1 < rep_count:
            block = ring(block, "dp")
    weights = weights.reshape(width, q_cols + kv_cols)

    gain_row = norm_gain[0]
    freq_row = time_freq[0]
    table = contact_table[0]
    gate_local = lax.dynamic_slice_in_dim(attn_gate[0], seq_idx * q_cols, q_cols)
    table_local = lax.dynamic_slice_in_dim(table, seq_idx * q_cols, q_cols, 1)
    bias_local = lax.dynamic_slice_in_dim(key_bias[0], seq_idx * heads_local, heads_local)
    contact_all = lax.all_gather(contacts[:, 0, :], "seq", axis=1, tiled=True)
    key_all = keyframes[:, 0, :]
    step_all = timesteps[:, 0]
    labels = jnp.arange(table.shape[0], dtype=jnp.int32)
    cot_all = lax.all_gather(head_cotangent[0, :, 0], "seq", axis=1, tiled=True)

    lag = 2 if section_count == 2 else 1
    if lag == 2:
        steps = turns + 1
    else:
        steps = turns

    def turn_at(step):
        if lag == 1:
            return jnp.int32(step)
        return jnp.clip(step - section_idx, 0, turns - 1)

    outputs = []
    handed = {}
    for step in range(steps):
        turn = turn_at(step)
        fresh = lax.dynamic_index_in_dim(incoming[0, :, 0], turn, 0, keepdims=False)
        current = lax.all_gather(fresh, "seq", axis=0, tiled=True)
        if step in handed:
            current = jnp.where((section_idx == 0) | (turn == 0), current, handed[step])
        batch_idx = turn - section_idx + section_count - 1
        contact_rows = lax.dynamic_index_in_dim(contact_all, batch_idx, 0, keepdims=False)
        key_flags = lax.dynamic_index_in_dim(key_all, batch_idx, 0, keepdims=False).astype(
            jnp.float32
        )
        timestep = lax.dynamic_index_in_dim(step_all, batch_idx, 0, keepdims=False).astype(
            jnp.float32
        )
        onehot = (contact_rows[:, None] == labels[None, :]).astype(jnp.bfloat16)
        hidden = current.astype(jnp.float32) + jnp.dot(
            onehot, table, preferred_element_type=jnp.float32
        )
        root_mean = jnp.sqrt(jnp.mean(hidden * hidden, axis=-1, keepdims=True) + epsilon)
        modulation = gain_row * (1.0 + 0.5 * jnp.sin(timestep * freq_row))
        normed = (hidden / root_mean * modulation[None, :]).astype(jnp.bfloat16)
        projected = jnp.dot(normed, weights, preferred_element_type=jnp.float32).astype(
            jnp.bfloat16
        )
        query_heads = projected[:, :q_cols].reshape(frames, heads_local, head_size)
        keyval_heads = projected[:, q_cols:].reshape(frames, kv_local, 2, head_size)
        head_outputs = []
        for head in range(heads_local):
            key_rows = keyval_heads[:, head // group_size, 0]
            value_rows = keyval_heads[:, head // group_size, 1]
            scores = (
                lax.dot_general(
                    query_heads[:, head],
                    key_rows,
                    (((1,), (1,)), ((), ())),
                    preferred_element_type=jnp.float32,
                )
                * score_scale
            )
            scores = scores + bias_local[head] * key_flags[None, :]
            row_max = jnp.max(scores, axis=-1, keepdims=True)
            exponent = jnp.exp(scores - row_max)
            probabilities = (exponent / jnp.sum(exponent, axis=-1, keepdims=True)).astype(
                jnp.bfloat16
            )
            head_outputs.append(
                jnp.dot(probabilities, value_rows, preferred_element_type=jnp.float32).astype(
                    jnp.bfloat16
                )
            )
        attended = jnp.concatenate(head_outputs, axis=1)
        hidden_local = lax.dynamic_slice_in_dim(current, seq_idx * q_cols, q_cols, 1).astype(
            jnp.float32
        ) + jnp.dot(onehot, table_local, preferred_element_type=jnp.float32)
        output = (hidden_local + gate_local[None, :] * attended.astype(jnp.float32)).astype(
            jnp.bfloat16
        )
        outputs.append(output)
        if step + lag < steps:
            piece = passed_along(output, "pipe", 1)
            handed[step + lag] = lax.all_gather(piece, "seq", axis=1, tiled=True)

    factor = float(turns * rep_count * frames) ** (-0.5)
    total = None
    rows_out = []
    for turn in range(turns):
        if lag == 2:
            own = jnp.where(section_idx == 0, outputs[turn], outputs[turn + 1])
        else:
            own = outputs[turn]
        term = lax.dot_general(
            own, cot_all[turn], (((0,), (0,)), ((), ())), preferred_element_type=jnp.float32
        )
        total = term if total is None else total + term
        rows_out.append(lax.all_to_all(own, "seq", split_axis=0, concat_axis=1, tiled=True))
    section_out = jnp.stack(rows_out)[None, :, None]
    grad_parts = lax.all_to_all(
        (total * factor).astype(jnp.bfloat16).reshape(rep_count, q_cols // rep_count, feat_count),
        "dp",
        split_axis=0,
        concat_axis=0,
        tiled=True,
    )
    grad_rows = jnp.sum(grad_parts.astype(jnp.float32), axis=0)
    return (section_out, grad_rows[None])


def solution(mesh):
    in_specs = (
        P("pipe", None, "dp", "seq", None),
        P(None, "dp", "seq"),
        P(None, "dp", None),
        P(None, "dp"),
        P("pipe", ("seq", "dp"), None),
        P("pipe", ("seq", "dp"), None),
        P("pipe", None),
        P("pipe", None),
        P("pipe", None, None),
        P("pipe", None),
        P("pipe", None),
        P("pipe", None, "dp", "seq", None),
    )
    out_specs = (P("pipe", None, "dp", "seq", None), P("pipe", ("seq", "dp"), None))
    return jax.shard_map(body, mesh=mesh, in_specs=in_specs, out_specs=out_specs, check_vma=False)
```

```python
import functools
import math

import jax
import jax.numpy as jnp
from jax import lax
from jax.experimental import pallas as pl
from jax.experimental.pallas import tpu as pltpu
from jax.sharding import PartitionSpec as P

epsilon = 1e-06


def passed_along(value, axis, steps):
    count = lax.axis_size(axis)
    first, last = (max(0, -steps), min(count, count - steps))
    return lax.ppermute(value, axis, [(source, source + steps) for source in range(first, last)])


def ring(value, axis):
    count = lax.axis_size(axis)
    return lax.ppermute(value, axis, [(source, (source + 1) % count) for source in range(count)])


def swap(value, bit):
    count = lax.axis_size("seq")
    return lax.ppermute(value, "seq", [(source, source ^ bit) for source in range(count)])


def shifted(value, axis, shift):
    count = lax.axis_size(axis)
    return lax.ppermute(value, axis, [(source, (source + shift) % count) for source in range(count)])


def offsets_of(count):
    offsets = [0]
    bit = count // 2
    while bit:
        offsets = offsets + [offset ^ bit for offset in offsets]
        bit //= 2
    return offsets


def turn_and_batch(step, turns):
    section = lax.axis_index("pipe")
    turn = jnp.clip(step - section, 0, turns - 1)
    return turn, turn - section + 1


def pack_kernel(wq, wkv, own, *outs):
    cols = outs[0].shape[1] // 2
    seq = lax.axis_index("seq")
    targets = (own.at[0],) + outs
    for m, out in enumerate(targets):
        start = pl.multiple_of((seq ^ m) * cols, 128)
        out[:, :cols] = wq[0, :, pl.ds(start, cols)]
        out[:, cols:] = wkv[0, :, pl.ds(start, cols)]


def pair_kernel(own, other, out):
    out[0] = own[0]
    out[1] = other[...]


def stack_kernel(dep, a, b, out):
    out[0] = a[...]
    out[1] = b[...]


def first_kernel(turns, dep, incoming, contacts, out, states):
    rows = incoming.shape[3]
    for turn in range(2):
        out[turn * rows : (turn + 1) * rows] = incoming[0, turn, 0]
    states[...] = jnp.zeros_like(states)
    for step in range(turns + 1):
        _, batch = turn_and_batch(step, turns)
        states[step : step + 1] = contacts[batch].astype(jnp.float32)
    out[2 * rows :, : states.shape[1]] = states[...].astype(jnp.bfloat16)


def second_kernel(dep, incoming, cotangent, out):
    turns, rows, feats = cotangent.shape[1], cotangent.shape[3], cotangent.shape[4]
    out[:rows] = incoming[0, 2, 0]
    for turn in range(turns):
        out[rows:, turn * feats : (turn + 1) * feats] = cotangent[0, turn, 0]


def step_kernel(cfg, *refs):
    step, has_relay, first_step = cfg["step"], cfg["has_relay"], cfg["first_step"]
    pieces, hops, head, turns = cfg["pieces"], cfg["hops"], cfg["head"], cfg["turns"]
    heads, group, halves = cfg["heads"], cfg["group"], cfg["halves"]
    refs = list(refs)

    def take(count):
        taken, refs[:count] = refs[:count], []
        return taken

    bias, times, table, gain, freq, gate, flags = take(7)
    first = take(pieces)
    second = take(pieces) if step >= 2 else None
    chunks = take(2 * hops) if first_step else None
    weights = None if first_step else take(1)[0]
    relay = take(pieces * halves) if has_relay else None
    outs = take(halves)
    if first_step:
        weights = take(1)[0]
    scaled, mod, square, own_hidden, proj, att, sem_w = take(7)
    offsets = offsets_of(pieces)
    frames, width = scaled.shape
    rows, cols = frames // pieces, att.shape[1]
    part = pieces // halves
    seq, rep, section = lax.axis_index("seq"), lax.axis_index("dp"), lax.axis_index("pipe")
    turn, batch = turn_and_batch(step, turns)

    w_copies = []
    if first_step:
        w_rows = chunks[0].shape[1]
        for ring in range(2):
            for hop in range(hops):
                for j in range(2):
                    block = (seq ^ (2 * ring + j)) * hops + lax.rem(rep + hops - hop, hops)
                    w_copies.append(
                        pltpu.make_async_copy(
                            chunks[ring * hops + hop].at[j],
                            weights.at[pl.ds(pl.multiple_of(block * w_rows, 16), w_rows)],
                            sem_w.at[len(w_copies)],
                        )
                    )
        for copy in w_copies:
            copy.start()

    labels = lax.broadcasted_iota(jnp.int32, (32, rows), 0)
    columns = []
    for i in range(pieces):
        state = first[i][2 * rows : 2 * rows + 16, :rows][step : step + 1]
        state = state.astype(jnp.float32).astype(jnp.int32)
        flag = flags[batch, :, pl.ds(pl.multiple_of((seq ^ offsets[i]) * rows, 128), rows)]
        one = jnp.where(labels == state, 1.0, 0.0)
        columns.append(jnp.where(labels == 16, flag.astype(jnp.float32), one).T)
    columns = jnp.concatenate(columns, axis=0)
    onehot = columns[:, : table.shape[1]].astype(jnp.bfloat16)
    flag_column = columns[:, 16:17]

    time = times[batch, 0].astype(jnp.float32)
    mod[...] = gain[...] * (1.0 + 0.5 * jnp.sin(time * freq[...]))

    def normalize(relayed):
        total = jnp.zeros((frames, 128), jnp.float32)
        for i in range(pieces):
            lanes = pl.ds(pl.multiple_of((seq ^ offsets[i]) * cols, 128), cols)
            blocks = []
            for p in range(pieces):
                if relayed:
                    j = offsets.index(offsets[i] ^ offsets[p])
                    blocks.append(relay[(j // part) * pieces + i][j % part])
                elif step < 2:
                    at = pl.multiple_of(jnp.minimum(turn, 1) * rows, 128)
                    blocks.append(first[p][pl.ds(at, rows), lanes])
                else:
                    blocks.append(second[p][:rows, lanes])
            hidden = jnp.concatenate(blocks, axis=0).astype(jnp.float32) + jnp.dot(
                onehot, table[0, :, lanes], preferred_element_type=jnp.float32
            )
            for lane in range(0, cols, 128):
                piece = hidden[:, lane : lane + 128]
                total = total + piece * piece
            scaled[:, lanes] = (hidden * mod[:, lanes]).astype(jnp.bfloat16)
            if i == 0:
                own_hidden[...] = hidden
        square[...] = total

    if has_relay:

        @pl.when(section == 0)
        def _():
            normalize(False)

        @pl.when(section != 0)
        def _():
            normalize(True)
    else:
        normalize(False)
    mean = jnp.sum(square[...], axis=1, keepdims=True) * (1.0 / width)
    scale = lax.rsqrt(mean + epsilon)
    for copy in w_copies:
        copy.wait()
    projected = jnp.dot(scaled[...], weights[...], preferred_element_type=jnp.float32) * scale
    score_scale = head ** (-0.5) * math.log2(math.e)
    proj[:, :cols] = (projected[:, :cols] * score_scale).astype(jnp.bfloat16)
    proj[:, cols : 2 * cols] = projected[:, cols:].astype(jnp.bfloat16)
    proj[:, 2 * cols :] = jnp.zeros((frames, 128), jnp.bfloat16)
    lanes = lax.broadcasted_iota(jnp.int32, (frames, 128), 1)
    row_lanes = lax.broadcasted_iota(jnp.int32, (1, 128), 1)
    flag_lanes = jnp.logical_or(lanes == head, lanes == head + 1)

    def part_of(at):
        return proj[:, at : at + 128].astype(jnp.float32)

    keys, values = [], []
    for kv in range(heads // group):
        base = cols + kv * 2 * head
        key = jnp.where(flag_lanes, flag_column, jnp.where(lanes < head, part_of(base), 0.0))
        value = jnp.where(lanes < head, part_of(base + head), jnp.where(lanes == head, 1.0, 0.0))
        keys.append(key.astype(jnp.bfloat16))
        values.append(value.astype(jnp.bfloat16))

    def scores_of(h):
        strength = jnp.zeros((1, 128), jnp.float32) + bias[0, seq * heads + h] * math.log2(math.e)
        coarse = strength.astype(jnp.bfloat16).astype(jnp.float32)
        tail = jnp.where(
            row_lanes == head, coarse, jnp.where(row_lanes == head + 1, strength - coarse, 0.0)
        )
        query = jnp.where(lanes < head, part_of(h * head), tail).astype(jnp.bfloat16)
        return lax.dot_general(
            query, keys[h // group], (((1,), (1,)), ((), ())), preferred_element_type=jnp.float32
        )

    scores = scores_of(0)
    for h in range(heads):
        ahead = scores_of(h + 1) if h + 1 < heads else None
        top = jnp.max(scores, axis=1, keepdims=True)
        weight = jnp.exp2(scores - top).astype(jnp.bfloat16)
        mixed = jnp.dot(weight, values[h // group], preferred_element_type=jnp.float32)
        att[:, h * head : (h + 1) * head] = mixed[:, :head] * (1.0 / mixed[:, head : head + 1])
        scores = ahead
    own = pl.ds(pl.multiple_of(seq * cols, 128), cols)
    attended = att[...].astype(jnp.bfloat16).astype(jnp.float32)
    output = (own_hidden[...] + gate[:, own] * attended).astype(jnp.bfloat16)
    blocks = output.reshape(pieces, rows, cols)
    for k in range(halves):
        outs[k][...] = blocks[k * part : (k + 1) * part]


def tie_kernel(count, *refs):
    pass


def grad_of(output, second, turn, rows, feats):
    cot = jnp.concatenate(
        [piece[rows : 2 * rows, turn * feats : (turn + 1) * feats] for piece in second], axis=0
    )
    return lax.dot_general(
        output, cot, (((0,), (0,)), ((), ())), preferred_element_type=jnp.float32
    )


def early_kernel(turns, pieces, halves, feats, *refs):
    outs, second = refs[: turns * halves], refs[turns * halves : turns * halves + pieces]
    sends, grad = refs[turns * halves + pieces : -1], refs[-1]
    section = lax.axis_index("pipe")
    offsets = offsets_of(pieces)
    part = pieces // halves
    rows = outs[0].shape[1]
    total = None
    for turn in range(turns - 1):
        blocks = []
        for p in range(pieces):
            k, j = p // part, p % part
            block = jnp.where(
                section == 0, outs[turn * halves + k][j], outs[(turn + 1) * halves + k][j]
            )
            sends[offsets[p]][turn] = block
            blocks.append(block)
        share = grad_of(jnp.concatenate(blocks, axis=0), second, turn, rows, feats)
        total = share if total is None else total + share
    grad[...] = total


def settle_kernel(turns, pieces, halves, hops, feats, *refs):
    refs = list(refs)

    def take(count):
        taken, refs[:count] = refs[:count], []
        return taken

    before, now, second, early = take(halves), take(halves), take(pieces), take(pieces)
    early_grad = take(1)[0]
    late, own_grad, grads = take(pieces), take(1)[0], take(hops - 1)
    section_out = take(1)[0]
    rows_out, total, sem = take(3)
    section, seq, rep = lax.axis_index("pipe"), lax.axis_index("seq"), lax.axis_index("dp")
    offsets = offsets_of(pieces)
    part = pieces // halves
    rows, cols = early[0].shape[1:]
    for m in range(pieces):
        lanes = pl.ds(pl.multiple_of((seq ^ m) * cols, 128), cols)
        for turn in range(turns - 1):
            rows_out[turn, :, lanes] = early[m][turn]
    copy = pltpu.make_async_copy(rows_out, section_out.at[pl.ds(0, turns - 1)], sem)
    copy.start()
    blocks = []
    for p in range(pieces):
        block = jnp.where(section == 0, before[p // part][p % part], now[p // part][p % part])
        late[offsets[p]][...] = block
        blocks.append(block)
    share = grad_of(jnp.concatenate(blocks, axis=0), second, turns - 1, rows, feats)
    factor = float(turns * hops * rows * pieces) ** (-0.5)
    total[...] = (share + early_grad[...]) * factor
    g_rows = cols // hops
    own_grad[...] = total[pl.ds(pl.multiple_of(rep * g_rows, 8), g_rows)]
    for shift in range(1, hops):
        at = pl.multiple_of(lax.rem(rep + shift, hops) * g_rows, 8)
        grads[shift - 1][...] = total[pl.ds(at, g_rows)].astype(jnp.bfloat16)
    copy.wait()


def finish_kernel(pieces, hops, *refs):
    held, late, refs = refs[0], refs[1 : pieces + 1], refs[pieces + 1 :]
    own_grad, parts, (section_out, grad, row_out, sem) = refs[0], refs[1:hops], refs[hops:]
    seq = lax.axis_index("seq")
    cols = late[0].shape[1]
    for m in range(pieces):
        lanes = pl.ds(pl.multiple_of((seq ^ m) * cols, 128), cols)
        row_out[:, lanes] = late[m][...]
    copy = pltpu.make_async_copy(row_out, section_out.at[section_out.shape[0] - 1], sem)
    copy.start()
    total = own_grad[...]
    for part in parts:
        total = total + part[...].astype(jnp.float32)
    grad[...] = total
    copy.wait()


HALVES = 2
MIB = 1024 * 1024


def paired_body(
    incoming,
    contacts,
    keyframes,
    timesteps,
    w_query,
    w_keyval,
    norm_gain,
    time_freq,
    contact_table,
    key_bias,
    attn_gate,
    head_cotangent,
):
    seq_count = lax.axis_size("seq")
    hops = lax.axis_size("dp")
    rows, width, turns = incoming.shape[3], incoming.shape[4], incoming.shape[1]
    frames = rows * seq_count
    heads_all = key_bias.shape[1]
    head = width // heads_all
    heads = heads_all // seq_count
    kv_heads = w_keyval.shape[2] // (2 * head * seq_count)
    feats = head_cotangent.shape[4]
    cols = width // seq_count
    w_rows = w_query.shape[1]
    steps = turns + 1
    part = seq_count // HALVES
    kind = jnp.bfloat16
    smem = pl.BlockSpec(memory_space=pltpu.SMEM)
    vmem = pl.BlockSpec(memory_space=pltpu.VMEM)
    anywhere = pl.BlockSpec(memory_space=pl.ANY)
    shape = jax.ShapeDtypeStruct

    def call(kernel, name, out_shape, in_specs, operands, scratch=(), limit=4, flops=0, **options):
        return pl.pallas_call(
            kernel,
            out_shape=out_shape,
            in_specs=in_specs,
            scratch_shapes=list(scratch),
            compiler_params=pltpu.CompilerParams(vmem_limit_bytes=limit * MIB),
            cost_estimate=pl.CostEstimate(
                flops=flops, bytes_accessed=flops // 512, transcendentals=0
            ),
            name=name,
            **options,
        )(*operands)

    block = shape((w_rows, 2 * cols), kind)
    pair = shape((2, w_rows, 2 * cols), kind)
    packed = call(
        pack_kernel,
        "pack",
        [pair] + [block] * (seq_count - 1),
        [vmem, vmem],
        [w_query, w_keyval],
        out_specs=[vmem] * seq_count,
    )
    blocks = [swap(packed[m], m) for m in range(1, seq_count)]
    near = call(
        pair_kernel, "near", pair, [vmem, vmem], [packed[0], blocks[0]], out_specs=vmem
    )
    far = call(
        stack_kernel, "far", pair, [anywhere, vmem, vmem], [near] + blocks[1:], out_specs=vmem
    )
    rings = [[near], [far]]
    for hop in range(1, hops):
        for ring in rings:
            ring.append(shifted(ring[-1], "dp", 1))

    mine = call(
        functools.partial(first_kernel, turns),
        "first",
        shape((2 * rows + 16, width), kind),
        [anywhere, vmem, vmem],
        [far, incoming, contacts],
        [pltpu.VMEM((16, 128), jnp.float32)],
        out_specs=vmem,
    )
    across = swap(mine, 2)
    first = [mine, across, swap(mine, 1), swap(across, 1)]
    mine = call(
        second_kernel,
        "second",
        shape((2 * rows, width), kind),
        [anywhere, vmem, vmem],
        [across, incoming, head_cotangent],
        out_specs=vmem,
    )
    across = swap(mine, 2)
    second = [mine, across, swap(mine, 1), swap(across, 1)]

    outputs = []
    relayed = {}
    weights = None
    for step in range(steps):
        cfg = {
            "step": step,
            "has_relay": step in relayed,
            "first_step": step == 0,
            "pieces": seq_count,
            "hops": hops,
            "head": head,
            "heads": heads,
            "group": heads // kv_heads,
            "turns": turns,
            "halves": HALVES,
        }
        operands = [key_bias, timesteps, contact_table, norm_gain, time_freq, attn_gate, keyframes]
        operands += first
        if step >= 2:
            operands += second
        operands += rings[0] + rings[1] if step == 0 else [weights]
        operands += relayed.get(step, [])
        out_shape = [shape((part, rows, cols), kind)] * HALVES
        if step == 0:
            out_shape += [shape((width, 2 * cols), kind)]
        results = call(
            functools.partial(step_kernel, cfg),
            "step%d" % step,
            out_shape,
            [smem, smem] + [vmem] * (len(operands) - 2),
            operands,
            [
                pltpu.VMEM((frames, width), kind),
                pltpu.VMEM((1, width), jnp.float32),
                pltpu.VMEM((frames, 128), jnp.float32),
                pltpu.VMEM((frames, cols), jnp.float32),
                pltpu.VMEM((frames, 2 * cols + 128), kind),
                pltpu.VMEM((frames, cols), jnp.float32),
                pltpu.SemaphoreType.DMA((4 * hops,)),
            ],
            20,
            2 * frames * width * 2 * cols + 4 * heads * frames * frames * head,
            out_specs=[vmem] * len(out_shape),
        )
        outputs.append(list(results[:HALVES]))
        if step == 0:
            weights = results[HALVES]
        if step == 2:
            pending = [piece for k in range(HALVES) for piece in (crossing[k][0], crossing[k][1])]
            tied = call(
                functools.partial(tie_kernel, len(pending)),
                "tie",
                [shape(piece.shape, kind) for piece in pending],
                [anywhere] * (len(pending) + 1),
                pending + [outputs[-1][0]],
                out_specs=[anywhere] * len(pending),
                input_output_aliases={i: i for i in range(len(pending))},
            )
            relayed[3] = []
            for k in range(HALVES):
                mine, across = tied[2 * k], tied[2 * k + 1]
                relayed[3] += [mine, across, swap(mine, 1), swap(across, 1)]
            early = call(
                functools.partial(early_kernel, turns, seq_count, HALVES, feats),
                "early",
                [shape((turns - 1, rows, cols), kind)] * seq_count
                + [shape((cols, feats), jnp.float32)],
                [vmem] * (turns * HALVES + seq_count),
                [half for output in outputs for half in output] + second,
                limit=8,
                out_specs=[vmem] * (seq_count + 1),
            )
            early, early_grad = list(early[:-1]), early[-1]
            early = [early[0]] + [swap(early[m], m) for m in range(1, seq_count)]
        if step + 2 < steps:
            pieces = [passed_along(half, "pipe", 1) for half in outputs[-1]]
            crossing = [(piece, swap(piece, 2)) for piece in pieces]
            if step == 0:
                relayed[2] = []
                for mine, across in crossing:
                    relayed[2] += [mine, across, swap(mine, 1), swap(across, 1)]

    g_shape = (cols // hops, feats)
    operands = outputs[-2] + outputs[-1] + second + early + [early_grad]
    settled = call(
        functools.partial(settle_kernel, turns, seq_count, HALVES, hops, feats),
        "settle",
        [shape((rows, cols), kind)] * seq_count
        + [shape(g_shape, jnp.float32)]
        + [shape(g_shape, kind)] * (hops - 1)
        + [shape((turns, rows, width), kind)],
        [vmem] * len(operands),
        operands,
        [
            pltpu.VMEM((turns - 1, rows, width), kind),
            pltpu.VMEM((cols, feats), jnp.float32),
            pltpu.SemaphoreType.DMA,
        ],
        8,
        out_specs=[vmem] * (seq_count + hops) + [anywhere],
    )
    late, grads, held = settled[:seq_count], settled[seq_count:-1], settled[-1]
    late = [late[0]] + [swap(late[m], m) for m in range(1, seq_count)]
    grads = [grads[0]] + [shifted(grads[k], "dp", k) for k in range(1, hops)]
    section_out, grad_rows = call(
        functools.partial(finish_kernel, seq_count, hops),
        "finish",
        [shape((turns, rows, width), kind), shape(g_shape, jnp.float32)],
        [anywhere] + [vmem] * (seq_count + hops),
        [held] + late + grads,
        [pltpu.VMEM((rows, width), kind), pltpu.SemaphoreType.DMA],
        out_specs=[anywhere, vmem],
        input_output_aliases={0: 0},
    )
    return (section_out[None, :, None], grad_rows[None])


def body(incoming, contacts, keyframes, timesteps, w_query, *others):
    count = lax.axis_size("seq")
    cols = w_query.shape[2] // count
    paired = (
        lax.axis_size("pipe") == 2
        and count == 4
        and cols % 128 == 0
        and w_query.shape[1] % 16 == 0
        and incoming.shape[3] == 128
        and incoming.shape[1] == 3
    )
    chosen = paired_body if paired else general_body
    return chosen(incoming, contacts, keyframes, timesteps, w_query, *others)


def general_body(
    incoming,
    contacts,
    keyframes,
    timesteps,
    w_query,
    w_keyval,
    norm_gain,
    time_freq,
    contact_table,
    key_bias,
    attn_gate,
    head_cotangent,
):
    section_idx = lax.axis_index("pipe")
    seq_idx = lax.axis_index("seq")
    rep_idx = lax.axis_index("dp")
    seq_count = lax.axis_size("seq")
    section_count = lax.axis_size("pipe")
    rep_count = lax.axis_size("dp")
    tok_rows = incoming.shape[3]
    width = incoming.shape[4]
    turns = incoming.shape[1]
    frames = tok_rows * seq_count
    heads_all = key_bias.shape[1]
    head_size = width // heads_all
    heads_local = heads_all // seq_count
    kv_width = w_keyval.shape[2]
    kv_local = kv_width // (2 * head_size * seq_count)
    group_size = heads_local // kv_local
    feat_count = head_cotangent.shape[4]
    score_scale = head_size ** (-0.5)
    q_cols = width // seq_count
    kv_cols = kv_width // seq_count
    w_rows = w_query.shape[1]

    w_parts = jnp.concatenate(
        [
            w_query[0].reshape(w_rows, seq_count, q_cols),
            w_keyval[0].reshape(w_rows, seq_count, kv_cols),
        ],
        axis=2,
    ).transpose(1, 0, 2)
    block = lax.all_to_all(w_parts, "seq", split_axis=0, concat_axis=0, tiled=True)
    weights = jnp.zeros((seq_count, rep_count, w_rows, q_cols + kv_cols), jnp.bfloat16)
    for hop in range(rep_count):
        owner = lax.rem(rep_idx + rep_count - hop, rep_count)
        weights = lax.dynamic_update_slice_in_dim(weights, block[:, None], owner, 1)
        if hop + 1 < rep_count:
            block = ring(block, "dp")
    weights = weights.reshape(width, q_cols + kv_cols)

    gain_row = norm_gain[0]
    freq_row = time_freq[0]
    table = contact_table[0]
    gate_local = lax.dynamic_slice_in_dim(attn_gate[0], seq_idx * q_cols, q_cols)
    table_local = lax.dynamic_slice_in_dim(table, seq_idx * q_cols, q_cols, 1)
    bias_local = lax.dynamic_slice_in_dim(key_bias[0], seq_idx * heads_local, heads_local)
    contact_all = lax.all_gather(contacts[:, 0, :], "seq", axis=1, tiled=True)
    key_all = keyframes[:, 0, :]
    step_all = timesteps[:, 0]
    labels = jnp.arange(table.shape[0], dtype=jnp.int32)
    cot_all = lax.all_gather(head_cotangent[0, :, 0], "seq", axis=1, tiled=True)

    lag = 2 if section_count == 2 else 1
    if lag == 2:
        steps = turns + 1
    else:
        steps = turns

    def turn_at(step):
        if lag == 1:
            return jnp.int32(step)
        return jnp.clip(step - section_idx, 0, turns - 1)

    outputs = []
    handed = {}
    for step in range(steps):
        turn = turn_at(step)
        fresh = lax.dynamic_index_in_dim(incoming[0, :, 0], turn, 0, keepdims=False)
        current = lax.all_gather(fresh, "seq", axis=0, tiled=True)
        if step in handed:
            current = jnp.where((section_idx == 0) | (turn == 0), current, handed[step])
        batch_idx = turn - section_idx + section_count - 1
        contact_rows = lax.dynamic_index_in_dim(contact_all, batch_idx, 0, keepdims=False)
        key_flags = lax.dynamic_index_in_dim(key_all, batch_idx, 0, keepdims=False).astype(
            jnp.float32
        )
        timestep = lax.dynamic_index_in_dim(step_all, batch_idx, 0, keepdims=False).astype(
            jnp.float32
        )
        onehot = (contact_rows[:, None] == labels[None, :]).astype(jnp.bfloat16)
        hidden = current.astype(jnp.float32) + jnp.dot(
            onehot, table, preferred_element_type=jnp.float32
        )
        root_mean = jnp.sqrt(jnp.mean(hidden * hidden, axis=-1, keepdims=True) + epsilon)
        modulation = gain_row * (1.0 + 0.5 * jnp.sin(timestep * freq_row))
        normed = (hidden / root_mean * modulation[None, :]).astype(jnp.bfloat16)
        projected = jnp.dot(normed, weights, preferred_element_type=jnp.float32).astype(
            jnp.bfloat16
        )
        query_heads = projected[:, :q_cols].reshape(frames, heads_local, head_size)
        keyval_heads = projected[:, q_cols:].reshape(frames, kv_local, 2, head_size)
        head_outputs = []
        for head in range(heads_local):
            key_rows = keyval_heads[:, head // group_size, 0]
            value_rows = keyval_heads[:, head // group_size, 1]
            scores = (
                lax.dot_general(
                    query_heads[:, head],
                    key_rows,
                    (((1,), (1,)), ((), ())),
                    preferred_element_type=jnp.float32,
                )
                * score_scale
            )
            scores = scores + bias_local[head] * key_flags[None, :]
            row_max = jnp.max(scores, axis=-1, keepdims=True)
            exponent = jnp.exp(scores - row_max)
            probabilities = (exponent / jnp.sum(exponent, axis=-1, keepdims=True)).astype(
                jnp.bfloat16
            )
            head_outputs.append(
                jnp.dot(probabilities, value_rows, preferred_element_type=jnp.float32).astype(
                    jnp.bfloat16
                )
            )
        attended = jnp.concatenate(head_outputs, axis=1)
        hidden_local = lax.dynamic_slice_in_dim(current, seq_idx * q_cols, q_cols, 1).astype(
            jnp.float32
        ) + jnp.dot(onehot, table_local, preferred_element_type=jnp.float32)
        output = (hidden_local + gate_local[None, :] * attended.astype(jnp.float32)).astype(
            jnp.bfloat16
        )
        outputs.append(output)
        if step + lag < steps:
            piece = passed_along(output, "pipe", 1)
            handed[step + lag] = lax.all_gather(piece, "seq", axis=1, tiled=True)

    factor = float(turns * rep_count * frames) ** (-0.5)
    total = None
    rows_out = []
    for turn in range(turns):
        if lag == 2:
            own = jnp.where(section_idx == 0, outputs[turn], outputs[turn + 1])
        else:
            own = outputs[turn]
        term = lax.dot_general(
            own, cot_all[turn], (((0,), (0,)), ((), ())), preferred_element_type=jnp.float32
        )
        total = term if total is None else total + term
        rows_out.append(lax.all_to_all(own, "seq", split_axis=0, concat_axis=1, tiled=True))
    section_out = jnp.stack(rows_out)[None, :, None]
    grad_parts = lax.all_to_all(
        (total * factor).astype(jnp.bfloat16).reshape(rep_count, q_cols // rep_count, feat_count),
        "dp",
        split_axis=0,
        concat_axis=0,
        tiled=True,
    )
    grad_rows = jnp.sum(grad_parts.astype(jnp.float32), axis=0)
    return (section_out, grad_rows[None])


def solution(mesh):
    in_specs = (
        P("pipe", None, "dp", "seq", None),
        P(None, "dp", "seq"),
        P(None, "dp", None),
        P(None, "dp"),
        P("pipe", ("seq", "dp"), None),
        P("pipe", ("seq", "dp"), None),
        P("pipe", None),
        P("pipe", None),
        P("pipe", None, None),
        P("pipe", None),
        P("pipe", None),
        P("pipe", None, "dp", "seq", None),
    )
    out_specs = (P("pipe", None, "dp", "seq", None), P("pipe", ("seq", "dp"), None))
    return jax.shard_map(body, mesh=mesh, in_specs=in_specs, out_specs=out_specs, check_vma=False)
```

```python
import functools
import math

import jax
import jax.numpy as jnp
from jax import lax
from jax.experimental import pallas as pl
from jax.experimental.pallas import tpu as pltpu
from jax.sharding import PartitionSpec as P

epsilon = 1e-06


def passed_along(value, axis, steps):
    count = lax.axis_size(axis)
    first, last = (max(0, -steps), min(count, count - steps))
    return lax.ppermute(value, axis, [(source, source + steps) for source in range(first, last)])


def ring(value, axis):
    count = lax.axis_size(axis)
    return lax.ppermute(value, axis, [(source, (source + 1) % count) for source in range(count)])


def swap(value, bit):
    count = lax.axis_size("seq")
    return lax.ppermute(value, "seq", [(source, source ^ bit) for source in range(count)])


def shifted(value, axis, shift):
    count = lax.axis_size(axis)
    return lax.ppermute(value, axis, [(source, (source + shift) % count) for source in range(count)])


def offsets_of(count):
    offsets = [0]
    bit = count // 2
    while bit:
        offsets = offsets + [offset ^ bit for offset in offsets]
        bit //= 2
    return offsets


def turn_and_batch(step, turns):
    section = lax.axis_index("pipe")
    turn = jnp.clip(step - section, 0, turns - 1)
    return turn, turn - section + 1


def pack_kernel(wq, wkv, *refs):
    outs, sems = refs[:-1], refs[-1]
    cols = outs[0].shape[1] // 2
    seq = lax.axis_index("seq")
    copies = []
    for m, out in enumerate(outs):
        start = pl.multiple_of((seq ^ m) * cols, 128)
        for k, source in enumerate((wq, wkv)):
            copies.append(
                pltpu.make_async_copy(
                    source.at[0, :, pl.ds(start, cols)],
                    out.at[:, pl.ds(k * cols, cols)],
                    sems.at[2 * m + k],
                )
            )
    for copy in copies:
        copy.start()
    for copy in copies:
        copy.wait()


def stack_kernel(a, b, out):
    out[0] = a[...]
    out[1] = b[...]


def first_kernel(turns, near, beside, far, incoming, contacts, out, states):
    rows = incoming.shape[3]
    for turn in range(2):
        out[turn * rows : (turn + 1) * rows] = incoming[0, turn, 0]
    states[...] = jnp.zeros_like(states)
    for step in range(turns + 1):
        _, batch = turn_and_batch(step, turns)
        states[step : step + 1] = contacts[batch].astype(jnp.float32)
    out[2 * rows :, : states.shape[1]] = states[...].astype(jnp.bfloat16)


def second_kernel(dep, incoming, cotangent, out):
    turns, rows, feats = cotangent.shape[1], cotangent.shape[3], cotangent.shape[4]
    out[:rows] = incoming[0, 2, 0]
    for turn in range(turns):
        out[rows:, turn * feats : (turn + 1) * feats] = cotangent[0, turn, 0]


def columns_of(rows_of, pieces, rows):
    labels = lax.broadcasted_iota(jnp.int32, (32, rows), 0)
    columns = []
    for i in range(pieces):
        state, flag = rows_of(i)
        one = jnp.zeros((32, rows), jnp.float32)
        if state is not None:
            one = jnp.where(labels == state, 1.0, 0.0)
        if flag is not None:
            one = jnp.where(labels == 16, flag, one)
        columns.append(one.T)
    return jnp.concatenate(columns, axis=0)


def modulation(step, turns, times, gain, freq):
    _, batch = turn_and_batch(step, turns)
    return gain[...] * (1.0 + 0.5 * jnp.sin(times[batch, 0].astype(jnp.float32) * freq[...]))


def norm_kernel(turns, pieces, times, table, gain, freq, *refs):
    first, refs = refs[:pieces], refs[pieces + 1 :]
    scaled, scales, owns, embeds, mod = refs[0:2], refs[2:4], refs[4:6], refs[6:8], refs[8]
    frames, width = scaled[0].shape
    rows, cols = frames // pieces, owns[0].shape[1]
    seq = lax.axis_index("seq")
    offsets = offsets_of(pieces)
    for step in range(turns + 1):

        def state_of(i):
            state = first[i][2 * rows : 2 * rows + 16, :rows][step : step + 1]
            return state.astype(jnp.float32).astype(jnp.int32), None

        onehot = columns_of(state_of, pieces, rows)[:, : table.shape[1]].astype(jnp.bfloat16)
        if step >= 2:
            for at in range(0, width, 256):
                embeds[step - 2][:, at : at + 256] = jnp.dot(
                    onehot, table[0, :, at : at + 256], preferred_element_type=jnp.float32
                ).astype(jnp.bfloat16)
            continue
        turn, _ = turn_and_batch(step, turns)
        at = pl.multiple_of(jnp.minimum(turn, 1) * rows, 128)
        mod[...] = modulation(step, turns, times, gain, freq)
        total = jnp.zeros((frames, 128), jnp.float32)
        for i in range(pieces):
            lanes = pl.ds(pl.multiple_of((seq ^ offsets[i]) * cols, 128), cols)
            current = jnp.concatenate([first[p][pl.ds(at, rows), lanes] for p in range(pieces)])
            hidden = current.astype(jnp.float32) + jnp.dot(
                onehot, table[0, :, lanes], preferred_element_type=jnp.float32
            )
            for lane in range(0, cols, 128):
                piece = hidden[:, lane : lane + 128]
                total = total + piece * piece
            scaled[step][:, lanes] = (hidden * mod[:, lanes]).astype(jnp.bfloat16)
            if i == 0:
                owns[step][...] = hidden
        mean = jnp.sum(total, axis=1, keepdims=True) * (1.0 / width)
        scales[step][...] = jnp.broadcast_to(lax.rsqrt(mean + epsilon), (frames, 128))


def step_kernel(cfg, *refs):
    step, has_relay = cfg["step"], cfg["has_relay"]
    pieces, hops, head, turns = cfg["pieces"], cfg["hops"], cfg["head"], cfg["turns"]
    heads, group, halves = cfg["heads"], cfg["group"], cfg["halves"]
    refs = list(refs)

    def take(count):
        taken, refs[:count] = refs[:count], []
        return taken

    bias, times, gain, freq, gate, flags = take(6)
    if has_relay:
        second, embed, relay = take(pieces), take(1)[0], take(pieces * halves)
    else:
        scaled, scales, own_hidden = take(3)
    chunks = take(3 * hops) if step == 0 else None
    weights = None if step == 0 else take(1)[0]
    outs = take(halves)
    if step == 0:
        weights = take(1)[0]
    proj, att = take(2)
    if has_relay:
        scaled, scales, own_hidden, mod = take(4)
    offsets = offsets_of(pieces)
    frames, width = scaled.shape
    rows, cols = frames // pieces, att.shape[1]
    part = pieces // halves
    seq, rep, section = lax.axis_index("seq"), lax.axis_index("dp"), lax.axis_index("pipe")
    _, batch = turn_and_batch(step, turns)

    if step == 0:
        w_rows = width // (pieces * hops)
        for m in range(pieces):
            for hop in range(hops):
                block = (seq ^ m) * hops + lax.rem(rep + hops - hop, hops)
                chunk = chunks[m * hops + hop] if m < 2 else chunks[2 * hops + hop].at[m - 2]
                weights[pl.ds(pl.multiple_of(block * w_rows, 16), w_rows)] = chunk[...]

    def normalize(relayed):
        total = jnp.zeros((frames, 128), jnp.float32)
        for i in range(pieces):
            lanes = pl.ds(pl.multiple_of((seq ^ offsets[i]) * cols, 128), cols)
            blocks = []
            for p in range(pieces):
                if relayed:
                    j = offsets.index(offsets[i] ^ offsets[p])
                    blocks.append(relay[(j // part) * pieces + i][j % part])
                else:
                    blocks.append(second[p][:rows, lanes])
            hidden = jnp.concatenate(blocks, axis=0).astype(jnp.float32)
            hidden = hidden + embed[:, lanes].astype(jnp.float32)
            for lane in range(0, cols, 128):
                piece = hidden[:, lane : lane + 128]
                total = total + piece * piece
            scaled[:, lanes] = (hidden * mod[:, lanes]).astype(jnp.bfloat16)
            if i == 0:
                own_hidden[...] = hidden
        scales[...] = total

    if has_relay:
        mod[...] = modulation(step, turns, times, gain, freq)

        @pl.when(section == 0)
        def _():
            normalize(False)

        @pl.when(section != 0)
        def _():
            normalize(True)

        mean = jnp.sum(scales[...], axis=1, keepdims=True) * (1.0 / width)
        scale = lax.rsqrt(mean + epsilon)
    else:
        scale = scales[:, :1]

    def flag_of(i):
        lanes = pl.ds(pl.multiple_of((seq ^ offsets[i]) * rows, 128), rows)
        return None, flags[batch, :, lanes].astype(jnp.float32)

    flag_column = columns_of(flag_of, pieces, rows)[:, 16:17]
    projected = jnp.dot(scaled[...], weights[...], preferred_element_type=jnp.float32) * scale
    score_scale = head ** (-0.5) * math.log2(math.e)
    proj[:, :cols] = (projected[:, :cols] * score_scale).astype(jnp.bfloat16)
    proj[:, cols : 2 * cols] = projected[:, cols:].astype(jnp.bfloat16)
    proj[:, 2 * cols :] = jnp.zeros((frames, 128), jnp.bfloat16)
    lanes = lax.broadcasted_iota(jnp.int32, (frames, 128), 1)
    row_lanes = lax.broadcasted_iota(jnp.int32, (1, 128), 1)
    flag_lanes = jnp.logical_or(lanes == head, lanes == head + 1)

    def part_of(at):
        return proj[:, at : at + 128].astype(jnp.float32)

    keys, values = [], []
    for kv in range(heads // group):
        base = cols + kv * 2 * head
        key = jnp.where(flag_lanes, flag_column, jnp.where(lanes < head, part_of(base), 0.0))
        value = jnp.where(lanes < head, part_of(base + head), jnp.where(lanes == head, 1.0, 0.0))
        keys.append(key.astype(jnp.bfloat16))
        values.append(value.astype(jnp.bfloat16))

    def scores_of(h):
        strength = jnp.zeros((1, 128), jnp.float32) + bias[0, seq * heads + h] * math.log2(math.e)
        coarse = strength.astype(jnp.bfloat16).astype(jnp.float32)
        tail = jnp.where(
            row_lanes == head, coarse, jnp.where(row_lanes == head + 1, strength - coarse, 0.0)
        )
        query = jnp.where(lanes < head, part_of(h * head), tail).astype(jnp.bfloat16)
        return lax.dot_general(
            query, keys[h // group], (((1,), (1,)), ((), ())), preferred_element_type=jnp.float32
        )

    scores = scores_of(0)
    for h in range(heads):
        ahead = scores_of(h + 1) if h + 1 < heads else None
        top = jnp.max(scores, axis=1, keepdims=True)
        weight = jnp.exp2(scores - top).astype(jnp.bfloat16)
        mixed = jnp.dot(weight, values[h // group], preferred_element_type=jnp.float32)
        att[:, h * head : (h + 1) * head] = mixed[:, :head] * (1.0 / mixed[:, head : head + 1])
        scores = ahead
    own = pl.ds(pl.multiple_of(seq * cols, 128), cols)
    attended = att[...].astype(jnp.bfloat16).astype(jnp.float32)
    output = (own_hidden[...] + gate[:, own] * attended).astype(jnp.bfloat16)
    blocks = output.reshape(pieces, rows, cols)
    for k in range(halves):
        outs[k][...] = blocks[k * part : (k + 1) * part]


def tie_kernel(*refs):
    pass


def grad_of(output, second, turn, rows, feats):
    cot = jnp.concatenate(
        [piece[rows : 2 * rows, turn * feats : (turn + 1) * feats] for piece in second], axis=0
    )
    return lax.dot_general(
        output, cot, (((0,), (0,)), ((), ())), preferred_element_type=jnp.float32
    )


def early_kernel(turns, pieces, halves, feats, *refs):
    outs, second = refs[: turns * halves], refs[turns * halves : turns * halves + pieces]
    sends, grad = refs[turns * halves + pieces : -1], refs[-1]
    section = lax.axis_index("pipe")
    offsets = offsets_of(pieces)
    part = pieces // halves
    rows = outs[0].shape[1]
    total = None
    for turn in range(turns - 1):
        blocks = []
        for p in range(pieces):
            k, j = p // part, p % part
            block = jnp.where(
                section == 0, outs[turn * halves + k][j], outs[(turn + 1) * halves + k][j]
            )
            sends[offsets[p]][turn] = block
            blocks.append(block)
        share = grad_of(jnp.concatenate(blocks, axis=0), second, turn, rows, feats)
        total = share if total is None else total + share
    grad[...] = total


def settle_kernel(turns, pieces, halves, hops, feats, *refs):
    refs = list(refs)

    def take(count):
        taken, refs[:count] = refs[:count], []
        return taken

    before, now, second, early = take(halves), take(halves), take(pieces), take(pieces)
    early_grad = take(1)[0]
    late, own_grad, grads = take(pieces), take(1)[0], take(hops - 1)
    section_out = take(1)[0]
    rows_out, total, sem = take(3)
    section, seq, rep = lax.axis_index("pipe"), lax.axis_index("seq"), lax.axis_index("dp")
    offsets = offsets_of(pieces)
    part = pieces // halves
    rows, cols = early[0].shape[1:]
    for m in range(pieces):
        lanes = pl.ds(pl.multiple_of((seq ^ m) * cols, 128), cols)
        for turn in range(turns - 1):
            rows_out[turn, :, lanes] = early[m][turn]
    copy = pltpu.make_async_copy(rows_out, section_out.at[pl.ds(0, turns - 1)], sem)
    copy.start()
    blocks = []
    for p in range(pieces):
        block = jnp.where(section == 0, before[p // part][p % part], now[p // part][p % part])
        late[offsets[p]][...] = block
        blocks.append(block)
    share = grad_of(jnp.concatenate(blocks, axis=0), second, turns - 1, rows, feats)
    factor = float(turns * hops * rows * pieces) ** (-0.5)
    total[...] = (share + early_grad[...]) * factor
    g_rows = cols // hops
    own_grad[...] = total[pl.ds(pl.multiple_of(rep * g_rows, 8), g_rows)]
    for shift in range(1, hops):
        at = pl.multiple_of(lax.rem(rep + shift, hops) * g_rows, 8)
        grads[shift - 1][...] = total[pl.ds(at, g_rows)].astype(jnp.bfloat16)
    copy.wait()


def finish_kernel(pieces, hops, *refs):
    held, late, refs = refs[0], refs[1 : pieces + 1], refs[pieces + 1 :]
    own_grad, parts, (section_out, grad, row_out, sem) = refs[0], refs[1:hops], refs[hops:]
    seq = lax.axis_index("seq")
    cols = late[0].shape[1]
    for m in range(pieces):
        lanes = pl.ds(pl.multiple_of((seq ^ m) * cols, 128), cols)
        row_out[:, lanes] = late[m][...]
    copy = pltpu.make_async_copy(row_out, section_out.at[section_out.shape[0] - 1], sem)
    copy.start()
    total = own_grad[...]
    for part in parts:
        total = total + part[...].astype(jnp.float32)
    grad[...] = total
    copy.wait()


HALVES = 2
MIB = 1024 * 1024


def paired_body(
    incoming,
    contacts,
    keyframes,
    timesteps,
    w_query,
    w_keyval,
    norm_gain,
    time_freq,
    contact_table,
    key_bias,
    attn_gate,
    head_cotangent,
):
    seq_count = lax.axis_size("seq")
    hops = lax.axis_size("dp")
    rows, width, turns = incoming.shape[3], incoming.shape[4], incoming.shape[1]
    frames = rows * seq_count
    heads_all = key_bias.shape[1]
    head = width // heads_all
    heads = heads_all // seq_count
    kv_heads = w_keyval.shape[2] // (2 * head * seq_count)
    feats = head_cotangent.shape[4]
    cols = width // seq_count
    w_rows = w_query.shape[1]
    steps = turns + 1
    part = seq_count // HALVES
    kind = jnp.bfloat16
    smem = pl.BlockSpec(memory_space=pltpu.SMEM)
    vmem = pl.BlockSpec(memory_space=pltpu.VMEM)
    anywhere = pl.BlockSpec(memory_space=pl.ANY)
    shape = jax.ShapeDtypeStruct

    def call(kernel, name, out_shape, in_specs, operands, scratch=(), limit=4, flops=0, **options):
        return pl.pallas_call(
            kernel,
            out_shape=out_shape,
            in_specs=in_specs,
            scratch_shapes=list(scratch),
            compiler_params=pltpu.CompilerParams(vmem_limit_bytes=limit * MIB),
            cost_estimate=pl.CostEstimate(
                flops=flops, bytes_accessed=flops // 512, transcendentals=0
            ),
            name=name,
            **options,
        )(*operands)

    def pin(value, space=pltpu.VMEM):
        return pltpu.with_memory_space_constraint(value, space)

    packed = call(
        pack_kernel,
        "pack",
        [pltpu.VMEM((w_rows, 2 * cols), kind)] * seq_count,
        [anywhere, anywhere],
        [pin(w_query, pltpu.HBM), pin(w_keyval, pltpu.HBM)],
        [pltpu.SemaphoreType.DMA((2 * seq_count,))],
        out_specs=[vmem] * seq_count,
    )
    blocks = [packed[0]] + [swap(packed[m], m) for m in range(1, seq_count)]
    far = call(
        stack_kernel,
        "far",
        pltpu.VMEM((2, w_rows, 2 * cols), kind),
        [vmem, vmem],
        blocks[2:],
        out_specs=vmem,
    )
    rings = [[blocks[0]], [blocks[1]], [far]]
    for hop in range(1, hops):
        for ring in rings:
            ring.append(shifted(ring[-1], "dp", 1))

    def tie(values, deps):
        return call(
            tie_kernel,
            "tie",
            [shape(value.shape, kind) for value in values],
            [anywhere] * (len(values) + len(deps)),
            list(values) + list(deps),
            out_specs=[anywhere] * len(values),
            input_output_aliases={i: i for i in range(len(values))},
        )

    mine = call(
        functools.partial(first_kernel, turns),
        "first",
        pltpu.VMEM((2 * rows + 16, width), kind),
        [anywhere] * 3 + [vmem, vmem],
        [rings[0][1], rings[1][1], far, incoming, contacts],
        [pltpu.VMEM((16, 128), jnp.float32)],
        out_specs=vmem,
    )
    across = swap(mine, 2)
    beside = swap(mine, 1)
    (across,) = tie([across], [ring[-2] for ring in rings])
    first = [mine, across, beside, swap(across, 1)]
    mine = call(
        second_kernel,
        "second",
        pltpu.VMEM((2 * rows, width), kind),
        [anywhere, vmem, vmem],
        [across, incoming, head_cotangent],
        out_specs=vmem,
    )
    across = swap(mine, 2)
    second = [mine, across, swap(mine, 1), swap(across, 1)]

    prepared = call(
        functools.partial(norm_kernel, turns, seq_count),
        "norm",
        [pltpu.VMEM((frames, width), kind)] * 2
        + [pltpu.VMEM((frames, 128), jnp.float32)] * 2
        + [pltpu.VMEM((frames, cols), jnp.float32)] * 2
        + [pltpu.VMEM((frames, width), kind)] * 2,
        [smem] + [vmem] * (3 + seq_count) + [anywhere],
        [timesteps, contact_table, norm_gain, time_freq]
        + [pin(piece) for piece in first]
        + [rings[0][-1]],
        [pltpu.VMEM((1, width), jnp.float32)],
        8,
        out_specs=[vmem] * 8,
    )

    outputs = []
    relayed = {}
    weights = None
    for step in range(steps):
        cfg = {
            "step": step,
            "has_relay": step in relayed,
            "pieces": seq_count,
            "hops": hops,
            "head": head,
            "heads": heads,
            "group": heads // kv_heads,
            "turns": turns,
            "halves": HALVES,
        }
        operands = [key_bias, timesteps, norm_gain, time_freq, attn_gate, keyframes]
        scratch = [
            pltpu.VMEM((frames, 2 * cols + 128), kind),
            pltpu.VMEM((frames, cols), jnp.float32),
        ]
        if step in relayed:
            large = second + [prepared[4 + step]] + relayed[step]
            scratch += [
                pltpu.VMEM((frames, width), kind),
                pltpu.VMEM((frames, 128), jnp.float32),
                pltpu.VMEM((frames, cols), jnp.float32),
                pltpu.VMEM((1, width), jnp.float32),
            ]
        else:
            large = [prepared[step], prepared[2 + step], prepared[4 + step]]
        large += rings[0] + rings[1] + rings[2] if step == 0 else [weights]
        operands += [pin(value) for value in large]
        out_shape = [pltpu.VMEM((part, rows, cols), kind)] * HALVES
        if step == 0:
            out_shape += [pltpu.VMEM((width, 2 * cols), kind)]
        results = call(
            functools.partial(step_kernel, cfg),
            "step%d" % step,
            out_shape,
            [smem, smem] + [vmem] * (len(operands) - 2),
            operands,
            scratch,
            16,
            2 * frames * width * 2 * cols + 4 * heads * frames * frames * head,
            out_specs=[vmem] * len(out_shape),
        )
        outputs.append(list(results[:HALVES]))
        if step == 0:
            weights = results[HALVES]
        if step == 2:
            pending = [piece for k in range(HALVES) for piece in (crossing[k][0], crossing[k][1])]
            tied = tie(pending, [outputs[-1][0]])
            relayed[3] = []
            for k in range(HALVES):
                mine, across = tied[2 * k], tied[2 * k + 1]
                relayed[3] += [mine, across, swap(mine, 1), swap(across, 1)]
            early = call(
                functools.partial(early_kernel, turns, seq_count, HALVES, feats),
                "early",
                [shape((turns - 1, rows, cols), kind)] * seq_count
                + [shape((cols, feats), jnp.float32)],
                [vmem] * (turns * HALVES + seq_count),
                [half for output in outputs for half in output] + second,
                limit=8,
                out_specs=[vmem] * (seq_count + 1),
            )
            early, early_grad = list(early[:-1]), early[-1]
            early = [early[0]] + [swap(early[m], m) for m in range(1, seq_count)]
        if step + 2 < steps:
            pieces = [passed_along(half, "pipe", 1) for half in outputs[-1]]
            crossing = [(piece, swap(piece, 2)) for piece in pieces]
            if step == 0:
                relayed[2] = []
                for mine, across in crossing:
                    relayed[2] += [mine, across, swap(mine, 1), swap(across, 1)]

    g_shape = (cols // hops, feats)
    operands = outputs[-2] + outputs[-1] + second + early + [early_grad]
    settled = call(
        functools.partial(settle_kernel, turns, seq_count, HALVES, hops, feats),
        "settle",
        [shape((rows, cols), kind)] * seq_count
        + [shape(g_shape, jnp.float32)]
        + [shape(g_shape, kind)] * (hops - 1)
        + [shape((turns, rows, width), kind)],
        [vmem] * len(operands),
        operands,
        [
            pltpu.VMEM((turns - 1, rows, width), kind),
            pltpu.VMEM((cols, feats), jnp.float32),
            pltpu.SemaphoreType.DMA,
        ],
        8,
        out_specs=[vmem] * (seq_count + hops) + [anywhere],
    )
    late, grads, held = settled[:seq_count], settled[seq_count:-1], settled[-1]
    late = [late[0]] + [swap(late[m], m) for m in range(1, seq_count)]
    grads = [grads[0]] + [shifted(grads[k], "dp", k) for k in range(1, hops)]
    section_out, grad_rows = call(
        functools.partial(finish_kernel, seq_count, hops),
        "finish",
        [shape((turns, rows, width), kind), shape(g_shape, jnp.float32)],
        [anywhere] + [vmem] * (seq_count + hops),
        [held] + late + grads,
        [pltpu.VMEM((rows, width), kind), pltpu.SemaphoreType.DMA],
        out_specs=[anywhere, vmem],
        input_output_aliases={0: 0},
    )
    return (section_out[None, :, None], grad_rows[None])


def body(incoming, contacts, keyframes, timesteps, w_query, *others):
    count = lax.axis_size("seq")
    cols = w_query.shape[2] // count
    paired = (
        lax.axis_size("pipe") == 2
        and count == 4
        and cols % 128 == 0
        and w_query.shape[1] % 16 == 0
        and incoming.shape[3] == 128
        and incoming.shape[1] == 3
    )
    chosen = paired_body if paired else general_body
    return chosen(incoming, contacts, keyframes, timesteps, w_query, *others)


def general_body(
    incoming,
    contacts,
    keyframes,
    timesteps,
    w_query,
    w_keyval,
    norm_gain,
    time_freq,
    contact_table,
    key_bias,
    attn_gate,
    head_cotangent,
):
    section_idx = lax.axis_index("pipe")
    seq_idx = lax.axis_index("seq")
    rep_idx = lax.axis_index("dp")
    seq_count = lax.axis_size("seq")
    section_count = lax.axis_size("pipe")
    rep_count = lax.axis_size("dp")
    tok_rows = incoming.shape[3]
    width = incoming.shape[4]
    turns = incoming.shape[1]
    frames = tok_rows * seq_count
    heads_all = key_bias.shape[1]
    head_size = width // heads_all
    heads_local = heads_all // seq_count
    kv_width = w_keyval.shape[2]
    kv_local = kv_width // (2 * head_size * seq_count)
    group_size = heads_local // kv_local
    feat_count = head_cotangent.shape[4]
    score_scale = head_size ** (-0.5)
    q_cols = width // seq_count
    kv_cols = kv_width // seq_count
    w_rows = w_query.shape[1]

    w_parts = jnp.concatenate(
        [
            w_query[0].reshape(w_rows, seq_count, q_cols),
            w_keyval[0].reshape(w_rows, seq_count, kv_cols),
        ],
        axis=2,
    ).transpose(1, 0, 2)
    block = lax.all_to_all(w_parts, "seq", split_axis=0, concat_axis=0, tiled=True)
    weights = jnp.zeros((seq_count, rep_count, w_rows, q_cols + kv_cols), jnp.bfloat16)
    for hop in range(rep_count):
        owner = lax.rem(rep_idx + rep_count - hop, rep_count)
        weights = lax.dynamic_update_slice_in_dim(weights, block[:, None], owner, 1)
        if hop + 1 < rep_count:
            block = ring(block, "dp")
    weights = weights.reshape(width, q_cols + kv_cols)

    gain_row = norm_gain[0]
    freq_row = time_freq[0]
    table = contact_table[0]
    gate_local = lax.dynamic_slice_in_dim(attn_gate[0], seq_idx * q_cols, q_cols)
    table_local = lax.dynamic_slice_in_dim(table, seq_idx * q_cols, q_cols, 1)
    bias_local = lax.dynamic_slice_in_dim(key_bias[0], seq_idx * heads_local, heads_local)
    contact_all = lax.all_gather(contacts[:, 0, :], "seq", axis=1, tiled=True)
    key_all = keyframes[:, 0, :]
    step_all = timesteps[:, 0]
    labels = jnp.arange(table.shape[0], dtype=jnp.int32)
    cot_all = lax.all_gather(head_cotangent[0, :, 0], "seq", axis=1, tiled=True)

    lag = 2 if section_count == 2 else 1
    if lag == 2:
        steps = turns + 1
    else:
        steps = turns

    def turn_at(step):
        if lag == 1:
            return jnp.int32(step)
        return jnp.clip(step - section_idx, 0, turns - 1)

    outputs = []
    handed = {}
    for step in range(steps):
        turn = turn_at(step)
        fresh = lax.dynamic_index_in_dim(incoming[0, :, 0], turn, 0, keepdims=False)
        current = lax.all_gather(fresh, "seq", axis=0, tiled=True)
        if step in handed:
            current = jnp.where((section_idx == 0) | (turn == 0), current, handed[step])
        batch_idx = turn - section_idx + section_count - 1
        contact_rows = lax.dynamic_index_in_dim(contact_all, batch_idx, 0, keepdims=False)
        key_flags = lax.dynamic_index_in_dim(key_all, batch_idx, 0, keepdims=False).astype(
            jnp.float32
        )
        timestep = lax.dynamic_index_in_dim(step_all, batch_idx, 0, keepdims=False).astype(
            jnp.float32
        )
        onehot = (contact_rows[:, None] == labels[None, :]).astype(jnp.bfloat16)
        hidden = current.astype(jnp.float32) + jnp.dot(
            onehot, table, preferred_element_type=jnp.float32
        )
        root_mean = jnp.sqrt(jnp.mean(hidden * hidden, axis=-1, keepdims=True) + epsilon)
        modulation = gain_row * (1.0 + 0.5 * jnp.sin(timestep * freq_row))
        normed = (hidden / root_mean * modulation[None, :]).astype(jnp.bfloat16)
        projected = jnp.dot(normed, weights, preferred_element_type=jnp.float32).astype(
            jnp.bfloat16
        )
        query_heads = projected[:, :q_cols].reshape(frames, heads_local, head_size)
        keyval_heads = projected[:, q_cols:].reshape(frames, kv_local, 2, head_size)
        head_outputs = []
        for head in range(heads_local):
            key_rows = keyval_heads[:, head // group_size, 0]
            value_rows = keyval_heads[:, head // group_size, 1]
            scores = (
                lax.dot_general(
                    query_heads[:, head],
                    key_rows,
                    (((1,), (1,)), ((), ())),
                    preferred_element_type=jnp.float32,
                )
                * score_scale
            )
            scores = scores + bias_local[head] * key_flags[None, :]
            row_max = jnp.max(scores, axis=-1, keepdims=True)
            exponent = jnp.exp(scores - row_max)
            probabilities = (exponent / jnp.sum(exponent, axis=-1, keepdims=True)).astype(
                jnp.bfloat16
            )
            head_outputs.append(
                jnp.dot(probabilities, value_rows, preferred_element_type=jnp.float32).astype(
                    jnp.bfloat16
                )
            )
        attended = jnp.concatenate(head_outputs, axis=1)
        hidden_local = lax.dynamic_slice_in_dim(current, seq_idx * q_cols, q_cols, 1).astype(
            jnp.float32
        ) + jnp.dot(onehot, table_local, preferred_element_type=jnp.float32)
        output = (hidden_local + gate_local[None, :] * attended.astype(jnp.float32)).astype(
            jnp.bfloat16
        )
        outputs.append(output)
        if step + lag < steps:
            piece = passed_along(output, "pipe", 1)
            handed[step + lag] = lax.all_gather(piece, "seq", axis=1, tiled=True)

    factor = float(turns * rep_count * frames) ** (-0.5)
    total = None
    rows_out = []
    for turn in range(turns):
        if lag == 2:
            own = jnp.where(section_idx == 0, outputs[turn], outputs[turn + 1])
        else:
            own = outputs[turn]
        term = lax.dot_general(
            own, cot_all[turn], (((0,), (0,)), ((), ())), preferred_element_type=jnp.float32
        )
        total = term if total is None else total + term
        rows_out.append(lax.all_to_all(own, "seq", split_axis=0, concat_axis=1, tiled=True))
    section_out = jnp.stack(rows_out)[None, :, None]
    grad_parts = lax.all_to_all(
        (total * factor).astype(jnp.bfloat16).reshape(rep_count, q_cols // rep_count, feat_count),
        "dp",
        split_axis=0,
        concat_axis=0,
        tiled=True,
    )
    grad_rows = jnp.sum(grad_parts.astype(jnp.float32), axis=0)
    return (section_out, grad_rows[None])


def solution(mesh):
    in_specs = (
        P("pipe", None, "dp", "seq", None),
        P(None, "dp", "seq"),
        P(None, "dp", None),
        P(None, "dp"),
        P("pipe", ("seq", "dp"), None),
        P("pipe", ("seq", "dp"), None),
        P("pipe", None),
        P("pipe", None),
        P("pipe", None, None),
        P("pipe", None),
        P("pipe", None),
        P("pipe", None, "dp", "seq", None),
    )
    out_specs = (P("pipe", None, "dp", "seq", None), P("pipe", ("seq", "dp"), None))
    return jax.shard_map(body, mesh=mesh, in_specs=in_specs, out_specs=out_specs, check_vma=False)
```

```python
import functools
import math

import jax
import jax.numpy as jnp
from jax import lax
from jax.experimental import pallas as pl
from jax.experimental.pallas import tpu as pltpu
from jax.sharding import PartitionSpec as P

epsilon = 1e-06


def passed_along(value, axis, steps):
    count = lax.axis_size(axis)
    first, last = (max(0, -steps), min(count, count - steps))
    return lax.ppermute(value, axis, [(source, source + steps) for source in range(first, last)])


def ring(value, axis):
    count = lax.axis_size(axis)
    return lax.ppermute(value, axis, [(source, (source + 1) % count) for source in range(count)])


def swap(value, bit):
    count = lax.axis_size("seq")
    return lax.ppermute(value, "seq", [(source, source ^ bit) for source in range(count)])


def shifted(value, axis, shift):
    count = lax.axis_size(axis)
    return lax.ppermute(value, axis, [(source, (source + shift) % count) for source in range(count)])


def offsets_of(count):
    offsets = [0]
    bit = count // 2
    while bit:
        offsets = offsets + [offset ^ bit for offset in offsets]
        bit //= 2
    return offsets


def turn_and_batch(step, turns):
    section = lax.axis_index("pipe")
    turn = jnp.clip(step - section, 0, turns - 1)
    return turn, turn - section + 1


def pack_kernel(wq, wkv, *refs):
    outs, sems = refs[:-1], refs[-1]
    cols = outs[0].shape[1] // 2
    seq = lax.axis_index("seq")
    copies = []
    for m, out in enumerate(outs):
        start = pl.multiple_of((seq ^ m) * cols, 128)
        for k, source in enumerate((wq, wkv)):
            copies.append(
                pltpu.make_async_copy(
                    source.at[0, :, pl.ds(start, cols)],
                    out.at[:, pl.ds(k * cols, cols)],
                    sems.at[2 * m + k],
                )
            )
    for copy in copies:
        copy.start()
    for copy in copies:
        copy.wait()


def stack_kernel(deps, *refs):
    out = refs[-1]
    at = 0
    for ref in refs[deps:-1]:
        if len(ref.shape) == 2:
            out[at] = ref[...]
            at += 1
        else:
            out[at : at + ref.shape[0]] = ref[...]
            at += ref.shape[0]


def place_kernel(hop, hops, *refs):
    weights, parts = refs[-1], refs[:-1]
    if hop > 0:
        parts = parts[:-1]
    place(hop, hops, parts, weights)


def place(hop, hops, parts, weights):
    seq, rep = lax.axis_index("seq"), lax.axis_index("dp")
    m = 0
    for part in parts:
        count, rows = part.shape[:2]
        for j in range(count):
            block = (seq ^ m) * hops + lax.rem(rep + hops - hop, hops)
            weights[pl.ds(pl.multiple_of(block * rows, 16), rows)] = part[j]
            m += 1


def first_kernel(turns, far, incoming, contacts, out, states):
    rows = incoming.shape[3]
    for turn in range(2):
        out[turn * rows : (turn + 1) * rows] = incoming[0, turn, 0]
    states[...] = jnp.zeros_like(states)
    for step in range(turns + 1):
        _, batch = turn_and_batch(step, turns)
        states[step : step + 1] = contacts[batch].astype(jnp.float32)
    out[2 * rows :, : states.shape[1]] = states[...].astype(jnp.bfloat16)


def second_kernel(dep, incoming, cotangent, out):
    turns, rows, feats = cotangent.shape[1], cotangent.shape[3], cotangent.shape[4]
    out[:rows] = incoming[0, 2, 0]
    for turn in range(turns):
        out[rows:, turn * feats : (turn + 1) * feats] = cotangent[0, turn, 0]


def columns_of(rows_of, pieces, rows):
    labels = lax.broadcasted_iota(jnp.int32, (32, rows), 0)
    columns = []
    for i in range(pieces):
        state, flag = rows_of(i)
        one = jnp.zeros((32, rows), jnp.float32)
        if state is not None:
            one = jnp.where(labels == state, 1.0, 0.0)
        if flag is not None:
            one = jnp.where(labels == 16, flag, one)
        columns.append(one.T)
    return jnp.concatenate(columns, axis=0)


def modulation(step, turns, times, gain, freq):
    _, batch = turn_and_batch(step, turns)
    return gain[...] * (1.0 + 0.5 * jnp.sin(times[batch, 0].astype(jnp.float32) * freq[...]))


def norm_kernel(turns, pieces, times, table, gain, freq, *refs):
    sources, refs = refs[:pieces], refs[pieces:]
    scaled, scales, owns, embeds, mod = refs[0:2], refs[2:4], refs[4:6], refs[6:8], refs[8]
    first, sems = refs[9 : 9 + pieces], refs[9 + pieces]
    copies = [
        pltpu.make_async_copy(sources[i], first[i], sems.at[i]) for i in range(pieces)
    ]
    for copy in copies:
        copy.start()
    for copy in copies:
        copy.wait()
    frames, width = scaled[0].shape
    rows, cols = frames // pieces, owns[0].shape[1]
    seq = lax.axis_index("seq")
    offsets = offsets_of(pieces)
    for step in range(turns + 1):

        def state_of(i):
            state = first[i][2 * rows : 2 * rows + 16, :rows][step : step + 1]
            return state.astype(jnp.float32).astype(jnp.int32), None

        onehot = columns_of(state_of, pieces, rows)[:, : table.shape[1]].astype(jnp.bfloat16)
        if step >= 2:
            for at in range(0, width, 256):
                embeds[step - 2][:, at : at + 256] = jnp.dot(
                    onehot, table[0, :, at : at + 256], preferred_element_type=jnp.float32
                ).astype(jnp.bfloat16)
            continue
        turn, _ = turn_and_batch(step, turns)
        at = pl.multiple_of(jnp.minimum(turn, 1) * rows, 128)
        mod[...] = modulation(step, turns, times, gain, freq)
        total = jnp.zeros((frames, 128), jnp.float32)
        for i in range(pieces):
            lanes = pl.ds(pl.multiple_of((seq ^ offsets[i]) * cols, 128), cols)
            current = jnp.concatenate([first[p][pl.ds(at, rows), lanes] for p in range(pieces)])
            hidden = current.astype(jnp.float32) + jnp.dot(
                onehot, table[0, :, lanes], preferred_element_type=jnp.float32
            )
            for lane in range(0, cols, 128):
                piece = hidden[:, lane : lane + 128]
                total = total + piece * piece
            scaled[step][:, lanes] = (hidden * mod[:, lanes]).astype(jnp.bfloat16)
            if i == 0:
                owns[step][...] = hidden
        mean = jnp.sum(total, axis=1, keepdims=True) * (1.0 / width)
        scales[step][...] = jnp.broadcast_to(lax.rsqrt(mean + epsilon), (frames, 128))


def step_kernel(cfg, *refs):
    step, has_relay = cfg["step"], cfg["has_relay"]
    pieces, hops, head, turns = cfg["pieces"], cfg["hops"], cfg["head"], cfg["turns"]
    heads, group, halves = cfg["heads"], cfg["group"], cfg["halves"]
    refs = list(refs)

    def take(count):
        taken, refs[:count] = refs[:count], []
        return taken

    bias, times, gain, freq, gate, flags = take(6)
    if has_relay:
        second, embed, relay = take(pieces), take(1)[0], take(pieces * halves)
    else:
        scaled, scales, own_hidden = take(3)
    chunk = take(1) if step == 0 else None
    weights = take(1)[0]
    outs = take(halves)
    if step == 0:
        weights = take(1)[0]
    proj, att = take(2)
    if has_relay:
        scaled, scales, own_hidden, mod = take(4)
    offsets = offsets_of(pieces)
    frames, width = scaled.shape
    rows, cols = frames // pieces, att.shape[1]
    part = pieces // halves
    seq, rep, section = lax.axis_index("seq"), lax.axis_index("dp"), lax.axis_index("pipe")
    _, batch = turn_and_batch(step, turns)

    if step == 0:
        place(hops - 1, hops, chunk, weights)

    def normalize(relayed):
        total = jnp.zeros((frames, 128), jnp.float32)
        for i in range(pieces):
            lanes = pl.ds(pl.multiple_of((seq ^ offsets[i]) * cols, 128), cols)
            blocks = []
            for p in range(pieces):
                if relayed:
                    j = offsets.index(offsets[i] ^ offsets[p])
                    blocks.append(relay[(j // part) * pieces + i][j % part])
                else:
                    blocks.append(second[p][:rows, lanes])
            hidden = jnp.concatenate(blocks, axis=0).astype(jnp.float32)
            hidden = hidden + embed[:, lanes].astype(jnp.float32)
            for lane in range(0, cols, 128):
                piece = hidden[:, lane : lane + 128]
                total = total + piece * piece
            scaled[:, lanes] = (hidden * mod[:, lanes]).astype(jnp.bfloat16)
            if i == 0:
                own_hidden[...] = hidden
        scales[...] = total

    if has_relay:
        mod[...] = modulation(step, turns, times, gain, freq)

        @pl.when(section == 0)
        def _():
            normalize(False)

        @pl.when(section != 0)
        def _():
            normalize(True)

        mean = jnp.sum(scales[...], axis=1, keepdims=True) * (1.0 / width)
        scale = lax.rsqrt(mean + epsilon)
    else:
        scale = scales[:, :1]

    def flag_of(i):
        lanes = pl.ds(pl.multiple_of((seq ^ offsets[i]) * rows, 128), rows)
        return None, flags[batch, :, lanes].astype(jnp.float32)

    flag_column = columns_of(flag_of, pieces, rows)[:, 16:17]
    projected = jnp.dot(scaled[...], weights[...], preferred_element_type=jnp.float32) * scale
    score_scale = head ** (-0.5) * math.log2(math.e)
    proj[:, :cols] = (projected[:, :cols] * score_scale).astype(jnp.bfloat16)
    proj[:, cols : 2 * cols] = projected[:, cols:].astype(jnp.bfloat16)
    proj[:, 2 * cols :] = jnp.zeros((frames, 128), jnp.bfloat16)
    lanes = lax.broadcasted_iota(jnp.int32, (frames, 128), 1)
    row_lanes = lax.broadcasted_iota(jnp.int32, (1, 128), 1)
    flag_lanes = jnp.logical_or(lanes == head, lanes == head + 1)

    def part_of(at):
        return proj[:, at : at + 128].astype(jnp.float32)

    keys, values = [], []
    for kv in range(heads // group):
        base = cols + kv * 2 * head
        key = jnp.where(flag_lanes, flag_column, jnp.where(lanes < head, part_of(base), 0.0))
        value = jnp.where(lanes < head, part_of(base + head), jnp.where(lanes == head, 1.0, 0.0))
        keys.append(key.astype(jnp.bfloat16))
        values.append(value.astype(jnp.bfloat16))

    def scores_of(h):
        strength = jnp.zeros((1, 128), jnp.float32) + bias[0, seq * heads + h] * math.log2(math.e)
        coarse = strength.astype(jnp.bfloat16).astype(jnp.float32)
        tail = jnp.where(
            row_lanes == head, coarse, jnp.where(row_lanes == head + 1, strength - coarse, 0.0)
        )
        query = jnp.where(lanes < head, part_of(h * head), tail).astype(jnp.bfloat16)
        return lax.dot_general(
            query, keys[h // group], (((1,), (1,)), ((), ())), preferred_element_type=jnp.float32
        )

    scores = scores_of(0)
    for h in range(heads):
        ahead = scores_of(h + 1) if h + 1 < heads else None
        top = jnp.max(scores, axis=1, keepdims=True)
        weight = jnp.exp2(scores - top).astype(jnp.bfloat16)
        mixed = jnp.dot(weight, values[h // group], preferred_element_type=jnp.float32)
        att[:, h * head : (h + 1) * head] = mixed[:, :head] * (1.0 / mixed[:, head : head + 1])
        scores = ahead
    own = pl.ds(pl.multiple_of(seq * cols, 128), cols)
    attended = att[...].astype(jnp.bfloat16).astype(jnp.float32)
    output = (own_hidden[...] + gate[:, own] * attended).astype(jnp.bfloat16)
    blocks = output.reshape(pieces, rows, cols)
    for k in range(halves):
        outs[k][...] = blocks[k * part : (k + 1) * part]


def tie_kernel(*refs):
    pass


def grad_of(output, second, turn, rows, feats):
    cot = jnp.concatenate(
        [piece[rows : 2 * rows, turn * feats : (turn + 1) * feats] for piece in second], axis=0
    )
    return lax.dot_general(
        output, cot, (((0,), (0,)), ((), ())), preferred_element_type=jnp.float32
    )


def early_kernel(turns, pieces, halves, feats, *refs):
    outs, second = refs[: turns * halves], refs[turns * halves : turns * halves + pieces]
    sends, grad = refs[turns * halves + pieces : -1], refs[-1]
    section = lax.axis_index("pipe")
    offsets = offsets_of(pieces)
    part = pieces // halves
    rows = outs[0].shape[1]
    total = None
    for turn in range(turns - 1):
        blocks = []
        for p in range(pieces):
            k, j = p // part, p % part
            block = jnp.where(
                section == 0, outs[turn * halves + k][j], outs[(turn + 1) * halves + k][j]
            )
            sends[offsets[p]][turn] = block
            blocks.append(block)
        share = grad_of(jnp.concatenate(blocks, axis=0), second, turn, rows, feats)
        total = share if total is None else total + share
    grad[...] = total


def settle_kernel(turns, pieces, halves, hops, feats, *refs):
    refs = list(refs)

    def take(count):
        taken, refs[:count] = refs[:count], []
        return taken

    before, now, second, early = take(halves), take(halves), take(pieces), take(pieces)
    early_grad = take(1)[0]
    late, own_grad, grads = take(pieces), take(1)[0], take(hops - 1)
    section_out = take(1)[0]
    rows_out, total, sem = take(3)
    section, seq, rep = lax.axis_index("pipe"), lax.axis_index("seq"), lax.axis_index("dp")
    offsets = offsets_of(pieces)
    part = pieces // halves
    rows, cols = early[0].shape[1:]
    for m in range(pieces):
        lanes = pl.ds(pl.multiple_of((seq ^ m) * cols, 128), cols)
        for turn in range(turns - 1):
            rows_out[turn, :, lanes] = early[m][turn]
    copy = pltpu.make_async_copy(rows_out, section_out.at[pl.ds(0, turns - 1)], sem)
    copy.start()
    blocks = []
    for p in range(pieces):
        block = jnp.where(section == 0, before[p // part][p % part], now[p // part][p % part])
        late[offsets[p]][...] = block
        blocks.append(block)
    share = grad_of(jnp.concatenate(blocks, axis=0), second, turns - 1, rows, feats)
    factor = float(turns * hops * rows * pieces) ** (-0.5)
    total[...] = (share + early_grad[...]) * factor
    g_rows = cols // hops
    own_grad[...] = total[pl.ds(pl.multiple_of(rep * g_rows, 8), g_rows)]
    for shift in range(1, hops):
        at = pl.multiple_of(lax.rem(rep + shift, hops) * g_rows, 8)
        grads[shift - 1][...] = total[pl.ds(at, g_rows)].astype(jnp.bfloat16)
    copy.wait()


def finish_kernel(pieces, hops, *refs):
    held, late, refs = refs[0], refs[1 : pieces + 1], refs[pieces + 1 :]
    own_grad, parts, (section_out, grad, row_out, sem) = refs[0], refs[1:hops], refs[hops:]
    seq = lax.axis_index("seq")
    cols = late[0].shape[1]
    for m in range(pieces):
        lanes = pl.ds(pl.multiple_of((seq ^ m) * cols, 128), cols)
        row_out[:, lanes] = late[m][...]
    copy = pltpu.make_async_copy(row_out, section_out.at[section_out.shape[0] - 1], sem)
    copy.start()
    total = own_grad[...]
    for part in parts:
        total = total + part[...].astype(jnp.float32)
    grad[...] = total
    copy.wait()


HALVES = 1
MIB = 1024 * 1024


def paired_body(
    incoming,
    contacts,
    keyframes,
    timesteps,
    w_query,
    w_keyval,
    norm_gain,
    time_freq,
    contact_table,
    key_bias,
    attn_gate,
    head_cotangent,
):
    seq_count = lax.axis_size("seq")
    hops = lax.axis_size("dp")
    rows, width, turns = incoming.shape[3], incoming.shape[4], incoming.shape[1]
    frames = rows * seq_count
    heads_all = key_bias.shape[1]
    head = width // heads_all
    heads = heads_all // seq_count
    kv_heads = w_keyval.shape[2] // (2 * head * seq_count)
    feats = head_cotangent.shape[4]
    cols = width // seq_count
    w_rows = w_query.shape[1]
    steps = turns + 1
    part = seq_count // HALVES
    kind = jnp.bfloat16
    smem = pl.BlockSpec(memory_space=pltpu.SMEM)
    vmem = pl.BlockSpec(memory_space=pltpu.VMEM)
    anywhere = pl.BlockSpec(memory_space=pl.ANY)
    shape = jax.ShapeDtypeStruct

    def call(kernel, name, out_shape, in_specs, operands, scratch=(), limit=4, flops=0, **options):
        return pl.pallas_call(
            kernel,
            out_shape=out_shape,
            in_specs=in_specs,
            scratch_shapes=list(scratch),
            compiler_params=pltpu.CompilerParams(vmem_limit_bytes=limit * MIB),
            cost_estimate=pl.CostEstimate(
                flops=flops, bytes_accessed=flops // 512, transcendentals=0
            ),
            name=name,
            **options,
        )(*operands)

    def pin(value, space=pltpu.VMEM):
        return pltpu.with_memory_space_constraint(value, space)

    packed = call(
        pack_kernel,
        "pack",
        [pltpu.VMEM((w_rows, 2 * cols), kind)] * seq_count,
        [anywhere, anywhere],
        [pin(w_query, pltpu.HBM), pin(w_keyval, pltpu.HBM)],
        [pltpu.SemaphoreType.DMA((2 * seq_count,))],
        out_specs=[vmem] * seq_count,
    )
    blocks = [packed[0]] + [swap(packed[m], m) for m in range(1, seq_count)]

    def stacked(name, count, deps, values):
        return call(
            functools.partial(stack_kernel, len(deps)),
            name,
            pltpu.VMEM((count, w_rows, 2 * cols), kind),
            [anywhere] * len(deps) + [vmem] * len(values),
            deps + values,
            out_specs=vmem,
        )

    weights = None

    def placed(hop, parts):
        operands = [pin(part) for part in parts] + ([pin(weights)] if hop else [])
        return call(
            functools.partial(place_kernel, hop, hops),
            "place%d" % hop,
            pltpu.VMEM((width, 2 * cols), kind),
            [vmem] * len(operands),
            operands,
            out_specs=vmem,
            input_output_aliases={len(parts): 0} if hop else {},
        )

    near = stacked("near", 2, [], blocks[:2])
    near_next = shifted(near, "dp", 1)
    far = stacked("far", 2, [near_next], blocks[2:])
    far_next = shifted(far, "dp", 1)
    weights = placed(0, [near, far])
    chunk = stacked("whole", seq_count, [], [near_next, far_next])
    weights = placed(1, [chunk])
    for hop in range(2, hops):
        chunk = shifted(chunk, "dp", 1)
        if hop + 1 < hops:
            weights = placed(hop, [chunk])
            late_chunk = chunk

    def tie(values, deps):
        return call(
            tie_kernel,
            "tie",
            [shape(value.shape, kind) for value in values],
            [anywhere] * (len(values) + len(deps)),
            list(values) + list(deps),
            out_specs=[anywhere] * len(values),
            input_output_aliases={i: i for i in range(len(values))},
        )

    mine = call(
        functools.partial(first_kernel, turns),
        "first",
        pltpu.VMEM((2 * rows + 16, width), kind),
        [anywhere, vmem, vmem],
        [far, incoming, contacts],
        [pltpu.VMEM((16, 128), jnp.float32)],
        out_specs=vmem,
    )
    across = swap(mine, 2)
    beside = swap(mine, 1)
    (across,) = tie([across], [late_chunk])
    first = [mine, across, beside, swap(across, 1)]
    prepared = call(
        functools.partial(norm_kernel, turns, seq_count),
        "norm",
        [pltpu.VMEM((frames, width), kind)] * 2
        + [pltpu.VMEM((frames, 128), jnp.float32)] * 2
        + [pltpu.VMEM((frames, cols), jnp.float32)] * 2
        + [pltpu.VMEM((frames, width), kind)] * 2,
        [smem] + [vmem] * 3 + [anywhere] * seq_count,
        [timesteps, contact_table, norm_gain, time_freq]
        + [pin(piece, pltpu.HBM) for piece in first],
        [pltpu.VMEM((1, width), jnp.float32)]
        + [pltpu.VMEM((2 * rows + 16, width), kind)] * seq_count
        + [pltpu.SemaphoreType.DMA((seq_count,))],
        12,
        out_specs=[vmem] * 8,
    )

    mine = call(
        second_kernel,
        "second",
        pltpu.VMEM((2 * rows, width), kind),
        [anywhere, vmem, vmem],
        [prepared[2], incoming, head_cotangent],
        out_specs=vmem,
    )
    across = swap(mine, 2)
    second = [mine, across, swap(mine, 1), swap(across, 1)]

    outputs = []
    relayed = {}
    handed = []
    for step in range(steps):
        cfg = {
            "step": step,
            "has_relay": step in relayed,
            "pieces": seq_count,
            "hops": hops,
            "head": head,
            "heads": heads,
            "group": heads // kv_heads,
            "turns": turns,
            "halves": HALVES,
        }
        operands = [key_bias, timesteps, norm_gain, time_freq, attn_gate, keyframes]
        scratch = [
            pltpu.VMEM((frames, 2 * cols + 128), kind),
            pltpu.VMEM((frames, cols), jnp.float32),
        ]
        if step in relayed:
            large = second + [prepared[4 + step]] + relayed[step]
            scratch += [
                pltpu.VMEM((frames, width), kind),
                pltpu.VMEM((frames, 128), jnp.float32),
                pltpu.VMEM((frames, cols), jnp.float32),
                pltpu.VMEM((1, width), jnp.float32),
            ]
        else:
            large = [prepared[step], prepared[2 + step], prepared[4 + step]]
        large += [chunk, weights] if step == 0 else [weights]
        operands += [pin(value) for value in large]
        out_shape = [pltpu.VMEM((part, rows, cols), kind)] * HALVES
        if step == 0:
            out_shape += [pltpu.VMEM((width, 2 * cols), kind)]
        results = call(
            functools.partial(step_kernel, cfg),
            "step%d" % step,
            out_shape,
            [smem, smem] + [vmem] * (len(operands) - 2),
            operands,
            scratch,
            16,
            2 * frames * width * 2 * cols + 4 * heads * frames * frames * head,
            out_specs=[vmem] * len(out_shape),
            input_output_aliases={len(operands) - 1: HALVES} if step == 0 else {},
        )
        outputs.append(list(results[:HALVES]))
        if step == 0:
            weights = results[HALVES]
        if step == 2:
            pending = [piece for k in range(HALVES) for piece in (crossing[k][0], crossing[k][1])]
            tied = tie(pending, [outputs[-1][0]])
            relayed[3] = []
            for k in range(HALVES):
                mine, across = tied[2 * k], tied[2 * k + 1]
                relayed[3] += [mine, across, swap(mine, 1), swap(across, 1)]
            early = call(
                functools.partial(early_kernel, turns, seq_count, HALVES, feats),
                "early",
                [shape((turns - 1, rows, cols), kind)] * seq_count
                + [shape((cols, feats), jnp.float32)],
                [vmem] * (turns * HALVES + seq_count),
                [half for output in outputs for half in output] + second,
                limit=8,
                out_specs=[vmem] * (seq_count + 1),
            )
            early, early_grad = list(early[:-1]), early[-1]
            early = [early[0]] + [swap(early[m], m) for m in range(1, seq_count)]
        if step + 2 < steps:
            handed.append([passed_along(half, "pipe", 1) for half in outputs[-1]])
        if step == 1:
            relayed[2] = []
            for piece in tie(handed[0], [outputs[-1][0]]):
                across = swap(piece, 2)
                relayed[2] += [piece, across, swap(piece, 1), swap(across, 1)]
            crossing = [(piece, swap(piece, 2)) for piece in handed[1]]

    g_shape = (cols // hops, feats)
    operands = outputs[-2] + outputs[-1] + second + early + [early_grad]
    settled = call(
        functools.partial(settle_kernel, turns, seq_count, HALVES, hops, feats),
        "settle",
        [shape((rows, cols), kind)] * seq_count
        + [shape(g_shape, jnp.float32)]
        + [shape(g_shape, kind)] * (hops - 1)
        + [shape((turns, rows, width), kind)],
        [vmem] * len(operands),
        operands,
        [
            pltpu.VMEM((turns - 1, rows, width), kind),
            pltpu.VMEM((cols, feats), jnp.float32),
            pltpu.SemaphoreType.DMA,
        ],
        8,
        out_specs=[vmem] * (seq_count + hops) + [anywhere],
    )
    late, grads, held = settled[:seq_count], settled[seq_count:-1], settled[-1]
    late = [late[0]] + [swap(late[m], m) for m in range(1, seq_count)]
    grads = [grads[0]] + [shifted(grads[k], "dp", k) for k in range(1, hops)]
    section_out, grad_rows = call(
        functools.partial(finish_kernel, seq_count, hops),
        "finish",
        [shape((turns, rows, width), kind), shape(g_shape, jnp.float32)],
        [anywhere] + [vmem] * (seq_count + hops),
        [held] + late + grads,
        [pltpu.VMEM((rows, width), kind), pltpu.SemaphoreType.DMA],
        out_specs=[anywhere, vmem],
        input_output_aliases={0: 0},
    )
    return (section_out[None, :, None], grad_rows[None])


def body(incoming, contacts, keyframes, timesteps, w_query, *others):
    count = lax.axis_size("seq")
    cols = w_query.shape[2] // count
    paired = (
        lax.axis_size("pipe") == 2
        and count == 4
        and cols % 128 == 0
        and w_query.shape[1] % 16 == 0
        and incoming.shape[3] == 128
        and incoming.shape[1] == 3
    )
    chosen = paired_body if paired else general_body
    return chosen(incoming, contacts, keyframes, timesteps, w_query, *others)


def general_body(
    incoming,
    contacts,
    keyframes,
    timesteps,
    w_query,
    w_keyval,
    norm_gain,
    time_freq,
    contact_table,
    key_bias,
    attn_gate,
    head_cotangent,
):
    section_idx = lax.axis_index("pipe")
    seq_idx = lax.axis_index("seq")
    rep_idx = lax.axis_index("dp")
    seq_count = lax.axis_size("seq")
    section_count = lax.axis_size("pipe")
    rep_count = lax.axis_size("dp")
    tok_rows = incoming.shape[3]
    width = incoming.shape[4]
    turns = incoming.shape[1]
    frames = tok_rows * seq_count
    heads_all = key_bias.shape[1]
    head_size = width // heads_all
    heads_local = heads_all // seq_count
    kv_width = w_keyval.shape[2]
    kv_local = kv_width // (2 * head_size * seq_count)
    group_size = heads_local // kv_local
    feat_count = head_cotangent.shape[4]
    score_scale = head_size ** (-0.5)
    q_cols = width // seq_count
    kv_cols = kv_width // seq_count
    w_rows = w_query.shape[1]

    w_parts = jnp.concatenate(
        [
            w_query[0].reshape(w_rows, seq_count, q_cols),
            w_keyval[0].reshape(w_rows, seq_count, kv_cols),
        ],
        axis=2,
    ).transpose(1, 0, 2)
    block = lax.all_to_all(w_parts, "seq", split_axis=0, concat_axis=0, tiled=True)
    weights = jnp.zeros((seq_count, rep_count, w_rows, q_cols + kv_cols), jnp.bfloat16)
    for hop in range(rep_count):
        owner = lax.rem(rep_idx + rep_count - hop, rep_count)
        weights = lax.dynamic_update_slice_in_dim(weights, block[:, None], owner, 1)
        if hop + 1 < rep_count:
            block = ring(block, "dp")
    weights = weights.reshape(width, q_cols + kv_cols)

    gain_row = norm_gain[0]
    freq_row = time_freq[0]
    table = contact_table[0]
    gate_local = lax.dynamic_slice_in_dim(attn_gate[0], seq_idx * q_cols, q_cols)
    table_local = lax.dynamic_slice_in_dim(table, seq_idx * q_cols, q_cols, 1)
    bias_local = lax.dynamic_slice_in_dim(key_bias[0], seq_idx * heads_local, heads_local)
    contact_all = lax.all_gather(contacts[:, 0, :], "seq", axis=1, tiled=True)
    key_all = keyframes[:, 0, :]
    step_all = timesteps[:, 0]
    labels = jnp.arange(table.shape[0], dtype=jnp.int32)
    cot_all = lax.all_gather(head_cotangent[0, :, 0], "seq", axis=1, tiled=True)

    lag = 2 if section_count == 2 else 1
    if lag == 2:
        steps = turns + 1
    else:
        steps = turns

    def turn_at(step):
        if lag == 1:
            return jnp.int32(step)
        return jnp.clip(step - section_idx, 0, turns - 1)

    outputs = []
    handed = {}
    for step in range(steps):
        turn = turn_at(step)
        fresh = lax.dynamic_index_in_dim(incoming[0, :, 0], turn, 0, keepdims=False)
        current = lax.all_gather(fresh, "seq", axis=0, tiled=True)
        if step in handed:
            current = jnp.where((section_idx == 0) | (turn == 0), current, handed[step])
        batch_idx = turn - section_idx + section_count - 1
        contact_rows = lax.dynamic_index_in_dim(contact_all, batch_idx, 0, keepdims=False)
        key_flags = lax.dynamic_index_in_dim(key_all, batch_idx, 0, keepdims=False).astype(
            jnp.float32
        )
        timestep = lax.dynamic_index_in_dim(step_all, batch_idx, 0, keepdims=False).astype(
            jnp.float32
        )
        onehot = (contact_rows[:, None] == labels[None, :]).astype(jnp.bfloat16)
        hidden = current.astype(jnp.float32) + jnp.dot(
            onehot, table, preferred_element_type=jnp.float32
        )
        root_mean = jnp.sqrt(jnp.mean(hidden * hidden, axis=-1, keepdims=True) + epsilon)
        modulation = gain_row * (1.0 + 0.5 * jnp.sin(timestep * freq_row))
        normed = (hidden / root_mean * modulation[None, :]).astype(jnp.bfloat16)
        projected = jnp.dot(normed, weights, preferred_element_type=jnp.float32).astype(
            jnp.bfloat16
        )
        query_heads = projected[:, :q_cols].reshape(frames, heads_local, head_size)
        keyval_heads = projected[:, q_cols:].reshape(frames, kv_local, 2, head_size)
        head_outputs = []
        for head in range(heads_local):
            key_rows = keyval_heads[:, head // group_size, 0]
            value_rows = keyval_heads[:, head // group_size, 1]
            scores = (
                lax.dot_general(
                    query_heads[:, head],
                    key_rows,
                    (((1,), (1,)), ((), ())),
                    preferred_element_type=jnp.float32,
                )
                * score_scale
            )
            scores = scores + bias_local[head] * key_flags[None, :]
            row_max = jnp.max(scores, axis=-1, keepdims=True)
            exponent = jnp.exp(scores - row_max)
            probabilities = (exponent / jnp.sum(exponent, axis=-1, keepdims=True)).astype(
                jnp.bfloat16
            )
            head_outputs.append(
                jnp.dot(probabilities, value_rows, preferred_element_type=jnp.float32).astype(
                    jnp.bfloat16
                )
            )
        attended = jnp.concatenate(head_outputs, axis=1)
        hidden_local = lax.dynamic_slice_in_dim(current, seq_idx * q_cols, q_cols, 1).astype(
            jnp.float32
        ) + jnp.dot(onehot, table_local, preferred_element_type=jnp.float32)
        output = (hidden_local + gate_local[None, :] * attended.astype(jnp.float32)).astype(
            jnp.bfloat16
        )
        outputs.append(output)
        if step + lag < steps:
            piece = passed_along(output, "pipe", 1)
            handed[step + lag] = lax.all_gather(piece, "seq", axis=1, tiled=True)

    factor = float(turns * rep_count * frames) ** (-0.5)
    total = None
    rows_out = []
    for turn in range(turns):
        if lag == 2:
            own = jnp.where(section_idx == 0, outputs[turn], outputs[turn + 1])
        else:
            own = outputs[turn]
        term = lax.dot_general(
            own, cot_all[turn], (((0,), (0,)), ((), ())), preferred_element_type=jnp.float32
        )
        total = term if total is None else total + term
        rows_out.append(lax.all_to_all(own, "seq", split_axis=0, concat_axis=1, tiled=True))
    section_out = jnp.stack(rows_out)[None, :, None]
    grad_parts = lax.all_to_all(
        (total * factor).astype(jnp.bfloat16).reshape(rep_count, q_cols // rep_count, feat_count),
        "dp",
        split_axis=0,
        concat_axis=0,
        tiled=True,
    )
    grad_rows = jnp.sum(grad_parts.astype(jnp.float32), axis=0)
    return (section_out, grad_rows[None])


def solution(mesh):
    in_specs = (
        P("pipe", None, "dp", "seq", None),
        P(None, "dp", "seq"),
        P(None, "dp", None),
        P(None, "dp"),
        P("pipe", ("seq", "dp"), None),
        P("pipe", ("seq", "dp"), None),
        P("pipe", None),
        P("pipe", None),
        P("pipe", None, None),
        P("pipe", None),
        P("pipe", None),
        P("pipe", None, "dp", "seq", None),
    )
    out_specs = (P("pipe", None, "dp", "seq", None), P("pipe", ("seq", "dp"), None))
    return jax.shard_map(body, mesh=mesh, in_specs=in_specs, out_specs=out_specs, check_vma=False)
```

```python
import functools
import math

import jax
import jax.numpy as jnp
from jax import lax
from jax.experimental import pallas as pl
from jax.experimental.pallas import tpu as pltpu
from jax.sharding import PartitionSpec as P

epsilon = 1e-06


def passed_along(value, axis, steps):
    count = lax.axis_size(axis)
    first, last = (max(0, -steps), min(count, count - steps))
    return lax.ppermute(value, axis, [(source, source + steps) for source in range(first, last)])


def ring(value, axis):
    count = lax.axis_size(axis)
    return lax.ppermute(value, axis, [(source, (source + 1) % count) for source in range(count)])


def swap(value, bit):
    count = lax.axis_size("seq")
    return lax.ppermute(value, "seq", [(source, source ^ bit) for source in range(count)])


def swap_within(section, value, bit):
    count = lax.axis_size("seq")
    pairs = [(section * count + i, section * count + (i ^ bit)) for i in range(count)]
    return lax.ppermute(value, ("pipe", "seq"), pairs)


def shifted(value, axis, shift):
    count = lax.axis_size(axis)
    return lax.ppermute(value, axis, [(source, (source + shift) % count) for source in range(count)])


def offsets_of(count):
    offsets = [0]
    bit = count // 2
    while bit:
        offsets = offsets + [offset ^ bit for offset in offsets]
        bit //= 2
    return offsets


def turn_and_batch(step, turns):
    section = lax.axis_index("pipe")
    turn = jnp.clip(step - section, 0, turns - 1)
    return turn, turn - section + 1


def pack_kernel(wq, wkv, *refs):
    outs, sems = refs[:-1], refs[-1]
    cols = outs[0].shape[1] // 2
    seq = lax.axis_index("seq")
    copies = []
    for m, out in enumerate(outs):
        start = pl.multiple_of((seq ^ m) * cols, 128)
        for k, source in enumerate((wq, wkv)):
            copies.append(
                pltpu.make_async_copy(
                    source.at[0, :, pl.ds(start, cols)],
                    out.at[:, pl.ds(k * cols, cols)],
                    sems.at[2 * m + k],
                )
            )
    for copy in copies:
        copy.start()
    for copy in copies:
        copy.wait()


def stack_kernel(deps, *refs):
    out = refs[-1]
    at = 0
    for ref in refs[deps:-1]:
        if len(ref.shape) == 2:
            out[at] = ref[...]
            at += 1
        else:
            out[at : at + ref.shape[0]] = ref[...]
            at += ref.shape[0]


def place_kernel(hop, hops, *refs):
    weights, parts = refs[-1], refs[:-1]
    if hop > 0:
        parts = parts[:-1]
    place(hop, hops, parts, weights)


def place(hop, hops, parts, weights):
    seq, rep = lax.axis_index("seq"), lax.axis_index("dp")
    m = 0
    for part in parts:
        count, rows = part.shape[:2]
        for j in range(count):
            block = (seq ^ m) * hops + lax.rem(rep + hops - hop, hops)
            weights[pl.ds(pl.multiple_of(block * rows, 16), rows)] = part[j]
            m += 1


def first_kernel(turns, far, incoming, contacts, out, states):
    rows = incoming.shape[3]
    for turn in range(2):
        out[turn * rows : (turn + 1) * rows] = incoming[0, turn, 0]
    states[...] = jnp.zeros_like(states)
    for step in range(turns + 1):
        _, batch = turn_and_batch(step, turns)
        states[step : step + 1] = contacts[batch].astype(jnp.float32)
    out[2 * rows :, : states.shape[1]] = states[...].astype(jnp.bfloat16)


def second_kernel(dep, incoming, cotangent, out):
    turns, rows, feats = cotangent.shape[1], cotangent.shape[3], cotangent.shape[4]
    out[:rows] = incoming[0, 2, 0]
    for turn in range(turns):
        out[rows:, turn * feats : (turn + 1) * feats] = cotangent[0, turn, 0]


def columns_of(rows_of, pieces, rows):
    labels = lax.broadcasted_iota(jnp.int32, (32, rows), 0)
    columns = []
    for i in range(pieces):
        state, flag = rows_of(i)
        one = jnp.zeros((32, rows), jnp.float32)
        if state is not None:
            one = jnp.where(labels == state, 1.0, 0.0)
        if flag is not None:
            one = jnp.where(labels == 16, flag, one)
        columns.append(one.T)
    return jnp.concatenate(columns, axis=0)


def modulation(step, turns, times, gain, freq):
    _, batch = turn_and_batch(step, turns)
    return gain[...] * (1.0 + 0.5 * jnp.sin(times[batch, 0].astype(jnp.float32) * freq[...]))


def norm_kernel(turns, pieces, times, table, gain, freq, *refs):
    sources, refs = refs[:pieces], refs[pieces + 1 :]
    scaled, scales, owns, embeds, mod = refs[0:2], refs[2:4], refs[4:6], refs[6:8], refs[8]
    first, sems = refs[9 : 9 + pieces], refs[9 + pieces]
    copies = [
        pltpu.make_async_copy(sources[i], first[i], sems.at[i]) for i in range(pieces)
    ]
    for copy in copies:
        copy.start()
    for copy in copies:
        copy.wait()
    frames, width = scaled[0].shape
    rows, cols = frames // pieces, owns[0].shape[1]
    seq = lax.axis_index("seq")
    offsets = offsets_of(pieces)
    for step in range(turns + 1):

        def state_of(i):
            state = first[i][2 * rows : 2 * rows + 16, :rows][step : step + 1]
            return state.astype(jnp.float32).astype(jnp.int32), None

        onehot = columns_of(state_of, pieces, rows)[:, : table.shape[1]].astype(jnp.bfloat16)
        if step >= 2:
            for at in range(0, width, 256):
                embeds[step - 2][:, at : at + 256] = jnp.dot(
                    onehot, table[0, :, at : at + 256], preferred_element_type=jnp.float32
                ).astype(jnp.bfloat16)
            continue
        turn, _ = turn_and_batch(step, turns)
        at = pl.multiple_of(jnp.minimum(turn, 1) * rows, 128)
        mod[...] = modulation(step, turns, times, gain, freq)
        total = jnp.zeros((frames, 128), jnp.float32)
        for i in range(pieces):
            lanes = pl.ds(pl.multiple_of((seq ^ offsets[i]) * cols, 128), cols)
            current = jnp.concatenate([first[p][pl.ds(at, rows), lanes] for p in range(pieces)])
            hidden = current.astype(jnp.float32) + jnp.dot(
                onehot, table[0, :, lanes], preferred_element_type=jnp.float32
            )
            for lane in range(0, cols, 128):
                piece = hidden[:, lane : lane + 128]
                total = total + piece * piece
            scaled[step][:, lanes] = (hidden * mod[:, lanes]).astype(jnp.bfloat16)
            if i == 0:
                owns[step][...] = hidden
        mean = jnp.sum(total, axis=1, keepdims=True) * (1.0 / width)
        scales[step][...] = jnp.broadcast_to(lax.rsqrt(mean + epsilon), (frames, 128))


def step_kernel(cfg, *refs):
    step, has_relay = cfg["step"], cfg["has_relay"]
    pieces, hops, head, turns = cfg["pieces"], cfg["hops"], cfg["head"], cfg["turns"]
    heads, group, halves = cfg["heads"], cfg["group"], cfg["halves"]
    refs = list(refs)

    def take(count):
        taken, refs[:count] = refs[:count], []
        return taken

    bias, times, gain, freq, gate, flags = take(6)
    if has_relay:
        second, embed, relay = take(pieces), take(1)[0], take(pieces * halves)
    else:
        scaled, scales, own_hidden = take(3)
    chunk = take(2) if step == 0 else None
    weights = take(1)[0]
    outs = take(halves)
    if step == 0:
        weights = take(1)[0]
    proj, att = take(2)
    if has_relay:
        scaled, scales, own_hidden, mod = take(4)
    offsets = offsets_of(pieces)
    frames, width = scaled.shape
    rows, cols = frames // pieces, att.shape[1]
    part = pieces // halves
    seq, rep, section = lax.axis_index("seq"), lax.axis_index("dp"), lax.axis_index("pipe")
    _, batch = turn_and_batch(step, turns)

    if step == 0:
        place(hops - 1, hops, chunk, weights)

    def normalize(relayed):
        total = jnp.zeros((frames, 128), jnp.float32)
        for i in range(pieces):
            lanes = pl.ds(pl.multiple_of((seq ^ offsets[i]) * cols, 128), cols)
            blocks = []
            for p in range(pieces):
                if relayed:
                    j = offsets.index(offsets[i] ^ offsets[p])
                    blocks.append(relay[(j // part) * pieces + i][j % part])
                else:
                    blocks.append(second[p][:rows, lanes])
            hidden = jnp.concatenate(blocks, axis=0).astype(jnp.float32)
            hidden = hidden + embed[:, lanes].astype(jnp.float32)
            for lane in range(0, cols, 128):
                piece = hidden[:, lane : lane + 128]
                total = total + piece * piece
            scaled[:, lanes] = (hidden * mod[:, lanes]).astype(jnp.bfloat16)
            if i == 0:
                own_hidden[...] = hidden
        scales[...] = total

    if has_relay:
        mod[...] = modulation(step, turns, times, gain, freq)

        @pl.when(section == 0)
        def _():
            normalize(False)

        @pl.when(section != 0)
        def _():
            normalize(True)

        mean = jnp.sum(scales[...], axis=1, keepdims=True) * (1.0 / width)
        scale = lax.rsqrt(mean + epsilon)
    else:
        scale = scales[:, :1]

    def flag_of(i):
        lanes = pl.ds(pl.multiple_of((seq ^ offsets[i]) * rows, 128), rows)
        return None, flags[batch, :, lanes].astype(jnp.float32)

    flag_column = columns_of(flag_of, pieces, rows)[:, 16:17]
    projected = jnp.dot(scaled[...], weights[...], preferred_element_type=jnp.float32) * scale
    score_scale = head ** (-0.5) * math.log2(math.e)
    proj[:, :cols] = (projected[:, :cols] * score_scale).astype(jnp.bfloat16)
    proj[:, cols : 2 * cols] = projected[:, cols:].astype(jnp.bfloat16)
    proj[:, 2 * cols :] = jnp.zeros((frames, 128), jnp.bfloat16)
    lanes = lax.broadcasted_iota(jnp.int32, (frames, 128), 1)
    row_lanes = lax.broadcasted_iota(jnp.int32, (1, 128), 1)
    flag_lanes = jnp.logical_or(lanes == head, lanes == head + 1)

    def part_of(at):
        return proj[:, at : at + 128].astype(jnp.float32)

    keys, values = [], []
    for kv in range(heads // group):
        base = cols + kv * 2 * head
        key = jnp.where(flag_lanes, flag_column, jnp.where(lanes < head, part_of(base), 0.0))
        value = jnp.where(lanes < head, part_of(base + head), jnp.where(lanes == head, 1.0, 0.0))
        keys.append(key.astype(jnp.bfloat16))
        values.append(value.astype(jnp.bfloat16))

    def scores_of(h):
        strength = jnp.zeros((1, 128), jnp.float32) + bias[0, seq * heads + h] * math.log2(math.e)
        coarse = strength.astype(jnp.bfloat16).astype(jnp.float32)
        tail = jnp.where(
            row_lanes == head, coarse, jnp.where(row_lanes == head + 1, strength - coarse, 0.0)
        )
        query = jnp.where(lanes < head, part_of(h * head), tail).astype(jnp.bfloat16)
        return lax.dot_general(
            query, keys[h // group], (((1,), (1,)), ((), ())), preferred_element_type=jnp.float32
        )

    scores = scores_of(0)
    for h in range(heads):
        ahead = scores_of(h + 1) if h + 1 < heads else None
        top = jnp.max(scores, axis=1, keepdims=True)
        weight = jnp.exp2(scores - top).astype(jnp.bfloat16)
        mixed = jnp.dot(weight, values[h // group], preferred_element_type=jnp.float32)
        att[:, h * head : (h + 1) * head] = mixed[:, :head] * (1.0 / mixed[:, head : head + 1])
        scores = ahead
    own = pl.ds(pl.multiple_of(seq * cols, 128), cols)
    attended = att[...].astype(jnp.bfloat16).astype(jnp.float32)
    output = (own_hidden[...] + gate[:, own] * attended).astype(jnp.bfloat16)
    blocks = output.reshape(pieces, rows, cols)
    for k in range(halves):
        outs[k][...] = blocks[k * part : (k + 1) * part]


def tie_kernel(*refs):
    pass


def grad_of(output, second, turn, rows, feats):
    cot = jnp.concatenate(
        [piece[rows : 2 * rows, turn * feats : (turn + 1) * feats] for piece in second], axis=0
    )
    return lax.dot_general(
        output, cot, (((0,), (0,)), ((), ())), preferred_element_type=jnp.float32
    )


def early_kernel(turns, pieces, halves, feats, *refs):
    outs, second = refs[: turns * halves], refs[turns * halves : turns * halves + pieces]
    sends, grad = refs[turns * halves + pieces : -1], refs[-1]
    section = lax.axis_index("pipe")
    offsets = offsets_of(pieces)
    part = pieces // halves
    rows = outs[0].shape[1]
    total = None
    for turn in range(turns - 1):
        blocks = []
        for p in range(pieces):
            k, j = p // part, p % part
            block = jnp.where(
                section == 0, outs[turn * halves + k][j], outs[(turn + 1) * halves + k][j]
            )
            sends[offsets[p]][turn] = block
            blocks.append(block)
        share = grad_of(jnp.concatenate(blocks, axis=0), second, turn, rows, feats)
        total = share if total is None else total + share
    grad[...] = total


def settle_kernel(turns, pieces, halves, hops, feats, *refs):
    refs = list(refs)

    def take(count):
        taken, refs[:count] = refs[:count], []
        return taken

    before, now, second, early = take(halves), take(halves), take(pieces), take(pieces)
    early_grad = take(1)[0]
    late, own_grad, grads = take(pieces), take(1)[0], take(hops - 1)
    section_out = take(1)[0]
    rows_out, total, sem = take(3)
    section, seq, rep = lax.axis_index("pipe"), lax.axis_index("seq"), lax.axis_index("dp")
    offsets = offsets_of(pieces)
    part = pieces // halves
    rows, cols = early[0].shape[1:]
    for m in range(pieces):
        lanes = pl.ds(pl.multiple_of((seq ^ m) * cols, 128), cols)
        for turn in range(turns - 1):
            rows_out[turn, :, lanes] = early[m][turn]
    copy = pltpu.make_async_copy(rows_out, section_out.at[pl.ds(0, turns - 1)], sem)
    copy.start()
    blocks = []
    for p in range(pieces):
        block = jnp.where(section == 0, before[p // part][p % part], now[p // part][p % part])
        late[offsets[p]][...] = block
        blocks.append(block)
    share = grad_of(jnp.concatenate(blocks, axis=0), second, turns - 1, rows, feats)
    factor = float(turns * hops * rows * pieces) ** (-0.5)
    total[...] = (share + early_grad[...]) * factor
    g_rows = cols // hops
    own_grad[...] = total[pl.ds(pl.multiple_of(rep * g_rows, 8), g_rows)]
    for shift in range(1, hops):
        at = pl.multiple_of(lax.rem(rep + shift, hops) * g_rows, 8)
        grads[shift - 1][...] = total[pl.ds(at, g_rows)].astype(jnp.bfloat16)
    copy.wait()


def finish_kernel(pieces, hops, *refs):
    held, late, refs = refs[0], refs[1 : pieces + 1], refs[pieces + 1 :]
    own_grad, parts, (section_out, grad, row_out, sem) = refs[0], refs[1:hops], refs[hops:]
    seq = lax.axis_index("seq")
    cols = late[0].shape[1]
    for m in range(pieces):
        lanes = pl.ds(pl.multiple_of((seq ^ m) * cols, 128), cols)
        row_out[:, lanes] = late[m][...]
    copy = pltpu.make_async_copy(row_out, section_out.at[section_out.shape[0] - 1], sem)
    copy.start()
    total = own_grad[...]
    for part in parts:
        total = total + part[...].astype(jnp.float32)
    grad[...] = total
    copy.wait()


HALVES = 2
MIB = 1024 * 1024


def paired_body(
    incoming,
    contacts,
    keyframes,
    timesteps,
    w_query,
    w_keyval,
    norm_gain,
    time_freq,
    contact_table,
    key_bias,
    attn_gate,
    head_cotangent,
):
    seq_count = lax.axis_size("seq")
    hops = lax.axis_size("dp")
    rows, width, turns = incoming.shape[3], incoming.shape[4], incoming.shape[1]
    frames = rows * seq_count
    heads_all = key_bias.shape[1]
    head = width // heads_all
    heads = heads_all // seq_count
    kv_heads = w_keyval.shape[2] // (2 * head * seq_count)
    feats = head_cotangent.shape[4]
    cols = width // seq_count
    w_rows = w_query.shape[1]
    steps = turns + 1
    part = seq_count // HALVES
    kind = jnp.bfloat16
    smem = pl.BlockSpec(memory_space=pltpu.SMEM)
    vmem = pl.BlockSpec(memory_space=pltpu.VMEM)
    anywhere = pl.BlockSpec(memory_space=pl.ANY)
    shape = jax.ShapeDtypeStruct

    def call(kernel, name, out_shape, in_specs, operands, scratch=(), limit=4, flops=0, **options):
        return pl.pallas_call(
            kernel,
            out_shape=out_shape,
            in_specs=in_specs,
            scratch_shapes=list(scratch),
            compiler_params=pltpu.CompilerParams(vmem_limit_bytes=limit * MIB),
            cost_estimate=pl.CostEstimate(
                flops=flops, bytes_accessed=flops // 512, transcendentals=0
            ),
            name=name,
            **options,
        )(*operands)

    def pin(value, space=pltpu.VMEM):
        return pltpu.with_memory_space_constraint(value, space)

    packed = call(
        pack_kernel,
        "pack",
        [pltpu.VMEM((w_rows, 2 * cols), kind)] * seq_count,
        [anywhere, anywhere],
        [pin(w_query, pltpu.HBM), pin(w_keyval, pltpu.HBM)],
        [pltpu.SemaphoreType.DMA((2 * seq_count,))],
        out_specs=[vmem] * seq_count,
    )
    blocks = [packed[0]] + [swap(packed[m], m) for m in range(1, seq_count)]

    def stacked(name, count, deps, values):
        return call(
            functools.partial(stack_kernel, len(deps)),
            name,
            pltpu.VMEM((count, w_rows, 2 * cols), kind),
            [anywhere] * len(deps) + [vmem] * len(values),
            deps + values,
            out_specs=vmem,
        )

    weights = None

    def placed(hop, parts):
        operands = [pin(part) for part in parts] + ([pin(weights)] if hop else [])
        return call(
            functools.partial(place_kernel, hop, hops),
            "place%d" % hop,
            pltpu.VMEM((width, 2 * cols), kind),
            [vmem] * len(operands),
            operands,
            out_specs=vmem,
            input_output_aliases={len(parts): 0} if hop else {},
        )

    near = stacked("near", 2, [], blocks[:2])
    near_next = shifted(near, "dp", 1)
    far = stacked("far", 2, [near_next], blocks[2:])
    far_next = shifted(far, "dp", 1)
    rings = [[near, near_next], [far, far_next]]
    for hop in range(2, hops - 1):
        for chunks in rings:
            chunks.append(shifted(chunks[-1], "dp", 1))
    last_chunk = [shifted(chunks[-1], "dp", 1) for chunks in rings]
    for hop in range(hops - 1):
        weights = placed(hop, [chunks[hop] for chunks in rings])

    def tie(values, deps):
        return call(
            tie_kernel,
            "tie",
            [shape(value.shape, kind) for value in values],
            [anywhere] * (len(values) + len(deps)),
            list(values) + list(deps),
            out_specs=[anywhere] * len(values),
            input_output_aliases={i: i for i in range(len(values))},
        )

    mine = call(
        functools.partial(first_kernel, turns),
        "first",
        pltpu.VMEM((2 * rows + 16, width), kind),
        [anywhere, vmem, vmem],
        [far, incoming, contacts],
        [pltpu.VMEM((16, 128), jnp.float32)],
        out_specs=vmem,
    )
    across = swap(mine, 2)
    beside = swap(mine, 1)
    (across,) = tie([across], [chunks[-1] for chunks in rings])
    first = [mine, across, beside, swap(across, 1)]
    prepared = call(
        functools.partial(norm_kernel, turns, seq_count),
        "norm",
        [pltpu.VMEM((frames, width), kind)] * 2
        + [pltpu.VMEM((frames, 128), jnp.float32)] * 2
        + [pltpu.VMEM((frames, cols), jnp.float32)] * 2
        + [pltpu.VMEM((frames, width), kind)] * 2,
        [smem] + [vmem] * 3 + [anywhere] * (seq_count + 1),
        [timesteps, contact_table, norm_gain, time_freq]
        + [pin(piece, pltpu.HBM) for piece in first]
        + [weights],
        [pltpu.VMEM((1, width), jnp.float32)]
        + [pltpu.VMEM((2 * rows + 16, width), kind)] * seq_count
        + [pltpu.SemaphoreType.DMA((seq_count,))],
        12,
        out_specs=[vmem] * 8,
    )

    mine = call(
        second_kernel,
        "second",
        pltpu.VMEM((2 * rows, width), kind),
        [anywhere, vmem, vmem],
        [across, incoming, head_cotangent],
        out_specs=vmem,
    )
    second = [mine, swap(mine, 2), swap(mine, 1)]

    outputs = []
    relayed = {}
    for step in range(steps):
        cfg = {
            "step": step,
            "has_relay": step in relayed,
            "pieces": seq_count,
            "hops": hops,
            "head": head,
            "heads": heads,
            "group": heads // kv_heads,
            "turns": turns,
            "halves": HALVES,
        }
        operands = [key_bias, timesteps, norm_gain, time_freq, attn_gate, keyframes]
        scratch = [
            pltpu.VMEM((frames, 2 * cols + 128), kind),
            pltpu.VMEM((frames, cols), jnp.float32),
        ]
        if step in relayed:
            large = second + [prepared[4 + step]] + relayed[step]
            scratch += [
                pltpu.VMEM((frames, width), kind),
                pltpu.VMEM((frames, 128), jnp.float32),
                pltpu.VMEM((frames, cols), jnp.float32),
                pltpu.VMEM((1, width), jnp.float32),
            ]
        else:
            large = [prepared[step], prepared[2 + step], prepared[4 + step]]
        large += last_chunk + [weights] if step == 0 else [weights]
        operands += [pin(value) for value in large]
        out_shape = [pltpu.VMEM((part, rows, cols), kind)] * HALVES
        if step == 0:
            out_shape += [pltpu.VMEM((width, 2 * cols), kind)]
        results = call(
            functools.partial(step_kernel, cfg),
            "step%d" % step,
            out_shape,
            [smem, smem] + [vmem] * (len(operands) - 2),
            operands,
            scratch,
            16,
            2 * frames * width * 2 * cols + 4 * heads * frames * frames * head,
            out_specs=[vmem] * len(out_shape),
            input_output_aliases={len(operands) - 1: HALVES} if step == 0 else {},
        )
        outputs.append(list(results[:HALVES]))
        if step == 0:
            weights = results[HALVES]
            (second[1],) = tie([second[1]], [outputs[-1][0]])
            second.append(swap(second[1], 1))
        if step == 2:
            pending = [piece for k in range(HALVES) for piece in (crossing[k][0], crossing[k][1])]
            tied = tie(pending, [outputs[-1][0]])
            relayed[3] = []
            for k in range(HALVES):
                mine, across = tied[2 * k], tied[2 * k + 1]
                relayed[3] += [mine, across, swap_within(1, mine, 1), swap_within(1, across, 1)]
            early = call(
                functools.partial(early_kernel, turns, seq_count, HALVES, feats),
                "early",
                [shape((turns - 1, rows, cols), kind)] * seq_count
                + [shape((cols, feats), jnp.float32)],
                [vmem] * (turns * HALVES + seq_count),
                [half for output in outputs for half in output] + second,
                limit=8,
                out_specs=[vmem] * (seq_count + 1),
            )
            early, early_grad = list(early[:-1]), early[-1]
            early = [early[0]] + [swap(early[m], m) for m in range(1, seq_count)]
        if step + 2 < steps:
            crossing = []
            for k, half in enumerate(outputs[-1]):
                piece = passed_along(half, "pipe", 1)
                if step == 1 and k == 1:
                    across = passed_along(swap_within(0, half, 2), "pipe", 1)
                else:
                    across = swap_within(1, piece, 2)
                crossing.append((piece, across))
            if step == 0:
                relayed[2] = []
                for mine, across in crossing:
                    relayed[2] += [
                        mine,
                        across,
                        swap_within(1, mine, 1),
                        swap_within(1, across, 1),
                    ]

    g_shape = (cols // hops, feats)
    operands = outputs[-2] + outputs[-1] + second + early + [early_grad]
    settled = call(
        functools.partial(settle_kernel, turns, seq_count, HALVES, hops, feats),
        "settle",
        [shape((rows, cols), kind)] * seq_count
        + [shape(g_shape, jnp.float32)]
        + [shape(g_shape, kind)] * (hops - 1)
        + [shape((turns, rows, width), kind)],
        [vmem] * len(operands),
        operands,
        [
            pltpu.VMEM((turns - 1, rows, width), kind),
            pltpu.VMEM((cols, feats), jnp.float32),
            pltpu.SemaphoreType.DMA,
        ],
        8,
        out_specs=[vmem] * (seq_count + hops) + [anywhere],
    )
    late, grads, held = settled[:seq_count], settled[seq_count:-1], settled[-1]
    late = [late[0]] + [swap(late[m], m) for m in range(1, seq_count)]
    grads = [grads[0]] + [shifted(grads[k], "dp", k) for k in range(1, hops)]
    section_out, grad_rows = call(
        functools.partial(finish_kernel, seq_count, hops),
        "finish",
        [shape((turns, rows, width), kind), shape(g_shape, jnp.float32)],
        [anywhere] + [vmem] * (seq_count + hops),
        [held] + late + grads,
        [pltpu.VMEM((rows, width), kind), pltpu.SemaphoreType.DMA],
        out_specs=[anywhere, vmem],
        input_output_aliases={0: 0},
    )
    return (section_out[None, :, None], grad_rows[None])


def body(incoming, contacts, keyframes, timesteps, w_query, *others):
    count = lax.axis_size("seq")
    cols = w_query.shape[2] // count
    paired = (
        lax.axis_size("pipe") == 2
        and count == 4
        and cols % 128 == 0
        and w_query.shape[1] % 16 == 0
        and incoming.shape[3] == 128
        and incoming.shape[1] == 3
    )
    chosen = paired_body if paired else general_body
    return chosen(incoming, contacts, keyframes, timesteps, w_query, *others)


def general_body(
    incoming,
    contacts,
    keyframes,
    timesteps,
    w_query,
    w_keyval,
    norm_gain,
    time_freq,
    contact_table,
    key_bias,
    attn_gate,
    head_cotangent,
):
    section_idx = lax.axis_index("pipe")
    seq_idx = lax.axis_index("seq")
    rep_idx = lax.axis_index("dp")
    seq_count = lax.axis_size("seq")
    section_count = lax.axis_size("pipe")
    rep_count = lax.axis_size("dp")
    tok_rows = incoming.shape[3]
    width = incoming.shape[4]
    turns = incoming.shape[1]
    frames = tok_rows * seq_count
    heads_all = key_bias.shape[1]
    head_size = width // heads_all
    heads_local = heads_all // seq_count
    kv_width = w_keyval.shape[2]
    kv_local = kv_width // (2 * head_size * seq_count)
    group_size = heads_local // kv_local
    feat_count = head_cotangent.shape[4]
    score_scale = head_size ** (-0.5)
    q_cols = width // seq_count
    kv_cols = kv_width // seq_count
    w_rows = w_query.shape[1]

    w_parts = jnp.concatenate(
        [
            w_query[0].reshape(w_rows, seq_count, q_cols),
            w_keyval[0].reshape(w_rows, seq_count, kv_cols),
        ],
        axis=2,
    ).transpose(1, 0, 2)
    block = lax.all_to_all(w_parts, "seq", split_axis=0, concat_axis=0, tiled=True)
    weights = jnp.zeros((seq_count, rep_count, w_rows, q_cols + kv_cols), jnp.bfloat16)
    for hop in range(rep_count):
        owner = lax.rem(rep_idx + rep_count - hop, rep_count)
        weights = lax.dynamic_update_slice_in_dim(weights, block[:, None], owner, 1)
        if hop + 1 < rep_count:
            block = ring(block, "dp")
    weights = weights.reshape(width, q_cols + kv_cols)

    gain_row = norm_gain[0]
    freq_row = time_freq[0]
    table = contact_table[0]
    gate_local = lax.dynamic_slice_in_dim(attn_gate[0], seq_idx * q_cols, q_cols)
    table_local = lax.dynamic_slice_in_dim(table, seq_idx * q_cols, q_cols, 1)
    bias_local = lax.dynamic_slice_in_dim(key_bias[0], seq_idx * heads_local, heads_local)
    contact_all = lax.all_gather(contacts[:, 0, :], "seq", axis=1, tiled=True)
    key_all = keyframes[:, 0, :]
    step_all = timesteps[:, 0]
    labels = jnp.arange(table.shape[0], dtype=jnp.int32)
    cot_all = lax.all_gather(head_cotangent[0, :, 0], "seq", axis=1, tiled=True)

    lag = 2 if section_count == 2 else 1
    if lag == 2:
        steps = turns + 1
    else:
        steps = turns

    def turn_at(step):
        if lag == 1:
            return jnp.int32(step)
        return jnp.clip(step - section_idx, 0, turns - 1)

    outputs = []
    handed = {}
    for step in range(steps):
        turn = turn_at(step)
        fresh = lax.dynamic_index_in_dim(incoming[0, :, 0], turn, 0, keepdims=False)
        current = lax.all_gather(fresh, "seq", axis=0, tiled=True)
        if step in handed:
            current = jnp.where((section_idx == 0) | (turn == 0), current, handed[step])
        batch_idx = turn - section_idx + section_count - 1
        contact_rows = lax.dynamic_index_in_dim(contact_all, batch_idx, 0, keepdims=False)
        key_flags = lax.dynamic_index_in_dim(key_all, batch_idx, 0, keepdims=False).astype(
            jnp.float32
        )
        timestep = lax.dynamic_index_in_dim(step_all, batch_idx, 0, keepdims=False).astype(
            jnp.float32
        )
        onehot = (contact_rows[:, None] == labels[None, :]).astype(jnp.bfloat16)
        hidden = current.astype(jnp.float32) + jnp.dot(
            onehot, table, preferred_element_type=jnp.float32
        )
        root_mean = jnp.sqrt(jnp.mean(hidden * hidden, axis=-1, keepdims=True) + epsilon)
        modulation = gain_row * (1.0 + 0.5 * jnp.sin(timestep * freq_row))
        normed = (hidden / root_mean * modulation[None, :]).astype(jnp.bfloat16)
        projected = jnp.dot(normed, weights, preferred_element_type=jnp.float32).astype(
            jnp.bfloat16
        )
        query_heads = projected[:, :q_cols].reshape(frames, heads_local, head_size)
        keyval_heads = projected[:, q_cols:].reshape(frames, kv_local, 2, head_size)
        head_outputs = []
        for head in range(heads_local):
            key_rows = keyval_heads[:, head // group_size, 0]
            value_rows = keyval_heads[:, head // group_size, 1]
            scores = (
                lax.dot_general(
                    query_heads[:, head],
                    key_rows,
                    (((1,), (1,)), ((), ())),
                    preferred_element_type=jnp.float32,
                )
                * score_scale
            )
            scores = scores + bias_local[head] * key_flags[None, :]
            row_max = jnp.max(scores, axis=-1, keepdims=True)
            exponent = jnp.exp(scores - row_max)
            probabilities = (exponent / jnp.sum(exponent, axis=-1, keepdims=True)).astype(
                jnp.bfloat16
            )
            head_outputs.append(
                jnp.dot(probabilities, value_rows, preferred_element_type=jnp.float32).astype(
                    jnp.bfloat16
                )
            )
        attended = jnp.concatenate(head_outputs, axis=1)
        hidden_local = lax.dynamic_slice_in_dim(current, seq_idx * q_cols, q_cols, 1).astype(
            jnp.float32
        ) + jnp.dot(onehot, table_local, preferred_element_type=jnp.float32)
        output = (hidden_local + gate_local[None, :] * attended.astype(jnp.float32)).astype(
            jnp.bfloat16
        )
        outputs.append(output)
        if step + lag < steps:
            piece = passed_along(output, "pipe", 1)
            handed[step + lag] = lax.all_gather(piece, "seq", axis=1, tiled=True)

    factor = float(turns * rep_count * frames) ** (-0.5)
    total = None
    rows_out = []
    for turn in range(turns):
        if lag == 2:
            own = jnp.where(section_idx == 0, outputs[turn], outputs[turn + 1])
        else:
            own = outputs[turn]
        term = lax.dot_general(
            own, cot_all[turn], (((0,), (0,)), ((), ())), preferred_element_type=jnp.float32
        )
        total = term if total is None else total + term
        rows_out.append(lax.all_to_all(own, "seq", split_axis=0, concat_axis=1, tiled=True))
    section_out = jnp.stack(rows_out)[None, :, None]
    grad_parts = lax.all_to_all(
        (total * factor).astype(jnp.bfloat16).reshape(rep_count, q_cols // rep_count, feat_count),
        "dp",
        split_axis=0,
        concat_axis=0,
        tiled=True,
    )
    grad_rows = jnp.sum(grad_parts.astype(jnp.float32), axis=0)
    return (section_out, grad_rows[None])


def solution(mesh):
    in_specs = (
        P("pipe", None, "dp", "seq", None),
        P(None, "dp", "seq"),
        P(None, "dp", None),
        P(None, "dp"),
        P("pipe", ("seq", "dp"), None),
        P("pipe", ("seq", "dp"), None),
        P("pipe", None),
        P("pipe", None),
        P("pipe", None, None),
        P("pipe", None),
        P("pipe", None),
        P("pipe", None, "dp", "seq", None),
    )
    out_specs = (P("pipe", None, "dp", "seq", None), P("pipe", ("seq", "dp"), None))
    return jax.shard_map(body, mesh=mesh, in_specs=in_specs, out_specs=out_specs, check_vma=False)
```

```python
import functools
import math

import jax
import jax.numpy as jnp
from jax import lax
from jax.experimental import pallas as pl
from jax.experimental.pallas import tpu as pltpu
from jax.sharding import PartitionSpec as P

epsilon = 1e-06


def passed_along(value, axis, steps):
    count = lax.axis_size(axis)
    first, last = (max(0, -steps), min(count, count - steps))
    return lax.ppermute(value, axis, [(source, source + steps) for source in range(first, last)])


def ring(value, axis):
    count = lax.axis_size(axis)
    return lax.ppermute(value, axis, [(source, (source + 1) % count) for source in range(count)])


def swap(value, bit):
    count = lax.axis_size("seq")
    return lax.ppermute(value, "seq", [(source, source ^ bit) for source in range(count)])


def swap_within(section, value, bit):
    count = lax.axis_size("seq")
    pairs = [(section * count + i, section * count + (i ^ bit)) for i in range(count)]
    return lax.ppermute(value, ("pipe", "seq"), pairs)


def handed_over(value):
    return lax.ppermute(value, "pipe", [(0, 1), (1, 0)])


def shifted(value, axis, shift):
    count = lax.axis_size(axis)
    return lax.ppermute(value, axis, [(source, (source + shift) % count) for source in range(count)])


def offsets_of(count):
    offsets = [0]
    bit = count // 2
    while bit:
        offsets = offsets + [offset ^ bit for offset in offsets]
        bit //= 2
    return offsets


def turn_and_batch(step, turns):
    section = lax.axis_index("pipe")
    turn = jnp.clip(step - section, 0, turns - 1)
    return turn, turn - section + 1


def pack_kernel(wq, wkv, *refs):
    outs, sems = refs[:-1], refs[-1]
    cols = outs[0].shape[1] // 2
    seq = lax.axis_index("seq")
    copies = []
    for m, out in enumerate(outs):
        start = pl.multiple_of((seq ^ m) * cols, 128)
        for k, source in enumerate((wq, wkv)):
            copies.append(
                pltpu.make_async_copy(
                    source.at[0, :, pl.ds(start, cols)],
                    out.at[:, pl.ds(k * cols, cols)],
                    sems.at[2 * m + k],
                )
            )
    for copy in copies:
        copy.start()
    for copy in copies:
        copy.wait()


def stack_kernel(deps, *refs):
    out = refs[-1]
    at = 0
    for ref in refs[deps:-1]:
        if len(ref.shape) == 2:
            out[at] = ref[...]
            at += 1
        else:
            out[at : at + ref.shape[0]] = ref[...]
            at += ref.shape[0]


def place_kernel(hop, hops, *refs):
    weights, parts = refs[-1], refs[:-1]
    if hop > 0:
        parts = parts[:-1]
    place(hop, hops, parts, weights)


def place(hop, hops, parts, weights):
    seq, rep = lax.axis_index("seq"), lax.axis_index("dp")
    m = 0
    for part in parts:
        count, rows = part.shape[:2]
        for j in range(count):
            block = (seq ^ m) * hops + lax.rem(rep + hops - hop, hops)
            weights[pl.ds(pl.multiple_of(block * rows, 16), rows)] = part[j]
            m += 1


def first_kernel(turns, far, incoming, contacts, out, states):
    rows = incoming.shape[3]
    for turn in range(2):
        out[turn * rows : (turn + 1) * rows] = incoming[0, turn, 0]
    states[...] = jnp.zeros_like(states)
    for step in range(turns + 1):
        _, batch = turn_and_batch(step, turns)
        states[step : step + 1] = contacts[batch].astype(jnp.float32)
    out[2 * rows :, : states.shape[1]] = states[...].astype(jnp.bfloat16)


def second_kernel(dep, incoming, cotangent, out):
    turns, rows, feats = cotangent.shape[1], cotangent.shape[3], cotangent.shape[4]
    out[:rows] = incoming[0, 2, 0]
    for turn in range(turns):
        out[rows:, turn * feats : (turn + 1) * feats] = cotangent[0, turn, 0]


def columns_of(rows_of, pieces, rows):
    labels = lax.broadcasted_iota(jnp.int32, (32, rows), 0)
    columns = []
    for i in range(pieces):
        state, flag = rows_of(i)
        one = jnp.zeros((32, rows), jnp.float32)
        if state is not None:
            one = jnp.where(labels == state, 1.0, 0.0)
        if flag is not None:
            one = jnp.where(labels == 16, flag, one)
        columns.append(one.T)
    return jnp.concatenate(columns, axis=0)


def modulation(step, turns, times, gain, freq):
    _, batch = turn_and_batch(step, turns)
    return gain[...] * (1.0 + 0.5 * jnp.sin(times[batch, 0].astype(jnp.float32) * freq[...]))


def norm_kernel(turns, pieces, times, table, gain, freq, *refs):
    sources, refs = refs[:pieces], refs[pieces + 1 :]
    scaled, scales, owns, embeds, mod = refs[0:2], refs[2:4], refs[4:6], refs[6:8], refs[8]
    first, sems = refs[9 : 9 + pieces], refs[9 + pieces]
    copies = [
        pltpu.make_async_copy(sources[i], first[i], sems.at[i]) for i in range(pieces)
    ]
    for copy in copies:
        copy.start()
    for copy in copies:
        copy.wait()
    frames, width = scaled[0].shape
    rows, cols = frames // pieces, owns[0].shape[1]
    seq = lax.axis_index("seq")
    offsets = offsets_of(pieces)
    for step in range(turns + 1):

        def state_of(i):
            state = first[i][2 * rows : 2 * rows + 16, :rows][step : step + 1]
            return state.astype(jnp.float32).astype(jnp.int32), None

        onehot = columns_of(state_of, pieces, rows)[:, : table.shape[1]].astype(jnp.bfloat16)
        if step >= 2:
            for at in range(0, width, 256):
                embeds[step - 2][:, at : at + 256] = jnp.dot(
                    onehot, table[0, :, at : at + 256], preferred_element_type=jnp.float32
                ).astype(jnp.bfloat16)
            continue
        turn, _ = turn_and_batch(step, turns)
        at = pl.multiple_of(jnp.minimum(turn, 1) * rows, 128)
        mod[...] = modulation(step, turns, times, gain, freq)
        total = jnp.zeros((frames, 128), jnp.float32)
        for i in range(pieces):
            lanes = pl.ds(pl.multiple_of((seq ^ offsets[i]) * cols, 128), cols)
            current = jnp.concatenate([first[p][pl.ds(at, rows), lanes] for p in range(pieces)])
            hidden = current.astype(jnp.float32) + jnp.dot(
                onehot, table[0, :, lanes], preferred_element_type=jnp.float32
            )
            for lane in range(0, cols, 128):
                piece = hidden[:, lane : lane + 128]
                total = total + piece * piece
            scaled[step][:, lanes] = (hidden * mod[:, lanes]).astype(jnp.bfloat16)
            if i == 0:
                owns[step][...] = hidden
        mean = jnp.sum(total, axis=1, keepdims=True) * (1.0 / width)
        scales[step][...] = jnp.broadcast_to(lax.rsqrt(mean + epsilon), (frames, 128))


def step_kernel(cfg, *refs):
    step, has_relay = cfg["step"], cfg["has_relay"]
    pieces, hops, head, turns = cfg["pieces"], cfg["hops"], cfg["head"], cfg["turns"]
    heads, group, halves = cfg["heads"], cfg["group"], cfg["halves"]
    refs = list(refs)

    def take(count):
        taken, refs[:count] = refs[:count], []
        return taken

    bias, times, gain, freq, gate, flags = take(6)
    if has_relay:
        second, embed, relay = take(pieces), take(1)[0], take(pieces * halves)
    else:
        scaled, scales, own_hidden = take(3)
    chunk = take(2) if step == 0 else None
    weights = take(1)[0]
    outs = take(halves)
    if step == 0:
        weights = take(1)[0]
    proj, att = take(2)
    if has_relay:
        scaled, scales, own_hidden, mod = take(4)
    offsets = offsets_of(pieces)
    frames, width = scaled.shape
    rows, cols = frames // pieces, att.shape[1]
    part = pieces // halves
    seq, rep, section = lax.axis_index("seq"), lax.axis_index("dp"), lax.axis_index("pipe")
    _, batch = turn_and_batch(step, turns)

    if step == 0:
        place(hops - 1, hops, chunk, weights)

    def normalize(relayed):
        total = jnp.zeros((frames, 128), jnp.float32)
        for i in range(pieces):
            lanes = pl.ds(pl.multiple_of((seq ^ offsets[i]) * cols, 128), cols)
            blocks = []
            for p in range(pieces):
                if relayed:
                    j = offsets.index(offsets[i] ^ offsets[p])
                    blocks.append(relay[(j // part) * pieces + i][j % part])
                else:
                    blocks.append(second[p][:rows, lanes])
            hidden = jnp.concatenate(blocks, axis=0).astype(jnp.float32)
            hidden = hidden + embed[:, lanes].astype(jnp.float32)
            for lane in range(0, cols, 128):
                piece = hidden[:, lane : lane + 128]
                total = total + piece * piece
            scaled[:, lanes] = (hidden * mod[:, lanes]).astype(jnp.bfloat16)
            if i == 0:
                own_hidden[...] = hidden
        scales[...] = total

    if has_relay:
        mod[...] = modulation(step, turns, times, gain, freq)

        @pl.when(section == 0)
        def _():
            normalize(False)

        @pl.when(section != 0)
        def _():
            normalize(True)

        mean = jnp.sum(scales[...], axis=1, keepdims=True) * (1.0 / width)
        scale = lax.rsqrt(mean + epsilon)
    else:
        scale = scales[:, :1]

    def flag_of(i):
        lanes = pl.ds(pl.multiple_of((seq ^ offsets[i]) * rows, 128), rows)
        return None, flags[batch, :, lanes].astype(jnp.float32)

    flag_column = columns_of(flag_of, pieces, rows)[:, 16:17]
    projected = jnp.dot(scaled[...], weights[...], preferred_element_type=jnp.float32) * scale
    score_scale = head ** (-0.5) * math.log2(math.e)
    proj[:, :cols] = (projected[:, :cols] * score_scale).astype(jnp.bfloat16)
    proj[:, cols : 2 * cols] = projected[:, cols:].astype(jnp.bfloat16)
    proj[:, 2 * cols :] = jnp.zeros((frames, 128), jnp.bfloat16)
    lanes = lax.broadcasted_iota(jnp.int32, (frames, 128), 1)
    row_lanes = lax.broadcasted_iota(jnp.int32, (1, 128), 1)
    flag_lanes = jnp.logical_or(lanes == head, lanes == head + 1)

    def part_of(at):
        return proj[:, at : at + 128].astype(jnp.float32)

    keys, values = [], []
    for kv in range(heads // group):
        base = cols + kv * 2 * head
        key = jnp.where(flag_lanes, flag_column, jnp.where(lanes < head, part_of(base), 0.0))
        value = jnp.where(lanes < head, part_of(base + head), jnp.where(lanes == head, 1.0, 0.0))
        keys.append(key.astype(jnp.bfloat16))
        values.append(value.astype(jnp.bfloat16))

    def scores_of(h):
        strength = jnp.zeros((1, 128), jnp.float32) + bias[0, seq * heads + h] * math.log2(math.e)
        coarse = strength.astype(jnp.bfloat16).astype(jnp.float32)
        tail = jnp.where(
            row_lanes == head, coarse, jnp.where(row_lanes == head + 1, strength - coarse, 0.0)
        )
        query = jnp.where(lanes < head, part_of(h * head), tail).astype(jnp.bfloat16)
        return lax.dot_general(
            query, keys[h // group], (((1,), (1,)), ((), ())), preferred_element_type=jnp.float32
        )

    scores = scores_of(0)
    for h in range(heads):
        ahead = scores_of(h + 1) if h + 1 < heads else None
        top = jnp.max(scores, axis=1, keepdims=True)
        weight = jnp.exp2(scores - top).astype(jnp.bfloat16)
        mixed = jnp.dot(weight, values[h // group], preferred_element_type=jnp.float32)
        att[:, h * head : (h + 1) * head] = mixed[:, :head] * (1.0 / mixed[:, head : head + 1])
        scores = ahead
    own = pl.ds(pl.multiple_of(seq * cols, 128), cols)
    attended = att[...].astype(jnp.bfloat16).astype(jnp.float32)
    output = (own_hidden[...] + gate[:, own] * attended).astype(jnp.bfloat16)
    blocks = output.reshape(pieces, rows, cols)
    for k in range(halves):
        outs[k][...] = blocks[k * part : (k + 1) * part]


def tie_kernel(*refs):
    pass


def grad_of(output, second, turn, rows, feats):
    cot = jnp.concatenate(
        [piece[rows : 2 * rows, turn * feats : (turn + 1) * feats] for piece in second], axis=0
    )
    return lax.dot_general(
        output, cot, (((0,), (0,)), ((), ())), preferred_element_type=jnp.float32
    )


def early_kernel(turns, pieces, halves, feats, *refs):
    outs, second = refs[: turns * halves], refs[turns * halves : turns * halves + pieces]
    sends, grad = refs[turns * halves + pieces : -1], refs[-1]
    section = lax.axis_index("pipe")
    offsets = offsets_of(pieces)
    part = pieces // halves
    rows = outs[0].shape[1]
    total = None
    for turn in range(turns - 1):
        blocks = []
        for p in range(pieces):
            k, j = p // part, p % part
            block = jnp.where(
                section == 0, outs[turn * halves + k][j], outs[(turn + 1) * halves + k][j]
            )
            sends[offsets[p]][turn] = block
            blocks.append(block)
        share = grad_of(jnp.concatenate(blocks, axis=0), second, turn, rows, feats)
        total = share if total is None else total + share
    grad[...] = total


def settle_kernel(turns, pieces, halves, hops, feats, *refs):
    refs = list(refs)

    def take(count):
        taken, refs[:count] = refs[:count], []
        return taken

    before, now, second, early = take(halves), take(halves), take(pieces), take(pieces)
    early_grad = take(1)[0]
    late, own_grad, grads = take(pieces), take(1)[0], take(hops - 1)
    section_out = take(1)[0]
    rows_out, total, sem = take(3)
    section, seq, rep = lax.axis_index("pipe"), lax.axis_index("seq"), lax.axis_index("dp")
    offsets = offsets_of(pieces)
    part = pieces // halves
    rows, cols = early[0].shape[1:]
    for m in range(pieces):
        lanes = pl.ds(pl.multiple_of((seq ^ m) * cols, 128), cols)
        for turn in range(turns - 1):
            rows_out[turn, :, lanes] = early[m][turn]
    copy = pltpu.make_async_copy(rows_out, section_out.at[pl.ds(0, turns - 1)], sem)
    copy.start()
    blocks = []
    for p in range(pieces):
        block = jnp.where(section == 0, before[p // part][p % part], now[p // part][p % part])
        late[offsets[p]][...] = block
        blocks.append(block)
    share = grad_of(jnp.concatenate(blocks, axis=0), second, turns - 1, rows, feats)
    factor = float(turns * hops * rows * pieces) ** (-0.5)
    total[...] = (share + early_grad[...]) * factor
    g_rows = cols // hops
    own_grad[...] = total[pl.ds(pl.multiple_of(rep * g_rows, 8), g_rows)]
    for shift in range(1, hops):
        at = pl.multiple_of(lax.rem(rep + shift, hops) * g_rows, 8)
        grads[shift - 1][...] = total[pl.ds(at, g_rows)].astype(jnp.bfloat16)
    copy.wait()


def finish_kernel(pieces, hops, *refs):
    held, late, refs = refs[0], refs[1 : pieces + 1], refs[pieces + 1 :]
    own_grad, parts, (section_out, grad, row_out, sem) = refs[0], refs[1:hops], refs[hops:]
    seq = lax.axis_index("seq")
    cols = late[0].shape[1]
    for m in range(pieces):
        lanes = pl.ds(pl.multiple_of((seq ^ m) * cols, 128), cols)
        row_out[:, lanes] = late[m][...]
    copy = pltpu.make_async_copy(row_out, section_out.at[section_out.shape[0] - 1], sem)
    copy.start()
    total = own_grad[...]
    for part in parts:
        total = total + part[...].astype(jnp.float32)
    grad[...] = total
    copy.wait()


HALVES = 2
MIB = 1024 * 1024


def paired_body(
    incoming,
    contacts,
    keyframes,
    timesteps,
    w_query,
    w_keyval,
    norm_gain,
    time_freq,
    contact_table,
    key_bias,
    attn_gate,
    head_cotangent,
):
    seq_count = lax.axis_size("seq")
    hops = lax.axis_size("dp")
    rows, width, turns = incoming.shape[3], incoming.shape[4], incoming.shape[1]
    frames = rows * seq_count
    heads_all = key_bias.shape[1]
    head = width // heads_all
    heads = heads_all // seq_count
    kv_heads = w_keyval.shape[2] // (2 * head * seq_count)
    feats = head_cotangent.shape[4]
    cols = width // seq_count
    w_rows = w_query.shape[1]
    steps = turns + 1
    part = seq_count // HALVES
    kind = jnp.bfloat16
    smem = pl.BlockSpec(memory_space=pltpu.SMEM)
    vmem = pl.BlockSpec(memory_space=pltpu.VMEM)
    anywhere = pl.BlockSpec(memory_space=pl.ANY)
    shape = jax.ShapeDtypeStruct

    def call(kernel, name, out_shape, in_specs, operands, scratch=(), limit=4, flops=0, **options):
        return pl.pallas_call(
            kernel,
            out_shape=out_shape,
            in_specs=in_specs,
            scratch_shapes=list(scratch),
            compiler_params=pltpu.CompilerParams(vmem_limit_bytes=limit * MIB),
            cost_estimate=pl.CostEstimate(
                flops=flops, bytes_accessed=flops // 512, transcendentals=0
            ),
            name=name,
            **options,
        )(*operands)

    def pin(value, space=pltpu.VMEM):
        return pltpu.with_memory_space_constraint(value, space)

    packed = call(
        pack_kernel,
        "pack",
        [pltpu.VMEM((w_rows, 2 * cols), kind)] * seq_count,
        [anywhere, anywhere],
        [pin(w_query, pltpu.HBM), pin(w_keyval, pltpu.HBM)],
        [pltpu.SemaphoreType.DMA((2 * seq_count,))],
        out_specs=[vmem] * seq_count,
    )
    blocks = [packed[0]] + [swap(packed[m], m) for m in range(1, seq_count)]

    def stacked(name, count, deps, values):
        return call(
            functools.partial(stack_kernel, len(deps)),
            name,
            pltpu.VMEM((count, w_rows, 2 * cols), kind),
            [anywhere] * len(deps) + [vmem] * len(values),
            deps + values,
            out_specs=vmem,
        )

    weights = None

    def placed(hop, parts):
        operands = [pin(part) for part in parts] + ([pin(weights)] if hop else [])
        return call(
            functools.partial(place_kernel, hop, hops),
            "place%d" % hop,
            pltpu.VMEM((width, 2 * cols), kind),
            [vmem] * len(operands),
            operands,
            out_specs=vmem,
            input_output_aliases={len(parts): 0} if hop else {},
        )

    near = stacked("near", 2, [], blocks[:2])
    near_next = shifted(near, "dp", 1)
    far = stacked("far", 2, [near_next], blocks[2:])
    far_next = shifted(far, "dp", 1)
    rings = [[near, near_next], [far, far_next]]
    for hop in range(2, hops - 1):
        for chunks in rings:
            chunks.append(shifted(chunks[-1], "dp", 1))
    last_chunk = [shifted(chunks[-1], "dp", 1) for chunks in rings]
    for hop in range(hops - 1):
        weights = placed(hop, [chunks[hop] for chunks in rings])

    def tie(values, deps):
        return call(
            tie_kernel,
            "tie",
            [shape(value.shape, kind) for value in values],
            [anywhere] * (len(values) + len(deps)),
            list(values) + list(deps),
            out_specs=[anywhere] * len(values),
            input_output_aliases={i: i for i in range(len(values))},
        )

    mine = call(
        functools.partial(first_kernel, turns),
        "first",
        pltpu.VMEM((2 * rows + 16, width), kind),
        [anywhere, vmem, vmem],
        [far, incoming, contacts],
        [pltpu.VMEM((16, 128), jnp.float32)],
        out_specs=vmem,
    )
    across = swap(mine, 2)
    beside = swap(mine, 1)
    (across,) = tie([across], [chunks[-1] for chunks in rings])
    first = [mine, across, beside, swap(across, 1)]
    prepared = call(
        functools.partial(norm_kernel, turns, seq_count),
        "norm",
        [pltpu.VMEM((frames, width), kind)] * 2
        + [pltpu.VMEM((frames, 128), jnp.float32)] * 2
        + [pltpu.VMEM((frames, cols), jnp.float32)] * 2
        + [pltpu.VMEM((frames, width), kind)] * 2,
        [smem] + [vmem] * 3 + [anywhere] * (seq_count + 1),
        [timesteps, contact_table, norm_gain, time_freq]
        + [pin(piece, pltpu.HBM) for piece in first]
        + [weights],
        [pltpu.VMEM((1, width), jnp.float32)]
        + [pltpu.VMEM((2 * rows + 16, width), kind)] * seq_count
        + [pltpu.SemaphoreType.DMA((seq_count,))],
        12,
        out_specs=[vmem] * 8,
    )

    mine = call(
        second_kernel,
        "second",
        pltpu.VMEM((2 * rows, width), kind),
        [anywhere, vmem, vmem],
        [across, incoming, head_cotangent],
        out_specs=vmem,
    )
    second = [mine, swap(mine, 2), swap(mine, 1)]

    outputs = []
    relayed = {}
    for step in range(steps):
        cfg = {
            "step": step,
            "has_relay": step in relayed,
            "pieces": seq_count,
            "hops": hops,
            "head": head,
            "heads": heads,
            "group": heads // kv_heads,
            "turns": turns,
            "halves": HALVES,
        }
        operands = [key_bias, timesteps, norm_gain, time_freq, attn_gate, keyframes]
        scratch = [
            pltpu.VMEM((frames, 2 * cols + 128), kind),
            pltpu.VMEM((frames, cols), jnp.float32),
        ]
        if step in relayed:
            large = second + [prepared[4 + step]] + relayed[step]
            scratch += [
                pltpu.VMEM((frames, width), kind),
                pltpu.VMEM((frames, 128), jnp.float32),
                pltpu.VMEM((frames, cols), jnp.float32),
                pltpu.VMEM((1, width), jnp.float32),
            ]
        else:
            large = [prepared[step], prepared[2 + step], prepared[4 + step]]
        large += last_chunk + [weights] if step == 0 else [weights]
        operands += [pin(value) for value in large]
        out_shape = [pltpu.VMEM((part, rows, cols), kind)] * HALVES
        if step == 0:
            out_shape += [pltpu.VMEM((width, 2 * cols), kind)]
        results = call(
            functools.partial(step_kernel, cfg),
            "step%d" % step,
            out_shape,
            [smem, smem] + [vmem] * (len(operands) - 2),
            operands,
            scratch,
            16,
            2 * frames * width * 2 * cols + 4 * heads * frames * frames * head,
            out_specs=[vmem] * len(out_shape),
            input_output_aliases={len(operands) - 1: HALVES} if step == 0 else {},
        )
        outputs.append(list(results[:HALVES]))
        if step == 0:
            weights = results[HALVES]
            (second[1],) = tie([second[1]], [outputs[-1][0]])
            second.append(swap(second[1], 1))
        if step == 2:
            pending = [piece for k in range(HALVES) for piece in (crossing[k][0], crossing[k][1])]
            tied = tie(pending, [outputs[-1][0]])
            relayed[3] = []
            for k in range(HALVES):
                mine, across = tied[2 * k], tied[2 * k + 1]
                relayed[3] += [mine, across, swap(mine, 1), swap(across, 1)]
            early = call(
                functools.partial(early_kernel, turns, seq_count, HALVES, feats),
                "early",
                [shape((turns - 1, rows, cols), kind)] * seq_count
                + [shape((cols, feats), jnp.float32)],
                [vmem] * (turns * HALVES + seq_count),
                [half for output in outputs for half in output] + second,
                limit=8,
                out_specs=[vmem] * (seq_count + 1),
            )
            early, early_grad = list(early[:-1]), early[-1]
            early = [early[0]] + [swap(early[m], m) for m in range(1, seq_count)]
        if step + 2 < steps:
            crossing = []
            for k, half in enumerate(outputs[-1]):
                piece = handed_over(half)
                if step == 1 and k == 1:
                    across = handed_over(swap_within(0, half, 2))
                else:
                    across = swap(piece, 2)
                crossing.append((piece, across))
            if step == 0:
                relayed[2] = []
                for mine, across in crossing:
                    relayed[2] += [mine, across, swap(mine, 1), swap(across, 1)]

    g_shape = (cols // hops, feats)
    operands = outputs[-2] + outputs[-1] + second + early + [early_grad]
    settled = call(
        functools.partial(settle_kernel, turns, seq_count, HALVES, hops, feats),
        "settle",
        [shape((rows, cols), kind)] * seq_count
        + [shape(g_shape, jnp.float32)]
        + [shape(g_shape, kind)] * (hops - 1)
        + [shape((turns, rows, width), kind)],
        [vmem] * len(operands),
        operands,
        [
            pltpu.VMEM((turns - 1, rows, width), kind),
            pltpu.VMEM((cols, feats), jnp.float32),
            pltpu.SemaphoreType.DMA,
        ],
        8,
        out_specs=[vmem] * (seq_count + hops) + [anywhere],
    )
    late, grads, held = settled[:seq_count], settled[seq_count:-1], settled[-1]
    late = [late[0]] + [swap(late[m], m) for m in range(1, seq_count)]
    grads = [grads[0]] + [shifted(grads[k], "dp", k) for k in range(1, hops)]
    section_out, grad_rows = call(
        functools.partial(finish_kernel, seq_count, hops),
        "finish",
        [shape((turns, rows, width), kind), shape(g_shape, jnp.float32)],
        [anywhere] + [vmem] * (seq_count + hops),
        [held] + late + grads,
        [pltpu.VMEM((rows, width), kind), pltpu.SemaphoreType.DMA],
        out_specs=[anywhere, vmem],
        input_output_aliases={0: 0},
    )
    return (section_out[None, :, None], grad_rows[None])


def body(incoming, contacts, keyframes, timesteps, w_query, *others):
    count = lax.axis_size("seq")
    cols = w_query.shape[2] // count
    paired = (
        lax.axis_size("pipe") == 2
        and count == 4
        and cols % 128 == 0
        and w_query.shape[1] % 16 == 0
        and incoming.shape[3] == 128
        and incoming.shape[1] == 3
    )
    chosen = paired_body if paired else general_body
    return chosen(incoming, contacts, keyframes, timesteps, w_query, *others)


def general_body(
    incoming,
    contacts,
    keyframes,
    timesteps,
    w_query,
    w_keyval,
    norm_gain,
    time_freq,
    contact_table,
    key_bias,
    attn_gate,
    head_cotangent,
):
    section_idx = lax.axis_index("pipe")
    seq_idx = lax.axis_index("seq")
    rep_idx = lax.axis_index("dp")
    seq_count = lax.axis_size("seq")
    section_count = lax.axis_size("pipe")
    rep_count = lax.axis_size("dp")
    tok_rows = incoming.shape[3]
    width = incoming.shape[4]
    turns = incoming.shape[1]
    frames = tok_rows * seq_count
    heads_all = key_bias.shape[1]
    head_size = width // heads_all
    heads_local = heads_all // seq_count
    kv_width = w_keyval.shape[2]
    kv_local = kv_width // (2 * head_size * seq_count)
    group_size = heads_local // kv_local
    feat_count = head_cotangent.shape[4]
    score_scale = head_size ** (-0.5)
    q_cols = width // seq_count
    kv_cols = kv_width // seq_count
    w_rows = w_query.shape[1]

    w_parts = jnp.concatenate(
        [
            w_query[0].reshape(w_rows, seq_count, q_cols),
            w_keyval[0].reshape(w_rows, seq_count, kv_cols),
        ],
        axis=2,
    ).transpose(1, 0, 2)
    block = lax.all_to_all(w_parts, "seq", split_axis=0, concat_axis=0, tiled=True)
    weights = jnp.zeros((seq_count, rep_count, w_rows, q_cols + kv_cols), jnp.bfloat16)
    for hop in range(rep_count):
        owner = lax.rem(rep_idx + rep_count - hop, rep_count)
        weights = lax.dynamic_update_slice_in_dim(weights, block[:, None], owner, 1)
        if hop + 1 < rep_count:
            block = ring(block, "dp")
    weights = weights.reshape(width, q_cols + kv_cols)

    gain_row = norm_gain[0]
    freq_row = time_freq[0]
    table = contact_table[0]
    gate_local = lax.dynamic_slice_in_dim(attn_gate[0], seq_idx * q_cols, q_cols)
    table_local = lax.dynamic_slice_in_dim(table, seq_idx * q_cols, q_cols, 1)
    bias_local = lax.dynamic_slice_in_dim(key_bias[0], seq_idx * heads_local, heads_local)
    contact_all = lax.all_gather(contacts[:, 0, :], "seq", axis=1, tiled=True)
    key_all = keyframes[:, 0, :]
    step_all = timesteps[:, 0]
    labels = jnp.arange(table.shape[0], dtype=jnp.int32)
    cot_all = lax.all_gather(head_cotangent[0, :, 0], "seq", axis=1, tiled=True)

    lag = 2 if section_count == 2 else 1
    if lag == 2:
        steps = turns + 1
    else:
        steps = turns

    def turn_at(step):
        if lag == 1:
            return jnp.int32(step)
        return jnp.clip(step - section_idx, 0, turns - 1)

    outputs = []
    handed = {}
    for step in range(steps):
        turn = turn_at(step)
        fresh = lax.dynamic_index_in_dim(incoming[0, :, 0], turn, 0, keepdims=False)
        current = lax.all_gather(fresh, "seq", axis=0, tiled=True)
        if step in handed:
            current = jnp.where((section_idx == 0) | (turn == 0), current, handed[step])
        batch_idx = turn - section_idx + section_count - 1
        contact_rows = lax.dynamic_index_in_dim(contact_all, batch_idx, 0, keepdims=False)
        key_flags = lax.dynamic_index_in_dim(key_all, batch_idx, 0, keepdims=False).astype(
            jnp.float32
        )
        timestep = lax.dynamic_index_in_dim(step_all, batch_idx, 0, keepdims=False).astype(
            jnp.float32
        )
        onehot = (contact_rows[:, None] == labels[None, :]).astype(jnp.bfloat16)
        hidden = current.astype(jnp.float32) + jnp.dot(
            onehot, table, preferred_element_type=jnp.float32
        )
        root_mean = jnp.sqrt(jnp.mean(hidden * hidden, axis=-1, keepdims=True) + epsilon)
        modulation = gain_row * (1.0 + 0.5 * jnp.sin(timestep * freq_row))
        normed = (hidden / root_mean * modulation[None, :]).astype(jnp.bfloat16)
        projected = jnp.dot(normed, weights, preferred_element_type=jnp.float32).astype(
            jnp.bfloat16
        )
        query_heads = projected[:, :q_cols].reshape(frames, heads_local, head_size)
        keyval_heads = projected[:, q_cols:].reshape(frames, kv_local, 2, head_size)
        head_outputs = []
        for head in range(heads_local):
            key_rows = keyval_heads[:, head // group_size, 0]
            value_rows = keyval_heads[:, head // group_size, 1]
            scores = (
                lax.dot_general(
                    query_heads[:, head],
                    key_rows,
                    (((1,), (1,)), ((), ())),
                    preferred_element_type=jnp.float32,
                )
                * score_scale
            )
            scores = scores + bias_local[head] * key_flags[None, :]
            row_max = jnp.max(scores, axis=-1, keepdims=True)
            exponent = jnp.exp(scores - row_max)
            probabilities = (exponent / jnp.sum(exponent, axis=-1, keepdims=True)).astype(
                jnp.bfloat16
            )
            head_outputs.append(
                jnp.dot(probabilities, value_rows, preferred_element_type=jnp.float32).astype(
                    jnp.bfloat16
                )
            )
        attended = jnp.concatenate(head_outputs, axis=1)
        hidden_local = lax.dynamic_slice_in_dim(current, seq_idx * q_cols, q_cols, 1).astype(
            jnp.float32
        ) + jnp.dot(onehot, table_local, preferred_element_type=jnp.float32)
        output = (hidden_local + gate_local[None, :] * attended.astype(jnp.float32)).astype(
            jnp.bfloat16
        )
        outputs.append(output)
        if step + lag < steps:
            piece = passed_along(output, "pipe", 1)
            handed[step + lag] = lax.all_gather(piece, "seq", axis=1, tiled=True)

    factor = float(turns * rep_count * frames) ** (-0.5)
    total = None
    rows_out = []
    for turn in range(turns):
        if lag == 2:
            own = jnp.where(section_idx == 0, outputs[turn], outputs[turn + 1])
        else:
            own = outputs[turn]
        term = lax.dot_general(
            own, cot_all[turn], (((0,), (0,)), ((), ())), preferred_element_type=jnp.float32
        )
        total = term if total is None else total + term
        rows_out.append(lax.all_to_all(own, "seq", split_axis=0, concat_axis=1, tiled=True))
    section_out = jnp.stack(rows_out)[None, :, None]
    grad_parts = lax.all_to_all(
        (total * factor).astype(jnp.bfloat16).reshape(rep_count, q_cols // rep_count, feat_count),
        "dp",
        split_axis=0,
        concat_axis=0,
        tiled=True,
    )
    grad_rows = jnp.sum(grad_parts.astype(jnp.float32), axis=0)
    return (section_out, grad_rows[None])


def solution(mesh):
    in_specs = (
        P("pipe", None, "dp", "seq", None),
        P(None, "dp", "seq"),
        P(None, "dp", None),
        P(None, "dp"),
        P("pipe", ("seq", "dp"), None),
        P("pipe", ("seq", "dp"), None),
        P("pipe", None),
        P("pipe", None),
        P("pipe", None, None),
        P("pipe", None),
        P("pipe", None),
        P("pipe", None, "dp", "seq", None),
    )
    out_specs = (P("pipe", None, "dp", "seq", None), P("pipe", ("seq", "dp"), None))
    return jax.shard_map(body, mesh=mesh, in_specs=in_specs, out_specs=out_specs, check_vma=False)
```

```python
import functools
import math

import jax
import jax.numpy as jnp
from jax import lax
from jax.experimental import pallas as pl
from jax.experimental.pallas import tpu as pltpu
from jax.sharding import PartitionSpec as P

epsilon = 1e-06


def passed_along(value, axis, steps):
    count = lax.axis_size(axis)
    first, last = (max(0, -steps), min(count, count - steps))
    return lax.ppermute(value, axis, [(source, source + steps) for source in range(first, last)])


def ring(value, axis):
    count = lax.axis_size(axis)
    return lax.ppermute(value, axis, [(source, (source + 1) % count) for source in range(count)])


def swap(value, bit):
    count = lax.axis_size("seq")
    return lax.ppermute(value, "seq", [(source, source ^ bit) for source in range(count)])


def handed_over(value):
    return lax.ppermute(value, "pipe", [(0, 1), (1, 0)])


def shifted(value, axis, shift):
    count = lax.axis_size(axis)
    return lax.ppermute(value, axis, [(source, (source + shift) % count) for source in range(count)])


def offsets_of(count):
    offsets = [0]
    bit = count // 2
    while bit:
        offsets = offsets + [offset ^ bit for offset in offsets]
        bit //= 2
    return offsets


def turn_and_batch(step, turns):
    section = lax.axis_index("pipe")
    turn = jnp.clip(step - section, 0, turns - 1)
    return turn, turn - section + 1


def pack_kernel(wq, wkv, *refs):
    outs, sems = refs[:-1], refs[-1]
    cols = outs[0].shape[1] // 2
    seq = lax.axis_index("seq")
    copies = []
    for m, out in enumerate(outs):
        start = pl.multiple_of((seq ^ m) * cols, 128)
        for k, source in enumerate((wq, wkv)):
            copies.append(
                pltpu.make_async_copy(
                    source.at[0, :, pl.ds(start, cols)],
                    out.at[:, pl.ds(k * cols, cols)],
                    sems.at[2 * m + k],
                )
            )
    for copy in copies:
        copy.start()
    for copy in copies:
        copy.wait()


def stack_kernel(deps, *refs):
    out = refs[-1]
    at = 0
    for ref in refs[deps:-1]:
        if len(ref.shape) == 2:
            out[at] = ref[...]
            at += 1
        else:
            out[at : at + ref.shape[0]] = ref[...]
            at += ref.shape[0]


def place_kernel(hop, hops, *refs):
    weights, parts = refs[-1], refs[:-1]
    if hop > 0:
        parts = parts[:-1]
    place(hop, hops, parts, weights)


def place(hop, hops, parts, weights):
    seq, rep = lax.axis_index("seq"), lax.axis_index("dp")
    m = 0
    for part in parts:
        count, rows = part.shape[:2]
        for j in range(count):
            block = (seq ^ m) * hops + lax.rem(rep + hops - hop, hops)
            weights[pl.ds(pl.multiple_of(block * rows, 16), rows)] = part[j]
            m += 1


def first_kernel(turns, far, incoming, contacts, out, states):
    rows = incoming.shape[3]
    for turn in range(2):
        out[turn * rows : (turn + 1) * rows] = incoming[0, turn, 0]
    states[...] = jnp.zeros_like(states)
    for step in range(turns + 1):
        _, batch = turn_and_batch(step, turns)
        states[step : step + 1] = contacts[batch].astype(jnp.float32)
    out[2 * rows :, : states.shape[1]] = states[...].astype(jnp.bfloat16)


def second_kernel(dep, incoming, cotangent, out):
    turns, rows, feats = cotangent.shape[1], cotangent.shape[3], cotangent.shape[4]
    out[:rows] = incoming[0, 2, 0]
    for turn in range(turns):
        out[rows:, turn * feats : (turn + 1) * feats] = cotangent[0, turn, 0]


def columns_of(rows_of, pieces, rows):
    labels = lax.broadcasted_iota(jnp.int32, (32, rows), 0)
    columns = []
    for i in range(pieces):
        state, flag = rows_of(i)
        one = jnp.zeros((32, rows), jnp.float32)
        if state is not None:
            one = jnp.where(labels == state, 1.0, 0.0)
        if flag is not None:
            one = jnp.where(labels == 16, flag, one)
        columns.append(one.T)
    return jnp.concatenate(columns, axis=0)


def modulation(step, turns, times, gain, freq):
    _, batch = turn_and_batch(step, turns)
    return gain[...] * (1.0 + 0.5 * jnp.sin(times[batch, 0].astype(jnp.float32) * freq[...]))


def norm_kernel(turns, pieces, times, table, gain, freq, *refs):
    sources, refs = refs[:pieces], refs[pieces + 2 :]
    scaled, scales, owns, embeds, mod = refs[0:2], refs[2:4], refs[4:6], refs[6:8], refs[8]
    first, sems = refs[9 : 9 + pieces], refs[9 + pieces]
    copies = [
        pltpu.make_async_copy(sources[i], first[i], sems.at[i]) for i in range(pieces)
    ]
    for copy in copies:
        copy.start()
    for copy in copies:
        copy.wait()
    frames, width = scaled[0].shape
    rows, cols = frames // pieces, owns[0].shape[1]
    seq = lax.axis_index("seq")
    offsets = offsets_of(pieces)
    for step in range(turns + 1):

        def state_of(i):
            state = first[i][2 * rows : 2 * rows + 16, :rows][step : step + 1]
            return state.astype(jnp.float32).astype(jnp.int32), None

        onehot = columns_of(state_of, pieces, rows)[:, : table.shape[1]].astype(jnp.bfloat16)
        if step >= 2:
            for at in range(0, width, 256):
                embeds[step - 2][:, at : at + 256] = jnp.dot(
                    onehot, table[0, :, at : at + 256], preferred_element_type=jnp.float32
                ).astype(jnp.bfloat16)
            continue
        turn, _ = turn_and_batch(step, turns)
        at = pl.multiple_of(jnp.minimum(turn, 1) * rows, 128)
        mod[...] = modulation(step, turns, times, gain, freq)
        total = jnp.zeros((frames, 128), jnp.float32)
        for i in range(pieces):
            lanes = pl.ds(pl.multiple_of((seq ^ offsets[i]) * cols, 128), cols)
            current = jnp.concatenate([first[p][pl.ds(at, rows), lanes] for p in range(pieces)])
            hidden = current.astype(jnp.float32) + jnp.dot(
                onehot, table[0, :, lanes], preferred_element_type=jnp.float32
            )
            for lane in range(0, cols, 128):
                piece = hidden[:, lane : lane + 128]
                total = total + piece * piece
            scaled[step][:, lanes] = (hidden * mod[:, lanes]).astype(jnp.bfloat16)
            if i == 0:
                owns[step][...] = hidden
        mean = jnp.sum(total, axis=1, keepdims=True) * (1.0 / width)
        scales[step][...] = jnp.broadcast_to(lax.rsqrt(mean + epsilon), (frames, 128))


def step_kernel(cfg, *refs):
    step, has_relay = cfg["step"], cfg["has_relay"]
    pieces, hops, head, turns = cfg["pieces"], cfg["hops"], cfg["head"], cfg["turns"]
    heads, group, halves = cfg["heads"], cfg["group"], cfg["halves"]
    refs = list(refs)

    def take(count):
        taken, refs[:count] = refs[:count], []
        return taken

    bias, times, gain, freq, gate, flags = take(6)
    if has_relay:
        second, embed, relay = take(pieces), take(1)[0], take(pieces * halves)
    else:
        scaled, scales, own_hidden = take(3)
    chunk = take(2) if step == 0 else None
    weights = take(1)[0]
    outs = take(halves)
    if step == 0:
        weights = take(1)[0]
    proj, att = take(2)
    if has_relay:
        scaled, scales, own_hidden, mod = take(4)
    offsets = offsets_of(pieces)
    frames, width = scaled.shape
    rows, cols = frames // pieces, att.shape[1]
    part = pieces // halves
    seq, rep, section = lax.axis_index("seq"), lax.axis_index("dp"), lax.axis_index("pipe")
    _, batch = turn_and_batch(step, turns)

    if step == 0:
        place(hops - 1, hops, chunk, weights)

    def normalize(relayed):
        total = jnp.zeros((frames, 128), jnp.float32)
        for i in range(pieces):
            lanes = pl.ds(pl.multiple_of((seq ^ offsets[i]) * cols, 128), cols)
            blocks = []
            for p in range(pieces):
                if relayed:
                    j = offsets.index(offsets[i] ^ offsets[p])
                    blocks.append(relay[(j // part) * pieces + i][j % part])
                else:
                    blocks.append(second[p][:rows, lanes])
            hidden = jnp.concatenate(blocks, axis=0).astype(jnp.float32)
            hidden = hidden + embed[:, lanes].astype(jnp.float32)
            for lane in range(0, cols, 128):
                piece = hidden[:, lane : lane + 128]
                total = total + piece * piece
            scaled[:, lanes] = (hidden * mod[:, lanes]).astype(jnp.bfloat16)
            if i == 0:
                own_hidden[...] = hidden
        scales[...] = total

    if has_relay:
        mod[...] = modulation(step, turns, times, gain, freq)

        @pl.when(section == 0)
        def _():
            normalize(False)

        @pl.when(section != 0)
        def _():
            normalize(True)

        mean = jnp.sum(scales[...], axis=1, keepdims=True) * (1.0 / width)
        scale = lax.rsqrt(mean + epsilon)
    else:
        scale = scales[:, :1]

    def flag_of(i):
        lanes = pl.ds(pl.multiple_of((seq ^ offsets[i]) * rows, 128), rows)
        return None, flags[batch, :, lanes].astype(jnp.float32)

    flag_column = columns_of(flag_of, pieces, rows)[:, 16:17]
    projected = jnp.dot(scaled[...], weights[...], preferred_element_type=jnp.float32) * scale
    score_scale = head ** (-0.5) * math.log2(math.e)
    proj[:, :cols] = (projected[:, :cols] * score_scale).astype(jnp.bfloat16)
    proj[:, cols : 2 * cols] = projected[:, cols:].astype(jnp.bfloat16)
    proj[:, 2 * cols :] = jnp.zeros((frames, 128), jnp.bfloat16)
    lanes = lax.broadcasted_iota(jnp.int32, (frames, 128), 1)
    row_lanes = lax.broadcasted_iota(jnp.int32, (1, 128), 1)
    flag_lanes = jnp.logical_or(lanes == head, lanes == head + 1)

    def part_of(at):
        return proj[:, at : at + 128].astype(jnp.float32)

    keys, values = [], []
    for kv in range(heads // group):
        base = cols + kv * 2 * head
        key = jnp.where(flag_lanes, flag_column, jnp.where(lanes < head, part_of(base), 0.0))
        value = jnp.where(lanes < head, part_of(base + head), jnp.where(lanes == head, 1.0, 0.0))
        keys.append(key.astype(jnp.bfloat16))
        values.append(value.astype(jnp.bfloat16))

    queries = []
    for h in range(heads):
        strength = jnp.zeros((1, 128), jnp.float32) + bias[0, seq * heads + h] * math.log2(math.e)
        coarse = strength.astype(jnp.bfloat16).astype(jnp.float32)
        tail = jnp.where(
            row_lanes == head, coarse, jnp.where(row_lanes == head + 1, strength - coarse, 0.0)
        )
        queries.append(jnp.where(lanes < head, part_of(h * head), tail).astype(jnp.bfloat16))

    def scores_of(h, at):
        return lax.dot_general(
            queries[h][at : at + rows],
            keys[h // group],
            (((1,), (1,)), ((), ())),
            preferred_element_type=jnp.float32,
        )

    tasks = [(h, at) for h in range(heads) for at in range(0, frames, rows)]
    scores = scores_of(*tasks[0])
    for index, (h, at) in enumerate(tasks):
        ahead = scores_of(*tasks[index + 1]) if index + 1 < len(tasks) else None
        top = jnp.max(scores, axis=1, keepdims=True)
        weight = jnp.exp2(scores - top).astype(jnp.bfloat16)
        mixed = jnp.dot(weight, values[h // group], preferred_element_type=jnp.float32)
        att[at : at + rows, h * head : (h + 1) * head] = mixed[:, :head] * (
            1.0 / mixed[:, head : head + 1]
        )
        scores = ahead
    own = pl.ds(pl.multiple_of(seq * cols, 128), cols)
    attended = att[...].astype(jnp.bfloat16).astype(jnp.float32)
    output = (own_hidden[...] + gate[:, own] * attended).astype(jnp.bfloat16)
    blocks = output.reshape(pieces, rows, cols)
    for k in range(halves):
        outs[k][...] = blocks[k * part : (k + 1) * part]


def tie_kernel(*refs):
    pass


def grad_of(output, second, turn, rows, feats):
    cot = jnp.concatenate(
        [piece[rows : 2 * rows, turn * feats : (turn + 1) * feats] for piece in second], axis=0
    )
    return lax.dot_general(
        output, cot, (((0,), (0,)), ((), ())), preferred_element_type=jnp.float32
    )


def early_kernel(turns, pieces, halves, feats, *refs):
    outs, second = refs[: turns * halves], refs[turns * halves : turns * halves + pieces]
    sends, grad = refs[turns * halves + pieces : -1], refs[-1]
    section = lax.axis_index("pipe")
    offsets = offsets_of(pieces)
    part = pieces // halves
    rows = outs[0].shape[1]
    total = None
    for turn in range(turns - 1):
        blocks = []
        for p in range(pieces):
            k, j = p // part, p % part
            block = jnp.where(
                section == 0, outs[turn * halves + k][j], outs[(turn + 1) * halves + k][j]
            )
            sends[offsets[p]][turn] = block
            blocks.append(block)
        share = grad_of(jnp.concatenate(blocks, axis=0), second, turn, rows, feats)
        total = share if total is None else total + share
    grad[...] = total


def settle_kernel(turns, pieces, halves, hops, feats, *refs):
    refs = list(refs)

    def take(count):
        taken, refs[:count] = refs[:count], []
        return taken

    before, now, second, early = take(halves), take(halves), take(pieces), take(pieces)
    early_grad = take(1)[0]
    late, own_grad, grads = take(pieces), take(1)[0], take(hops - 1)
    section_out = take(1)[0]
    rows_out, total, sem = take(3)
    section, seq, rep = lax.axis_index("pipe"), lax.axis_index("seq"), lax.axis_index("dp")
    offsets = offsets_of(pieces)
    part = pieces // halves
    rows, cols = early[0].shape[1:]
    for m in range(pieces):
        lanes = pl.ds(pl.multiple_of((seq ^ m) * cols, 128), cols)
        for turn in range(turns - 1):
            rows_out[turn, :, lanes] = early[m][turn]
    copy = pltpu.make_async_copy(rows_out, section_out.at[pl.ds(0, turns - 1)], sem)
    copy.start()
    blocks = []
    for p in range(pieces):
        block = jnp.where(section == 0, before[p // part][p % part], now[p // part][p % part])
        late[offsets[p]][...] = block
        blocks.append(block)
    share = grad_of(jnp.concatenate(blocks, axis=0), second, turns - 1, rows, feats)
    factor = float(turns * hops * rows * pieces) ** (-0.5)
    total[...] = (share + early_grad[...]) * factor
    g_rows = cols // hops
    own_grad[...] = total[pl.ds(pl.multiple_of(rep * g_rows, 8), g_rows)]
    for shift in range(1, hops):
        at = pl.multiple_of(lax.rem(rep + shift, hops) * g_rows, 8)
        grads[shift - 1][...] = total[pl.ds(at, g_rows)].astype(jnp.bfloat16)
    copy.wait()


def finish_kernel(pieces, hops, *refs):
    held, late, refs = refs[0], refs[1 : pieces + 1], refs[pieces + 1 :]
    own_grad, parts, (section_out, grad, row_out, sem) = refs[0], refs[1:hops], refs[hops:]
    seq = lax.axis_index("seq")
    cols = late[0].shape[1]
    for m in range(pieces):
        lanes = pl.ds(pl.multiple_of((seq ^ m) * cols, 128), cols)
        row_out[:, lanes] = late[m][...]
    copy = pltpu.make_async_copy(row_out, section_out.at[section_out.shape[0] - 1], sem)
    copy.start()
    total = own_grad[...]
    for part in parts:
        total = total + part[...].astype(jnp.float32)
    grad[...] = total
    copy.wait()


HALVES = 2
MIB = 1024 * 1024


def paired_body(
    incoming,
    contacts,
    keyframes,
    timesteps,
    w_query,
    w_keyval,
    norm_gain,
    time_freq,
    contact_table,
    key_bias,
    attn_gate,
    head_cotangent,
):
    seq_count = lax.axis_size("seq")
    hops = lax.axis_size("dp")
    rows, width, turns = incoming.shape[3], incoming.shape[4], incoming.shape[1]
    frames = rows * seq_count
    heads_all = key_bias.shape[1]
    head = width // heads_all
    heads = heads_all // seq_count
    kv_heads = w_keyval.shape[2] // (2 * head * seq_count)
    feats = head_cotangent.shape[4]
    cols = width // seq_count
    w_rows = w_query.shape[1]
    steps = turns + 1
    part = seq_count // HALVES
    kind = jnp.bfloat16
    smem = pl.BlockSpec(memory_space=pltpu.SMEM)
    vmem = pl.BlockSpec(memory_space=pltpu.VMEM)
    anywhere = pl.BlockSpec(memory_space=pl.ANY)
    shape = jax.ShapeDtypeStruct

    def call(kernel, name, out_shape, in_specs, operands, scratch=(), limit=4, flops=0, **options):
        return pl.pallas_call(
            kernel,
            out_shape=out_shape,
            in_specs=in_specs,
            scratch_shapes=list(scratch),
            compiler_params=pltpu.CompilerParams(vmem_limit_bytes=limit * MIB),
            cost_estimate=pl.CostEstimate(
                flops=flops, bytes_accessed=flops // 512, transcendentals=0
            ),
            name=name,
            **options,
        )(*operands)

    def pin(value, space=pltpu.VMEM):
        return pltpu.with_memory_space_constraint(value, space)

    packed = call(
        pack_kernel,
        "pack",
        [pltpu.VMEM((w_rows, 2 * cols), kind)] * seq_count,
        [anywhere, anywhere],
        [pin(w_query, pltpu.HBM), pin(w_keyval, pltpu.HBM)],
        [pltpu.SemaphoreType.DMA((2 * seq_count,))],
        out_specs=[vmem] * seq_count,
    )
    blocks = [packed[0]] + [swap(packed[m], m) for m in range(1, seq_count)]

    def stacked(name, count, deps, values):
        return call(
            functools.partial(stack_kernel, len(deps)),
            name,
            pltpu.VMEM((count, w_rows, 2 * cols), kind),
            [anywhere] * len(deps) + [vmem] * len(values),
            deps + values,
            out_specs=vmem,
        )

    weights = None

    def placed(hop, parts):
        operands = [pin(part) for part in parts] + ([pin(weights)] if hop else [])
        return call(
            functools.partial(place_kernel, hop, hops),
            "place%d" % hop,
            pltpu.VMEM((width, 2 * cols), kind),
            [vmem] * len(operands),
            operands,
            out_specs=vmem,
            input_output_aliases={len(parts): 0} if hop else {},
        )

    near = stacked("near", 2, [], blocks[:2])
    near_next = shifted(near, "dp", 1)
    far = stacked("far", 2, [near_next], blocks[2:])
    far_next = shifted(far, "dp", 1)
    rings = [[near, near_next], [far, far_next]]
    for hop in range(2, hops - 1):
        for chunks in rings:
            chunks.append(shifted(chunks[-1], "dp", 1))
    last_chunk = [shifted(chunks[-1], "dp", 1) for chunks in rings]
    for hop in range(hops - 1):
        weights = placed(hop, [chunks[hop] for chunks in rings])

    def tie(values, deps):
        return call(
            tie_kernel,
            "tie",
            [shape(value.shape, kind) for value in values],
            [anywhere] * (len(values) + len(deps)),
            list(values) + list(deps),
            out_specs=[anywhere] * len(values),
            input_output_aliases={i: i for i in range(len(values))},
        )

    mine = call(
        functools.partial(first_kernel, turns),
        "first",
        pltpu.VMEM((2 * rows + 16, width), kind),
        [anywhere, vmem, vmem],
        [far, incoming, contacts],
        [pltpu.VMEM((16, 128), jnp.float32)],
        out_specs=vmem,
    )
    across = swap(mine, 2)
    beside = swap(mine, 1)
    (across,) = tie([across], [last_chunk[0], rings[1][-1]])
    first = [mine, across, beside, swap(across, 1)]
    prepared = call(
        functools.partial(norm_kernel, turns, seq_count),
        "norm",
        [pltpu.VMEM((frames, width), kind)] * 2
        + [pltpu.VMEM((frames, 128), jnp.float32)] * 2
        + [pltpu.VMEM((frames, cols), jnp.float32)] * 2
        + [pltpu.VMEM((frames, width), kind)] * 2,
        [smem] + [vmem] * 3 + [anywhere] * (seq_count + 2),
        [timesteps, contact_table, norm_gain, time_freq]
        + [pin(piece, pltpu.HBM) for piece in first]
        + [weights, last_chunk[0]],
        [pltpu.VMEM((1, width), jnp.float32)]
        + [pltpu.VMEM((2 * rows + 16, width), kind)] * seq_count
        + [pltpu.SemaphoreType.DMA((seq_count,))],
        12,
        out_specs=[vmem] * 8,
    )

    mine = call(
        second_kernel,
        "second",
        pltpu.VMEM((2 * rows, width), kind),
        [anywhere, vmem, vmem],
        [across, incoming, head_cotangent],
        out_specs=vmem,
    )
    second = [mine, swap(mine, 2), swap(mine, 1)]

    outputs = []
    relayed = {}
    for step in range(steps):
        cfg = {
            "step": step,
            "has_relay": step in relayed,
            "pieces": seq_count,
            "hops": hops,
            "head": head,
            "heads": heads,
            "group": heads // kv_heads,
            "turns": turns,
            "halves": HALVES,
        }
        operands = [key_bias, timesteps, norm_gain, time_freq, attn_gate, keyframes]
        scratch = [
            pltpu.VMEM((frames, 2 * cols + 128), kind),
            pltpu.VMEM((frames, cols), jnp.float32),
        ]
        if step in relayed:
            large = second + [prepared[4 + step]] + relayed[step]
            scratch += [
                pltpu.VMEM((frames, width), kind),
                pltpu.VMEM((frames, 128), jnp.float32),
                pltpu.VMEM((frames, cols), jnp.float32),
                pltpu.VMEM((1, width), jnp.float32),
            ]
        else:
            large = [prepared[step], prepared[2 + step], prepared[4 + step]]
        large += last_chunk + [weights] if step == 0 else [weights]
        operands += [pin(value) for value in large]
        out_shape = [pltpu.VMEM((part, rows, cols), kind)] * HALVES
        if step == 0:
            out_shape += [pltpu.VMEM((width, 2 * cols), kind)]
        results = call(
            functools.partial(step_kernel, cfg),
            "step%d" % step,
            out_shape,
            [smem, smem] + [vmem] * (len(operands) - 2),
            operands,
            scratch,
            16,
            2 * frames * width * 2 * cols + 4 * heads * frames * frames * head,
            out_specs=[vmem] * len(out_shape),
            input_output_aliases={len(operands) - 1: HALVES} if step == 0 else {},
        )
        outputs.append(list(results[:HALVES]))
        if step == 0:
            weights = results[HALVES]
            (second[1],) = tie([second[1]], [outputs[-1][0]])
            second.append(swap(second[1], 1))
        if step == 2:
            pending = [piece for k in range(HALVES) for piece in (crossing[k][0], crossing[k][1])]
            tied = tie(pending, [outputs[-1][0]])
            relayed[3] = []
            for k in range(HALVES):
                mine, across = tied[2 * k], tied[2 * k + 1]
                relayed[3] += [mine, across, swap(mine, 1), swap(across, 1)]
            early = call(
                functools.partial(early_kernel, turns, seq_count, HALVES, feats),
                "early",
                [shape((turns - 1, rows, cols), kind)] * seq_count
                + [shape((cols, feats), jnp.float32)],
                [vmem] * (turns * HALVES + seq_count),
                [half for output in outputs for half in output] + second,
                limit=8,
                out_specs=[vmem] * (seq_count + 1),
            )
            early, early_grad = list(early[:-1]), early[-1]
            early = [early[0]] + [swap(early[m], m) for m in range(1, seq_count)]
        if step + 2 < steps:
            crossing = []
            for half in outputs[-1]:
                piece = handed_over(half)
                crossing.append((piece, swap(piece, 2)))
            if step == 0:
                relayed[2] = []
                for mine, across in crossing:
                    relayed[2] += [mine, across, swap(mine, 1), swap(across, 1)]

    g_shape = (cols // hops, feats)
    operands = outputs[-2] + outputs[-1] + second + early + [early_grad]
    settled = call(
        functools.partial(settle_kernel, turns, seq_count, HALVES, hops, feats),
        "settle",
        [shape((rows, cols), kind)] * seq_count
        + [shape(g_shape, jnp.float32)]
        + [shape(g_shape, kind)] * (hops - 1)
        + [shape((turns, rows, width), kind)],
        [vmem] * len(operands),
        operands,
        [
            pltpu.VMEM((turns - 1, rows, width), kind),
            pltpu.VMEM((cols, feats), jnp.float32),
            pltpu.SemaphoreType.DMA,
        ],
        8,
        out_specs=[vmem] * (seq_count + hops) + [anywhere],
    )
    late, grads, held = settled[:seq_count], settled[seq_count:-1], settled[-1]
    late = [late[0]] + [swap(late[m], m) for m in range(1, seq_count)]
    grads = [grads[0]] + [shifted(grads[k], "dp", k) for k in range(1, hops)]
    section_out, grad_rows = call(
        functools.partial(finish_kernel, seq_count, hops),
        "finish",
        [shape((turns, rows, width), kind), shape(g_shape, jnp.float32)],
        [anywhere] + [vmem] * (seq_count + hops),
        [held] + late + grads,
        [pltpu.VMEM((rows, width), kind), pltpu.SemaphoreType.DMA],
        out_specs=[anywhere, vmem],
        input_output_aliases={0: 0},
    )
    return (section_out[None, :, None], grad_rows[None])


def body(incoming, contacts, keyframes, timesteps, w_query, *others):
    count = lax.axis_size("seq")
    cols = w_query.shape[2] // count
    paired = (
        lax.axis_size("pipe") == 2
        and count == 4
        and cols % 128 == 0
        and w_query.shape[1] % 16 == 0
        and incoming.shape[3] == 128
        and incoming.shape[1] == 3
    )
    chosen = paired_body if paired else general_body
    return chosen(incoming, contacts, keyframes, timesteps, w_query, *others)


def general_body(
    incoming,
    contacts,
    keyframes,
    timesteps,
    w_query,
    w_keyval,
    norm_gain,
    time_freq,
    contact_table,
    key_bias,
    attn_gate,
    head_cotangent,
):
    section_idx = lax.axis_index("pipe")
    seq_idx = lax.axis_index("seq")
    rep_idx = lax.axis_index("dp")
    seq_count = lax.axis_size("seq")
    section_count = lax.axis_size("pipe")
    rep_count = lax.axis_size("dp")
    tok_rows = incoming.shape[3]
    width = incoming.shape[4]
    turns = incoming.shape[1]
    frames = tok_rows * seq_count
    heads_all = key_bias.shape[1]
    head_size = width // heads_all
    heads_local = heads_all // seq_count
    kv_width = w_keyval.shape[2]
    kv_local = kv_width // (2 * head_size * seq_count)
    group_size = heads_local // kv_local
    feat_count = head_cotangent.shape[4]
    score_scale = head_size ** (-0.5)
    q_cols = width // seq_count
    kv_cols = kv_width // seq_count
    w_rows = w_query.shape[1]

    w_parts = jnp.concatenate(
        [
            w_query[0].reshape(w_rows, seq_count, q_cols),
            w_keyval[0].reshape(w_rows, seq_count, kv_cols),
        ],
        axis=2,
    ).transpose(1, 0, 2)
    block = lax.all_to_all(w_parts, "seq", split_axis=0, concat_axis=0, tiled=True)
    weights = jnp.zeros((seq_count, rep_count, w_rows, q_cols + kv_cols), jnp.bfloat16)
    for hop in range(rep_count):
        owner = lax.rem(rep_idx + rep_count - hop, rep_count)
        weights = lax.dynamic_update_slice_in_dim(weights, block[:, None], owner, 1)
        if hop + 1 < rep_count:
            block = ring(block, "dp")
    weights = weights.reshape(width, q_cols + kv_cols)

    gain_row = norm_gain[0]
    freq_row = time_freq[0]
    table = contact_table[0]
    gate_local = lax.dynamic_slice_in_dim(attn_gate[0], seq_idx * q_cols, q_cols)
    table_local = lax.dynamic_slice_in_dim(table, seq_idx * q_cols, q_cols, 1)
    bias_local = lax.dynamic_slice_in_dim(key_bias[0], seq_idx * heads_local, heads_local)
    contact_all = lax.all_gather(contacts[:, 0, :], "seq", axis=1, tiled=True)
    key_all = keyframes[:, 0, :]
    step_all = timesteps[:, 0]
    labels = jnp.arange(table.shape[0], dtype=jnp.int32)
    cot_all = lax.all_gather(head_cotangent[0, :, 0], "seq", axis=1, tiled=True)

    lag = 2 if section_count == 2 else 1
    if lag == 2:
        steps = turns + 1
    else:
        steps = turns

    def turn_at(step):
        if lag == 1:
            return jnp.int32(step)
        return jnp.clip(step - section_idx, 0, turns - 1)

    outputs = []
    handed = {}
    for step in range(steps):
        turn = turn_at(step)
        fresh = lax.dynamic_index_in_dim(incoming[0, :, 0], turn, 0, keepdims=False)
        current = lax.all_gather(fresh, "seq", axis=0, tiled=True)
        if step in handed:
            current = jnp.where((section_idx == 0) | (turn == 0), current, handed[step])
        batch_idx = turn - section_idx + section_count - 1
        contact_rows = lax.dynamic_index_in_dim(contact_all, batch_idx, 0, keepdims=False)
        key_flags = lax.dynamic_index_in_dim(key_all, batch_idx, 0, keepdims=False).astype(
            jnp.float32
        )
        timestep = lax.dynamic_index_in_dim(step_all, batch_idx, 0, keepdims=False).astype(
            jnp.float32
        )
        onehot = (contact_rows[:, None] == labels[None, :]).astype(jnp.bfloat16)
        hidden = current.astype(jnp.float32) + jnp.dot(
            onehot, table, preferred_element_type=jnp.float32
        )
        root_mean = jnp.sqrt(jnp.mean(hidden * hidden, axis=-1, keepdims=True) + epsilon)
        modulation = gain_row * (1.0 + 0.5 * jnp.sin(timestep * freq_row))
        normed = (hidden / root_mean * modulation[None, :]).astype(jnp.bfloat16)
        projected = jnp.dot(normed, weights, preferred_element_type=jnp.float32).astype(
            jnp.bfloat16
        )
        query_heads = projected[:, :q_cols].reshape(frames, heads_local, head_size)
        keyval_heads = projected[:, q_cols:].reshape(frames, kv_local, 2, head_size)
        head_outputs = []
        for head in range(heads_local):
            key_rows = keyval_heads[:, head // group_size, 0]
            value_rows = keyval_heads[:, head // group_size, 1]
            scores = (
                lax.dot_general(
                    query_heads[:, head],
                    key_rows,
                    (((1,), (1,)), ((), ())),
                    preferred_element_type=jnp.float32,
                )
                * score_scale
            )
            scores = scores + bias_local[head] * key_flags[None, :]
            row_max = jnp.max(scores, axis=-1, keepdims=True)
            exponent = jnp.exp(scores - row_max)
            probabilities = (exponent / jnp.sum(exponent, axis=-1, keepdims=True)).astype(
                jnp.bfloat16
            )
            head_outputs.append(
                jnp.dot(probabilities, value_rows, preferred_element_type=jnp.float32).astype(
                    jnp.bfloat16
                )
            )
        attended = jnp.concatenate(head_outputs, axis=1)
        hidden_local = lax.dynamic_slice_in_dim(current, seq_idx * q_cols, q_cols, 1).astype(
            jnp.float32
        ) + jnp.dot(onehot, table_local, preferred_element_type=jnp.float32)
        output = (hidden_local + gate_local[None, :] * attended.astype(jnp.float32)).astype(
            jnp.bfloat16
        )
        outputs.append(output)
        if step + lag < steps:
            piece = passed_along(output, "pipe", 1)
            handed[step + lag] = lax.all_gather(piece, "seq", axis=1, tiled=True)

    factor = float(turns * rep_count * frames) ** (-0.5)
    total = None
    rows_out = []
    for turn in range(turns):
        if lag == 2:
            own = jnp.where(section_idx == 0, outputs[turn], outputs[turn + 1])
        else:
            own = outputs[turn]
        term = lax.dot_general(
            own, cot_all[turn], (((0,), (0,)), ((), ())), preferred_element_type=jnp.float32
        )
        total = term if total is None else total + term
        rows_out.append(lax.all_to_all(own, "seq", split_axis=0, concat_axis=1, tiled=True))
    section_out = jnp.stack(rows_out)[None, :, None]
    grad_parts = lax.all_to_all(
        (total * factor).astype(jnp.bfloat16).reshape(rep_count, q_cols // rep_count, feat_count),
        "dp",
        split_axis=0,
        concat_axis=0,
        tiled=True,
    )
    grad_rows = jnp.sum(grad_parts.astype(jnp.float32), axis=0)
    return (section_out, grad_rows[None])


def solution(mesh):
    in_specs = (
        P("pipe", None, "dp", "seq", None),
        P(None, "dp", "seq"),
        P(None, "dp", None),
        P(None, "dp"),
        P("pipe", ("seq", "dp"), None),
        P("pipe", ("seq", "dp"), None),
        P("pipe", None),
        P("pipe", None),
        P("pipe", None, None),
        P("pipe", None),
        P("pipe", None),
        P("pipe", None, "dp", "seq", None),
    )
    out_specs = (P("pipe", None, "dp", "seq", None), P("pipe", ("seq", "dp"), None))
    return jax.shard_map(body, mesh=mesh, in_specs=in_specs, out_specs=out_specs, check_vma=False)
```

```python
import functools
import math

import jax
import jax.numpy as jnp
from jax import lax
from jax.experimental import pallas as pl
from jax.experimental.pallas import tpu as pltpu
from jax.sharding import PartitionSpec as P

epsilon = 1e-06


def passed_along(value, axis, steps):
    count = lax.axis_size(axis)
    first, last = (max(0, -steps), min(count, count - steps))
    return lax.ppermute(value, axis, [(source, source + steps) for source in range(first, last)])


def ring(value, axis):
    count = lax.axis_size(axis)
    return lax.ppermute(value, axis, [(source, (source + 1) % count) for source in range(count)])


def swap(value, bit):
    count = lax.axis_size("seq")
    return lax.ppermute(value, "seq", [(source, source ^ bit) for source in range(count)])


def handed_over(value):
    return lax.ppermute(value, "pipe", [(0, 1), (1, 0)])


def shifted(value, axis, shift):
    count = lax.axis_size(axis)
    return lax.ppermute(value, axis, [(source, (source + shift) % count) for source in range(count)])


def fold(index):
    return index ^ (index >> 1)


def ring_step(value):
    count = lax.axis_size("dp")
    pairs = [(fold(place), fold((place + 1) % count)) for place in range(count)]
    return lax.ppermute(value, "dp", pairs)


def offsets_of(count):
    offsets = [0]
    bit = count // 2
    while bit:
        offsets = offsets + [offset ^ bit for offset in offsets]
        bit //= 2
    return offsets


def turn_and_batch(step, turns):
    section = lax.axis_index("pipe")
    turn = jnp.clip(step - section, 0, turns - 1)
    return turn, turn - section + 1


def pack_kernel(wq, wkv, *refs):
    outs, sems = refs[:-1], refs[-1]
    cols = outs[0].shape[1] // 2
    seq = lax.axis_index("seq")
    copies = []
    for m, out in enumerate(outs):
        start = pl.multiple_of((seq ^ m) * cols, 128)
        for k, source in enumerate((wq, wkv)):
            copies.append(
                pltpu.make_async_copy(
                    source.at[0, :, pl.ds(start, cols)],
                    out.at[:, pl.ds(k * cols, cols)],
                    sems.at[2 * m + k],
                )
            )
    for copy in copies:
        copy.start()
    for copy in copies:
        copy.wait()


def stack_kernel(deps, *refs):
    out = refs[-1]
    at = 0
    for ref in refs[deps:-1]:
        if len(ref.shape) == 2:
            out[at] = ref[...]
            at += 1
        else:
            out[at : at + ref.shape[0]] = ref[...]
            at += ref.shape[0]


def place_kernel(hop, hops, *refs):
    weights, parts = refs[-1], refs[:-1]
    if hop > 0:
        parts = parts[:-1]
    place(hop, hops, parts, weights)


def place(hop, hops, parts, weights):
    seq, rep = lax.axis_index("seq"), lax.axis_index("dp")
    m = 0
    for part in parts:
        count, rows = part.shape[:2]
        for j in range(count):
            block = (seq ^ m) * hops + fold(lax.rem(fold(rep) + hops - hop, hops))
            weights[pl.ds(pl.multiple_of(block * rows, 16), rows)] = part[j]
            m += 1


def first_kernel(turns, far, incoming, contacts, out, states):
    rows = incoming.shape[3]
    for turn in range(2):
        out[turn * rows : (turn + 1) * rows] = incoming[0, turn, 0]
    states[...] = jnp.zeros_like(states)
    for step in range(turns + 1):
        _, batch = turn_and_batch(step, turns)
        states[step : step + 1] = contacts[batch].astype(jnp.float32)
    out[2 * rows :, : states.shape[1]] = states[...].astype(jnp.bfloat16)


def second_kernel(dep, incoming, cotangent, out):
    turns, rows, feats = cotangent.shape[1], cotangent.shape[3], cotangent.shape[4]
    out[:rows] = incoming[0, 2, 0]
    for turn in range(turns):
        out[rows:, turn * feats : (turn + 1) * feats] = cotangent[0, turn, 0]


def columns_of(rows_of, pieces, rows):
    labels = lax.broadcasted_iota(jnp.int32, (32, rows), 0)
    columns = []
    for i in range(pieces):
        state, flag = rows_of(i)
        one = jnp.zeros((32, rows), jnp.float32)
        if state is not None:
            one = jnp.where(labels == state, 1.0, 0.0)
        if flag is not None:
            one = jnp.where(labels == 16, flag, one)
        columns.append(one.T)
    return jnp.concatenate(columns, axis=0)


def modulation(step, turns, times, gain, freq):
    _, batch = turn_and_batch(step, turns)
    return gain[...] * (1.0 + 0.5 * jnp.sin(times[batch, 0].astype(jnp.float32) * freq[...]))


def norm_kernel(turns, pieces, times, table, gain, freq, *refs):
    sources, refs = refs[:pieces], refs[pieces + 1 :]
    scaled, scales, owns, embeds, mod = refs[0:2], refs[2:4], refs[4:6], refs[6:8], refs[8]
    first, sems = refs[9 : 9 + pieces], refs[9 + pieces]
    copies = [
        pltpu.make_async_copy(sources[i], first[i], sems.at[i]) for i in range(pieces)
    ]
    for copy in copies:
        copy.start()
    for copy in copies:
        copy.wait()
    frames, width = scaled[0].shape
    rows, cols = frames // pieces, owns[0].shape[1]
    seq = lax.axis_index("seq")
    offsets = offsets_of(pieces)
    for step in range(turns + 1):

        def state_of(i):
            state = first[i][2 * rows : 2 * rows + 16, :rows][step : step + 1]
            return state.astype(jnp.float32).astype(jnp.int32), None

        onehot = columns_of(state_of, pieces, rows)[:, : table.shape[1]].astype(jnp.bfloat16)
        if step >= 2:
            for at in range(0, width, 256):
                embeds[step - 2][:, at : at + 256] = jnp.dot(
                    onehot, table[0, :, at : at + 256], preferred_element_type=jnp.float32
                ).astype(jnp.bfloat16)
            continue
        turn, _ = turn_and_batch(step, turns)
        at = pl.multiple_of(jnp.minimum(turn, 1) * rows, 128)
        mod[...] = modulation(step, turns, times, gain, freq)
        total = jnp.zeros((frames, 128), jnp.float32)
        for i in range(pieces):
            lanes = pl.ds(pl.multiple_of((seq ^ offsets[i]) * cols, 128), cols)
            current = jnp.concatenate([first[p][pl.ds(at, rows), lanes] for p in range(pieces)])
            hidden = current.astype(jnp.float32) + jnp.dot(
                onehot, table[0, :, lanes], preferred_element_type=jnp.float32
            )
            for lane in range(0, cols, 128):
                piece = hidden[:, lane : lane + 128]
                total = total + piece * piece
            scaled[step][:, lanes] = (hidden * mod[:, lanes]).astype(jnp.bfloat16)
            if i == 0:
                owns[step][...] = hidden
        mean = jnp.sum(total, axis=1, keepdims=True) * (1.0 / width)
        scales[step][...] = jnp.broadcast_to(lax.rsqrt(mean + epsilon), (frames, 128))


def step_kernel(cfg, *refs):
    step, has_relay = cfg["step"], cfg["has_relay"]
    pieces, hops, head, turns = cfg["pieces"], cfg["hops"], cfg["head"], cfg["turns"]
    heads, group, halves = cfg["heads"], cfg["group"], cfg["halves"]
    refs = list(refs)

    def take(count):
        taken, refs[:count] = refs[:count], []
        return taken

    bias, times, gain, freq, gate, flags = take(6)
    if has_relay:
        second, embed, relay = take(pieces), take(1)[0], take(pieces * halves)
    else:
        scaled, scales, own_hidden = take(3)
    chunk = take(2) if step == 0 else None
    weights = take(1)[0]
    outs = take(halves)
    if step == 0:
        weights = take(1)[0]
    proj, att = take(2)
    if has_relay:
        scaled, scales, own_hidden, mod = take(4)
    offsets = offsets_of(pieces)
    frames, width = scaled.shape
    rows, cols = frames // pieces, att.shape[1]
    part = pieces // halves
    seq, rep, section = lax.axis_index("seq"), lax.axis_index("dp"), lax.axis_index("pipe")
    _, batch = turn_and_batch(step, turns)

    if step == 0:
        place(hops - 1, hops, chunk, weights)

    def normalize(relayed):
        total = jnp.zeros((frames, 128), jnp.float32)
        for i in range(pieces):
            lanes = pl.ds(pl.multiple_of((seq ^ offsets[i]) * cols, 128), cols)
            blocks = []
            for p in range(pieces):
                if relayed:
                    j = offsets.index(offsets[i] ^ offsets[p])
                    blocks.append(relay[(j // part) * pieces + i][j % part])
                else:
                    blocks.append(second[p][:rows, lanes])
            hidden = jnp.concatenate(blocks, axis=0).astype(jnp.float32)
            hidden = hidden + embed[:, lanes].astype(jnp.float32)
            for lane in range(0, cols, 128):
                piece = hidden[:, lane : lane + 128]
                total = total + piece * piece
            scaled[:, lanes] = (hidden * mod[:, lanes]).astype(jnp.bfloat16)
            if i == 0:
                own_hidden[...] = hidden
        scales[...] = total

    if has_relay:
        mod[...] = modulation(step, turns, times, gain, freq)

        @pl.when(section == 0)
        def _():
            normalize(False)

        @pl.when(section != 0)
        def _():
            normalize(True)

        mean = jnp.sum(scales[...], axis=1, keepdims=True) * (1.0 / width)
        scale = lax.rsqrt(mean + epsilon)
    else:
        scale = scales[:, :1]

    def flag_of(i):
        lanes = pl.ds(pl.multiple_of((seq ^ offsets[i]) * rows, 128), rows)
        return None, flags[batch, :, lanes].astype(jnp.float32)

    flag_column = columns_of(flag_of, pieces, rows)[:, 16:17]
    projected = jnp.dot(scaled[...], weights[...], preferred_element_type=jnp.float32) * scale
    score_scale = head ** (-0.5) * math.log2(math.e)
    proj[:, :cols] = (projected[:, :cols] * score_scale).astype(jnp.bfloat16)
    proj[:, cols : 2 * cols] = projected[:, cols:].astype(jnp.bfloat16)
    proj[:, 2 * cols :] = jnp.zeros((frames, 128), jnp.bfloat16)
    lanes = lax.broadcasted_iota(jnp.int32, (frames, 128), 1)
    row_lanes = lax.broadcasted_iota(jnp.int32, (1, 128), 1)
    flag_lanes = jnp.logical_or(lanes == head, lanes == head + 1)

    def part_of(at):
        return proj[:, at : at + 128].astype(jnp.float32)

    keys, values = [], []
    for kv in range(heads // group):
        base = cols + kv * 2 * head
        key = jnp.where(flag_lanes, flag_column, jnp.where(lanes < head, part_of(base), 0.0))
        value = jnp.where(lanes < head, part_of(base + head), jnp.where(lanes == head, 1.0, 0.0))
        keys.append(key.astype(jnp.bfloat16))
        values.append(value.astype(jnp.bfloat16))

    def scores_of(h):
        strength = jnp.zeros((1, 128), jnp.float32) + bias[0, seq * heads + h] * math.log2(math.e)
        coarse = strength.astype(jnp.bfloat16).astype(jnp.float32)
        tail = jnp.where(
            row_lanes == head, coarse, jnp.where(row_lanes == head + 1, strength - coarse, 0.0)
        )
        query = jnp.where(lanes < head, part_of(h * head), tail).astype(jnp.bfloat16)
        return lax.dot_general(
            query, keys[h // group], (((1,), (1,)), ((), ())), preferred_element_type=jnp.float32
        )

    scores = scores_of(0)
    for h in range(heads):
        ahead = scores_of(h + 1) if h + 1 < heads else None
        top = jnp.max(scores, axis=1, keepdims=True)
        weight = jnp.exp2((scores - top).astype(jnp.bfloat16))
        mixed = jnp.dot(weight, values[h // group], preferred_element_type=jnp.float32)
        att[:, h * head : (h + 1) * head] = mixed[:, :head] * (1.0 / mixed[:, head : head + 1])
        scores = ahead
    own = pl.ds(pl.multiple_of(seq * cols, 128), cols)
    attended = att[...].astype(jnp.bfloat16).astype(jnp.float32)
    output = (own_hidden[...] + gate[:, own] * attended).astype(jnp.bfloat16)
    blocks = output.reshape(pieces, rows, cols)
    for k in range(halves):
        outs[k][...] = blocks[k * part : (k + 1) * part]


def tie_kernel(*refs):
    pass


def grad_of(output, second, turn, rows, feats):
    cot = jnp.concatenate(
        [piece[rows : 2 * rows, turn * feats : (turn + 1) * feats] for piece in second], axis=0
    )
    return lax.dot_general(
        output, cot, (((0,), (0,)), ((), ())), preferred_element_type=jnp.float32
    )


def early_kernel(turns, pieces, halves, feats, *refs):
    outs, second = refs[: turns * halves], refs[turns * halves : turns * halves + pieces]
    sends, grad = refs[turns * halves + pieces : -1], refs[-1]
    section = lax.axis_index("pipe")
    offsets = offsets_of(pieces)
    part = pieces // halves
    rows = outs[0].shape[1]
    total = None
    for turn in range(turns - 1):
        blocks = []
        for p in range(pieces):
            k, j = p // part, p % part
            block = jnp.where(
                section == 0, outs[turn * halves + k][j], outs[(turn + 1) * halves + k][j]
            )
            sends[offsets[p]][turn] = block
            blocks.append(block)
        share = grad_of(jnp.concatenate(blocks, axis=0), second, turn, rows, feats)
        total = share if total is None else total + share
    grad[...] = total


def settle_kernel(turns, pieces, halves, hops, feats, *refs):
    refs = list(refs)

    def take(count):
        taken, refs[:count] = refs[:count], []
        return taken

    before, now, second, early = take(halves), take(halves), take(pieces), take(pieces)
    early_grad = take(1)[0]
    late, own_grad, grads = take(pieces), take(1)[0], take(hops - 1)
    section_out = take(1)[0]
    rows_out, total, sem = take(3)
    section, seq, rep = lax.axis_index("pipe"), lax.axis_index("seq"), lax.axis_index("dp")
    offsets = offsets_of(pieces)
    part = pieces // halves
    rows, cols = early[0].shape[1:]
    for m in range(pieces):
        lanes = pl.ds(pl.multiple_of((seq ^ m) * cols, 128), cols)
        for turn in range(turns - 1):
            rows_out[turn, :, lanes] = early[m][turn]
    copy = pltpu.make_async_copy(rows_out, section_out.at[pl.ds(0, turns - 1)], sem)
    copy.start()
    blocks = []
    for p in range(pieces):
        block = jnp.where(section == 0, before[p // part][p % part], now[p // part][p % part])
        late[offsets[p]][...] = block
        blocks.append(block)
    share = grad_of(jnp.concatenate(blocks, axis=0), second, turns - 1, rows, feats)
    factor = float(turns * hops * rows * pieces) ** (-0.5)
    total[...] = (share + early_grad[...]) * factor
    g_rows = cols // hops
    own_grad[...] = total[pl.ds(pl.multiple_of(rep * g_rows, 8), g_rows)]
    for shift in range(1, hops):
        at = pl.multiple_of(lax.rem(rep + shift, hops) * g_rows, 8)
        grads[shift - 1][...] = total[pl.ds(at, g_rows)].astype(jnp.bfloat16)
    copy.wait()


def finish_kernel(pieces, hops, *refs):
    held, late, refs = refs[0], refs[1 : pieces + 1], refs[pieces + 1 :]
    own_grad, parts, (section_out, grad, row_out, sem) = refs[0], refs[1:hops], refs[hops:]
    seq = lax.axis_index("seq")
    cols = late[0].shape[1]
    for m in range(pieces):
        lanes = pl.ds(pl.multiple_of((seq ^ m) * cols, 128), cols)
        row_out[:, lanes] = late[m][...]
    copy = pltpu.make_async_copy(row_out, section_out.at[section_out.shape[0] - 1], sem)
    copy.start()
    total = own_grad[...]
    for part in parts:
        total = total + part[...].astype(jnp.float32)
    grad[...] = total
    copy.wait()


HALVES = 2
MIB = 1024 * 1024


def paired_body(
    incoming,
    contacts,
    keyframes,
    timesteps,
    w_query,
    w_keyval,
    norm_gain,
    time_freq,
    contact_table,
    key_bias,
    attn_gate,
    head_cotangent,
):
    seq_count = lax.axis_size("seq")
    hops = lax.axis_size("dp")
    rows, width, turns = incoming.shape[3], incoming.shape[4], incoming.shape[1]
    frames = rows * seq_count
    heads_all = key_bias.shape[1]
    head = width // heads_all
    heads = heads_all // seq_count
    kv_heads = w_keyval.shape[2] // (2 * head * seq_count)
    feats = head_cotangent.shape[4]
    cols = width // seq_count
    w_rows = w_query.shape[1]
    steps = turns + 1
    part = seq_count // HALVES
    kind = jnp.bfloat16
    smem = pl.BlockSpec(memory_space=pltpu.SMEM)
    vmem = pl.BlockSpec(memory_space=pltpu.VMEM)
    anywhere = pl.BlockSpec(memory_space=pl.ANY)
    shape = jax.ShapeDtypeStruct

    def call(kernel, name, out_shape, in_specs, operands, scratch=(), limit=4, flops=0, **options):
        return pl.pallas_call(
            kernel,
            out_shape=out_shape,
            in_specs=in_specs,
            scratch_shapes=list(scratch),
            compiler_params=pltpu.CompilerParams(vmem_limit_bytes=limit * MIB),
            cost_estimate=pl.CostEstimate(
                flops=flops, bytes_accessed=flops // 512, transcendentals=0
            ),
            name=name,
            **options,
        )(*operands)

    def pin(value, space=pltpu.VMEM):
        return pltpu.with_memory_space_constraint(value, space)

    packed = call(
        pack_kernel,
        "pack",
        [pltpu.VMEM((w_rows, 2 * cols), kind)] * seq_count,
        [anywhere, anywhere],
        [pin(w_query, pltpu.HBM), pin(w_keyval, pltpu.HBM)],
        [pltpu.SemaphoreType.DMA((2 * seq_count,))],
        out_specs=[vmem] * seq_count,
    )
    blocks = [packed[0]] + [swap(packed[m], m) for m in range(1, seq_count)]

    def stacked(name, count, deps, values):
        return call(
            functools.partial(stack_kernel, len(deps)),
            name,
            pltpu.VMEM((count, w_rows, 2 * cols), kind),
            [anywhere] * len(deps) + [vmem] * len(values),
            deps + values,
            out_specs=vmem,
        )

    weights = None

    def placed(hop, parts):
        operands = [pin(part) for part in parts] + ([pin(weights)] if hop else [])
        return call(
            functools.partial(place_kernel, hop, hops),
            "place%d" % hop,
            pltpu.VMEM((width, 2 * cols), kind),
            [vmem] * len(operands),
            operands,
            out_specs=vmem,
            input_output_aliases={len(parts): 0} if hop else {},
        )

    near = stacked("near", 2, [], blocks[:2])
    near_next = ring_step(near)
    far = stacked("far", 2, [near_next], blocks[2:])
    far_next = ring_step(far)
    rings = [[near, near_next], [far, far_next]]
    for hop in range(2, hops - 1):
        for chunks in rings:
            chunks.append(ring_step(chunks[-1]))
    last_chunk = [ring_step(chunks[-1]) for chunks in rings]
    for hop in range(hops - 1):
        weights = placed(hop, [chunks[hop] for chunks in rings])

    def tie(values, deps):
        return call(
            tie_kernel,
            "tie",
            [shape(value.shape, kind) for value in values],
            [anywhere] * (len(values) + len(deps)),
            list(values) + list(deps),
            out_specs=[anywhere] * len(values),
            input_output_aliases={i: i for i in range(len(values))},
        )

    mine = call(
        functools.partial(first_kernel, turns),
        "first",
        pltpu.VMEM((2 * rows + 16, width), kind),
        [anywhere, vmem, vmem],
        [far, incoming, contacts],
        [pltpu.VMEM((16, 128), jnp.float32)],
        out_specs=vmem,
    )
    across = swap(mine, 2)
    beside = swap(mine, 1)
    (across,) = tie([across], [chunks[-1] for chunks in rings])
    first = [mine, across, beside, swap(across, 1)]
    prepared = call(
        functools.partial(norm_kernel, turns, seq_count),
        "norm",
        [pltpu.VMEM((frames, width), kind)] * 2
        + [pltpu.VMEM((frames, 128), jnp.float32)] * 2
        + [pltpu.VMEM((frames, cols), jnp.float32)] * 2
        + [pltpu.VMEM((frames, width), kind)] * 2,
        [smem] + [vmem] * 3 + [anywhere] * (seq_count + 1),
        [timesteps, contact_table, norm_gain, time_freq]
        + [pin(piece, pltpu.HBM) for piece in first]
        + [weights],
        [pltpu.VMEM((1, width), jnp.float32)]
        + [pltpu.VMEM((2 * rows + 16, width), kind)] * seq_count
        + [pltpu.SemaphoreType.DMA((seq_count,))],
        12,
        out_specs=[vmem] * 8,
    )

    mine = call(
        second_kernel,
        "second",
        pltpu.VMEM((2 * rows, width), kind),
        [anywhere, vmem, vmem],
        [across, incoming, head_cotangent],
        out_specs=vmem,
    )
    second = [mine, swap(mine, 2), swap(mine, 1)]

    outputs = []
    relayed = {}
    for step in range(steps):
        cfg = {
            "step": step,
            "has_relay": step in relayed,
            "pieces": seq_count,
            "hops": hops,
            "head": head,
            "heads": heads,
            "group": heads // kv_heads,
            "turns": turns,
            "halves": HALVES,
        }
        operands = [key_bias, timesteps, norm_gain, time_freq, attn_gate, keyframes]
        scratch = [
            pltpu.VMEM((frames, 2 * cols + 128), kind),
            pltpu.VMEM((frames, cols), jnp.float32),
        ]
        if step in relayed:
            large = second + [prepared[4 + step]] + relayed[step]
            scratch += [
                pltpu.VMEM((frames, width), kind),
                pltpu.VMEM((frames, 128), jnp.float32),
                pltpu.VMEM((frames, cols), jnp.float32),
                pltpu.VMEM((1, width), jnp.float32),
            ]
        else:
            large = [prepared[step], prepared[2 + step], prepared[4 + step]]
        large += last_chunk + [weights] if step == 0 else [weights]
        operands += [pin(value) for value in large]
        out_shape = [pltpu.VMEM((part, rows, cols), kind)] * HALVES
        if step == 0:
            out_shape += [pltpu.VMEM((width, 2 * cols), kind)]
        results = call(
            functools.partial(step_kernel, cfg),
            "step%d" % step,
            out_shape,
            [smem, smem] + [vmem] * (len(operands) - 2),
            operands,
            scratch,
            16,
            2 * frames * width * 2 * cols + 4 * heads * frames * frames * head,
            out_specs=[vmem] * len(out_shape),
            input_output_aliases={len(operands) - 1: HALVES} if step == 0 else {},
        )
        outputs.append(list(results[:HALVES]))
        if step == 0:
            weights = results[HALVES]
        if step == 0:
            (second[1],) = tie([second[1]], [outputs[-1][0]])
            second.append(swap(second[1], 1))
        if step == 2:
            pending = [piece for k in range(HALVES) for piece in (crossing[k][0], crossing[k][1])]
            tied = tie(pending, [outputs[-1][0]])
            relayed[3] = []
            for k in range(HALVES):
                mine, across = tied[2 * k], tied[2 * k + 1]
                relayed[3] += [mine, across, swap(mine, 1), swap(across, 1)]
            early = call(
                functools.partial(early_kernel, turns, seq_count, HALVES, feats),
                "early",
                [shape((turns - 1, rows, cols), kind)] * seq_count
                + [shape((cols, feats), jnp.float32)],
                [vmem] * (turns * HALVES + seq_count),
                [half for output in outputs for half in output] + second,
                limit=8,
                out_specs=[vmem] * (seq_count + 1),
            )
            early, early_grad = list(early[:-1]), early[-1]
            early = [early[0]] + [swap(early[m], m) for m in range(1, seq_count)]
        if step + 2 < steps:
            crossing = []
            for half in outputs[-1]:
                piece = handed_over(half)
                crossing.append((piece, swap(piece, 2)))
            if step == 0:
                relayed[2] = []
                for mine, across in crossing:
                    relayed[2] += [mine, across, swap(mine, 1), swap(across, 1)]

    g_shape = (cols // hops, feats)
    operands = outputs[-2] + outputs[-1] + second + early + [early_grad]
    settled = call(
        functools.partial(settle_kernel, turns, seq_count, HALVES, hops, feats),
        "settle",
        [shape((rows, cols), kind)] * seq_count
        + [shape(g_shape, jnp.float32)]
        + [shape(g_shape, kind)] * (hops - 1)
        + [shape((turns, rows, width), kind)],
        [vmem] * len(operands),
        operands,
        [
            pltpu.VMEM((turns - 1, rows, width), kind),
            pltpu.VMEM((cols, feats), jnp.float32),
            pltpu.SemaphoreType.DMA,
        ],
        8,
        out_specs=[vmem] * (seq_count + hops) + [anywhere],
    )
    late, grads, held = settled[:seq_count], settled[seq_count:-1], settled[-1]
    late = [late[0]] + [swap(late[m], m) for m in range(1, seq_count)]
    grads = [grads[0]] + [shifted(grads[k], "dp", k) for k in range(1, hops)]
    section_out, grad_rows = call(
        functools.partial(finish_kernel, seq_count, hops),
        "finish",
        [shape((turns, rows, width), kind), shape(g_shape, jnp.float32)],
        [anywhere] + [vmem] * (seq_count + hops),
        [held] + late + grads,
        [pltpu.VMEM((rows, width), kind), pltpu.SemaphoreType.DMA],
        out_specs=[anywhere, vmem],
        input_output_aliases={0: 0},
    )
    return (section_out[None, :, None], grad_rows[None])


def body(incoming, contacts, keyframes, timesteps, w_query, *others):
    count = lax.axis_size("seq")
    cols = w_query.shape[2] // count
    paired = (
        lax.axis_size("pipe") == 2
        and lax.axis_size("dp") == 4
        and count == 4
        and cols % 128 == 0
        and w_query.shape[1] % 16 == 0
        and incoming.shape[3] == 128
        and incoming.shape[1] == 3
    )
    chosen = paired_body if paired else general_body
    return chosen(incoming, contacts, keyframes, timesteps, w_query, *others)


def general_body(
    incoming,
    contacts,
    keyframes,
    timesteps,
    w_query,
    w_keyval,
    norm_gain,
    time_freq,
    contact_table,
    key_bias,
    attn_gate,
    head_cotangent,
):
    section_idx = lax.axis_index("pipe")
    seq_idx = lax.axis_index("seq")
    rep_idx = lax.axis_index("dp")
    seq_count = lax.axis_size("seq")
    section_count = lax.axis_size("pipe")
    rep_count = lax.axis_size("dp")
    tok_rows = incoming.shape[3]
    width = incoming.shape[4]
    turns = incoming.shape[1]
    frames = tok_rows * seq_count
    heads_all = key_bias.shape[1]
    head_size = width // heads_all
    heads_local = heads_all // seq_count
    kv_width = w_keyval.shape[2]
    kv_local = kv_width // (2 * head_size * seq_count)
    group_size = heads_local // kv_local
    feat_count = head_cotangent.shape[4]
    score_scale = head_size ** (-0.5)
    q_cols = width // seq_count
    kv_cols = kv_width // seq_count
    w_rows = w_query.shape[1]

    w_parts = jnp.concatenate(
        [
            w_query[0].reshape(w_rows, seq_count, q_cols),
            w_keyval[0].reshape(w_rows, seq_count, kv_cols),
        ],
        axis=2,
    ).transpose(1, 0, 2)
    block = lax.all_to_all(w_parts, "seq", split_axis=0, concat_axis=0, tiled=True)
    weights = jnp.zeros((seq_count, rep_count, w_rows, q_cols + kv_cols), jnp.bfloat16)
    for hop in range(rep_count):
        owner = lax.rem(rep_idx + rep_count - hop, rep_count)
        weights = lax.dynamic_update_slice_in_dim(weights, block[:, None], owner, 1)
        if hop + 1 < rep_count:
            block = ring(block, "dp")
    weights = weights.reshape(width, q_cols + kv_cols)

    gain_row = norm_gain[0]
    freq_row = time_freq[0]
    table = contact_table[0]
    gate_local = lax.dynamic_slice_in_dim(attn_gate[0], seq_idx * q_cols, q_cols)
    table_local = lax.dynamic_slice_in_dim(table, seq_idx * q_cols, q_cols, 1)
    bias_local = lax.dynamic_slice_in_dim(key_bias[0], seq_idx * heads_local, heads_local)
    contact_all = lax.all_gather(contacts[:, 0, :], "seq", axis=1, tiled=True)
    key_all = keyframes[:, 0, :]
    step_all = timesteps[:, 0]
    labels = jnp.arange(table.shape[0], dtype=jnp.int32)
    cot_all = lax.all_gather(head_cotangent[0, :, 0], "seq", axis=1, tiled=True)

    lag = 2 if section_count == 2 else 1
    if lag == 2:
        steps = turns + 1
    else:
        steps = turns

    def turn_at(step):
        if lag == 1:
            return jnp.int32(step)
        return jnp.clip(step - section_idx, 0, turns - 1)

    outputs = []
    handed = {}
    for step in range(steps):
        turn = turn_at(step)
        fresh = lax.dynamic_index_in_dim(incoming[0, :, 0], turn, 0, keepdims=False)
        current = lax.all_gather(fresh, "seq", axis=0, tiled=True)
        if step in handed:
            current = jnp.where((section_idx == 0) | (turn == 0), current, handed[step])
        batch_idx = turn - section_idx + section_count - 1
        contact_rows = lax.dynamic_index_in_dim(contact_all, batch_idx, 0, keepdims=False)
        key_flags = lax.dynamic_index_in_dim(key_all, batch_idx, 0, keepdims=False).astype(
            jnp.float32
        )
        timestep = lax.dynamic_index_in_dim(step_all, batch_idx, 0, keepdims=False).astype(
            jnp.float32
        )
        onehot = (contact_rows[:, None] == labels[None, :]).astype(jnp.bfloat16)
        hidden = current.astype(jnp.float32) + jnp.dot(
            onehot, table, preferred_element_type=jnp.float32
        )
        root_mean = jnp.sqrt(jnp.mean(hidden * hidden, axis=-1, keepdims=True) + epsilon)
        modulation = gain_row * (1.0 + 0.5 * jnp.sin(timestep * freq_row))
        normed = (hidden / root_mean * modulation[None, :]).astype(jnp.bfloat16)
        projected = jnp.dot(normed, weights, preferred_element_type=jnp.float32).astype(
            jnp.bfloat16
        )
        query_heads = projected[:, :q_cols].reshape(frames, heads_local, head_size)
        keyval_heads = projected[:, q_cols:].reshape(frames, kv_local, 2, head_size)
        head_outputs = []
        for head in range(heads_local):
            key_rows = keyval_heads[:, head // group_size, 0]
            value_rows = keyval_heads[:, head // group_size, 1]
            scores = (
                lax.dot_general(
                    query_heads[:, head],
                    key_rows,
                    (((1,), (1,)), ((), ())),
                    preferred_element_type=jnp.float32,
                )
                * score_scale
            )
            scores = scores + bias_local[head] * key_flags[None, :]
            row_max = jnp.max(scores, axis=-1, keepdims=True)
            exponent = jnp.exp(scores - row_max)
            probabilities = (exponent / jnp.sum(exponent, axis=-1, keepdims=True)).astype(
                jnp.bfloat16
            )
            head_outputs.append(
                jnp.dot(probabilities, value_rows, preferred_element_type=jnp.float32).astype(
                    jnp.bfloat16
                )
            )
        attended = jnp.concatenate(head_outputs, axis=1)
        hidden_local = lax.dynamic_slice_in_dim(current, seq_idx * q_cols, q_cols, 1).astype(
            jnp.float32
        ) + jnp.dot(onehot, table_local, preferred_element_type=jnp.float32)
        output = (hidden_local + gate_local[None, :] * attended.astype(jnp.float32)).astype(
            jnp.bfloat16
        )
        outputs.append(output)
        if step + lag < steps:
            piece = passed_along(output, "pipe", 1)
            handed[step + lag] = lax.all_gather(piece, "seq", axis=1, tiled=True)

    factor = float(turns * rep_count * frames) ** (-0.5)
    total = None
    rows_out = []
    for turn in range(turns):
        if lag == 2:
            own = jnp.where(section_idx == 0, outputs[turn], outputs[turn + 1])
        else:
            own = outputs[turn]
        term = lax.dot_general(
            own, cot_all[turn], (((0,), (0,)), ((), ())), preferred_element_type=jnp.float32
        )
        total = term if total is None else total + term
        rows_out.append(lax.all_to_all(own, "seq", split_axis=0, concat_axis=1, tiled=True))
    section_out = jnp.stack(rows_out)[None, :, None]
    grad_parts = lax.all_to_all(
        (total * factor).astype(jnp.bfloat16).reshape(rep_count, q_cols // rep_count, feat_count),
        "dp",
        split_axis=0,
        concat_axis=0,
        tiled=True,
    )
    grad_rows = jnp.sum(grad_parts.astype(jnp.float32), axis=0)
    return (section_out, grad_rows[None])


def solution(mesh):
    in_specs = (
        P("pipe", None, "dp", "seq", None),
        P(None, "dp", "seq"),
        P(None, "dp", None),
        P(None, "dp"),
        P("pipe", ("seq", "dp"), None),
        P("pipe", ("seq", "dp"), None),
        P("pipe", None),
        P("pipe", None),
        P("pipe", None, None),
        P("pipe", None),
        P("pipe", None),
        P("pipe", None, "dp", "seq", None),
    )
    out_specs = (P("pipe", None, "dp", "seq", None), P("pipe", ("seq", "dp"), None))
    return jax.shard_map(body, mesh=mesh, in_specs=in_specs, out_specs=out_specs, check_vma=False)
```

```python
import functools
import math

import jax
import jax.numpy as jnp
from jax import lax
from jax.experimental import pallas as pl
from jax.experimental.pallas import tpu as pltpu
from jax.sharding import PartitionSpec as P

epsilon = 1e-06


def passed_along(value, axis, steps):
    count = lax.axis_size(axis)
    first, last = (max(0, -steps), min(count, count - steps))
    return lax.ppermute(value, axis, [(source, source + steps) for source in range(first, last)])


def ring(value, axis):
    count = lax.axis_size(axis)
    return lax.ppermute(value, axis, [(source, (source + 1) % count) for source in range(count)])


def swap(value, bit):
    count = lax.axis_size("seq")
    return lax.ppermute(value, "seq", [(source, source ^ bit) for source in range(count)])


def handed_over(value):
    return lax.ppermute(value, "pipe", [(0, 1), (1, 0)])


def shifted(value, axis, shift):
    count = lax.axis_size(axis)
    return lax.ppermute(value, axis, [(source, (source + shift) % count) for source in range(count)])


def fold(index):
    return index ^ (index >> 1)


def ring_step(value):
    count = lax.axis_size("dp")
    pairs = [(fold(place), fold((place + 1) % count)) for place in range(count)]
    return lax.ppermute(value, "dp", pairs)


def offsets_of(count):
    offsets = [0]
    bit = count // 2
    while bit:
        offsets = offsets + [offset ^ bit for offset in offsets]
        bit //= 2
    return offsets


def turn_and_batch(step, turns):
    section = lax.axis_index("pipe")
    turn = jnp.clip(step - section, 0, turns - 1)
    return turn, turn - section + 1


def pack_kernel(wq, wkv, *refs):
    outs, sems = refs[:-1], refs[-1]
    cols = outs[0].shape[1] // 2
    seq = lax.axis_index("seq")
    copies = []
    for m, out in enumerate(outs):
        start = pl.multiple_of((seq ^ m) * cols, 128)
        for k, source in enumerate((wq, wkv)):
            copies.append(
                pltpu.make_async_copy(
                    source.at[0, :, pl.ds(start, cols)],
                    out.at[:, pl.ds(k * cols, cols)],
                    sems.at[2 * m + k],
                )
            )
    for copy in copies:
        copy.start()
    for copy in copies:
        copy.wait()


def stack_kernel(deps, *refs):
    out = refs[-1]
    at = 0
    for ref in refs[deps:-1]:
        if len(ref.shape) == 2:
            out[at] = ref[...]
            at += 1
        else:
            out[at : at + ref.shape[0]] = ref[...]
            at += ref.shape[0]


def place_kernel(hop, hops, *refs):
    weights, parts = refs[-1], refs[:-1]
    if hop > 0:
        parts = parts[:-1]
    place(hop, hops, parts, weights)


def place(hop, hops, parts, weights):
    seq, rep = lax.axis_index("seq"), lax.axis_index("dp")
    m = 0
    for part in parts:
        count, rows = part.shape[:2]
        for j in range(count):
            block = (seq ^ m) * hops + fold(lax.rem(fold(rep) + hops - hop, hops))
            weights[pl.ds(pl.multiple_of(block * rows, 16), rows)] = part[j]
            m += 1


def first_kernel(turns, far, incoming, contacts, out, states):
    rows = incoming.shape[3]
    for turn in range(2):
        out[turn * rows : (turn + 1) * rows] = incoming[0, turn, 0]
    states[...] = jnp.zeros_like(states)
    for step in range(turns + 1):
        _, batch = turn_and_batch(step, turns)
        states[step : step + 1] = contacts[batch].astype(jnp.float32)
    out[2 * rows :, : states.shape[1]] = states[...].astype(jnp.bfloat16)


def second_kernel(dep, incoming, cotangent, out):
    turns, rows, feats = cotangent.shape[1], cotangent.shape[3], cotangent.shape[4]
    out[:rows] = incoming[0, 2, 0]
    for turn in range(turns):
        out[rows:, turn * feats : (turn + 1) * feats] = cotangent[0, turn, 0]


def columns_of(rows_of, pieces, rows):
    labels = lax.broadcasted_iota(jnp.int32, (32, rows), 0)
    columns = []
    for i in range(pieces):
        state, flag = rows_of(i)
        one = jnp.zeros((32, rows), jnp.float32)
        if state is not None:
            one = jnp.where(labels == state, 1.0, 0.0)
        if flag is not None:
            one = jnp.where(labels == 16, flag, one)
        columns.append(one.T)
    return jnp.concatenate(columns, axis=0)


def modulation(step, turns, times, gain, freq):
    _, batch = turn_and_batch(step, turns)
    return gain[...] * (1.0 + 0.5 * jnp.sin(times[batch, 0].astype(jnp.float32) * freq[...]))


def norm_kernel(turns, pieces, times, table, gain, freq, *refs):
    sources, refs = refs[:pieces], refs[pieces + 1 :]
    scaled, scales, owns, embeds, mod = refs[0:2], refs[2:4], refs[4:6], refs[6:8], refs[8]
    first, sems = refs[9 : 9 + pieces], refs[9 + pieces]
    copies = [
        pltpu.make_async_copy(sources[i], first[i], sems.at[i]) for i in range(pieces)
    ]
    for copy in copies:
        copy.start()
    for copy in copies:
        copy.wait()
    frames, width = scaled[0].shape
    rows, cols = frames // pieces, owns[0].shape[1]
    seq = lax.axis_index("seq")
    offsets = offsets_of(pieces)
    for step in range(turns + 1):

        def state_of(i):
            state = first[i][2 * rows : 2 * rows + 16, :rows][step : step + 1]
            return state.astype(jnp.float32).astype(jnp.int32), None

        onehot = columns_of(state_of, pieces, rows)[:, : table.shape[1]].astype(jnp.bfloat16)
        if step >= 2:
            for at in range(0, width, 256):
                embeds[step - 2][:, at : at + 256] = jnp.dot(
                    onehot, table[0, :, at : at + 256], preferred_element_type=jnp.float32
                ).astype(jnp.bfloat16)
            continue
        turn, _ = turn_and_batch(step, turns)
        at = pl.multiple_of(jnp.minimum(turn, 1) * rows, 128)
        mod[...] = modulation(step, turns, times, gain, freq)
        total = jnp.zeros((frames, 128), jnp.float32)
        for i in range(pieces):
            lanes = pl.ds(pl.multiple_of((seq ^ offsets[i]) * cols, 128), cols)
            current = jnp.concatenate([first[p][pl.ds(at, rows), lanes] for p in range(pieces)])
            hidden = current.astype(jnp.float32) + jnp.dot(
                onehot, table[0, :, lanes], preferred_element_type=jnp.float32
            )
            for lane in range(0, cols, 128):
                piece = hidden[:, lane : lane + 128]
                total = total + piece * piece
            scaled[step][:, lanes] = (hidden * mod[:, lanes]).astype(jnp.bfloat16)
            if i == 0:
                owns[step][...] = hidden
        mean = jnp.sum(total, axis=1, keepdims=True) * (1.0 / width)
        scales[step][...] = jnp.broadcast_to(lax.rsqrt(mean + epsilon), (frames, 128))


def step_kernel(cfg, *refs):
    step, has_relay = cfg["step"], cfg["has_relay"]
    pieces, hops, head, turns = cfg["pieces"], cfg["hops"], cfg["head"], cfg["turns"]
    heads, group, halves = cfg["heads"], cfg["group"], cfg["halves"]
    refs = list(refs)

    def take(count):
        taken, refs[:count] = refs[:count], []
        return taken

    bias, times, gain, freq, gate, flags = take(6)
    if has_relay:
        second, embed, relay = take(pieces), take(1)[0], take(pieces * halves)
    else:
        scaled, scales, own_hidden = take(3)
    chunk = take(2) if step == 0 else None
    weights = take(1)[0]
    outs = take(halves)
    if step == 0:
        weights = take(1)[0]
    proj, att = take(2)
    if has_relay:
        scaled, scales, own_hidden, mod = take(4)
    offsets = offsets_of(pieces)
    frames, width = scaled.shape
    rows, cols = frames // pieces, att.shape[0]
    part = pieces // halves
    seq, rep, section = lax.axis_index("seq"), lax.axis_index("dp"), lax.axis_index("pipe")
    _, batch = turn_and_batch(step, turns)

    if step == 0:
        place(hops - 1, hops, chunk, weights)

    def normalize(relayed):
        total = jnp.zeros((frames, 128), jnp.float32)
        for i in range(pieces):
            lanes = pl.ds(pl.multiple_of((seq ^ offsets[i]) * cols, 128), cols)
            blocks = []
            for p in range(pieces):
                if relayed:
                    j = offsets.index(offsets[i] ^ offsets[p])
                    blocks.append(relay[(j // part) * pieces + i][j % part])
                else:
                    blocks.append(second[p][:rows, lanes])
            hidden = jnp.concatenate(blocks, axis=0).astype(jnp.float32)
            hidden = hidden + embed[:, lanes].astype(jnp.float32)
            for lane in range(0, cols, 128):
                piece = hidden[:, lane : lane + 128]
                total = total + piece * piece
            scaled[:, lanes] = (hidden * mod[:, lanes]).astype(jnp.bfloat16)
            if i == 0:
                own_hidden[...] = hidden
        scales[...] = total

    if has_relay:
        mod[...] = modulation(step, turns, times, gain, freq)

        @pl.when(section == 0)
        def _():
            normalize(False)

        @pl.when(section != 0)
        def _():
            normalize(True)

        mean = jnp.sum(scales[...], axis=1, keepdims=True) * (1.0 / width)
        scale = lax.rsqrt(mean + epsilon)
    else:
        scale = scales[:, :1]

    def flag_of(i):
        lanes = pl.ds(pl.multiple_of((seq ^ offsets[i]) * rows, 128), rows)
        return None, flags[batch, :, lanes].astype(jnp.float32)

    flag_column = columns_of(flag_of, pieces, rows)[:, 16:17]
    projected = jnp.dot(scaled[...], weights[...], preferred_element_type=jnp.float32) * scale
    score_scale = head ** (-0.5) * math.log2(math.e)
    proj[:, :cols] = (projected[:, :cols] * score_scale).astype(jnp.bfloat16)
    proj[:, cols : 2 * cols] = projected[:, cols:].astype(jnp.bfloat16)
    proj[:, 2 * cols :] = jnp.zeros((frames, 128), jnp.bfloat16)
    lanes = lax.broadcasted_iota(jnp.int32, (frames, 128), 1)
    row_lanes = lax.broadcasted_iota(jnp.int32, (1, 128), 1)
    flag_lanes = jnp.logical_or(lanes == head, lanes == head + 1)

    def part_of(at):
        return proj[:, at : at + 128].astype(jnp.float32)

    keys, values = [], []
    for kv in range(heads // group):
        base = cols + kv * 2 * head
        key = jnp.where(flag_lanes, flag_column, jnp.where(lanes < head, part_of(base), 0.0))
        value = jnp.where(lanes < head, part_of(base + head), jnp.where(lanes == head, 1.0, 0.0))
        keys.append(key.astype(jnp.bfloat16))
        values.append(value.T.astype(jnp.bfloat16))

    def scores_of(h):
        strength = jnp.zeros((1, 128), jnp.float32) + bias[0, seq * heads + h] * math.log2(math.e)
        coarse = strength.astype(jnp.bfloat16).astype(jnp.float32)
        tail = jnp.where(
            row_lanes == head, coarse, jnp.where(row_lanes == head + 1, strength - coarse, 0.0)
        )
        query = jnp.where(lanes < head, part_of(h * head), tail).astype(jnp.bfloat16)
        return lax.dot_general(
            keys[h // group], query, (((1,), (1,)), ((), ())), preferred_element_type=jnp.float32
        )

    scores = scores_of(0)
    for h in range(heads):
        ahead = scores_of(h + 1) if h + 1 < heads else None
        top = jnp.max(scores, axis=0, keepdims=True)
        weight = jnp.exp2(scores - top).astype(jnp.bfloat16)
        mixed = jnp.dot(values[h // group], weight, preferred_element_type=jnp.float32)
        att[h * head : (h + 1) * head, :] = mixed[:head] * (1.0 / mixed[head : head + 1])
        scores = ahead
    own = pl.ds(pl.multiple_of(seq * cols, 128), cols)
    attended = att[...].T.astype(jnp.bfloat16).astype(jnp.float32)
    output = (own_hidden[...] + gate[:, own] * attended).astype(jnp.bfloat16)
    blocks = output.reshape(pieces, rows, cols)
    for k in range(halves):
        outs[k][...] = blocks[k * part : (k + 1) * part]


def tie_kernel(*refs):
    pass


def grad_of(output, second, turn, rows, feats):
    cot = jnp.concatenate(
        [piece[rows : 2 * rows, turn * feats : (turn + 1) * feats] for piece in second], axis=0
    )
    return lax.dot_general(
        output, cot, (((0,), (0,)), ((), ())), preferred_element_type=jnp.float32
    )


def early_kernel(turns, pieces, halves, feats, *refs):
    outs, second = refs[: turns * halves], refs[turns * halves : turns * halves + pieces]
    sends, grad = refs[turns * halves + pieces : -1], refs[-1]
    section = lax.axis_index("pipe")
    offsets = offsets_of(pieces)
    part = pieces // halves
    rows = outs[0].shape[1]
    total = None
    for turn in range(turns - 1):
        blocks = []
        for p in range(pieces):
            k, j = p // part, p % part
            block = jnp.where(
                section == 0, outs[turn * halves + k][j], outs[(turn + 1) * halves + k][j]
            )
            sends[offsets[p]][turn] = block
            blocks.append(block)
        share = grad_of(jnp.concatenate(blocks, axis=0), second, turn, rows, feats)
        total = share if total is None else total + share
    grad[...] = total


def settle_kernel(turns, pieces, halves, hops, feats, *refs):
    refs = list(refs)

    def take(count):
        taken, refs[:count] = refs[:count], []
        return taken

    before, now, second, early = take(halves), take(halves), take(pieces), take(pieces - 1)
    early_grad = take(1)[0]
    late, own_grad, grads = take(pieces), take(1)[0], take(hops - 1)
    section_out = take(1)[0]
    rows_out, total, sem = take(3)
    section, seq, rep = lax.axis_index("pipe"), lax.axis_index("seq"), lax.axis_index("dp")
    offsets = offsets_of(pieces)
    part = pieces // halves
    rows, cols = early[0].shape[1:]
    for m in range(pieces - 1):
        lanes = pl.ds(pl.multiple_of((seq ^ m) * cols, 128), cols)
        for turn in range(turns - 1):
            rows_out[turn, :, lanes] = early[m][turn]
    copy = pltpu.make_async_copy(rows_out, section_out.at[pl.ds(0, turns - 1)], sem)
    copy.start()
    blocks = []
    for p in range(pieces):
        block = jnp.where(section == 0, before[p // part][p % part], now[p // part][p % part])
        late[offsets[p]][...] = block
        blocks.append(block)
    share = grad_of(jnp.concatenate(blocks, axis=0), second, turns - 1, rows, feats)
    factor = float(turns * hops * rows * pieces) ** (-0.5)
    total[...] = (share + early_grad[...]) * factor
    g_rows = cols // hops
    own_grad[...] = total[pl.ds(pl.multiple_of(rep * g_rows, 8), g_rows)]
    for shift in range(1, hops):
        at = pl.multiple_of(lax.rem(rep + shift, hops) * g_rows, 8)
        grads[shift - 1][...] = total[pl.ds(at, g_rows)].astype(jnp.bfloat16)
    copy.wait()


def finish_kernel(pieces, hops, *refs):
    held, early, late, refs = refs[0], refs[1], refs[2 : pieces + 2], refs[pieces + 2 :]
    own_grad, parts, (section_out, grad, row_out, sems) = refs[0], refs[1:hops], refs[hops:]
    seq = lax.axis_index("seq")
    cols = late[0].shape[1]
    last_lanes = pl.ds(pl.multiple_of((seq ^ (pieces - 1)) * cols, 128), cols)
    early_copy = pltpu.make_async_copy(
        early, section_out.at[pl.ds(0, early.shape[0]), :, last_lanes], sems.at[0]
    )
    early_copy.start()
    for m in range(pieces):
        lanes = pl.ds(pl.multiple_of((seq ^ m) * cols, 128), cols)
        row_out[:, lanes] = late[m][...]
    copy = pltpu.make_async_copy(row_out, section_out.at[section_out.shape[0] - 1], sems.at[1])
    copy.start()
    total = own_grad[...]
    for part in parts:
        total = total + part[...].astype(jnp.float32)
    grad[...] = total
    early_copy.wait()
    copy.wait()


HALVES = 2
MIB = 1024 * 1024


def paired_body(
    incoming,
    contacts,
    keyframes,
    timesteps,
    w_query,
    w_keyval,
    norm_gain,
    time_freq,
    contact_table,
    key_bias,
    attn_gate,
    head_cotangent,
):
    seq_count = lax.axis_size("seq")
    hops = lax.axis_size("dp")
    rows, width, turns = incoming.shape[3], incoming.shape[4], incoming.shape[1]
    frames = rows * seq_count
    heads_all = key_bias.shape[1]
    head = width // heads_all
    heads = heads_all // seq_count
    kv_heads = w_keyval.shape[2] // (2 * head * seq_count)
    feats = head_cotangent.shape[4]
    cols = width // seq_count
    w_rows = w_query.shape[1]
    steps = turns + 1
    part = seq_count // HALVES
    kind = jnp.bfloat16
    smem = pl.BlockSpec(memory_space=pltpu.SMEM)
    vmem = pl.BlockSpec(memory_space=pltpu.VMEM)
    anywhere = pl.BlockSpec(memory_space=pl.ANY)
    shape = jax.ShapeDtypeStruct

    def call(kernel, name, out_shape, in_specs, operands, scratch=(), limit=4, flops=0, **options):
        return pl.pallas_call(
            kernel,
            out_shape=out_shape,
            in_specs=in_specs,
            scratch_shapes=list(scratch),
            compiler_params=pltpu.CompilerParams(vmem_limit_bytes=limit * MIB),
            cost_estimate=pl.CostEstimate(
                flops=flops, bytes_accessed=flops // 512, transcendentals=0
            ),
            name=name,
            **options,
        )(*operands)

    def pin(value, space=pltpu.VMEM):
        return pltpu.with_memory_space_constraint(value, space)

    packed = call(
        pack_kernel,
        "pack",
        [pltpu.VMEM((w_rows, 2 * cols), kind)] * seq_count,
        [anywhere, anywhere],
        [pin(w_query, pltpu.HBM), pin(w_keyval, pltpu.HBM)],
        [pltpu.SemaphoreType.DMA((2 * seq_count,))],
        out_specs=[vmem] * seq_count,
    )
    blocks = [packed[0]] + [swap(packed[m], m) for m in range(1, seq_count)]

    def stacked(name, count, deps, values):
        return call(
            functools.partial(stack_kernel, len(deps)),
            name,
            pltpu.VMEM((count, w_rows, 2 * cols), kind),
            [anywhere] * len(deps) + [vmem] * len(values),
            deps + values,
            out_specs=vmem,
        )

    weights = None

    def placed(hop, parts):
        operands = [pin(part) for part in parts] + ([pin(weights)] if hop else [])
        return call(
            functools.partial(place_kernel, hop, hops),
            "place%d" % hop,
            pltpu.VMEM((width, 2 * cols), kind),
            [vmem] * len(operands),
            operands,
            out_specs=vmem,
            input_output_aliases={len(parts): 0} if hop else {},
        )

    near = stacked("near", 2, [], blocks[:2])
    near_next = ring_step(near)
    far = stacked("far", 2, [near_next], blocks[2:])
    far_next = ring_step(far)
    rings = [[near, near_next], [far, far_next]]
    for hop in range(2, hops - 1):
        for chunks in rings:
            chunks.append(ring_step(chunks[-1]))
    last_chunk = [ring_step(chunks[-1]) for chunks in rings]
    for hop in range(hops - 1):
        weights = placed(hop, [chunks[hop] for chunks in rings])

    def tie(values, deps):
        return call(
            tie_kernel,
            "tie",
            [shape(value.shape, kind) for value in values],
            [anywhere] * (len(values) + len(deps)),
            list(values) + list(deps),
            out_specs=[anywhere] * len(values),
            input_output_aliases={i: i for i in range(len(values))},
        )

    mine = call(
        functools.partial(first_kernel, turns),
        "first",
        pltpu.VMEM((2 * rows + 16, width), kind),
        [anywhere, vmem, vmem],
        [far, incoming, contacts],
        [pltpu.VMEM((16, 128), jnp.float32)],
        out_specs=vmem,
    )
    across = swap(mine, 2)
    beside = swap(mine, 1)
    (across,) = tie([across], [chunks[-1] for chunks in rings])
    first = [mine, across, beside, swap(across, 1)]
    prepared = call(
        functools.partial(norm_kernel, turns, seq_count),
        "norm",
        [pltpu.VMEM((frames, width), kind)] * 2
        + [pltpu.VMEM((frames, 128), jnp.float32)] * 2
        + [pltpu.VMEM((frames, cols), jnp.float32)] * 2
        + [pltpu.VMEM((frames, width), kind)] * 2,
        [smem] + [vmem] * 3 + [anywhere] * (seq_count + 1),
        [timesteps, contact_table, norm_gain, time_freq]
        + [pin(piece, pltpu.HBM) for piece in first]
        + [weights],
        [pltpu.VMEM((1, width), jnp.float32)]
        + [pltpu.VMEM((2 * rows + 16, width), kind)] * seq_count
        + [pltpu.SemaphoreType.DMA((seq_count,))],
        12,
        out_specs=[vmem] * 8,
    )

    mine = call(
        second_kernel,
        "second",
        pltpu.VMEM((2 * rows, width), kind),
        [anywhere, vmem, vmem],
        [across, incoming, head_cotangent],
        out_specs=vmem,
    )
    second = [mine, swap(mine, 2), swap(mine, 1)]

    outputs = []
    relayed = {}
    for step in range(steps):
        cfg = {
            "step": step,
            "has_relay": step in relayed,
            "pieces": seq_count,
            "hops": hops,
            "head": head,
            "heads": heads,
            "group": heads // kv_heads,
            "turns": turns,
            "halves": HALVES,
        }
        operands = [key_bias, timesteps, norm_gain, time_freq, attn_gate, keyframes]
        scratch = [
            pltpu.VMEM((frames, 2 * cols + 128), kind),
            pltpu.VMEM((cols, frames), jnp.float32),
        ]
        if step in relayed:
            large = second + [prepared[4 + step]] + relayed[step]
            scratch += [
                pltpu.VMEM((frames, width), kind),
                pltpu.VMEM((frames, 128), jnp.float32),
                pltpu.VMEM((frames, cols), jnp.float32),
                pltpu.VMEM((1, width), jnp.float32),
            ]
        else:
            large = [prepared[step], prepared[2 + step], prepared[4 + step]]
        large += last_chunk + [weights] if step == 0 else [weights]
        operands += [pin(value) for value in large]
        out_shape = [pltpu.VMEM((part, rows, cols), kind)] * HALVES
        if step == 0:
            out_shape += [pltpu.VMEM((width, 2 * cols), kind)]
        results = call(
            functools.partial(step_kernel, cfg),
            "step%d" % step,
            out_shape,
            [smem, smem] + [vmem] * (len(operands) - 2),
            operands,
            scratch,
            16,
            2 * frames * width * 2 * cols + 4 * heads * frames * frames * head,
            out_specs=[vmem] * len(out_shape),
            input_output_aliases={len(operands) - 1: HALVES} if step == 0 else {},
        )
        outputs.append(list(results[:HALVES]))
        if step == 0:
            weights = results[HALVES]
        if step == 0:
            (second[1],) = tie([second[1]], [outputs[-1][0]])
            second.append(swap(second[1], 1))
        if step == 2:
            pending = [piece for k in range(HALVES) for piece in (crossing[k][0], crossing[k][1])]
            tied = tie(pending, [outputs[-1][0]])
            relayed[3] = []
            for k in range(HALVES):
                mine, across = tied[2 * k], tied[2 * k + 1]
                relayed[3] += [mine, across, swap(mine, 1), swap(across, 1)]
            early = call(
                functools.partial(early_kernel, turns, seq_count, HALVES, feats),
                "early",
                [shape((turns - 1, rows, cols), kind)] * seq_count
                + [shape((cols, feats), jnp.float32)],
                [vmem] * (turns * HALVES + seq_count),
                [half for output in outputs for half in output] + second,
                limit=8,
                out_specs=[vmem] * (seq_count + 1),
            )
            early, early_grad = list(early[:-1]), early[-1]
            early = [early[0]] + [swap(early[m], m) for m in range(1, seq_count)]
        if step + 2 < steps:
            crossing = []
            for half in outputs[-1]:
                piece = handed_over(half)
                crossing.append((piece, swap(piece, 2)))
            if step == 0:
                relayed[2] = []
                for mine, across in crossing:
                    relayed[2] += [mine, across, swap(mine, 1), swap(across, 1)]

    g_shape = (cols // hops, feats)
    operands = outputs[-2] + outputs[-1] + second + early[:-1] + [early_grad]
    settled = call(
        functools.partial(settle_kernel, turns, seq_count, HALVES, hops, feats),
        "settle",
        [shape((rows, cols), kind)] * seq_count
        + [shape(g_shape, jnp.float32)]
        + [shape(g_shape, kind)] * (hops - 1)
        + [shape((turns, rows, width), kind)],
        [vmem] * len(operands),
        operands,
        [
            pltpu.VMEM((turns - 1, rows, width), kind),
            pltpu.VMEM((cols, feats), jnp.float32),
            pltpu.SemaphoreType.DMA,
        ],
        8,
        out_specs=[vmem] * (seq_count + hops) + [anywhere],
    )
    late, grads, held = settled[:seq_count], settled[seq_count:-1], settled[-1]
    late = [late[0]] + [swap(late[m], m) for m in range(1, seq_count)]
    grads = [grads[0]] + [shifted(grads[k], "dp", k) for k in range(1, hops)]
    section_out, grad_rows = call(
        functools.partial(finish_kernel, seq_count, hops),
        "finish",
        [shape((turns, rows, width), kind), shape(g_shape, jnp.float32)],
        [anywhere] + [vmem] * (seq_count + hops + 1),
        [held, early[-1]] + late + grads,
        [pltpu.VMEM((rows, width), kind), pltpu.SemaphoreType.DMA((2,))],
        out_specs=[anywhere, vmem],
        input_output_aliases={0: 0},
    )
    return (section_out[None, :, None], grad_rows[None])


def body(incoming, contacts, keyframes, timesteps, w_query, *others):
    count = lax.axis_size("seq")
    cols = w_query.shape[2] // count
    paired = (
        lax.axis_size("pipe") == 2
        and lax.axis_size("dp") == 4
        and count == 4
        and cols % 128 == 0
        and w_query.shape[1] % 16 == 0
        and incoming.shape[3] == 128
        and incoming.shape[1] == 3
    )
    chosen = paired_body if paired else general_body
    return chosen(incoming, contacts, keyframes, timesteps, w_query, *others)


def general_body(
    incoming,
    contacts,
    keyframes,
    timesteps,
    w_query,
    w_keyval,
    norm_gain,
    time_freq,
    contact_table,
    key_bias,
    attn_gate,
    head_cotangent,
):
    section_idx = lax.axis_index("pipe")
    seq_idx = lax.axis_index("seq")
    rep_idx = lax.axis_index("dp")
    seq_count = lax.axis_size("seq")
    section_count = lax.axis_size("pipe")
    rep_count = lax.axis_size("dp")
    tok_rows = incoming.shape[3]
    width = incoming.shape[4]
    turns = incoming.shape[1]
    frames = tok_rows * seq_count
    heads_all = key_bias.shape[1]
    head_size = width // heads_all
    heads_local = heads_all // seq_count
    kv_width = w_keyval.shape[2]
    kv_local = kv_width // (2 * head_size * seq_count)
    group_size = heads_local // kv_local
    feat_count = head_cotangent.shape[4]
    score_scale = head_size ** (-0.5)
    q_cols = width // seq_count
    kv_cols = kv_width // seq_count
    w_rows = w_query.shape[1]

    w_parts = jnp.concatenate(
        [
            w_query[0].reshape(w_rows, seq_count, q_cols),
            w_keyval[0].reshape(w_rows, seq_count, kv_cols),
        ],
        axis=2,
    ).transpose(1, 0, 2)
    block = lax.all_to_all(w_parts, "seq", split_axis=0, concat_axis=0, tiled=True)
    weights = jnp.zeros((seq_count, rep_count, w_rows, q_cols + kv_cols), jnp.bfloat16)
    for hop in range(rep_count):
        owner = lax.rem(rep_idx + rep_count - hop, rep_count)
        weights = lax.dynamic_update_slice_in_dim(weights, block[:, None], owner, 1)
        if hop + 1 < rep_count:
            block = ring(block, "dp")
    weights = weights.reshape(width, q_cols + kv_cols)

    gain_row = norm_gain[0]
    freq_row = time_freq[0]
    table = contact_table[0]
    gate_local = lax.dynamic_slice_in_dim(attn_gate[0], seq_idx * q_cols, q_cols)
    table_local = lax.dynamic_slice_in_dim(table, seq_idx * q_cols, q_cols, 1)
    bias_local = lax.dynamic_slice_in_dim(key_bias[0], seq_idx * heads_local, heads_local)
    contact_all = lax.all_gather(contacts[:, 0, :], "seq", axis=1, tiled=True)
    key_all = keyframes[:, 0, :]
    step_all = timesteps[:, 0]
    labels = jnp.arange(table.shape[0], dtype=jnp.int32)
    cot_all = lax.all_gather(head_cotangent[0, :, 0], "seq", axis=1, tiled=True)

    lag = 2 if section_count == 2 else 1
    if lag == 2:
        steps = turns + 1
    else:
        steps = turns

    def turn_at(step):
        if lag == 1:
            return jnp.int32(step)
        return jnp.clip(step - section_idx, 0, turns - 1)

    outputs = []
    handed = {}
    for step in range(steps):
        turn = turn_at(step)
        fresh = lax.dynamic_index_in_dim(incoming[0, :, 0], turn, 0, keepdims=False)
        current = lax.all_gather(fresh, "seq", axis=0, tiled=True)
        if step in handed:
            current = jnp.where((section_idx == 0) | (turn == 0), current, handed[step])
        batch_idx = turn - section_idx + section_count - 1
        contact_rows = lax.dynamic_index_in_dim(contact_all, batch_idx, 0, keepdims=False)
        key_flags = lax.dynamic_index_in_dim(key_all, batch_idx, 0, keepdims=False).astype(
            jnp.float32
        )
        timestep = lax.dynamic_index_in_dim(step_all, batch_idx, 0, keepdims=False).astype(
            jnp.float32
        )
        onehot = (contact_rows[:, None] == labels[None, :]).astype(jnp.bfloat16)
        hidden = current.astype(jnp.float32) + jnp.dot(
            onehot, table, preferred_element_type=jnp.float32
        )
        root_mean = jnp.sqrt(jnp.mean(hidden * hidden, axis=-1, keepdims=True) + epsilon)
        modulation = gain_row * (1.0 + 0.5 * jnp.sin(timestep * freq_row))
        normed = (hidden / root_mean * modulation[None, :]).astype(jnp.bfloat16)
        projected = jnp.dot(normed, weights, preferred_element_type=jnp.float32).astype(
            jnp.bfloat16
        )
        query_heads = projected[:, :q_cols].reshape(frames, heads_local, head_size)
        keyval_heads = projected[:, q_cols:].reshape(frames, kv_local, 2, head_size)
        head_outputs = []
        for head in range(heads_local):
            key_rows = keyval_heads[:, head // group_size, 0]
            value_rows = keyval_heads[:, head // group_size, 1]
            scores = (
                lax.dot_general(
                    query_heads[:, head],
                    key_rows,
                    (((1,), (1,)), ((), ())),
                    preferred_element_type=jnp.float32,
                )
                * score_scale
            )
            scores = scores + bias_local[head] * key_flags[None, :]
            row_max = jnp.max(scores, axis=-1, keepdims=True)
            exponent = jnp.exp(scores - row_max)
            probabilities = (exponent / jnp.sum(exponent, axis=-1, keepdims=True)).astype(
                jnp.bfloat16
            )
            head_outputs.append(
                jnp.dot(probabilities, value_rows, preferred_element_type=jnp.float32).astype(
                    jnp.bfloat16
                )
            )
        attended = jnp.concatenate(head_outputs, axis=1)
        hidden_local = lax.dynamic_slice_in_dim(current, seq_idx * q_cols, q_cols, 1).astype(
            jnp.float32
        ) + jnp.dot(onehot, table_local, preferred_element_type=jnp.float32)
        output = (hidden_local + gate_local[None, :] * attended.astype(jnp.float32)).astype(
            jnp.bfloat16
        )
        outputs.append(output)
        if step + lag < steps:
            piece = passed_along(output, "pipe", 1)
            handed[step + lag] = lax.all_gather(piece, "seq", axis=1, tiled=True)

    factor = float(turns * rep_count * frames) ** (-0.5)
    total = None
    rows_out = []
    for turn in range(turns):
        if lag == 2:
            own = jnp.where(section_idx == 0, outputs[turn], outputs[turn + 1])
        else:
            own = outputs[turn]
        term = lax.dot_general(
            own, cot_all[turn], (((0,), (0,)), ((), ())), preferred_element_type=jnp.float32
        )
        total = term if total is None else total + term
        rows_out.append(lax.all_to_all(own, "seq", split_axis=0, concat_axis=1, tiled=True))
    section_out = jnp.stack(rows_out)[None, :, None]
    grad_parts = lax.all_to_all(
        (total * factor).astype(jnp.bfloat16).reshape(rep_count, q_cols // rep_count, feat_count),
        "dp",
        split_axis=0,
        concat_axis=0,
        tiled=True,
    )
    grad_rows = jnp.sum(grad_parts.astype(jnp.float32), axis=0)
    return (section_out, grad_rows[None])


def solution(mesh):
    in_specs = (
        P("pipe", None, "dp", "seq", None),
        P(None, "dp", "seq"),
        P(None, "dp", None),
        P(None, "dp"),
        P("pipe", ("seq", "dp"), None),
        P("pipe", ("seq", "dp"), None),
        P("pipe", None),
        P("pipe", None),
        P("pipe", None, None),
        P("pipe", None),
        P("pipe", None),
        P("pipe", None, "dp", "seq", None),
    )
    out_specs = (P("pipe", None, "dp", "seq", None), P("pipe", ("seq", "dp"), None))
    return jax.shard_map(body, mesh=mesh, in_specs=in_specs, out_specs=out_specs, check_vma=False)
```

```python
import functools
import math

import jax
import jax.numpy as jnp
from jax import lax
from jax.experimental import pallas as pl
from jax.experimental.pallas import tpu as pltpu
from jax.sharding import PartitionSpec as P

epsilon = 1e-06


def passed_along(value, axis, steps):
    count = lax.axis_size(axis)
    first, last = (max(0, -steps), min(count, count - steps))
    return lax.ppermute(value, axis, [(source, source + steps) for source in range(first, last)])


def ring(value, axis):
    count = lax.axis_size(axis)
    return lax.ppermute(value, axis, [(source, (source + 1) % count) for source in range(count)])


def swap(value, bit):
    count = lax.axis_size("seq")
    return lax.ppermute(value, "seq", [(source, source ^ bit) for source in range(count)])


def handed_over(value):
    return lax.ppermute(value, "pipe", [(0, 1), (1, 0)])


def shifted(value, axis, shift):
    count = lax.axis_size(axis)
    return lax.ppermute(value, axis, [(source, (source + shift) % count) for source in range(count)])


def fold(index):
    return index ^ (index >> 1)


def ring_step(value):
    count = lax.axis_size("dp")
    pairs = [(fold(place), fold((place + 1) % count)) for place in range(count)]
    return lax.ppermute(value, "dp", pairs)


def offsets_of(count):
    offsets = [0]
    bit = count // 2
    while bit:
        offsets = offsets + [offset ^ bit for offset in offsets]
        bit //= 2
    return offsets


def turn_and_batch(step, turns):
    section = lax.axis_index("pipe")
    turn = jnp.clip(step - section, 0, turns - 1)
    return turn, turn - section + 1


def pack_kernel(wq, wkv, *refs):
    outs, sems = refs[:-1], refs[-1]
    cols = outs[0].shape[1] // 2
    seq = lax.axis_index("seq")
    copies = []
    for m, out in enumerate(outs):
        start = pl.multiple_of((seq ^ m) * cols, 128)
        for k, source in enumerate((wq, wkv)):
            copies.append(
                pltpu.make_async_copy(
                    source.at[0, :, pl.ds(start, cols)],
                    out.at[:, pl.ds(k * cols, cols)],
                    sems.at[2 * m + k],
                )
            )
    for copy in copies:
        copy.start()
    for copy in copies:
        copy.wait()


def stack_kernel(deps, *refs):
    out = refs[-1]
    at = 0
    for ref in refs[deps:-1]:
        if len(ref.shape) == 2:
            out[at] = ref[...]
            at += 1
        else:
            out[at : at + ref.shape[0]] = ref[...]
            at += ref.shape[0]


def place_kernel(hop, hops, *refs):
    weights, parts = refs[-1], refs[:-1]
    if hop > 0:
        parts = parts[:-1]
    place(hop, hops, parts, weights)


def place(hop, hops, parts, weights):
    seq, rep = lax.axis_index("seq"), lax.axis_index("dp")
    m = 0
    for part in parts:
        count, rows = part.shape[:2]
        for j in range(count):
            block = (seq ^ m) * hops + fold(lax.rem(fold(rep) + hops - hop, hops))
            weights[pl.ds(pl.multiple_of(block * rows, 16), rows)] = part[j]
            m += 1


def first_kernel(turns, far, incoming, contacts, out, states):
    rows = incoming.shape[3]
    for turn in range(2):
        out[turn * rows : (turn + 1) * rows] = incoming[0, turn, 0]
    states[...] = jnp.zeros_like(states)
    for step in range(turns + 1):
        _, batch = turn_and_batch(step, turns)
        states[step : step + 1] = contacts[batch].astype(jnp.float32)
    out[2 * rows :, : states.shape[1]] = states[...].astype(jnp.bfloat16)


def second_kernel(dep, incoming, cotangent, out):
    turns, rows, feats = cotangent.shape[1], cotangent.shape[3], cotangent.shape[4]
    out[:rows] = incoming[0, 2, 0]
    for turn in range(turns):
        out[rows:, turn * feats : (turn + 1) * feats] = cotangent[0, turn, 0]


def columns_of(rows_of, pieces, rows):
    labels = lax.broadcasted_iota(jnp.int32, (32, rows), 0)
    columns = []
    for i in range(pieces):
        state, flag = rows_of(i)
        one = jnp.zeros((32, rows), jnp.float32)
        if state is not None:
            one = jnp.where(labels == state, 1.0, 0.0)
        if flag is not None:
            one = jnp.where(labels == 16, flag, one)
        columns.append(one.T)
    return jnp.concatenate(columns, axis=0)


def modulation(step, turns, times, gain, freq):
    _, batch = turn_and_batch(step, turns)
    return gain[...] * (1.0 + 0.5 * jnp.sin(times[batch, 0].astype(jnp.float32) * freq[...]))


def norm_kernel(turns, pieces, times, table, gain, freq, *refs):
    sources, refs = refs[:pieces], refs[pieces:]
    scaled, scales, owns, embeds, mod = refs[0:2], refs[2:4], refs[4:6], refs[6:8], refs[8]
    first, sems = refs[9 : 9 + pieces], refs[9 + pieces]
    copies = [
        pltpu.make_async_copy(sources[i], first[i], sems.at[i]) for i in range(pieces)
    ]
    for copy in copies:
        copy.start()
    for copy in copies:
        copy.wait()
    frames, width = scaled[0].shape
    rows, cols = frames // pieces, owns[0].shape[1]
    seq = lax.axis_index("seq")
    offsets = offsets_of(pieces)
    for step in range(turns + 1):

        def state_of(i):
            state = first[i][2 * rows : 2 * rows + 16, :rows][step : step + 1]
            return state.astype(jnp.float32).astype(jnp.int32), None

        onehot = columns_of(state_of, pieces, rows)[:, : table.shape[1]].astype(jnp.bfloat16)
        if step >= 2:
            for at in range(0, width, 256):
                embeds[step - 2][:, at : at + 256] = jnp.dot(
                    onehot, table[0, :, at : at + 256], preferred_element_type=jnp.float32
                ).astype(jnp.bfloat16)
            continue
        turn, _ = turn_and_batch(step, turns)
        at = pl.multiple_of(jnp.minimum(turn, 1) * rows, 128)
        mod[...] = modulation(step, turns, times, gain, freq)
        total = jnp.zeros((frames, 128), jnp.float32)
        for i in range(pieces):
            lanes = pl.ds(pl.multiple_of((seq ^ offsets[i]) * cols, 128), cols)
            current = jnp.concatenate([first[p][pl.ds(at, rows), lanes] for p in range(pieces)])
            hidden = current.astype(jnp.float32) + jnp.dot(
                onehot, table[0, :, lanes], preferred_element_type=jnp.float32
            )
            for lane in range(0, cols, 128):
                piece = hidden[:, lane : lane + 128]
                total = total + piece * piece
            scaled[step][:, lanes] = (hidden * mod[:, lanes]).astype(jnp.bfloat16)
            if i == 0:
                owns[step][...] = hidden
        mean = jnp.sum(total, axis=1, keepdims=True) * (1.0 / width)
        scales[step][...] = jnp.broadcast_to(lax.rsqrt(mean + epsilon), (frames, 128))


def step_kernel(cfg, *refs):
    step, has_relay = cfg["step"], cfg["has_relay"]
    pieces, hops, head, turns = cfg["pieces"], cfg["hops"], cfg["head"], cfg["turns"]
    heads, group, halves = cfg["heads"], cfg["group"], cfg["halves"]
    refs = list(refs)

    def take(count):
        taken, refs[:count] = refs[:count], []
        return taken

    bias, times, gain, freq, gate, flags = take(6)
    if has_relay:
        second, embed, relay = take(pieces), take(1)[0], take(pieces * halves)
    else:
        scaled, scales, own_hidden = take(3)
    chunk = take(2) if step == 0 else None
    weights = take(1)[0]
    outs = take(halves)
    if step == 0:
        weights = take(1)[0]
    proj, att = take(2)
    if has_relay:
        scaled, scales, own_hidden, mod = take(4)
    offsets = offsets_of(pieces)
    frames, width = scaled.shape
    rows, cols = frames // pieces, att.shape[0]
    part = pieces // halves
    seq, rep, section = lax.axis_index("seq"), lax.axis_index("dp"), lax.axis_index("pipe")
    _, batch = turn_and_batch(step, turns)

    if step == 0:
        place(hops - 1, hops, chunk, weights)

    def normalize(relayed):
        total = jnp.zeros((frames, 128), jnp.float32)
        for i in range(pieces):
            lanes = pl.ds(pl.multiple_of((seq ^ offsets[i]) * cols, 128), cols)
            blocks = []
            for p in range(pieces):
                if relayed:
                    j = offsets.index(offsets[i] ^ offsets[p])
                    blocks.append(relay[(j // part) * pieces + i][j % part])
                else:
                    blocks.append(second[p][:rows, lanes])
            hidden = jnp.concatenate(blocks, axis=0).astype(jnp.float32)
            hidden = hidden + embed[:, lanes].astype(jnp.float32)
            for lane in range(0, cols, 128):
                piece = hidden[:, lane : lane + 128]
                total = total + piece * piece
            scaled[:, lanes] = (hidden * mod[:, lanes]).astype(jnp.bfloat16)
            if i == 0:
                own_hidden[...] = hidden
        scales[...] = total

    if has_relay:
        mod[...] = modulation(step, turns, times, gain, freq)

        @pl.when(section == 0)
        def _():
            normalize(False)

        @pl.when(section != 0)
        def _():
            normalize(True)

        mean = jnp.sum(scales[...], axis=1, keepdims=True) * (1.0 / width)
        scale = lax.rsqrt(mean + epsilon)
    else:
        scale = scales[:, :1]

    def flag_of(i):
        lanes = pl.ds(pl.multiple_of((seq ^ offsets[i]) * rows, 128), rows)
        return None, flags[batch, :, lanes].astype(jnp.float32)

    flag_column = columns_of(flag_of, pieces, rows)[:, 16:17]
    score_scale = head ** (-0.5) * math.log2(math.e)
    for at in range(0, 2 * cols, 256):
        lane = at + lax.broadcasted_iota(jnp.int32, (1, 256), 1)
        factor = jnp.where(lane < cols, score_scale, 1.0)
        projected = jnp.dot(
            scaled[...], weights[:, at : at + 256], preferred_element_type=jnp.float32
        )
        proj[:, at : at + 256] = (projected * scale * factor).astype(jnp.bfloat16)
    proj[:, 2 * cols :] = jnp.zeros((frames, 128), jnp.bfloat16)
    lanes = lax.broadcasted_iota(jnp.int32, (frames, 128), 1)
    row_lanes = lax.broadcasted_iota(jnp.int32, (1, 128), 1)
    flag_lanes = jnp.logical_or(lanes == head, lanes == head + 1)

    def part_of(at):
        return proj[:, at : at + 128].astype(jnp.float32)

    keys, values = [], []
    for kv in range(heads // group):
        base = cols + kv * 2 * head
        key = jnp.where(flag_lanes, flag_column, jnp.where(lanes < head, part_of(base), 0.0))
        value = jnp.where(lanes < head, part_of(base + head), jnp.where(lanes == head, 1.0, 0.0))
        keys.append(key.astype(jnp.bfloat16))
        values.append(value.T.astype(jnp.bfloat16))

    def scores_of(h):
        strength = jnp.zeros((1, 128), jnp.float32) + bias[0, seq * heads + h] * math.log2(math.e)
        coarse = strength.astype(jnp.bfloat16).astype(jnp.float32)
        tail = jnp.where(
            row_lanes == head, coarse, jnp.where(row_lanes == head + 1, strength - coarse, 0.0)
        )
        query = jnp.where(lanes < head, part_of(h * head), tail).astype(jnp.bfloat16)
        return lax.dot_general(
            keys[h // group], query, (((1,), (1,)), ((), ())), preferred_element_type=jnp.float32
        )

    scores = scores_of(0)
    for h in range(heads):
        ahead = scores_of(h + 1) if h + 1 < heads else None
        top = jnp.max(scores, axis=0, keepdims=True)
        weight = jnp.exp2(scores - top).astype(jnp.bfloat16)
        mixed = jnp.dot(values[h // group], weight, preferred_element_type=jnp.float32)
        att[h * head : (h + 1) * head, :] = mixed[:head] * (1.0 / mixed[head : head + 1])
        scores = ahead
    own = pl.ds(pl.multiple_of(seq * cols, 128), cols)
    attended = att[...].T.astype(jnp.bfloat16).astype(jnp.float32)
    output = (own_hidden[...] + gate[:, own] * attended).astype(jnp.bfloat16)
    blocks = output.reshape(pieces, rows, cols)
    for k in range(halves):
        outs[k][...] = blocks[k * part : (k + 1) * part]


def tie_kernel(*refs):
    pass


def grad_of(output, second, turn, rows, feats):
    cot = jnp.concatenate(
        [piece[rows : 2 * rows, turn * feats : (turn + 1) * feats] for piece in second], axis=0
    )
    return lax.dot_general(
        output, cot, (((0,), (0,)), ((), ())), preferred_element_type=jnp.float32
    )


def early_kernel(turns, pieces, halves, feats, *refs):
    outs, second = refs[: turns * halves], refs[turns * halves : turns * halves + pieces]
    sends, grad = refs[turns * halves + pieces : -1], refs[-1]
    section = lax.axis_index("pipe")
    offsets = offsets_of(pieces)
    part = pieces // halves
    rows = outs[0].shape[1]
    total = None
    for turn in range(turns - 1):
        blocks = []
        for p in range(pieces):
            k, j = p // part, p % part
            block = jnp.where(
                section == 0, outs[turn * halves + k][j], outs[(turn + 1) * halves + k][j]
            )
            sends[offsets[p]][turn] = block
            blocks.append(block)
        share = grad_of(jnp.concatenate(blocks, axis=0), second, turn, rows, feats)
        total = share if total is None else total + share
    grad[...] = total


def settle_kernel(turns, pieces, halves, hops, feats, *refs):
    refs = list(refs)

    def take(count):
        taken, refs[:count] = refs[:count], []
        return taken

    before, now, second, early = take(halves), take(halves), take(pieces), take(pieces - 1)
    early_grad = take(1)[0]
    late, own_grad, grads = take(pieces), take(1)[0], take(hops - 1)
    section_out = take(1)[0]
    rows_out, total, sem = take(3)
    section, seq, rep = lax.axis_index("pipe"), lax.axis_index("seq"), lax.axis_index("dp")
    offsets = offsets_of(pieces)
    part = pieces // halves
    rows, cols = early[0].shape[1:]
    for m in range(pieces - 1):
        lanes = pl.ds(pl.multiple_of((seq ^ m) * cols, 128), cols)
        for turn in range(turns - 1):
            rows_out[turn, :, lanes] = early[m][turn]
    copy = pltpu.make_async_copy(rows_out, section_out.at[pl.ds(0, turns - 1)], sem)
    copy.start()
    blocks = []
    for p in range(pieces):
        block = jnp.where(section == 0, before[p // part][p % part], now[p // part][p % part])
        late[offsets[p]][...] = block
        blocks.append(block)
    share = grad_of(jnp.concatenate(blocks, axis=0), second, turns - 1, rows, feats)
    factor = float(turns * hops * rows * pieces) ** (-0.5)
    total[...] = (share + early_grad[...]) * factor
    g_rows = cols // hops
    own_grad[...] = total[pl.ds(pl.multiple_of(rep * g_rows, 8), g_rows)]
    for shift in range(1, hops):
        at = pl.multiple_of(lax.rem(rep + shift, hops) * g_rows, 8)
        grads[shift - 1][...] = total[pl.ds(at, g_rows)].astype(jnp.bfloat16)
    copy.wait()


def finish_kernel(pieces, hops, *refs):
    held, early, late, refs = refs[0], refs[1], refs[2 : pieces + 2], refs[pieces + 2 :]
    own_grad, parts, (section_out, grad, row_out, sems) = refs[0], refs[1:hops], refs[hops:]
    seq = lax.axis_index("seq")
    cols = late[0].shape[1]
    last_lanes = pl.ds(pl.multiple_of((seq ^ (pieces - 1)) * cols, 128), cols)
    early_copy = pltpu.make_async_copy(
        early, section_out.at[pl.ds(0, early.shape[0]), :, last_lanes], sems.at[0]
    )
    early_copy.start()
    for m in range(pieces):
        lanes = pl.ds(pl.multiple_of((seq ^ m) * cols, 128), cols)
        row_out[:, lanes] = late[m][...]
    copy = pltpu.make_async_copy(row_out, section_out.at[section_out.shape[0] - 1], sems.at[1])
    copy.start()
    total = own_grad[...]
    for part in parts:
        total = total + part[...].astype(jnp.float32)
    grad[...] = total
    early_copy.wait()
    copy.wait()


HALVES = 2
MIB = 1024 * 1024


def paired_body(
    incoming,
    contacts,
    keyframes,
    timesteps,
    w_query,
    w_keyval,
    norm_gain,
    time_freq,
    contact_table,
    key_bias,
    attn_gate,
    head_cotangent,
):
    seq_count = lax.axis_size("seq")
    hops = lax.axis_size("dp")
    rows, width, turns = incoming.shape[3], incoming.shape[4], incoming.shape[1]
    frames = rows * seq_count
    heads_all = key_bias.shape[1]
    head = width // heads_all
    heads = heads_all // seq_count
    kv_heads = w_keyval.shape[2] // (2 * head * seq_count)
    feats = head_cotangent.shape[4]
    cols = width // seq_count
    w_rows = w_query.shape[1]
    steps = turns + 1
    part = seq_count // HALVES
    kind = jnp.bfloat16
    smem = pl.BlockSpec(memory_space=pltpu.SMEM)
    vmem = pl.BlockSpec(memory_space=pltpu.VMEM)
    anywhere = pl.BlockSpec(memory_space=pl.ANY)
    shape = jax.ShapeDtypeStruct

    def call(kernel, name, out_shape, in_specs, operands, scratch=(), limit=4, flops=0, **options):
        return pl.pallas_call(
            kernel,
            out_shape=out_shape,
            in_specs=in_specs,
            scratch_shapes=list(scratch),
            compiler_params=pltpu.CompilerParams(vmem_limit_bytes=limit * MIB),
            cost_estimate=pl.CostEstimate(
                flops=flops, bytes_accessed=flops // 512, transcendentals=0
            ),
            name=name,
            **options,
        )(*operands)

    def pin(value, space=pltpu.VMEM):
        return pltpu.with_memory_space_constraint(value, space)

    packed = call(
        pack_kernel,
        "pack",
        [pltpu.VMEM((w_rows, 2 * cols), kind)] * seq_count,
        [anywhere, anywhere],
        [pin(w_query, pltpu.HBM), pin(w_keyval, pltpu.HBM)],
        [pltpu.SemaphoreType.DMA((2 * seq_count,))],
        out_specs=[vmem] * seq_count,
    )
    blocks = [packed[0]] + [swap(packed[m], m) for m in range(1, seq_count)]

    def stacked(name, count, deps, values):
        return call(
            functools.partial(stack_kernel, len(deps)),
            name,
            pltpu.VMEM((count, w_rows, 2 * cols), kind),
            [anywhere] * len(deps) + [vmem] * len(values),
            deps + values,
            out_specs=vmem,
        )

    weights = None

    def placed(hop, parts):
        operands = [pin(part) for part in parts] + ([pin(weights)] if hop else [])
        return call(
            functools.partial(place_kernel, hop, hops),
            "place%d" % hop,
            pltpu.VMEM((width, 2 * cols), kind),
            [vmem] * len(operands),
            operands,
            out_specs=vmem,
            input_output_aliases={len(parts): 0} if hop else {},
        )

    near = stacked("near", 2, [], blocks[:2])
    near_next = ring_step(near)
    far = stacked("far", 2, [near_next], blocks[2:])
    far_next = ring_step(far)
    rings = [[near, near_next], [far, far_next]]
    for hop in range(2, hops - 1):
        for chunks in rings:
            chunks.append(ring_step(chunks[-1]))
    last_chunk = [ring_step(chunks[-1]) for chunks in rings]
    for hop in range(hops - 1):
        weights = placed(hop, [chunks[hop] for chunks in rings])

    def tie(values, deps):
        return call(
            tie_kernel,
            "tie",
            [shape(value.shape, kind) for value in values],
            [anywhere] * (len(values) + len(deps)),
            list(values) + list(deps),
            out_specs=[anywhere] * len(values),
            input_output_aliases={i: i for i in range(len(values))},
        )

    mine = call(
        functools.partial(first_kernel, turns),
        "first",
        pltpu.VMEM((2 * rows + 16, width), kind),
        [anywhere, vmem, vmem],
        [far, incoming, contacts],
        [pltpu.VMEM((16, 128), jnp.float32)],
        out_specs=vmem,
    )
    across = swap(mine, 2)
    beside = swap(mine, 1)
    (across,) = tie([across], [chunks[-1] for chunks in rings])
    first = [mine, across, beside, swap(across, 1)]
    prepared = call(
        functools.partial(norm_kernel, turns, seq_count),
        "norm",
        [pltpu.VMEM((frames, width), kind)] * 2
        + [pltpu.VMEM((frames, 128), jnp.float32)] * 2
        + [pltpu.VMEM((frames, cols), jnp.float32)] * 2
        + [pltpu.VMEM((frames, width), kind)] * 2,
        [smem] + [vmem] * 3 + [anywhere] * seq_count,
        [timesteps, contact_table, norm_gain, time_freq]
        + first,
        [pltpu.VMEM((1, width), jnp.float32)]
        + [pltpu.VMEM((2 * rows + 16, width), kind)] * seq_count
        + [pltpu.SemaphoreType.DMA((seq_count,))],
        12,
        out_specs=[vmem] * 8,
    )

    mine = call(
        second_kernel,
        "second",
        pltpu.VMEM((2 * rows, width), kind),
        [anywhere, vmem, vmem],
        [across, incoming, head_cotangent],
        out_specs=vmem,
    )
    second = [mine, swap(mine, 2), swap(mine, 1)]

    outputs = []
    relayed = {}
    for step in range(steps):
        cfg = {
            "step": step,
            "has_relay": step in relayed,
            "pieces": seq_count,
            "hops": hops,
            "head": head,
            "heads": heads,
            "group": heads // kv_heads,
            "turns": turns,
            "halves": HALVES,
        }
        operands = [key_bias, timesteps, norm_gain, time_freq, attn_gate, keyframes]
        scratch = [
            pltpu.VMEM((frames, 2 * cols + 128), kind),
            pltpu.VMEM((cols, frames), jnp.float32),
        ]
        if step in relayed:
            large = second + [prepared[4 + step]] + relayed[step]
            scratch += [
                pltpu.VMEM((frames, width), kind),
                pltpu.VMEM((frames, 128), jnp.float32),
                pltpu.VMEM((frames, cols), jnp.float32),
                pltpu.VMEM((1, width), jnp.float32),
            ]
        else:
            large = [prepared[step], prepared[2 + step], prepared[4 + step]]
        large += last_chunk + [weights] if step == 0 else [weights]
        operands += [pin(value) for value in large]
        out_shape = [pltpu.VMEM((part, rows, cols), kind)] * HALVES
        if step == 0:
            out_shape += [pltpu.VMEM((width, 2 * cols), kind)]
        results = call(
            functools.partial(step_kernel, cfg),
            "step%d" % step,
            out_shape,
            [smem, smem] + [vmem] * (len(operands) - 2),
            operands,
            scratch,
            16,
            2 * frames * width * 2 * cols + 4 * heads * frames * frames * head,
            out_specs=[vmem] * len(out_shape),
            input_output_aliases={len(operands) - 1: HALVES} if step == 0 else {},
        )
        outputs.append(list(results[:HALVES]))
        if step == 0:
            weights = results[HALVES]
        if step == 0:
            (second[1],) = tie([second[1]], [outputs[-1][0]])
            second.append(swap(second[1], 1))
        if step == 2:
            early = call(
                functools.partial(early_kernel, turns, seq_count, HALVES, feats),
                "early",
                [shape((turns - 1, rows, cols), kind)] * seq_count
                + [shape((cols, feats), jnp.float32)],
                [vmem] * (turns * HALVES + seq_count),
                [half for output in outputs for half in output] + second,
                limit=8,
                out_specs=[vmem] * (seq_count + 1),
            )
            early, early_grad = list(early[:-1]), early[-1]
            early = [early[0]] + [swap(early[m], m) for m in range(1, seq_count)]
            pending = [piece for k in range(HALVES) for piece in (crossing[k][0], crossing[k][1])]
            tied = tie(pending, [early_grad])
            relayed[3] = []
            for k in range(HALVES):
                mine, across = tied[2 * k], tied[2 * k + 1]
                relayed[3] += [mine, across, swap(mine, 1), swap(across, 1)]
        if step + 2 < steps:
            crossing = []
            for half in outputs[-1]:
                piece = handed_over(half)
                crossing.append((piece, swap(piece, 2)))
            if step == 0:
                relayed[2] = []
                for mine, across in crossing:
                    relayed[2] += [mine, across, swap(mine, 1), swap(across, 1)]

    g_shape = (cols // hops, feats)
    operands = outputs[-2] + outputs[-1] + second + early[:-1] + [early_grad]
    settled = call(
        functools.partial(settle_kernel, turns, seq_count, HALVES, hops, feats),
        "settle",
        [shape((rows, cols), kind)] * seq_count
        + [shape(g_shape, jnp.float32)]
        + [shape(g_shape, kind)] * (hops - 1)
        + [shape((turns, rows, width), kind)],
        [vmem] * len(operands),
        operands,
        [
            pltpu.VMEM((turns - 1, rows, width), kind),
            pltpu.VMEM((cols, feats), jnp.float32),
            pltpu.SemaphoreType.DMA,
        ],
        8,
        out_specs=[vmem] * (seq_count + hops) + [anywhere],
    )
    late, grads, held = settled[:seq_count], settled[seq_count:-1], settled[-1]
    late = [late[0]] + [swap(late[m], m) for m in range(1, seq_count)]
    grads = [grads[0]] + [shifted(grads[k], "dp", k) for k in range(1, hops)]
    section_out, grad_rows = call(
        functools.partial(finish_kernel, seq_count, hops),
        "finish",
        [shape((turns, rows, width), kind), shape(g_shape, jnp.float32)],
        [anywhere] + [vmem] * (seq_count + hops + 1),
        [held, early[-1]] + late + grads,
        [pltpu.VMEM((rows, width), kind), pltpu.SemaphoreType.DMA((2,))],
        out_specs=[anywhere, vmem],
        input_output_aliases={0: 0},
    )
    return (section_out[None, :, None], grad_rows[None])


def body(incoming, contacts, keyframes, timesteps, w_query, *others):
    count = lax.axis_size("seq")
    cols = w_query.shape[2] // count
    paired = (
        lax.axis_size("pipe") == 2
        and lax.axis_size("dp") == 4
        and count == 4
        and cols % 128 == 0
        and w_query.shape[1] % 16 == 0
        and incoming.shape[3] == 128
        and incoming.shape[1] == 3
    )
    chosen = paired_body if paired else general_body
    return chosen(incoming, contacts, keyframes, timesteps, w_query, *others)


def general_body(
    incoming,
    contacts,
    keyframes,
    timesteps,
    w_query,
    w_keyval,
    norm_gain,
    time_freq,
    contact_table,
    key_bias,
    attn_gate,
    head_cotangent,
):
    section_idx = lax.axis_index("pipe")
    seq_idx = lax.axis_index("seq")
    rep_idx = lax.axis_index("dp")
    seq_count = lax.axis_size("seq")
    section_count = lax.axis_size("pipe")
    rep_count = lax.axis_size("dp")
    tok_rows = incoming.shape[3]
    width = incoming.shape[4]
    turns = incoming.shape[1]
    frames = tok_rows * seq_count
    heads_all = key_bias.shape[1]
    head_size = width // heads_all
    heads_local = heads_all // seq_count
    kv_width = w_keyval.shape[2]
    kv_local = kv_width // (2 * head_size * seq_count)
    group_size = heads_local // kv_local
    feat_count = head_cotangent.shape[4]
    score_scale = head_size ** (-0.5)
    q_cols = width // seq_count
    kv_cols = kv_width // seq_count
    w_rows = w_query.shape[1]

    w_parts = jnp.concatenate(
        [
            w_query[0].reshape(w_rows, seq_count, q_cols),
            w_keyval[0].reshape(w_rows, seq_count, kv_cols),
        ],
        axis=2,
    ).transpose(1, 0, 2)
    block = lax.all_to_all(w_parts, "seq", split_axis=0, concat_axis=0, tiled=True)
    weights = jnp.zeros((seq_count, rep_count, w_rows, q_cols + kv_cols), jnp.bfloat16)
    for hop in range(rep_count):
        owner = lax.rem(rep_idx + rep_count - hop, rep_count)
        weights = lax.dynamic_update_slice_in_dim(weights, block[:, None], owner, 1)
        if hop + 1 < rep_count:
            block = ring(block, "dp")
    weights = weights.reshape(width, q_cols + kv_cols)

    gain_row = norm_gain[0]
    freq_row = time_freq[0]
    table = contact_table[0]
    gate_local = lax.dynamic_slice_in_dim(attn_gate[0], seq_idx * q_cols, q_cols)
    table_local = lax.dynamic_slice_in_dim(table, seq_idx * q_cols, q_cols, 1)
    bias_local = lax.dynamic_slice_in_dim(key_bias[0], seq_idx * heads_local, heads_local)
    contact_all = lax.all_gather(contacts[:, 0, :], "seq", axis=1, tiled=True)
    key_all = keyframes[:, 0, :]
    step_all = timesteps[:, 0]
    labels = jnp.arange(table.shape[0], dtype=jnp.int32)
    cot_all = lax.all_gather(head_cotangent[0, :, 0], "seq", axis=1, tiled=True)

    lag = 2 if section_count == 2 else 1
    if lag == 2:
        steps = turns + 1
    else:
        steps = turns

    def turn_at(step):
        if lag == 1:
            return jnp.int32(step)
        return jnp.clip(step - section_idx, 0, turns - 1)

    outputs = []
    handed = {}
    for step in range(steps):
        turn = turn_at(step)
        fresh = lax.dynamic_index_in_dim(incoming[0, :, 0], turn, 0, keepdims=False)
        current = lax.all_gather(fresh, "seq", axis=0, tiled=True)
        if step in handed:
            current = jnp.where((section_idx == 0) | (turn == 0), current, handed[step])
        batch_idx = turn - section_idx + section_count - 1
        contact_rows = lax.dynamic_index_in_dim(contact_all, batch_idx, 0, keepdims=False)
        key_flags = lax.dynamic_index_in_dim(key_all, batch_idx, 0, keepdims=False).astype(
            jnp.float32
        )
        timestep = lax.dynamic_index_in_dim(step_all, batch_idx, 0, keepdims=False).astype(
            jnp.float32
        )
        onehot = (contact_rows[:, None] == labels[None, :]).astype(jnp.bfloat16)
        hidden = current.astype(jnp.float32) + jnp.dot(
            onehot, table, preferred_element_type=jnp.float32
        )
        root_mean = jnp.sqrt(jnp.mean(hidden * hidden, axis=-1, keepdims=True) + epsilon)
        modulation = gain_row * (1.0 + 0.5 * jnp.sin(timestep * freq_row))
        normed = (hidden / root_mean * modulation[None, :]).astype(jnp.bfloat16)
        projected = jnp.dot(normed, weights, preferred_element_type=jnp.float32).astype(
            jnp.bfloat16
        )
        query_heads = projected[:, :q_cols].reshape(frames, heads_local, head_size)
        keyval_heads = projected[:, q_cols:].reshape(frames, kv_local, 2, head_size)
        head_outputs = []
        for head in range(heads_local):
            key_rows = keyval_heads[:, head // group_size, 0]
            value_rows = keyval_heads[:, head // group_size, 1]
            scores = (
                lax.dot_general(
                    query_heads[:, head],
                    key_rows,
                    (((1,), (1,)), ((), ())),
                    preferred_element_type=jnp.float32,
                )
                * score_scale
            )
            scores = scores + bias_local[head] * key_flags[None, :]
            row_max = jnp.max(scores, axis=-1, keepdims=True)
            exponent = jnp.exp(scores - row_max)
            probabilities = (exponent / jnp.sum(exponent, axis=-1, keepdims=True)).astype(
                jnp.bfloat16
            )
            head_outputs.append(
                jnp.dot(probabilities, value_rows, preferred_element_type=jnp.float32).astype(
                    jnp.bfloat16
                )
            )
        attended = jnp.concatenate(head_outputs, axis=1)
        hidden_local = lax.dynamic_slice_in_dim(current, seq_idx * q_cols, q_cols, 1).astype(
            jnp.float32
        ) + jnp.dot(onehot, table_local, preferred_element_type=jnp.float32)
        output = (hidden_local + gate_local[None, :] * attended.astype(jnp.float32)).astype(
            jnp.bfloat16
        )
        outputs.append(output)
        if step + lag < steps:
            piece = passed_along(output, "pipe", 1)
            handed[step + lag] = lax.all_gather(piece, "seq", axis=1, tiled=True)

    factor = float(turns * rep_count * frames) ** (-0.5)
    total = None
    rows_out = []
    for turn in range(turns):
        if lag == 2:
            own = jnp.where(section_idx == 0, outputs[turn], outputs[turn + 1])
        else:
            own = outputs[turn]
        term = lax.dot_general(
            own, cot_all[turn], (((0,), (0,)), ((), ())), preferred_element_type=jnp.float32
        )
        total = term if total is None else total + term
        rows_out.append(lax.all_to_all(own, "seq", split_axis=0, concat_axis=1, tiled=True))
    section_out = jnp.stack(rows_out)[None, :, None]
    grad_parts = lax.all_to_all(
        (total * factor).astype(jnp.bfloat16).reshape(rep_count, q_cols // rep_count, feat_count),
        "dp",
        split_axis=0,
        concat_axis=0,
        tiled=True,
    )
    grad_rows = jnp.sum(grad_parts.astype(jnp.float32), axis=0)
    return (section_out, grad_rows[None])


def solution(mesh):
    in_specs = (
        P("pipe", None, "dp", "seq", None),
        P(None, "dp", "seq"),
        P(None, "dp", None),
        P(None, "dp"),
        P("pipe", ("seq", "dp"), None),
        P("pipe", ("seq", "dp"), None),
        P("pipe", None),
        P("pipe", None),
        P("pipe", None, None),
        P("pipe", None),
        P("pipe", None),
        P("pipe", None, "dp", "seq", None),
    )
    out_specs = (P("pipe", None, "dp", "seq", None), P("pipe", ("seq", "dp"), None))
    return jax.shard_map(body, mesh=mesh, in_specs=in_specs, out_specs=out_specs, check_vma=False)
```

```python
import functools
import math

import jax
import jax.numpy as jnp
from jax import lax
from jax.experimental import pallas as pl
from jax.experimental.pallas import tpu as pltpu
from jax.sharding import PartitionSpec as P

epsilon = 1e-06


def passed_along(value, axis, steps):
    count = lax.axis_size(axis)
    first, last = (max(0, -steps), min(count, count - steps))
    return lax.ppermute(value, axis, [(source, source + steps) for source in range(first, last)])


def ring(value, axis):
    count = lax.axis_size(axis)
    return lax.ppermute(value, axis, [(source, (source + 1) % count) for source in range(count)])


def swap(value, bit):
    count = lax.axis_size("seq")
    return lax.ppermute(value, "seq", [(source, source ^ bit) for source in range(count)])


def handed_over(value):
    return lax.ppermute(value, "pipe", [(0, 1), (1, 0)])


def shifted(value, axis, shift):
    count = lax.axis_size(axis)
    return lax.ppermute(value, axis, [(source, (source + shift) % count) for source in range(count)])


def fold(index):
    return index ^ (index >> 1)


def ring_step(value):
    count = lax.axis_size("dp")
    pairs = [(fold(place), fold((place + 1) % count)) for place in range(count)]
    return lax.ppermute(value, "dp", pairs)


def offsets_of(count):
    offsets = [0]
    bit = count // 2
    while bit:
        offsets = offsets + [offset ^ bit for offset in offsets]
        bit //= 2
    return offsets


def turn_and_batch(step, turns):
    section = lax.axis_index("pipe")
    turn = jnp.clip(step - section, 0, turns - 1)
    return turn, turn - section + 1


def pack_kernel(wq, wkv, *refs):
    outs, (queries, keyvals, sems) = refs[:-3], refs[-3:]
    parts, _, cols = outs[0].shape
    half = cols // 2
    seq = lax.axis_index("seq")
    copies = []
    for m in range(len(outs)):
        start = pl.multiple_of((seq ^ m) * cols, 128)
        for k, (source, held) in enumerate(((wq, queries), (wkv, keyvals))):
            copies.append(
                pltpu.make_async_copy(
                    source.at[0, :, pl.ds(start, cols)], held.at[m], sems.at[2 * m + k]
                )
            )
    for copy in copies:
        copy.start()
    for m, out in enumerate(outs):
        copies[2 * m].wait()
        copies[2 * m + 1].wait()
        for part in range(parts):
            lanes = slice(part * half, (part + 1) * half)
            out[part] = jnp.concatenate([queries[m][:, lanes], keyvals[m][:, lanes]], axis=1)


def pair_kernel(deps, *refs):
    out = refs[-1]
    for at, ref in enumerate(refs[deps:-1]):
        out[at] = ref[...]


def part_kernel(part, near, far, out):
    for at in range(2):
        out[at] = near[at, part]
        out[at + 2] = far[at, part]


def place(hop, hops, blocks, weights):
    seq, rep = lax.axis_index("seq"), lax.axis_index("dp")
    for m, block in enumerate(blocks):
        rows = block.shape[0]
        at = (seq ^ m) * hops + fold(lax.rem(fold(rep) + hops - hop, hops))
        weights[pl.ds(pl.multiple_of(at * rows, 16), rows)] = block[...]


def place_kernel(part, hops, near, far, chunk, weights):
    place(0, hops, [near.at[0, part], near.at[1, part], far.at[0, part], far.at[1, part]], weights)
    place(1, hops, [chunk.at[m] for m in range(4)], weights)


def first_kernel(turns, far, incoming, contacts, out, states):
    rows = incoming.shape[3]
    for turn in range(2):
        out[turn * rows : (turn + 1) * rows] = incoming[0, turn, 0]
    states[...] = jnp.zeros_like(states)
    for step in range(turns + 1):
        _, batch = turn_and_batch(step, turns)
        states[step : step + 1] = contacts[batch].astype(jnp.float32)
    out[2 * rows :, : states.shape[1]] = states[...].astype(jnp.bfloat16)


def second_kernel(dep, incoming, cotangent, out):
    turns, rows, feats = cotangent.shape[1], cotangent.shape[3], cotangent.shape[4]
    out[:rows] = incoming[0, 2, 0]
    for turn in range(turns):
        out[rows:, turn * feats : (turn + 1) * feats] = cotangent[0, turn, 0]


def columns_of(rows_of, pieces, rows):
    labels = lax.broadcasted_iota(jnp.int32, (32, rows), 0)
    columns = []
    for i in range(pieces):
        state, flag = rows_of(i)
        one = jnp.zeros((32, rows), jnp.float32)
        if state is not None:
            one = jnp.where(labels == state, 1.0, 0.0)
        if flag is not None:
            one = jnp.where(labels == 16, flag, one)
        columns.append(one.T)
    return jnp.concatenate(columns, axis=0)


def modulation(step, turns, times, gain, freq):
    _, batch = turn_and_batch(step, turns)
    return gain[...] * (1.0 + 0.5 * jnp.sin(times[batch, 0].astype(jnp.float32) * freq[...]))


def norm_kernel(turns, pieces, times, table, gain, freq, *refs):
    sources, refs = refs[:pieces], refs[pieces:]
    scaled, scales, owns, embeds, mod = refs[0:2], refs[2:4], refs[4:6], refs[6:8], refs[8]
    first, sems = refs[9 : 9 + pieces], refs[9 + pieces]
    copies = [
        pltpu.make_async_copy(sources[i], first[i], sems.at[i]) for i in range(pieces)
    ]
    for copy in copies:
        copy.start()
    for copy in copies:
        copy.wait()
    frames, width = scaled[0].shape
    rows, cols = frames // pieces, owns[0].shape[1]
    seq = lax.axis_index("seq")
    offsets = offsets_of(pieces)
    for step in range(turns + 1):

        def state_of(i):
            state = first[i][2 * rows : 2 * rows + 16, :rows][step : step + 1]
            return state.astype(jnp.float32).astype(jnp.int32), None

        onehot = columns_of(state_of, pieces, rows)[:, : table.shape[1]].astype(jnp.bfloat16)
        if step >= 2:
            for at in range(0, width, 256):
                embeds[step - 2][:, at : at + 256] = jnp.dot(
                    onehot, table[0, :, at : at + 256], preferred_element_type=jnp.float32
                ).astype(jnp.bfloat16)
            continue
        turn, _ = turn_and_batch(step, turns)
        at = pl.multiple_of(jnp.minimum(turn, 1) * rows, 128)
        mod[...] = modulation(step, turns, times, gain, freq)
        total = jnp.zeros((frames, 128), jnp.float32)
        for i in range(pieces):
            lanes = pl.ds(pl.multiple_of((seq ^ offsets[i]) * cols, 128), cols)
            current = jnp.concatenate([first[p][pl.ds(at, rows), lanes] for p in range(pieces)])
            hidden = current.astype(jnp.float32) + jnp.dot(
                onehot, table[0, :, lanes], preferred_element_type=jnp.float32
            )
            for lane in range(0, cols, 128):
                piece = hidden[:, lane : lane + 128]
                total = total + piece * piece
            scaled[step][:, lanes] = (hidden * mod[:, lanes]).astype(jnp.bfloat16)
            if i == 0:
                owns[step][...] = hidden
        mean = jnp.sum(total, axis=1, keepdims=True) * (1.0 / width)
        scales[step][...] = jnp.broadcast_to(lax.rsqrt(mean + epsilon), (frames, 128))


def dense(value, lead):
    frames = value.shape[0]
    rest = value[:, :64] if lead else value[:, 128:]
    full = value[:, 64:] if lead else value[:, :128]
    rest = jnp.concatenate([rest[: frames // 2], rest[frames // 2 :]], axis=1)
    return jnp.concatenate([full, rest], axis=0)


def undense(left, right, frames):
    middle = []
    for ref in (left, right):
        rest = ref[frames:]
        middle.append(jnp.concatenate([rest[:, :64], rest[:, 64:]], axis=0))
    return jnp.concatenate([left[:frames], jnp.concatenate(middle, axis=1), right[:frames]], axis=1)


def step_kernel(cfg, *refs):
    step, has_relay, parts = cfg["step"], cfg["has_relay"], cfg["parts"]
    pieces, hops, head, turns = cfg["pieces"], cfg["hops"], cfg["head"], cfg["turns"]
    heads, group = cfg["heads"], cfg["group"]
    refs = list(refs)

    def take(count):
        taken, refs[:count] = refs[:count], []
        return taken

    bias, times, gain, freq, gate, flags = take(6)
    if has_relay:
        second, embed, relay = take(pieces), take(1)[0], take(2 * pieces)
    else:
        scaled, scales, own_hidden = take(3)
    chunks = take(2) if step == 0 else None
    weights = take(len(parts))
    left = take(1)[0] if parts == (1,) else None
    sends = take(1)[0] if len(parts) == 1 else None
    out = take(1)[0]
    if step == 0:
        weights = take(1)
    proj, att = take(2)
    if has_relay:
        scaled, scales, own_hidden, mod = take(4)
    offsets = offsets_of(pieces)
    frames, width = scaled.shape
    cols = att.shape[0]
    half = cols // 2
    rows = frames // pieces
    seq, section = lax.axis_index("seq"), lax.axis_index("pipe")
    _, batch = turn_and_batch(step, turns)

    if step == 0:
        for hop, chunk in zip((2, 3), chunks):
            place(hop, hops, [chunk.at[m] for m in range(pieces)], weights[0])

    def normalize(relayed):
        total = jnp.zeros((frames, 128), jnp.float32)
        for i in range(pieces):
            lanes = pl.ds(pl.multiple_of((seq ^ offsets[i]) * cols, 128), cols)
            if relayed:
                value = undense(relay[i], relay[pieces + i], frames)
                order = [offsets.index(offsets[i] ^ offsets[p]) for p in range(pieces)]
                blocks = [value[j * rows : (j + 1) * rows] for j in order]
            else:
                blocks = [second[p][:rows, lanes] for p in range(pieces)]
            hidden = jnp.concatenate(blocks, axis=0).astype(jnp.float32)
            hidden = hidden + embed[:, lanes].astype(jnp.float32)
            for lane in range(0, cols, 128):
                piece = hidden[:, lane : lane + 128]
                total = total + piece * piece
            scaled[:, lanes] = (hidden * mod[:, lanes]).astype(jnp.bfloat16)
            if i == 0:
                own_hidden[...] = hidden
        scales[...] = total

    if has_relay:
        mod[...] = modulation(step, turns, times, gain, freq)

        @pl.when(section == 0)
        def _():
            normalize(False)

        @pl.when(section != 0)
        def _():
            normalize(True)

        mean = jnp.sum(scales[...], axis=1, keepdims=True) * (1.0 / width)
        scale = lax.rsqrt(mean + epsilon)
    else:
        scale = scales[:, :1]

    def flag_of(i):
        lanes = pl.ds(pl.multiple_of((seq ^ offsets[i]) * rows, 128), rows)
        return None, flags[batch, :, lanes].astype(jnp.float32)

    flag_column = columns_of(flag_of, pieces, rows)[:, 16:17]
    score_scale = head ** (-0.5) * math.log2(math.e)
    lanes = lax.broadcasted_iota(jnp.int32, (frames, 128), 1)
    row_lanes = lax.broadcasted_iota(jnp.int32, (1, 128), 1)
    flag_lanes = jnp.logical_or(lanes == head, lanes == head + 1)
    pitch = cols + 128

    for k, part in enumerate(parts):
        base = k * pitch
        for at in range(0, cols, 256):
            size = min(256, cols - at)
            lane = at + lax.broadcasted_iota(jnp.int32, (1, size), 1)
            factor = jnp.where(lane < half, score_scale, 1.0)
            projected = jnp.dot(
                scaled[...], weights[k][:, at : at + size], preferred_element_type=jnp.float32
            )
            proj[:, base + at : base + at + size] = (projected * scale * factor).astype(
                jnp.bfloat16
            )
        proj[:, base + cols : base + pitch] = jnp.zeros((frames, 128), jnp.bfloat16)

    def slice_of(at):
        return proj[:, at : at + 128].astype(jnp.float32)

    keys, values = [], []
    for k in range(len(parts)):
        at = k * pitch + half
        key = jnp.where(flag_lanes, flag_column, jnp.where(lanes < head, slice_of(at), 0.0))
        value = jnp.where(
            lanes < head, slice_of(at + head), jnp.where(lanes == head, 1.0, 0.0)
        )
        keys.append(key.astype(jnp.bfloat16))
        values.append(value.T.astype(jnp.bfloat16))

    def scores_of(k, h):
        strength = bias[0, seq * heads + parts[k] * group + h] * math.log2(math.e)
        strength = jnp.zeros((1, 128), jnp.float32) + strength
        coarse = strength.astype(jnp.bfloat16).astype(jnp.float32)
        tail = jnp.where(
            row_lanes == head, coarse, jnp.where(row_lanes == head + 1, strength - coarse, 0.0)
        )
        query = jnp.where(lanes < head, slice_of(k * pitch + h * head), tail).astype(jnp.bfloat16)
        return lax.dot_general(
            keys[k], query, (((1,), (1,)), ((), ())), preferred_element_type=jnp.float32
        )

    tasks = [(k, h) for k in range(len(parts)) for h in range(group)]
    scores = scores_of(*tasks[0])
    for index, (k, h) in enumerate(tasks):
        ahead = scores_of(*tasks[index + 1]) if index + 1 < len(tasks) else None
        top = jnp.max(scores, axis=0, keepdims=True)
        weight = jnp.exp2(scores - top).astype(jnp.bfloat16)
        mixed = jnp.dot(values[k], weight, preferred_element_type=jnp.float32)
        at = (parts[k] * group + h) * head
        att[at : at + head, :] = mixed[:head] * (1.0 / mixed[head : head + 1])
        scores = ahead
    gates = gate[:, pl.ds(pl.multiple_of(seq * cols, 128), cols)]
    first, last = parts[0] * half, (parts[-1] + 1) * half
    attended = att[first:last].T.astype(jnp.bfloat16).astype(jnp.float32)
    output = own_hidden[...][:, first:last] + gates[:, first:last] * attended
    if parts == (0,):
        out[:, :half] = output.astype(jnp.bfloat16)
    elif parts == (1,):
        output_both = jnp.concatenate([left[:, :half].astype(jnp.float32), output], axis=1)
        out[...] = output_both.astype(jnp.bfloat16).reshape(pieces, rows, cols)
    else:
        out[...] = output.astype(jnp.bfloat16).reshape(pieces, rows, cols)
    if sends is not None:
        sends[...] = dense(output, parts == (1,)).astype(jnp.bfloat16)


def tie_kernel(*refs):
    pass


def grad_of(output, second, turn, rows, feats):
    cot = jnp.concatenate(
        [piece[rows : 2 * rows, turn * feats : (turn + 1) * feats] for piece in second], axis=0
    )
    return lax.dot_general(
        output, cot, (((0,), (0,)), ((), ())), preferred_element_type=jnp.float32
    )


def early_kernel(turns, pieces, halves, feats, *refs):
    outs, second = refs[: turns * halves], refs[turns * halves : turns * halves + pieces]
    sends, grad = refs[turns * halves + pieces : -1], refs[-1]
    section = lax.axis_index("pipe")
    offsets = offsets_of(pieces)
    part = pieces // halves
    rows = outs[0].shape[1]
    total = None
    for turn in range(turns - 1):
        blocks = []
        for p in range(pieces):
            k, j = p // part, p % part
            block = jnp.where(
                section == 0, outs[turn * halves + k][j], outs[(turn + 1) * halves + k][j]
            )
            sends[offsets[p]][turn] = block
            blocks.append(block)
        share = grad_of(jnp.concatenate(blocks, axis=0), second, turn, rows, feats)
        total = share if total is None else total + share
    grad[...] = total


def settle_kernel(turns, pieces, halves, hops, feats, *refs):
    refs = list(refs)

    def take(count):
        taken, refs[:count] = refs[:count], []
        return taken

    before, now, second, early = take(halves), take(halves), take(pieces), take(pieces - 1)
    early_grad = take(1)[0]
    late, own_grad, grads = take(pieces), take(1)[0], take(hops - 1)
    section_out = take(1)[0]
    rows_out, total, sem = take(3)
    section, seq, rep = lax.axis_index("pipe"), lax.axis_index("seq"), lax.axis_index("dp")
    offsets = offsets_of(pieces)
    part = pieces // halves
    rows, cols = early[0].shape[1:]
    for m in range(pieces - 1):
        lanes = pl.ds(pl.multiple_of((seq ^ m) * cols, 128), cols)
        for turn in range(turns - 1):
            rows_out[turn, :, lanes] = early[m][turn]
    copy = pltpu.make_async_copy(rows_out, section_out.at[pl.ds(0, turns - 1)], sem)
    copy.start()
    blocks = []
    for p in range(pieces):
        block = jnp.where(section == 0, before[p // part][p % part], now[p // part][p % part])
        late[offsets[p]][...] = block
        blocks.append(block)
    share = grad_of(jnp.concatenate(blocks, axis=0), second, turns - 1, rows, feats)
    factor = float(turns * hops * rows * pieces) ** (-0.5)
    total[...] = (share + early_grad[...]) * factor
    g_rows = cols // hops
    own_grad[...] = total[pl.ds(pl.multiple_of(rep * g_rows, 8), g_rows)]
    for shift in range(1, hops):
        at = pl.multiple_of(lax.rem(rep + shift, hops) * g_rows, 8)
        grads[shift - 1][...] = total[pl.ds(at, g_rows)].astype(jnp.bfloat16)
    copy.wait()


def finish_kernel(pieces, hops, *refs):
    held, early, late, refs = refs[0], refs[1], refs[2 : pieces + 2], refs[pieces + 2 :]
    own_grad, parts, (section_out, grad, row_out, sems) = refs[0], refs[1:hops], refs[hops:]
    seq = lax.axis_index("seq")
    cols = late[0].shape[1]
    last_lanes = pl.ds(pl.multiple_of((seq ^ (pieces - 1)) * cols, 128), cols)
    early_copy = pltpu.make_async_copy(
        early, section_out.at[pl.ds(0, early.shape[0]), :, last_lanes], sems.at[0]
    )
    early_copy.start()
    for m in range(pieces):
        lanes = pl.ds(pl.multiple_of((seq ^ m) * cols, 128), cols)
        row_out[:, lanes] = late[m][...]
    copy = pltpu.make_async_copy(row_out, section_out.at[section_out.shape[0] - 1], sems.at[1])
    copy.start()
    total = own_grad[...]
    for part in parts:
        total = total + part[...].astype(jnp.float32)
    grad[...] = total
    early_copy.wait()
    copy.wait()


MIB = 1024 * 1024


def paired_body(
    incoming,
    contacts,
    keyframes,
    timesteps,
    w_query,
    w_keyval,
    norm_gain,
    time_freq,
    contact_table,
    key_bias,
    attn_gate,
    head_cotangent,
):
    seq_count = lax.axis_size("seq")
    hops = lax.axis_size("dp")
    rows, width, turns = incoming.shape[3], incoming.shape[4], incoming.shape[1]
    frames = rows * seq_count
    heads_all = key_bias.shape[1]
    head = width // heads_all
    heads = heads_all // seq_count
    kv_heads = w_keyval.shape[2] // (2 * head * seq_count)
    feats = head_cotangent.shape[4]
    cols = width // seq_count
    w_rows = w_query.shape[1]
    kind = jnp.bfloat16
    smem = pl.BlockSpec(memory_space=pltpu.SMEM)
    vmem = pl.BlockSpec(memory_space=pltpu.VMEM)
    anywhere = pl.BlockSpec(memory_space=pl.ANY)
    shape = jax.ShapeDtypeStruct

    def call(kernel, name, out_shape, in_specs, operands, scratch=(), limit=4, flops=0, **options):
        return pl.pallas_call(
            kernel,
            out_shape=out_shape,
            in_specs=in_specs,
            scratch_shapes=list(scratch),
            compiler_params=pltpu.CompilerParams(vmem_limit_bytes=limit * MIB),
            cost_estimate=pl.CostEstimate(
                flops=flops, bytes_accessed=flops // 512, transcendentals=0
            ),
            name=name,
            **options,
        )(*operands)

    def pin(value, space=pltpu.VMEM):
        return pltpu.with_memory_space_constraint(value, space)

    packed = call(
        pack_kernel,
        "pack",
        [pltpu.VMEM((2, w_rows, cols), kind)] * seq_count,
        [anywhere, anywhere],
        [pin(w_query, pltpu.HBM), pin(w_keyval, pltpu.HBM)],
        [pltpu.VMEM((seq_count, w_rows, cols), kind)] * 2
        + [pltpu.SemaphoreType.DMA((2 * seq_count,))],
        out_specs=[vmem] * seq_count,
    )
    blocks = [packed[0]] + [swap(packed[m], m) for m in range(1, seq_count)]

    def paired(name, deps, values):
        return call(
            functools.partial(pair_kernel, len(deps)),
            name,
            pltpu.VMEM((2, 2, w_rows, cols), kind),
            [anywhere] * len(deps) + [vmem] * 2,
            deps + values,
            out_specs=vmem,
        )

    near = paired("near", [], blocks[:2])
    near_next = ring_step(near)
    far = paired("far", [near_next], blocks[2:])
    far_next = ring_step(far)
    rings, partial = [], []
    for part in range(2):
        chunk = call(
            functools.partial(part_kernel, part),
            "part%d" % part,
            pltpu.VMEM((seq_count, w_rows, cols), kind),
            [vmem, vmem],
            [near_next, far_next],
            out_specs=vmem,
        )
        rings.append([chunk])
        partial.append(
            call(
                functools.partial(place_kernel, part, hops),
                "place%d" % part,
                pltpu.VMEM((width, cols), kind),
                [vmem] * 3,
                [pin(near), pin(far), pin(chunk)],
                out_specs=vmem,
            )
        )
    for hop in range(2):
        for ring in rings:
            ring.append(ring_step(ring[-1]))

    def tie(values, deps):
        return call(
            tie_kernel,
            "tie",
            [shape(value.shape, kind) for value in values],
            [anywhere] * (len(values) + len(deps)),
            list(values) + list(deps),
            out_specs=[anywhere] * len(values),
            input_output_aliases={i: i for i in range(len(values))},
        )

    mine = call(
        functools.partial(first_kernel, turns),
        "first",
        pltpu.VMEM((2 * rows + 16, width), kind),
        [anywhere, vmem, vmem],
        [far, incoming, contacts],
        [pltpu.VMEM((16, 128), jnp.float32)],
        out_specs=vmem,
    )
    across = swap(mine, 2)
    beside = swap(mine, 1)
    (across,) = tie([across], [ring[1] for ring in rings])
    first = [mine, across, beside, swap(across, 1)]
    prepared = call(
        functools.partial(norm_kernel, turns, seq_count),
        "norm",
        [pltpu.VMEM((frames, width), kind)] * 2
        + [pltpu.VMEM((frames, 128), jnp.float32)] * 2
        + [pltpu.VMEM((frames, cols), jnp.float32)] * 2
        + [pltpu.VMEM((frames, width), kind)] * 2,
        [smem] + [vmem] * 3 + [anywhere] * seq_count,
        [timesteps, contact_table, norm_gain, time_freq]
        + first,
        [pltpu.VMEM((1, width), jnp.float32)]
        + [pltpu.VMEM((2 * rows + 16, width), kind)] * seq_count
        + [pltpu.SemaphoreType.DMA((seq_count,))],
        12,
        out_specs=[vmem] * 8,
    )

    mine = call(
        second_kernel,
        "second",
        pltpu.VMEM((2 * rows, width), kind),
        [anywhere, vmem, vmem],
        [across, incoming, head_cotangent],
        out_specs=vmem,
    )
    second = [mine, swap(mine, 2), swap(mine, 1)]

    common = [key_bias, timesteps, norm_gain, time_freq, attn_gate, keyframes]

    def run_step(step, parts, large, out_shape, aliases):
        cfg = {
            "step": step,
            "has_relay": step >= 2,
            "parts": parts,
            "pieces": seq_count,
            "hops": hops,
            "head": head,
            "heads": heads,
            "group": heads // kv_heads,
            "turns": turns,
        }
        scratch = [
            pltpu.VMEM((frames, len(parts) * (cols + 128)), kind),
            pltpu.VMEM((cols, frames), jnp.float32),
        ]
        if step >= 2:
            scratch += [
                pltpu.VMEM((frames, width), kind),
                pltpu.VMEM((frames, 128), jnp.float32),
                pltpu.VMEM((frames, cols), jnp.float32),
                pltpu.VMEM((1, width), jnp.float32),
            ]
        operands = common + [pin(value) for value in large]
        return call(
            functools.partial(step_kernel, cfg),
            "step%d%s" % (step, "".join("ab"[part] for part in parts)),
            out_shape,
            [smem, smem] + [vmem] * (len(operands) - 2),
            operands,
            scratch,
            16,
            len(parts) * frames * (2 * width * cols + 2 * heads * frames * head),
            out_specs=[vmem] * len(out_shape),
            input_output_aliases=aliases,
        )

    whole = pltpu.VMEM((seq_count, rows, cols), kind)
    sent = pltpu.VMEM((frames * 3 // 2, 128), kind)
    weights = list(partial)
    relays, lefts, outputs = ([], []), [], []
    for part in range(2):
        for step in range(2):
            large = [prepared[step], prepared[2 + step], prepared[4 + step]]
            if step == 0:
                chunks = rings[part][1:]
                if part:
                    (last_chunk,) = tie(chunks[1:], [relays[0][0][0], lefts[1]])
                    chunks = [chunks[0], last_chunk]
                large += chunks
            large += [weights[part]]
            aliases = {len(common) + len(large) - 1: 2} if step == 0 else {}
            out_shape = [sent, whole if part else pltpu.VMEM((frames, 256), kind)]
            if step == 0:
                out_shape += [pltpu.VMEM((width, cols), kind)]
            if part:
                left = lefts[step]
                if step == 1:
                    (left,) = tie([left], [relays[1][0][0], relays[0][0][1]])
                large += [left]
            results = run_step(step, (part,), large, out_shape, aliases)
            if step == 0:
                weights[part] = results[2]
            (outputs if part else lefts).append(results[1])
            piece = handed_over(results[0])
            relays[step].append((piece, swap(piece, 2)))
    (second[1],) = tie([second[1]], [outputs[0]])
    second.append(swap(second[1], 1))

    def complete(crossing):
        return [
            piece
            for mine, across in crossing
            for piece in (mine, across, swap(mine, 1), swap(across, 1))
        ]

    relay = complete(relays[0])
    (output,) = run_step(2, (0, 1), second + [prepared[6]] + relay + weights, [whole], {})
    outputs.append(output)
    early = call(
        functools.partial(early_kernel, turns, seq_count, 1, feats),
        "early",
        [shape((turns - 1, rows, cols), kind)] * seq_count + [shape((cols, feats), jnp.float32)],
        [vmem] * (turns + seq_count),
        outputs + second,
        limit=8,
        out_specs=[vmem] * (seq_count + 1),
    )
    early, early_grad = list(early[:-1]), early[-1]
    early = [early[0]] + [swap(early[m], m) for m in range(1, seq_count)]
    tied = tie([piece for pair in relays[1] for piece in pair], [early_grad])
    relay = complete([(tied[0], tied[1]), (tied[2], tied[3])])
    (output,) = run_step(3, (0, 1), second + [prepared[7]] + relay + weights, [whole], {})
    outputs.append(output)

    g_shape = (cols // hops, feats)
    operands = outputs[-2:] + second + early[:-1] + [early_grad]
    settled = call(
        functools.partial(settle_kernel, turns, seq_count, 1, hops, feats),
        "settle",
        [shape((rows, cols), kind)] * seq_count
        + [shape(g_shape, jnp.float32)]
        + [shape(g_shape, kind)] * (hops - 1)
        + [shape((turns, rows, width), kind)],
        [vmem] * len(operands),
        operands,
        [
            pltpu.VMEM((turns - 1, rows, width), kind),
            pltpu.VMEM((cols, feats), jnp.float32),
            pltpu.SemaphoreType.DMA,
        ],
        8,
        out_specs=[vmem] * (seq_count + hops) + [anywhere],
    )
    late, grads, held = settled[:seq_count], settled[seq_count:-1], settled[-1]
    late = [late[0]] + [swap(late[m], m) for m in range(1, seq_count)]
    grads = [grads[0]] + [shifted(grads[k], "dp", k) for k in range(1, hops)]
    section_out, grad_rows = call(
        functools.partial(finish_kernel, seq_count, hops),
        "finish",
        [shape((turns, rows, width), kind), shape(g_shape, jnp.float32)],
        [anywhere] + [vmem] * (seq_count + hops + 1),
        [held, early[-1]] + late + grads,
        [pltpu.VMEM((rows, width), kind), pltpu.SemaphoreType.DMA((2,))],
        out_specs=[anywhere, vmem],
        input_output_aliases={0: 0},
    )
    return (section_out[None, :, None], grad_rows[None])


def body(incoming, contacts, keyframes, timesteps, w_query, *others):
    count = lax.axis_size("seq")
    cols = w_query.shape[2] // count
    paired = (
        lax.axis_size("pipe") == 2
        and lax.axis_size("dp") == 4
        and count == 4
        and cols % 128 == 0
        and w_query.shape[1] % 16 == 0
        and incoming.shape[3] == 128
        and incoming.shape[1] == 3
    )
    chosen = paired_body if paired else general_body
    return chosen(incoming, contacts, keyframes, timesteps, w_query, *others)


def general_body(
    incoming,
    contacts,
    keyframes,
    timesteps,
    w_query,
    w_keyval,
    norm_gain,
    time_freq,
    contact_table,
    key_bias,
    attn_gate,
    head_cotangent,
):
    section_idx = lax.axis_index("pipe")
    seq_idx = lax.axis_index("seq")
    rep_idx = lax.axis_index("dp")
    seq_count = lax.axis_size("seq")
    section_count = lax.axis_size("pipe")
    rep_count = lax.axis_size("dp")
    tok_rows = incoming.shape[3]
    width = incoming.shape[4]
    turns = incoming.shape[1]
    frames = tok_rows * seq_count
    heads_all = key_bias.shape[1]
    head_size = width // heads_all
    heads_local = heads_all // seq_count
    kv_width = w_keyval.shape[2]
    kv_local = kv_width // (2 * head_size * seq_count)
    group_size = heads_local // kv_local
    feat_count = head_cotangent.shape[4]
    score_scale = head_size ** (-0.5)
    q_cols = width // seq_count
    kv_cols = kv_width // seq_count
    w_rows = w_query.shape[1]

    w_parts = jnp.concatenate(
        [
            w_query[0].reshape(w_rows, seq_count, q_cols),
            w_keyval[0].reshape(w_rows, seq_count, kv_cols),
        ],
        axis=2,
    ).transpose(1, 0, 2)
    block = lax.all_to_all(w_parts, "seq", split_axis=0, concat_axis=0, tiled=True)
    weights = jnp.zeros((seq_count, rep_count, w_rows, q_cols + kv_cols), jnp.bfloat16)
    for hop in range(rep_count):
        owner = lax.rem(rep_idx + rep_count - hop, rep_count)
        weights = lax.dynamic_update_slice_in_dim(weights, block[:, None], owner, 1)
        if hop + 1 < rep_count:
            block = ring(block, "dp")
    weights = weights.reshape(width, q_cols + kv_cols)

    gain_row = norm_gain[0]
    freq_row = time_freq[0]
    table = contact_table[0]
    gate_local = lax.dynamic_slice_in_dim(attn_gate[0], seq_idx * q_cols, q_cols)
    table_local = lax.dynamic_slice_in_dim(table, seq_idx * q_cols, q_cols, 1)
    bias_local = lax.dynamic_slice_in_dim(key_bias[0], seq_idx * heads_local, heads_local)
    contact_all = lax.all_gather(contacts[:, 0, :], "seq", axis=1, tiled=True)
    key_all = keyframes[:, 0, :]
    step_all = timesteps[:, 0]
    labels = jnp.arange(table.shape[0], dtype=jnp.int32)
    cot_all = lax.all_gather(head_cotangent[0, :, 0], "seq", axis=1, tiled=True)

    lag = 2 if section_count == 2 else 1
    if lag == 2:
        steps = turns + 1
    else:
        steps = turns

    def turn_at(step):
        if lag == 1:
            return jnp.int32(step)
        return jnp.clip(step - section_idx, 0, turns - 1)

    outputs = []
    handed = {}
    for step in range(steps):
        turn = turn_at(step)
        fresh = lax.dynamic_index_in_dim(incoming[0, :, 0], turn, 0, keepdims=False)
        current = lax.all_gather(fresh, "seq", axis=0, tiled=True)
        if step in handed:
            current = jnp.where((section_idx == 0) | (turn == 0), current, handed[step])
        batch_idx = turn - section_idx + section_count - 1
        contact_rows = lax.dynamic_index_in_dim(contact_all, batch_idx, 0, keepdims=False)
        key_flags = lax.dynamic_index_in_dim(key_all, batch_idx, 0, keepdims=False).astype(
            jnp.float32
        )
        timestep = lax.dynamic_index_in_dim(step_all, batch_idx, 0, keepdims=False).astype(
            jnp.float32
        )
        onehot = (contact_rows[:, None] == labels[None, :]).astype(jnp.bfloat16)
        hidden = current.astype(jnp.float32) + jnp.dot(
            onehot, table, preferred_element_type=jnp.float32
        )
        root_mean = jnp.sqrt(jnp.mean(hidden * hidden, axis=-1, keepdims=True) + epsilon)
        modulation = gain_row * (1.0 + 0.5 * jnp.sin(timestep * freq_row))
        normed = (hidden / root_mean * modulation[None, :]).astype(jnp.bfloat16)
        projected = jnp.dot(normed, weights, preferred_element_type=jnp.float32).astype(
            jnp.bfloat16
        )
        query_heads = projected[:, :q_cols].reshape(frames, heads_local, head_size)
        keyval_heads = projected[:, q_cols:].reshape(frames, kv_local, 2, head_size)
        head_outputs = []
        for head in range(heads_local):
            key_rows = keyval_heads[:, head // group_size, 0]
            value_rows = keyval_heads[:, head // group_size, 1]
            scores = (
                lax.dot_general(
                    query_heads[:, head],
                    key_rows,
                    (((1,), (1,)), ((), ())),
                    preferred_element_type=jnp.float32,
                )
                * score_scale
            )
            scores = scores + bias_local[head] * key_flags[None, :]
            row_max = jnp.max(scores, axis=-1, keepdims=True)
            exponent = jnp.exp(scores - row_max)
            probabilities = (exponent / jnp.sum(exponent, axis=-1, keepdims=True)).astype(
                jnp.bfloat16
            )
            head_outputs.append(
                jnp.dot(probabilities, value_rows, preferred_element_type=jnp.float32).astype(
                    jnp.bfloat16
                )
            )
        attended = jnp.concatenate(head_outputs, axis=1)
        hidden_local = lax.dynamic_slice_in_dim(current, seq_idx * q_cols, q_cols, 1).astype(
            jnp.float32
        ) + jnp.dot(onehot, table_local, preferred_element_type=jnp.float32)
        output = (hidden_local + gate_local[None, :] * attended.astype(jnp.float32)).astype(
            jnp.bfloat16
        )
        outputs.append(output)
        if step + lag < steps:
            piece = passed_along(output, "pipe", 1)
            handed[step + lag] = lax.all_gather(piece, "seq", axis=1, tiled=True)

    factor = float(turns * rep_count * frames) ** (-0.5)
    total = None
    rows_out = []
    for turn in range(turns):
        if lag == 2:
            own = jnp.where(section_idx == 0, outputs[turn], outputs[turn + 1])
        else:
            own = outputs[turn]
        term = lax.dot_general(
            own, cot_all[turn], (((0,), (0,)), ((), ())), preferred_element_type=jnp.float32
        )
        total = term if total is None else total + term
        rows_out.append(lax.all_to_all(own, "seq", split_axis=0, concat_axis=1, tiled=True))
    section_out = jnp.stack(rows_out)[None, :, None]
    grad_parts = lax.all_to_all(
        (total * factor).astype(jnp.bfloat16).reshape(rep_count, q_cols // rep_count, feat_count),
        "dp",
        split_axis=0,
        concat_axis=0,
        tiled=True,
    )
    grad_rows = jnp.sum(grad_parts.astype(jnp.float32), axis=0)
    return (section_out, grad_rows[None])


def solution(mesh):
    in_specs = (
        P("pipe", None, "dp", "seq", None),
        P(None, "dp", "seq"),
        P(None, "dp", None),
        P(None, "dp"),
        P("pipe", ("seq", "dp"), None),
        P("pipe", ("seq", "dp"), None),
        P("pipe", None),
        P("pipe", None),
        P("pipe", None, None),
        P("pipe", None),
        P("pipe", None),
        P("pipe", None, "dp", "seq", None),
    )
    out_specs = (P("pipe", None, "dp", "seq", None), P("pipe", ("seq", "dp"), None))
    return jax.shard_map(body, mesh=mesh, in_specs=in_specs, out_specs=out_specs, check_vma=False)
```

```python
import functools
import math

import jax
import jax.numpy as jnp
from jax import lax
from jax.experimental import pallas as pl
from jax.experimental.pallas import tpu as pltpu
from jax.sharding import PartitionSpec as P

epsilon = 1e-06


def passed_along(value, axis, steps):
    count = lax.axis_size(axis)
    first, last = (max(0, -steps), min(count, count - steps))
    return lax.ppermute(value, axis, [(source, source + steps) for source in range(first, last)])


def ring(value, axis):
    count = lax.axis_size(axis)
    return lax.ppermute(value, axis, [(source, (source + 1) % count) for source in range(count)])


def swap(value, bit):
    count = lax.axis_size("seq")
    return lax.ppermute(value, "seq", [(source, source ^ bit) for source in range(count)])


def handed_over(value):
    return lax.ppermute(value, "pipe", [(0, 1), (1, 0)])


def shifted(value, axis, shift):
    count = lax.axis_size(axis)
    return lax.ppermute(value, axis, [(source, (source + shift) % count) for source in range(count)])


def fold(index):
    return index ^ (index >> 1)


def ring_step(value):
    count = lax.axis_size("dp")
    pairs = [(fold(place), fold((place + 1) % count)) for place in range(count)]
    return lax.ppermute(value, "dp", pairs)


def offsets_of(count):
    offsets = [0]
    bit = count // 2
    while bit:
        offsets = offsets + [offset ^ bit for offset in offsets]
        bit //= 2
    return offsets


def turn_and_batch(step, turns):
    section = lax.axis_index("pipe")
    turn = jnp.clip(step - section, 0, turns - 1)
    return turn, turn - section + 1


def pack_kernel(wq, wkv, *refs):
    outs, (queries, keyvals, sems) = refs[:-3], refs[-3:]
    parts, _, cols = outs[0].shape
    half = cols // 2
    seq = lax.axis_index("seq")
    copies = []
    for m in range(len(outs)):
        start = pl.multiple_of((seq ^ m) * cols, 128)
        for k, (source, held) in enumerate(((wq, queries), (wkv, keyvals))):
            copies.append(
                pltpu.make_async_copy(
                    source.at[0, :, pl.ds(start, cols)], held.at[m], sems.at[2 * m + k]
                )
            )
    for copy in copies:
        copy.start()
    for m, out in enumerate(outs):
        copies[2 * m].wait()
        copies[2 * m + 1].wait()
        for part in range(parts):
            lanes = slice(part * half, (part + 1) * half)
            out[part] = jnp.concatenate([queries[m][:, lanes], keyvals[m][:, lanes]], axis=1)


def pair_kernel(deps, *refs):
    out = refs[-1]
    for at, ref in enumerate(refs[deps:-1]):
        out[at] = ref[...]


def part_kernel(part, near, far, out):
    for at in range(2):
        out[at] = near[at, part]
        out[at + 2] = far[at, part]


def place(hop, hops, blocks, weights):
    seq, rep = lax.axis_index("seq"), lax.axis_index("dp")
    for m, block in enumerate(blocks):
        rows = block.shape[0]
        at = (seq ^ m) * hops + fold(lax.rem(fold(rep) + hops - hop, hops))
        weights[pl.ds(pl.multiple_of(at * rows, 16), rows)] = block[...]


def place_kernel(part, hops, near, far, chunk, weights):
    place(0, hops, [near.at[0, part], near.at[1, part], far.at[0, part], far.at[1, part]], weights)
    place(1, hops, [chunk.at[m] for m in range(4)], weights)


def first_kernel(turns, far, incoming, contacts, out, states):
    rows = incoming.shape[3]
    for turn in range(2):
        out[turn * rows : (turn + 1) * rows] = incoming[0, turn, 0]
    states[...] = jnp.zeros_like(states)
    for step in range(turns + 1):
        _, batch = turn_and_batch(step, turns)
        states[step : step + 1] = contacts[batch].astype(jnp.float32)
    out[2 * rows :, : states.shape[1]] = states[...].astype(jnp.bfloat16)


def second_kernel(dep, incoming, cotangent, out):
    turns, rows, feats = cotangent.shape[1], cotangent.shape[3], cotangent.shape[4]
    out[:rows] = incoming[0, 2, 0]
    for turn in range(turns):
        out[rows:, turn * feats : (turn + 1) * feats] = cotangent[0, turn, 0]


def columns_of(rows_of, pieces, rows):
    labels = lax.broadcasted_iota(jnp.int32, (32, rows), 0)
    columns = []
    for i in range(pieces):
        state, flag = rows_of(i)
        one = jnp.zeros((32, rows), jnp.float32)
        if state is not None:
            one = jnp.where(labels == state, 1.0, 0.0)
        if flag is not None:
            one = jnp.where(labels == 16, flag, one)
        columns.append(one.T)
    return jnp.concatenate(columns, axis=0)


def modulation(step, turns, times, gain, freq):
    _, batch = turn_and_batch(step, turns)
    return gain[...] * (1.0 + 0.5 * jnp.sin(times[0, batch].astype(jnp.float32) * freq[...]))


def norm_kernel(turns, pieces, times, table, gain, freq, *refs):
    sources, refs = refs[:pieces], refs[pieces:]
    scaled, scales, owns, embeds, mod = refs[0:2], refs[2:4], refs[4:6], refs[6:8], refs[8]
    first, sems = refs[9 : 9 + pieces], refs[9 + pieces]
    copies = [
        pltpu.make_async_copy(sources[i], first[i], sems.at[i]) for i in range(pieces)
    ]
    for copy in copies:
        copy.start()
    for copy in copies:
        copy.wait()
    frames, width = scaled[0].shape
    rows, cols = frames // pieces, owns[0].shape[1]
    seq = lax.axis_index("seq")
    offsets = offsets_of(pieces)
    for step in range(turns + 1):

        def state_of(i):
            state = first[i][2 * rows : 2 * rows + 16, :rows][step : step + 1]
            return state.astype(jnp.float32).astype(jnp.int32), None

        onehot = columns_of(state_of, pieces, rows)[:, : table.shape[1]].astype(jnp.bfloat16)
        if step >= 2:
            for at in range(0, width, 256):
                embeds[step - 2][:, at : at + 256] = jnp.dot(
                    onehot, table[0, :, at : at + 256], preferred_element_type=jnp.float32
                ).astype(jnp.bfloat16)
            continue
        turn, _ = turn_and_batch(step, turns)
        at = pl.multiple_of(jnp.minimum(turn, 1) * rows, 128)
        mod[...] = modulation(step, turns, times, gain, freq)
        total = jnp.zeros((frames, 128), jnp.float32)
        for i in range(pieces):
            lanes = pl.ds(pl.multiple_of((seq ^ offsets[i]) * cols, 128), cols)
            current = jnp.concatenate([first[p][pl.ds(at, rows), lanes] for p in range(pieces)])
            hidden = current.astype(jnp.float32) + jnp.dot(
                onehot, table[0, :, lanes], preferred_element_type=jnp.float32
            )
            for lane in range(0, cols, 128):
                piece = hidden[:, lane : lane + 128]
                total = total + piece * piece
            scaled[step][:, lanes] = (hidden * mod[:, lanes]).astype(jnp.bfloat16)
            if i == 0:
                owns[step][...] = hidden
        mean = jnp.sum(total, axis=1, keepdims=True) * (1.0 / width)
        scales[step][...] = jnp.broadcast_to(lax.rsqrt(mean + epsilon), (frames, 128))


def dense(value, lead):
    frames = value.shape[0]
    rest = value[:, :64] if lead else value[:, 128:]
    full = value[:, 64:] if lead else value[:, :128]
    rest = jnp.concatenate([rest[: frames // 2], rest[frames // 2 :]], axis=1)
    return jnp.concatenate([full, rest], axis=0)


def undense(left, right, frames):
    middle = []
    for ref in (left, right):
        rest = ref[frames:]
        middle.append(jnp.concatenate([rest[:, :64], rest[:, 64:]], axis=0))
    return jnp.concatenate([left[:frames], jnp.concatenate(middle, axis=1), right[:frames]], axis=1)


def second_pair_kernel(dep, mine, across, out):
    out[0] = mine[...]
    out[1] = across[...]


def opened(pieces):
    return list(pieces[:2]) + [pieces[2].at[0], pieces[2].at[1]]


def step_kernel(cfg, *refs):
    step, has_relay, parts = cfg["step"], cfg["has_relay"], cfg["parts"]
    pieces, hops, head, turns = cfg["pieces"], cfg["hops"], cfg["head"], cfg["turns"]
    heads, group = cfg["heads"], cfg["group"]
    refs = list(refs)

    def take(count):
        taken, refs[:count] = refs[:count], []
        return taken

    bias, times, gain, freq, gate, flags = take(6)
    if has_relay:
        second, embed, relay = opened(take(3)), take(1)[0], take(2 * pieces)
    else:
        scaled, scales, own_hidden = take(3)
    chunks = take(2) if step == 0 else None
    weights = take(len(parts))
    left = take(1)[0] if parts == (1,) else None
    sends = take(1)[0] if len(parts) == 1 else None
    out = take(1)[0]
    if step == 0:
        weights = take(1)
    proj, att = take(2)
    if has_relay:
        scaled, scales, own_hidden, mod = take(4)
    offsets = offsets_of(pieces)
    frames, width = scaled.shape
    cols = att.shape[0]
    half = cols // 2
    rows = frames // pieces
    seq, section = lax.axis_index("seq"), lax.axis_index("pipe")
    _, batch = turn_and_batch(step, turns)

    if step == 0:
        for hop, chunk in zip((2, 3), chunks):
            place(hop, hops, [chunk.at[m] for m in range(pieces)], weights[0])

    def normalize(relayed):
        total = jnp.zeros((frames, 128), jnp.float32)
        for i in range(pieces):
            lanes = pl.ds(pl.multiple_of((seq ^ offsets[i]) * cols, 128), cols)
            if relayed:
                value = undense(relay[i], relay[pieces + i], frames)
                order = [offsets.index(offsets[i] ^ offsets[p]) for p in range(pieces)]
                blocks = [value[j * rows : (j + 1) * rows] for j in order]
            else:
                blocks = [second[p][:rows, lanes] for p in range(pieces)]
            hidden = jnp.concatenate(blocks, axis=0).astype(jnp.float32)
            hidden = hidden + embed[:, lanes].astype(jnp.float32)
            for lane in range(0, cols, 128):
                piece = hidden[:, lane : lane + 128]
                total = total + piece * piece
            scaled[:, lanes] = (hidden * mod[:, lanes]).astype(jnp.bfloat16)
            if i == 0:
                own_hidden[...] = hidden
        scales[...] = total

    if has_relay:
        mod[...] = modulation(step, turns, times, gain, freq)

        @pl.when(section == 0)
        def _():
            normalize(False)

        @pl.when(section != 0)
        def _():
            normalize(True)

        mean = jnp.sum(scales[...], axis=1, keepdims=True) * (1.0 / width)
        scale = lax.rsqrt(mean + epsilon)
    else:
        scale = scales[:, :1]

    def flag_of(i):
        lanes = pl.ds(pl.multiple_of((seq ^ offsets[i]) * rows, 128), rows)
        return None, flags[batch, :, lanes].astype(jnp.float32)

    flag_column = columns_of(flag_of, pieces, rows)[:, 16:17]
    score_scale = head ** (-0.5) * math.log2(math.e)
    lanes = lax.broadcasted_iota(jnp.int32, (frames, 128), 1)
    row_lanes = lax.broadcasted_iota(jnp.int32, (1, 128), 1)
    flag_lanes = jnp.logical_or(lanes == head, lanes == head + 1)
    pitch = cols + 128

    for k, part in enumerate(parts):
        base = k * pitch
        for at in range(0, cols, 256):
            size = min(256, cols - at)
            lane = at + lax.broadcasted_iota(jnp.int32, (1, size), 1)
            factor = jnp.where(lane < half, score_scale, 1.0)
            projected = jnp.dot(
                scaled[...], weights[k][:, at : at + size], preferred_element_type=jnp.float32
            )
            proj[:, base + at : base + at + size] = (projected * scale * factor).astype(
                jnp.bfloat16
            )
        proj[:, base + cols : base + pitch] = jnp.zeros((frames, 128), jnp.bfloat16)

    def slice_of(at):
        return proj[:, at : at + 128].astype(jnp.float32)

    keys, values = [], []
    for k in range(len(parts)):
        at = k * pitch + half
        key = jnp.where(flag_lanes, flag_column, jnp.where(lanes < head, slice_of(at), 0.0))
        value = jnp.where(
            lanes < head, slice_of(at + head), jnp.where(lanes == head, 1.0, 0.0)
        )
        keys.append(key.astype(jnp.bfloat16))
        values.append(value.T.astype(jnp.bfloat16))

    def scores_of(k, h):
        strength = bias[0, seq * heads + parts[k] * group + h] * math.log2(math.e)
        strength = jnp.zeros((1, 128), jnp.float32) + strength
        coarse = strength.astype(jnp.bfloat16).astype(jnp.float32)
        tail = jnp.where(
            row_lanes == head, coarse, jnp.where(row_lanes == head + 1, strength - coarse, 0.0)
        )
        query = jnp.where(lanes < head, slice_of(k * pitch + h * head), tail).astype(jnp.bfloat16)
        return lax.dot_general(
            keys[k], query, (((1,), (1,)), ((), ())), preferred_element_type=jnp.float32
        )

    tasks = [(k, h) for k in range(len(parts)) for h in range(group)]
    scores = scores_of(*tasks[0])
    for index, (k, h) in enumerate(tasks):
        ahead = scores_of(*tasks[index + 1]) if index + 1 < len(tasks) else None
        top = jnp.max(scores, axis=0, keepdims=True)
        weight = jnp.exp2(scores - top).astype(jnp.bfloat16)
        mixed = jnp.dot(values[k], weight, preferred_element_type=jnp.float32)
        at = (parts[k] * group + h) * head
        att[at : at + head, :] = mixed[:head] * (1.0 / mixed[head : head + 1])
        scores = ahead
    gates = gate[:, pl.ds(pl.multiple_of(seq * cols, 128), cols)]
    first, last = parts[0] * half, (parts[-1] + 1) * half
    attended = att[first:last].T.astype(jnp.bfloat16).astype(jnp.float32)
    output = own_hidden[...][:, first:last] + gates[:, first:last] * attended
    if parts == (0,):
        out[:, :half] = output.astype(jnp.bfloat16)
    elif parts == (1,):
        output_both = jnp.concatenate([left[:, :half].astype(jnp.float32), output], axis=1)
        out[...] = output_both.astype(jnp.bfloat16).reshape(pieces, rows, cols)
    else:
        out[...] = output.astype(jnp.bfloat16).reshape(pieces, rows, cols)
    if sends is not None:
        sends[...] = dense(output, parts == (1,)).astype(jnp.bfloat16)


def tie_kernel(*refs):
    pass


def grad_of(output, second, turn, rows, feats):
    cot = jnp.concatenate(
        [piece[rows : 2 * rows, turn * feats : (turn + 1) * feats] for piece in second], axis=0
    )
    return lax.dot_general(
        output, cot, (((0,), (0,)), ((), ())), preferred_element_type=jnp.float32
    )


def early_kernel(turns, pieces, halves, feats, *refs):
    outs, second = refs[: turns * halves], opened(refs[turns * halves : turns * halves + 3])
    sends, grad = refs[turns * halves + 3 : -1], refs[-1]
    section = lax.axis_index("pipe")
    offsets = offsets_of(pieces)
    part = pieces // halves
    rows = outs[0].shape[1]
    total = None
    for turn in range(turns - 1):
        blocks = []
        for p in range(pieces):
            k, j = p // part, p % part
            block = jnp.where(
                section == 0, outs[turn * halves + k][j], outs[(turn + 1) * halves + k][j]
            )
            sends[offsets[p]][turn] = block
            blocks.append(block)
        share = grad_of(jnp.concatenate(blocks, axis=0), second, turn, rows, feats)
        total = share if total is None else total + share
    grad[...] = total


def settle_kernel(turns, pieces, halves, hops, feats, *refs):
    refs = list(refs)

    def take(count):
        taken, refs[:count] = refs[:count], []
        return taken

    before, now, second, early = take(halves), take(halves), opened(take(3)), take(pieces - 1)
    early_grad = take(1)[0]
    late, own_grad, grads = take(pieces), take(1)[0], take(hops - 1)
    section_out = take(1)[0]
    rows_out, total, sem = take(3)
    section, seq, rep = lax.axis_index("pipe"), lax.axis_index("seq"), lax.axis_index("dp")
    offsets = offsets_of(pieces)
    part = pieces // halves
    rows, cols = early[0].shape[1:]
    for m in range(pieces - 1):
        lanes = pl.ds(pl.multiple_of((seq ^ m) * cols, 128), cols)
        for turn in range(turns - 1):
            rows_out[turn, :, lanes] = early[m][turn]
    copy = pltpu.make_async_copy(rows_out, section_out.at[pl.ds(0, turns - 1)], sem)
    copy.start()
    blocks = []
    for p in range(pieces):
        block = jnp.where(section == 0, before[p // part][p % part], now[p // part][p % part])
        late[offsets[p]][...] = block
        blocks.append(block)
    share = grad_of(jnp.concatenate(blocks, axis=0), second, turns - 1, rows, feats)
    factor = float(turns * hops * rows * pieces) ** (-0.5)
    total[...] = (share + early_grad[...]) * factor
    g_rows = cols // hops
    own_grad[...] = total[pl.ds(pl.multiple_of(rep * g_rows, 8), g_rows)]
    for shift in range(1, hops):
        at = pl.multiple_of(lax.rem(rep + shift, hops) * g_rows, 8)
        grads[shift - 1][...] = total[pl.ds(at, g_rows)].astype(jnp.bfloat16)
    copy.wait()


def finish_kernel(pieces, hops, *refs):
    held, early, late, refs = refs[0], refs[1], refs[2 : pieces + 2], refs[pieces + 2 :]
    own_grad, parts, (section_out, grad, row_out, sems) = refs[0], refs[1:hops], refs[hops:]
    seq = lax.axis_index("seq")
    cols = late[0].shape[1]
    last_lanes = pl.ds(pl.multiple_of((seq ^ (pieces - 1)) * cols, 128), cols)
    early_copy = pltpu.make_async_copy(
        early, section_out.at[pl.ds(0, early.shape[0]), :, last_lanes], sems.at[0]
    )
    early_copy.start()
    for m in range(pieces):
        lanes = pl.ds(pl.multiple_of((seq ^ m) * cols, 128), cols)
        row_out[:, lanes] = late[m][...]
    copy = pltpu.make_async_copy(row_out, section_out.at[section_out.shape[0] - 1], sems.at[1])
    copy.start()
    total = own_grad[...]
    for part in parts:
        total = total + part[...].astype(jnp.float32)
    grad[...] = total
    early_copy.wait()
    copy.wait()


MIB = 1024 * 1024


def paired_body(
    incoming,
    contacts,
    keyframes,
    timesteps,
    w_query,
    w_keyval,
    norm_gain,
    time_freq,
    contact_table,
    key_bias,
    attn_gate,
    head_cotangent,
):
    seq_count = lax.axis_size("seq")
    hops = lax.axis_size("dp")
    rows, width, turns = incoming.shape[3], incoming.shape[4], incoming.shape[1]
    frames = rows * seq_count
    heads_all = key_bias.shape[1]
    head = width // heads_all
    heads = heads_all // seq_count
    kv_heads = w_keyval.shape[2] // (2 * head * seq_count)
    feats = head_cotangent.shape[4]
    cols = width // seq_count
    w_rows = w_query.shape[1]
    kind = jnp.bfloat16
    smem = pl.BlockSpec(memory_space=pltpu.SMEM)
    vmem = pl.BlockSpec(memory_space=pltpu.VMEM)
    anywhere = pl.BlockSpec(memory_space=pl.ANY)
    shape = jax.ShapeDtypeStruct

    def call(kernel, name, out_shape, in_specs, operands, scratch=(), limit=4, flops=0, **options):
        return pl.pallas_call(
            kernel,
            out_shape=out_shape,
            in_specs=in_specs,
            scratch_shapes=list(scratch),
            compiler_params=pltpu.CompilerParams(vmem_limit_bytes=limit * MIB),
            cost_estimate=pl.CostEstimate(
                flops=flops, bytes_accessed=flops // 512, transcendentals=0
            ),
            name=name,
            **options,
        )(*operands)

    timesteps = timesteps.reshape(1, timesteps.shape[0])

    def pin(value, space=pltpu.VMEM):
        return pltpu.with_memory_space_constraint(value, space)

    packed = call(
        pack_kernel,
        "pack",
        [pltpu.VMEM((2, w_rows, cols), kind)] * seq_count,
        [anywhere, anywhere],
        [pin(w_query, pltpu.HBM), pin(w_keyval, pltpu.HBM)],
        [pltpu.VMEM((seq_count, w_rows, cols), kind)] * 2
        + [pltpu.SemaphoreType.DMA((2 * seq_count,))],
        out_specs=[vmem] * seq_count,
    )
    blocks = [packed[0]] + [swap(packed[m], m) for m in range(1, seq_count)]

    def paired(name, deps, values):
        return call(
            functools.partial(pair_kernel, len(deps)),
            name,
            pltpu.VMEM((2, 2, w_rows, cols), kind),
            [anywhere] * len(deps) + [vmem] * 2,
            deps + values,
            out_specs=vmem,
        )

    near = paired("near", [], blocks[:2])
    near_next = ring_step(near)
    far = paired("far", [near_next], blocks[2:])
    far_next = ring_step(far)
    rings, partial = [], []
    for part in range(2):
        chunk = call(
            functools.partial(part_kernel, part),
            "part%d" % part,
            pltpu.VMEM((seq_count, w_rows, cols), kind),
            [vmem, vmem],
            [near_next, far_next],
            out_specs=vmem,
        )
        rings.append([chunk])
        partial.append(
            call(
                functools.partial(place_kernel, part, hops),
                "place%d" % part,
                pltpu.VMEM((width, cols), kind),
                [vmem] * 3,
                [pin(near), pin(far), pin(chunk)],
                out_specs=vmem,
            )
        )
    for hop in range(2):
        for ring in rings:
            ring.append(ring_step(ring[-1]))

    def tie(values, deps):
        return call(
            tie_kernel,
            "tie",
            [shape(value.shape, kind) for value in values],
            [anywhere] * (len(values) + len(deps)),
            list(values) + list(deps),
            out_specs=[anywhere] * len(values),
            input_output_aliases={i: i for i in range(len(values))},
        )

    mine = call(
        functools.partial(first_kernel, turns),
        "first",
        pltpu.VMEM((2 * rows + 16, width), kind),
        [anywhere, vmem, vmem],
        [far, incoming, contacts],
        [pltpu.VMEM((16, 128), jnp.float32)],
        out_specs=vmem,
    )
    across = swap(mine, 2)
    beside = swap(mine, 1)
    (across,) = tie([across], [ring[1] for ring in rings])
    first = [mine, across, beside, swap(across, 1)]
    prepared = call(
        functools.partial(norm_kernel, turns, seq_count),
        "norm",
        [pltpu.VMEM((frames, width), kind)] * 2
        + [pltpu.VMEM((frames, 128), jnp.float32)] * 2
        + [pltpu.VMEM((frames, cols), jnp.float32)] * 2
        + [pltpu.VMEM((frames, width), kind)] * 2,
        [smem] + [vmem] * 3 + [anywhere] * seq_count,
        [timesteps, contact_table, norm_gain, time_freq]
        + first,
        [pltpu.VMEM((1, width), jnp.float32)]
        + [pltpu.VMEM((2 * rows + 16, width), kind)] * seq_count
        + [pltpu.SemaphoreType.DMA((seq_count,))],
        12,
        out_specs=[vmem] * 8,
    )

    mine = call(
        second_kernel,
        "second",
        pltpu.VMEM((2 * rows, width), kind),
        [anywhere, vmem, vmem],
        [across, incoming, head_cotangent],
        out_specs=vmem,
    )
    second = [mine, swap(mine, 2)]

    common = [key_bias, timesteps, norm_gain, time_freq, attn_gate, keyframes]

    def run_step(step, parts, large, out_shape, aliases):
        cfg = {
            "step": step,
            "has_relay": step >= 2,
            "parts": parts,
            "pieces": seq_count,
            "hops": hops,
            "head": head,
            "heads": heads,
            "group": heads // kv_heads,
            "turns": turns,
        }
        scratch = [
            pltpu.VMEM((frames, len(parts) * (cols + 128)), kind),
            pltpu.VMEM((cols, frames), jnp.float32),
        ]
        if step >= 2:
            scratch += [
                pltpu.VMEM((frames, width), kind),
                pltpu.VMEM((frames, 128), jnp.float32),
                pltpu.VMEM((frames, cols), jnp.float32),
                pltpu.VMEM((1, width), jnp.float32),
            ]
        operands = common + [pin(value) for value in large]
        return call(
            functools.partial(step_kernel, cfg),
            "step%d%s" % (step, "".join("ab"[part] for part in parts)),
            out_shape,
            [smem, smem] + [vmem] * (len(operands) - 2),
            operands,
            scratch,
            16,
            len(parts) * frames * (2 * width * cols + 2 * heads * frames * head),
            out_specs=[vmem] * len(out_shape),
            input_output_aliases=aliases,
        )

    whole = pltpu.VMEM((seq_count, rows, cols), kind)
    sent = pltpu.VMEM((frames * 3 // 2, 128), kind)
    weights = list(partial)
    relays, lefts, outputs = ([], []), [], []
    for part in range(2):
        for step in range(2):
            large = [prepared[step], prepared[2 + step], prepared[4 + step]]
            if step == 0:
                chunks = rings[part][1:]
                if part:
                    (last_chunk,) = tie(chunks[1:], [relays[0][0][0], lefts[1]])
                    chunks = [chunks[0], last_chunk]
                large += chunks
            large += [weights[part]]
            aliases = {len(common) + len(large) - 1: 2} if step == 0 else {}
            out_shape = [sent, whole if part else pltpu.VMEM((frames, 256), kind)]
            if step == 0:
                out_shape += [pltpu.VMEM((width, cols), kind)]
            if part:
                large += [lefts[step]]
            results = run_step(step, (part,), large, out_shape, aliases)
            if step == 0:
                weights[part] = results[2]
            (outputs if part else lefts).append(results[1])
            piece = handed_over(results[0])
            relays[step].append([piece, None if part and not step else swap(piece, 2)])
    (piece,) = tie([relays[0][1][0]], [outputs[1]])
    relays[0][1] = [piece, swap(piece, 2)]
    beside = call(
        second_pair_kernel,
        "beside",
        pltpu.VMEM((2,) + second[0].shape, kind),
        [anywhere, vmem, vmem],
        [outputs[0]] + second,
        limit=8,
        out_specs=vmem,
    )
    second = [second[0], second[1], swap(beside, 1)]

    def complete(crossing):
        return [
            piece
            for mine, across in crossing
            for piece in (mine, across, swap(mine, 1), swap(across, 1))
        ]

    relay = complete(relays[0])
    (output,) = run_step(2, (0, 1), second + [prepared[6]] + relay + weights, [whole], {})
    outputs.append(output)
    early = call(
        functools.partial(early_kernel, turns, seq_count, 1, feats),
        "early",
        [shape((turns - 1, rows, cols), kind)] * seq_count + [shape((cols, feats), jnp.float32)],
        [vmem] * (turns + len(second)),
        outputs + second,
        limit=8,
        out_specs=[vmem] * (seq_count + 1),
    )
    early, early_grad = list(early[:-1]), early[-1]
    early = [early[0]] + [swap(early[m], m) for m in range(1, seq_count)]
    tied = tie([piece for pair in relays[1] for piece in pair], [early_grad])
    relay = complete([(tied[0], tied[1]), (tied[2], tied[3])])
    (output,) = run_step(3, (0, 1), second + [prepared[7]] + relay + weights, [whole], {})
    outputs.append(output)

    g_shape = (cols // hops, feats)
    operands = outputs[-2:] + second + early[:-1] + [early_grad]
    settled = call(
        functools.partial(settle_kernel, turns, seq_count, 1, hops, feats),
        "settle",
        [shape((rows, cols), kind)] * seq_count
        + [shape(g_shape, jnp.float32)]
        + [shape(g_shape, kind)] * (hops - 1)
        + [shape((turns, rows, width), kind)],
        [vmem] * len(operands),
        operands,
        [
            pltpu.VMEM((turns - 1, rows, width), kind),
            pltpu.VMEM((cols, feats), jnp.float32),
            pltpu.SemaphoreType.DMA,
        ],
        8,
        out_specs=[vmem] * (seq_count + hops) + [anywhere],
    )
    late, grads, held = settled[:seq_count], settled[seq_count:-1], settled[-1]
    late = [late[0]] + [swap(late[m], m) for m in range(1, seq_count)]
    grads = [grads[0]] + [shifted(grads[k], "dp", k) for k in range(1, hops)]
    section_out, grad_rows = call(
        functools.partial(finish_kernel, seq_count, hops),
        "finish",
        [shape((turns, rows, width), kind), shape(g_shape, jnp.float32)],
        [anywhere] + [vmem] * (seq_count + hops + 1),
        [held, early[-1]] + late + grads,
        [pltpu.VMEM((rows, width), kind), pltpu.SemaphoreType.DMA((2,))],
        out_specs=[anywhere, vmem],
        input_output_aliases={0: 0},
    )
    return (section_out[None, :, None], grad_rows[None])


def body(incoming, contacts, keyframes, timesteps, w_query, *others):
    count = lax.axis_size("seq")
    cols = w_query.shape[2] // count
    paired = (
        lax.axis_size("pipe") == 2
        and lax.axis_size("dp") == 4
        and count == 4
        and cols % 128 == 0
        and w_query.shape[1] % 16 == 0
        and incoming.shape[3] == 128
        and incoming.shape[1] == 3
    )
    chosen = paired_body if paired else general_body
    return chosen(incoming, contacts, keyframes, timesteps, w_query, *others)


def general_body(
    incoming,
    contacts,
    keyframes,
    timesteps,
    w_query,
    w_keyval,
    norm_gain,
    time_freq,
    contact_table,
    key_bias,
    attn_gate,
    head_cotangent,
):
    section_idx = lax.axis_index("pipe")
    seq_idx = lax.axis_index("seq")
    rep_idx = lax.axis_index("dp")
    seq_count = lax.axis_size("seq")
    section_count = lax.axis_size("pipe")
    rep_count = lax.axis_size("dp")
    tok_rows = incoming.shape[3]
    width = incoming.shape[4]
    turns = incoming.shape[1]
    frames = tok_rows * seq_count
    heads_all = key_bias.shape[1]
    head_size = width // heads_all
    heads_local = heads_all // seq_count
    kv_width = w_keyval.shape[2]
    kv_local = kv_width // (2 * head_size * seq_count)
    group_size = heads_local // kv_local
    feat_count = head_cotangent.shape[4]
    score_scale = head_size ** (-0.5)
    q_cols = width // seq_count
    kv_cols = kv_width // seq_count
    w_rows = w_query.shape[1]

    w_parts = jnp.concatenate(
        [
            w_query[0].reshape(w_rows, seq_count, q_cols),
            w_keyval[0].reshape(w_rows, seq_count, kv_cols),
        ],
        axis=2,
    ).transpose(1, 0, 2)
    block = lax.all_to_all(w_parts, "seq", split_axis=0, concat_axis=0, tiled=True)
    weights = jnp.zeros((seq_count, rep_count, w_rows, q_cols + kv_cols), jnp.bfloat16)
    for hop in range(rep_count):
        owner = lax.rem(rep_idx + rep_count - hop, rep_count)
        weights = lax.dynamic_update_slice_in_dim(weights, block[:, None], owner, 1)
        if hop + 1 < rep_count:
            block = ring(block, "dp")
    weights = weights.reshape(width, q_cols + kv_cols)

    gain_row = norm_gain[0]
    freq_row = time_freq[0]
    table = contact_table[0]
    gate_local = lax.dynamic_slice_in_dim(attn_gate[0], seq_idx * q_cols, q_cols)
    table_local = lax.dynamic_slice_in_dim(table, seq_idx * q_cols, q_cols, 1)
    bias_local = lax.dynamic_slice_in_dim(key_bias[0], seq_idx * heads_local, heads_local)
    contact_all = lax.all_gather(contacts[:, 0, :], "seq", axis=1, tiled=True)
    key_all = keyframes[:, 0, :]
    step_all = timesteps[:, 0]
    labels = jnp.arange(table.shape[0], dtype=jnp.int32)
    cot_all = lax.all_gather(head_cotangent[0, :, 0], "seq", axis=1, tiled=True)

    lag = 2 if section_count == 2 else 1
    if lag == 2:
        steps = turns + 1
    else:
        steps = turns

    def turn_at(step):
        if lag == 1:
            return jnp.int32(step)
        return jnp.clip(step - section_idx, 0, turns - 1)

    outputs = []
    handed = {}
    for step in range(steps):
        turn = turn_at(step)
        fresh = lax.dynamic_index_in_dim(incoming[0, :, 0], turn, 0, keepdims=False)
        current = lax.all_gather(fresh, "seq", axis=0, tiled=True)
        if step in handed:
            current = jnp.where((section_idx == 0) | (turn == 0), current, handed[step])
        batch_idx = turn - section_idx + section_count - 1
        contact_rows = lax.dynamic_index_in_dim(contact_all, batch_idx, 0, keepdims=False)
        key_flags = lax.dynamic_index_in_dim(key_all, batch_idx, 0, keepdims=False).astype(
            jnp.float32
        )
        timestep = lax.dynamic_index_in_dim(step_all, batch_idx, 0, keepdims=False).astype(
            jnp.float32
        )
        onehot = (contact_rows[:, None] == labels[None, :]).astype(jnp.bfloat16)
        hidden = current.astype(jnp.float32) + jnp.dot(
            onehot, table, preferred_element_type=jnp.float32
        )
        root_mean = jnp.sqrt(jnp.mean(hidden * hidden, axis=-1, keepdims=True) + epsilon)
        modulation = gain_row * (1.0 + 0.5 * jnp.sin(timestep * freq_row))
        normed = (hidden / root_mean * modulation[None, :]).astype(jnp.bfloat16)
        projected = jnp.dot(normed, weights, preferred_element_type=jnp.float32).astype(
            jnp.bfloat16
        )
        query_heads = projected[:, :q_cols].reshape(frames, heads_local, head_size)
        keyval_heads = projected[:, q_cols:].reshape(frames, kv_local, 2, head_size)
        head_outputs = []
        for head in range(heads_local):
            key_rows = keyval_heads[:, head // group_size, 0]
            value_rows = keyval_heads[:, head // group_size, 1]
            scores = (
                lax.dot_general(
                    query_heads[:, head],
                    key_rows,
                    (((1,), (1,)), ((), ())),
                    preferred_element_type=jnp.float32,
                )
                * score_scale
            )
            scores = scores + bias_local[head] * key_flags[None, :]
            row_max = jnp.max(scores, axis=-1, keepdims=True)
            exponent = jnp.exp(scores - row_max)
            probabilities = (exponent / jnp.sum(exponent, axis=-1, keepdims=True)).astype(
                jnp.bfloat16
            )
            head_outputs.append(
                jnp.dot(probabilities, value_rows, preferred_element_type=jnp.float32).astype(
                    jnp.bfloat16
                )
            )
        attended = jnp.concatenate(head_outputs, axis=1)
        hidden_local = lax.dynamic_slice_in_dim(current, seq_idx * q_cols, q_cols, 1).astype(
            jnp.float32
        ) + jnp.dot(onehot, table_local, preferred_element_type=jnp.float32)
        output = (hidden_local + gate_local[None, :] * attended.astype(jnp.float32)).astype(
            jnp.bfloat16
        )
        outputs.append(output)
        if step + lag < steps:
            piece = passed_along(output, "pipe", 1)
            handed[step + lag] = lax.all_gather(piece, "seq", axis=1, tiled=True)

    factor = float(turns * rep_count * frames) ** (-0.5)
    total = None
    rows_out = []
    for turn in range(turns):
        if lag == 2:
            own = jnp.where(section_idx == 0, outputs[turn], outputs[turn + 1])
        else:
            own = outputs[turn]
        term = lax.dot_general(
            own, cot_all[turn], (((0,), (0,)), ((), ())), preferred_element_type=jnp.float32
        )
        total = term if total is None else total + term
        rows_out.append(lax.all_to_all(own, "seq", split_axis=0, concat_axis=1, tiled=True))
    section_out = jnp.stack(rows_out)[None, :, None]
    grad_parts = lax.all_to_all(
        (total * factor).astype(jnp.bfloat16).reshape(rep_count, q_cols // rep_count, feat_count),
        "dp",
        split_axis=0,
        concat_axis=0,
        tiled=True,
    )
    grad_rows = jnp.sum(grad_parts.astype(jnp.float32), axis=0)
    return (section_out, grad_rows[None])


def solution(mesh):
    in_specs = (
        P("pipe", None, "dp", "seq", None),
        P(None, "dp", "seq"),
        P(None, "dp", None),
        P(None, "dp"),
        P("pipe", ("seq", "dp"), None),
        P("pipe", ("seq", "dp"), None),
        P("pipe", None),
        P("pipe", None),
        P("pipe", None, None),
        P("pipe", None),
        P("pipe", None),
        P("pipe", None, "dp", "seq", None),
    )
    out_specs = (P("pipe", None, "dp", "seq", None), P("pipe", ("seq", "dp"), None))
    return jax.shard_map(body, mesh=mesh, in_specs=in_specs, out_specs=out_specs, check_vma=False)
```

```python
import functools
import math

import jax
import jax.numpy as jnp
from jax import lax
from jax.experimental import pallas as pl
from jax.experimental.pallas import tpu as pltpu
from jax.sharding import PartitionSpec as P

epsilon = 1e-06


def passed_along(value, axis, steps):
    count = lax.axis_size(axis)
    first, last = (max(0, -steps), min(count, count - steps))
    return lax.ppermute(value, axis, [(source, source + steps) for source in range(first, last)])


def ring(value, axis):
    count = lax.axis_size(axis)
    return lax.ppermute(value, axis, [(source, (source + 1) % count) for source in range(count)])


def swap(value, bit):
    count = lax.axis_size("seq")
    return lax.ppermute(value, "seq", [(source, source ^ bit) for source in range(count)])


def handed_over(value):
    return lax.ppermute(value, "pipe", [(0, 1), (1, 0)])


def shifted(value, axis, shift):
    count = lax.axis_size(axis)
    return lax.ppermute(value, axis, [(source, (source + shift) % count) for source in range(count)])


def fold(index):
    return index ^ (index >> 1)


def ring_step(value):
    count = lax.axis_size("dp")
    pairs = [(fold(place), fold((place + 1) % count)) for place in range(count)]
    return lax.ppermute(value, "dp", pairs)


def offsets_of(count):
    offsets = [0]
    bit = count // 2
    while bit:
        offsets = offsets + [offset ^ bit for offset in offsets]
        bit //= 2
    return offsets


def turn_and_batch(step, turns):
    section = lax.axis_index("pipe")
    turn = jnp.clip(step - section, 0, turns - 1)
    return turn, turn - section + 1


def pack_kernel(wq, wkv, *refs):
    outs, (queries, keyvals, sems) = refs[:-3], refs[-3:]
    parts, _, cols = outs[0].shape
    half = cols // 2
    seq = lax.axis_index("seq")
    copies = []
    for m in range(len(outs)):
        start = pl.multiple_of((seq ^ m) * cols, 128)
        for k, (source, held) in enumerate(((wq, queries), (wkv, keyvals))):
            copies.append(
                pltpu.make_async_copy(
                    source.at[0, :, pl.ds(start, cols)], held.at[m], sems.at[2 * m + k]
                )
            )
    for copy in copies:
        copy.start()
    for m, out in enumerate(outs):
        copies[2 * m].wait()
        copies[2 * m + 1].wait()
        for part in range(parts):
            lanes = slice(part * half, (part + 1) * half)
            out[part] = jnp.concatenate([queries[m][:, lanes], keyvals[m][:, lanes]], axis=1)


def pair_kernel(deps, *refs):
    out = refs[-1]
    for at, ref in enumerate(refs[deps:-1]):
        out[at] = ref[...]


def part_kernel(part, near, far, out):
    for at in range(2):
        out[at] = near[at, part]
        out[at + 2] = far[at, part]


def place(hop, hops, blocks, weights):
    seq, rep = lax.axis_index("seq"), lax.axis_index("dp")
    for m, block in enumerate(blocks):
        rows = block.shape[0]
        at = (seq ^ m) * hops + fold(lax.rem(fold(rep) + hops - hop, hops))
        weights[pl.ds(pl.multiple_of(at * rows, 16), rows)] = block[...]


def place_kernel(part, hops, near, far, chunk, weights):
    place(0, hops, [near.at[0, part], near.at[1, part], far.at[0, part], far.at[1, part]], weights)
    place(1, hops, [chunk.at[m] for m in range(4)], weights)


def first_kernel(turns, far, incoming, contacts, out, states):
    rows = incoming.shape[3]
    for turn in range(2):
        out[turn * rows : (turn + 1) * rows] = incoming[0, turn, 0]
    states[...] = jnp.zeros_like(states)
    for step in range(turns + 1):
        _, batch = turn_and_batch(step, turns)
        states[step : step + 1] = contacts[batch].astype(jnp.float32)
    out[2 * rows :, : states.shape[1]] = states[...].astype(jnp.bfloat16)


def second_kernel(dep, incoming, cotangent, out):
    turns, rows, feats = cotangent.shape[1], cotangent.shape[3], cotangent.shape[4]
    out[:rows] = incoming[0, 2, 0]
    for turn in range(turns):
        out[rows:, turn * feats : (turn + 1) * feats] = cotangent[0, turn, 0]


def columns_of(rows_of, pieces, rows):
    labels = lax.broadcasted_iota(jnp.int32, (32, rows), 0)
    columns = []
    for i in range(pieces):
        state, flag = rows_of(i)
        one = jnp.zeros((32, rows), jnp.float32)
        if state is not None:
            one = jnp.where(labels == state, 1.0, 0.0)
        if flag is not None:
            one = jnp.where(labels == 16, flag, one)
        columns.append(one.T)
    return jnp.concatenate(columns, axis=0)


def modulation(step, turns, times, gain, freq):
    _, batch = turn_and_batch(step, turns)
    return gain[...] * (1.0 + 0.5 * jnp.sin(times[0, batch].astype(jnp.float32) * freq[...]))


def norm_kernel(turns, pieces, times, table, gain, freq, *refs):
    sources, refs = refs[:pieces], refs[pieces:]
    scaled, scales, owns, embeds, mod = refs[0:2], refs[2:4], refs[4:6], refs[6:8], refs[8]
    first, sems = refs[9 : 9 + pieces], refs[9 + pieces]
    copies = [
        pltpu.make_async_copy(sources[i], first[i], sems.at[i]) for i in range(pieces)
    ]
    for copy in copies:
        copy.start()
    for copy in copies:
        copy.wait()
    frames, width = scaled[0].shape
    rows, cols = frames // pieces, owns[0].shape[1]
    seq = lax.axis_index("seq")
    offsets = offsets_of(pieces)
    for step in range(turns + 1):

        def state_of(i):
            state = first[i][2 * rows : 2 * rows + 16, :rows][step : step + 1]
            return state.astype(jnp.float32).astype(jnp.int32), None

        onehot = columns_of(state_of, pieces, rows)[:, : table.shape[1]].astype(jnp.bfloat16)
        if step >= 2:
            for at in range(0, width, 256):
                embeds[step - 2][:, at : at + 256] = jnp.dot(
                    onehot, table[0, :, at : at + 256], preferred_element_type=jnp.float32
                ).astype(jnp.bfloat16)
            continue
        turn, _ = turn_and_batch(step, turns)
        at = pl.multiple_of(jnp.minimum(turn, 1) * rows, 128)
        mod[...] = modulation(step, turns, times, gain, freq)
        total = jnp.zeros((frames, 128), jnp.float32)
        for i in range(pieces):
            lanes = pl.ds(pl.multiple_of((seq ^ offsets[i]) * cols, 128), cols)
            current = jnp.concatenate([first[p][pl.ds(at, rows), lanes] for p in range(pieces)])
            hidden = current.astype(jnp.float32) + jnp.dot(
                onehot, table[0, :, lanes], preferred_element_type=jnp.float32
            )
            for lane in range(0, cols, 128):
                piece = hidden[:, lane : lane + 128]
                total = total + piece * piece
            scaled[step][:, lanes] = (hidden * mod[:, lanes]).astype(jnp.bfloat16)
            if i == 0:
                owns[step][...] = hidden
        mean = jnp.sum(total, axis=1, keepdims=True) * (1.0 / width)
        scales[step][...] = jnp.broadcast_to(lax.rsqrt(mean + epsilon), (frames, 128))


def dense(value, lead):
    frames = value.shape[0]
    rest = value[:, :64] if lead else value[:, 128:]
    full = value[:, 64:] if lead else value[:, :128]
    rest = jnp.concatenate([rest[: frames // 2], rest[frames // 2 :]], axis=1)
    return jnp.concatenate([full, rest], axis=0)


def undense(left, right, frames):
    middle = []
    for ref in (left, right):
        rest = ref[frames:]
        middle.append(jnp.concatenate([rest[:, :64], rest[:, 64:]], axis=0))
    return jnp.concatenate([left[:frames], jnp.concatenate(middle, axis=1), right[:frames]], axis=1)


def second_pair_kernel(dep, mine, across, out):
    out[0] = mine[...]
    out[1] = across[...]


def opened(pieces):
    return list(pieces[:2]) + [pieces[2].at[0], pieces[2].at[1]]


def step_kernel(cfg, *refs):
    step, has_relay, parts = cfg["step"], cfg["has_relay"], cfg["parts"]
    pieces, hops, head, turns = cfg["pieces"], cfg["hops"], cfg["head"], cfg["turns"]
    heads, group = cfg["heads"], cfg["group"]
    refs = list(refs)

    def take(count):
        taken, refs[:count] = refs[:count], []
        return taken

    bias, times, gain, freq, gate, flags = take(6)
    if has_relay:
        second, embed, relay = opened(take(3)), take(1)[0], take(2 * pieces)
    else:
        scaled, scales, own_hidden = take(3)
    chunks = take(2) if step == 0 else None
    weights = take(len(parts))
    left = take(1)[0] if parts == (1,) else None
    sends = take(1)[0] if len(parts) == 1 else None
    out = take(1)[0]
    if step == 0:
        weights = take(1)
    proj, att = take(2)
    if has_relay:
        scaled, scales, own_hidden, mod = take(4)
    offsets = offsets_of(pieces)
    frames, width = scaled.shape
    cols = att.shape[0]
    half = cols // 2
    rows = frames // pieces
    seq, section = lax.axis_index("seq"), lax.axis_index("pipe")
    _, batch = turn_and_batch(step, turns)

    if step == 0:
        for hop, chunk in zip((2, 3), chunks):
            place(hop, hops, [chunk.at[m] for m in range(pieces)], weights[0])

    def normalize(relayed):
        total = jnp.zeros((frames, 128), jnp.float32)
        for i in range(pieces):
            lanes = pl.ds(pl.multiple_of((seq ^ offsets[i]) * cols, 128), cols)
            if relayed:
                value = undense(relay[i], relay[pieces + i], frames)
                order = [offsets.index(offsets[i] ^ offsets[p]) for p in range(pieces)]
                blocks = [value[j * rows : (j + 1) * rows] for j in order]
            else:
                blocks = [second[p][:rows, lanes] for p in range(pieces)]
            hidden = jnp.concatenate(blocks, axis=0).astype(jnp.float32)
            hidden = hidden + embed[:, lanes].astype(jnp.float32)
            for lane in range(0, cols, 128):
                piece = hidden[:, lane : lane + 128]
                total = total + piece * piece
            scaled[:, lanes] = (hidden * mod[:, lanes]).astype(jnp.bfloat16)
            if i == 0:
                own_hidden[...] = hidden
        scales[...] = total

    if has_relay:
        mod[...] = modulation(step, turns, times, gain, freq)

        @pl.when(section == 0)
        def _():
            normalize(False)

        @pl.when(section != 0)
        def _():
            normalize(True)

        mean = jnp.sum(scales[...], axis=1, keepdims=True) * (1.0 / width)
        scale = lax.rsqrt(mean + epsilon)
    else:
        scale = scales[:, :1]

    def flag_of(i):
        lanes = pl.ds(pl.multiple_of((seq ^ offsets[i]) * rows, 128), rows)
        return None, flags[batch, :, lanes].astype(jnp.float32)

    flag_column = columns_of(flag_of, pieces, rows)[:, 16:17]
    score_scale = head ** (-0.5) * math.log2(math.e)
    lanes = lax.broadcasted_iota(jnp.int32, (frames, 128), 1)
    row_lanes = lax.broadcasted_iota(jnp.int32, (1, 128), 1)
    flag_lanes = jnp.logical_or(lanes == head, lanes == head + 1)
    pitch = cols + 128

    for k, part in enumerate(parts):
        base = k * pitch
        for at in range(0, cols, 256):
            size = min(256, cols - at)
            lane = at + lax.broadcasted_iota(jnp.int32, (1, size), 1)
            factor = jnp.where(lane < half, score_scale, 1.0)
            projected = jnp.dot(
                scaled[...], weights[k][:, at : at + size], preferred_element_type=jnp.float32
            )
            proj[:, base + at : base + at + size] = (projected * scale * factor).astype(
                jnp.bfloat16
            )
        proj[:, base + cols : base + pitch] = jnp.zeros((frames, 128), jnp.bfloat16)

    def slice_of(at):
        return proj[:, at : at + 128].astype(jnp.float32)

    keys, values = [], []
    for k in range(len(parts)):
        at = k * pitch + half
        key = jnp.where(flag_lanes, flag_column, jnp.where(lanes < head, slice_of(at), 0.0))
        value = jnp.where(
            lanes < head, slice_of(at + head), jnp.where(lanes == head, 1.0, 0.0)
        )
        keys.append(key.astype(jnp.bfloat16))
        values.append(value.T.astype(jnp.bfloat16))

    def scores_of(k, h):
        strength = bias[0, seq * heads + parts[k] * group + h] * math.log2(math.e)
        strength = jnp.zeros((1, 128), jnp.float32) + strength
        coarse = strength.astype(jnp.bfloat16).astype(jnp.float32)
        tail = jnp.where(
            row_lanes == head, coarse, jnp.where(row_lanes == head + 1, strength - coarse, 0.0)
        )
        query = jnp.where(lanes < head, slice_of(k * pitch + h * head), tail).astype(jnp.bfloat16)
        return lax.dot_general(
            keys[k], query, (((1,), (1,)), ((), ())), preferred_element_type=jnp.float32
        )

    tasks = [(k, h) for k in range(len(parts)) for h in range(group)]
    scores = scores_of(*tasks[0])
    for index, (k, h) in enumerate(tasks):
        ahead = scores_of(*tasks[index + 1]) if index + 1 < len(tasks) else None
        top = jnp.max(scores, axis=0, keepdims=True)
        weight = jnp.exp2(scores - top).astype(jnp.bfloat16)
        mixed = jnp.dot(values[k], weight, preferred_element_type=jnp.float32)
        at = (parts[k] * group + h) * head
        att[at : at + head, :] = mixed[:head] * (1.0 / mixed[head : head + 1])
        scores = ahead
    gates = gate[:, pl.ds(pl.multiple_of(seq * cols, 128), cols)]
    first, last = parts[0] * half, (parts[-1] + 1) * half
    attended = att[first:last].T.astype(jnp.bfloat16).astype(jnp.float32)
    output = own_hidden[...][:, first:last] + gates[:, first:last] * attended
    if parts == (0,):
        out[:, :half] = output.astype(jnp.bfloat16)
    elif parts == (1,):
        output_both = jnp.concatenate([left[:, :half].astype(jnp.float32), output], axis=1)
        out[...] = output_both.astype(jnp.bfloat16).reshape(pieces, rows, cols)
    else:
        out[...] = output.astype(jnp.bfloat16).reshape(pieces, rows, cols)
    if sends is not None:
        sends[...] = dense(output, parts == (1,)).astype(jnp.bfloat16)


def tie_kernel(*refs):
    pass


def grad_of(output, second, turn, rows, feats):
    cot = jnp.concatenate(
        [piece[rows : 2 * rows, turn * feats : (turn + 1) * feats] for piece in second], axis=0
    )
    return lax.dot_general(
        output, cot, (((0,), (0,)), ((), ())), preferred_element_type=jnp.float32
    )


def early_kernel(turns, pieces, halves, feats, *refs):
    outs, second = refs[: turns * halves], opened(refs[turns * halves : turns * halves + 3])
    sends, grad = refs[turns * halves + 3 : -1], refs[-1]
    section = lax.axis_index("pipe")
    offsets = offsets_of(pieces)
    part = pieces // halves
    rows = outs[0].shape[1]
    total = None
    for turn in range(turns - 1):
        blocks = []
        for p in range(pieces):
            k, j = p // part, p % part
            block = jnp.where(
                section == 0, outs[turn * halves + k][j], outs[(turn + 1) * halves + k][j]
            )
            sends[offsets[p]][turn] = block
            blocks.append(block)
        share = grad_of(jnp.concatenate(blocks, axis=0), second, turn, rows, feats)
        total = share if total is None else total + share
    grad[...] = total


def settle_kernel(turns, pieces, halves, hops, feats, *refs):
    refs = list(refs)

    def take(count):
        taken, refs[:count] = refs[:count], []
        return taken

    before, now, second, early = take(halves), take(halves), opened(take(3)), take(pieces - 1)
    early_grad = take(1)[0]
    late, own_grad, grads = take(pieces), take(1)[0], take(hops - 1)
    section_out = take(1)[0]
    rows_out, total, sem = take(3)
    section, seq, rep = lax.axis_index("pipe"), lax.axis_index("seq"), lax.axis_index("dp")
    offsets = offsets_of(pieces)
    part = pieces // halves
    rows, cols = early[0].shape[1:]
    for m in range(pieces - 1):
        lanes = pl.ds(pl.multiple_of((seq ^ m) * cols, 128), cols)
        for turn in range(turns - 1):
            rows_out[turn, :, lanes] = early[m][turn]
    copy = pltpu.make_async_copy(rows_out, section_out.at[pl.ds(0, turns - 1)], sem)
    copy.start()
    blocks = []
    for p in range(pieces):
        block = jnp.where(section == 0, before[p // part][p % part], now[p // part][p % part])
        late[offsets[p]][...] = block
        blocks.append(block)
    share = grad_of(jnp.concatenate(blocks, axis=0), second, turns - 1, rows, feats)
    factor = float(turns * hops * rows * pieces) ** (-0.5)
    total[...] = (share + early_grad[...]) * factor
    g_rows = cols // hops
    own_grad[...] = total[pl.ds(pl.multiple_of(rep * g_rows, 8), g_rows)]
    for shift in range(1, hops):
        at = pl.multiple_of(lax.rem(rep + shift, hops) * g_rows, 8)
        grads[shift - 1][...] = total[pl.ds(at, g_rows)].astype(jnp.bfloat16)
    copy.wait()


def finish_kernel(pieces, hops, *refs):
    held, early, late, refs = refs[0], refs[1], refs[2 : pieces + 2], refs[pieces + 2 :]
    own_grad, parts, (section_out, grad, row_out, sems) = refs[0], refs[1:hops], refs[hops:]
    seq = lax.axis_index("seq")
    cols = late[0].shape[1]
    last_lanes = pl.ds(pl.multiple_of((seq ^ (pieces - 1)) * cols, 128), cols)
    early_copy = pltpu.make_async_copy(
        early, section_out.at[pl.ds(0, early.shape[0]), :, last_lanes], sems.at[0]
    )
    early_copy.start()
    for m in range(pieces):
        lanes = pl.ds(pl.multiple_of((seq ^ m) * cols, 128), cols)
        row_out[:, lanes] = late[m][...]
    copy = pltpu.make_async_copy(row_out, section_out.at[section_out.shape[0] - 1], sems.at[1])
    copy.start()
    total = own_grad[...]
    for part in parts:
        total = total + part[...].astype(jnp.float32)
    grad[...] = total
    early_copy.wait()
    copy.wait()


MIB = 1024 * 1024


def paired_body(
    incoming,
    contacts,
    keyframes,
    timesteps,
    w_query,
    w_keyval,
    norm_gain,
    time_freq,
    contact_table,
    key_bias,
    attn_gate,
    head_cotangent,
):
    seq_count = lax.axis_size("seq")
    hops = lax.axis_size("dp")
    rows, width, turns = incoming.shape[3], incoming.shape[4], incoming.shape[1]
    frames = rows * seq_count
    heads_all = key_bias.shape[1]
    head = width // heads_all
    heads = heads_all // seq_count
    kv_heads = w_keyval.shape[2] // (2 * head * seq_count)
    feats = head_cotangent.shape[4]
    cols = width // seq_count
    w_rows = w_query.shape[1]
    kind = jnp.bfloat16
    smem = pl.BlockSpec(memory_space=pltpu.SMEM)
    vmem = pl.BlockSpec(memory_space=pltpu.VMEM)
    anywhere = pl.BlockSpec(memory_space=pl.ANY)
    shape = jax.ShapeDtypeStruct

    def call(kernel, name, out_shape, in_specs, operands, scratch=(), limit=4, flops=0, **options):
        return pl.pallas_call(
            kernel,
            out_shape=out_shape,
            in_specs=in_specs,
            scratch_shapes=list(scratch),
            compiler_params=pltpu.CompilerParams(vmem_limit_bytes=limit * MIB),
            cost_estimate=pl.CostEstimate(
                flops=flops, bytes_accessed=flops // 512, transcendentals=0
            ),
            name=name,
            **options,
        )(*operands)

    timesteps = timesteps.reshape(1, timesteps.shape[0])

    def pin(value, space=pltpu.VMEM):
        return pltpu.with_memory_space_constraint(value, space)

    packed = call(
        pack_kernel,
        "pack",
        [pltpu.VMEM((2, w_rows, cols), kind)] * seq_count,
        [anywhere, anywhere],
        [pin(w_query, pltpu.HBM), pin(w_keyval, pltpu.HBM)],
        [pltpu.VMEM((seq_count, w_rows, cols), kind)] * 2
        + [pltpu.SemaphoreType.DMA((2 * seq_count,))],
        out_specs=[vmem] * seq_count,
    )
    blocks = [packed[0]] + [swap(packed[m], m) for m in range(1, seq_count)]

    def paired(name, deps, values):
        return call(
            functools.partial(pair_kernel, len(deps)),
            name,
            pltpu.VMEM((2, 2, w_rows, cols), kind),
            [anywhere] * len(deps) + [vmem] * 2,
            deps + values,
            out_specs=vmem,
        )

    near = paired("near", [], blocks[:2])
    near_next = ring_step(near)
    far = paired("far", [near_next], blocks[2:])
    far_next = ring_step(far)
    rings, partial = [], []
    for part in range(2):
        chunk = call(
            functools.partial(part_kernel, part),
            "part%d" % part,
            pltpu.VMEM((seq_count, w_rows, cols), kind),
            [vmem, vmem],
            [near_next, far_next],
            out_specs=vmem,
        )
        rings.append([chunk])
        partial.append(
            call(
                functools.partial(place_kernel, part, hops),
                "place%d" % part,
                pltpu.VMEM((width, cols), kind),
                [vmem] * 3,
                [pin(near), pin(far), pin(chunk)],
                out_specs=vmem,
            )
        )
    for hop in range(2):
        for ring in rings:
            ring.append(ring_step(ring[-1]))

    def tie(values, deps):
        return call(
            tie_kernel,
            "tie",
            [shape(value.shape, kind) for value in values],
            [anywhere] * (len(values) + len(deps)),
            list(values) + list(deps),
            out_specs=[anywhere] * len(values),
            input_output_aliases={i: i for i in range(len(values))},
        )

    mine = call(
        functools.partial(first_kernel, turns),
        "first",
        pltpu.VMEM((2 * rows + 16, width), kind),
        [anywhere, vmem, vmem],
        [far, incoming, contacts],
        [pltpu.VMEM((16, 128), jnp.float32)],
        out_specs=vmem,
    )
    across = swap(mine, 2)
    beside = swap(mine, 1)
    (across,) = tie([across], [ring[1] for ring in rings])
    first = [mine, across, beside, swap(across, 1)]
    prepared = call(
        functools.partial(norm_kernel, turns, seq_count),
        "norm",
        [pltpu.VMEM((frames, width), kind)] * 2
        + [pltpu.VMEM((frames, 128), jnp.float32)] * 2
        + [pltpu.VMEM((frames, cols), jnp.float32)] * 2
        + [pltpu.VMEM((frames, width), kind)] * 2,
        [smem] + [vmem] * 3 + [anywhere] * seq_count,
        [timesteps, contact_table, norm_gain, time_freq]
        + first,
        [pltpu.VMEM((1, width), jnp.float32)]
        + [pltpu.VMEM((2 * rows + 16, width), kind)] * seq_count
        + [pltpu.SemaphoreType.DMA((seq_count,))],
        12,
        out_specs=[vmem] * 8,
    )

    mine = call(
        second_kernel,
        "second",
        pltpu.VMEM((2 * rows, width), kind),
        [anywhere, vmem, vmem],
        [across, incoming, head_cotangent],
        out_specs=vmem,
    )
    second = [mine, swap(mine, 2)]

    common = [key_bias, timesteps, norm_gain, time_freq, attn_gate, keyframes]

    def run_step(step, parts, large, out_shape, aliases):
        cfg = {
            "step": step,
            "has_relay": step >= 2,
            "parts": parts,
            "pieces": seq_count,
            "hops": hops,
            "head": head,
            "heads": heads,
            "group": heads // kv_heads,
            "turns": turns,
        }
        scratch = [
            pltpu.VMEM((frames, len(parts) * (cols + 128)), kind),
            pltpu.VMEM((cols, frames), jnp.float32),
        ]
        if step >= 2:
            scratch += [
                pltpu.VMEM((frames, width), kind),
                pltpu.VMEM((frames, 128), jnp.float32),
                pltpu.VMEM((frames, cols), jnp.float32),
                pltpu.VMEM((1, width), jnp.float32),
            ]
        operands = common + [pin(value) for value in large]
        return call(
            functools.partial(step_kernel, cfg),
            "step%d%s" % (step, "".join("ab"[part] for part in parts)),
            out_shape,
            [smem, smem] + [vmem] * (len(operands) - 2),
            operands,
            scratch,
            16,
            len(parts) * frames * (2 * width * cols + 2 * heads * frames * head),
            out_specs=[vmem] * len(out_shape),
            input_output_aliases=aliases,
        )

    whole = pltpu.VMEM((seq_count, rows, cols), kind)
    sent = pltpu.VMEM((frames * 3 // 2, 128), kind)
    weights = list(partial)
    relays, lefts, outputs = ([], []), [], []
    for part in range(2):
        for step in range(2):
            large = [prepared[step], prepared[2 + step], prepared[4 + step]]
            if step == 0:
                chunks = rings[part][1:]
                if part:
                    (last_chunk,) = tie(chunks[1:], [relays[0][0][1], relays[1][0][0]])
                    chunks = [chunks[0], last_chunk]
                large += chunks
            large += [weights[part]]
            aliases = {len(common) + len(large) - 1: 2} if step == 0 else {}
            out_shape = [sent, whole if part else pltpu.VMEM((frames, 256), kind)]
            if step == 0:
                out_shape += [pltpu.VMEM((width, cols), kind)]
            if part:
                large += [lefts[step]]
            results = run_step(step, (part,), large, out_shape, aliases)
            if step == 0:
                weights[part] = results[2]
            (outputs if part else lefts).append(results[1])
            piece = results[0]
            if step and not part:
                (piece,) = tie([piece], [relays[0][0][0]])
            piece = handed_over(piece)
            relays[step].append([piece, None if part and not step else swap(piece, 2)])
    (piece,) = tie([relays[0][1][0]], [outputs[1], relays[1][0][1]])
    relays[0][1] = [piece, swap(piece, 2)]
    beside = call(
        second_pair_kernel,
        "beside",
        pltpu.VMEM((2,) + second[0].shape, kind),
        [anywhere, vmem, vmem],
        [outputs[0]] + second,
        limit=8,
        out_specs=vmem,
    )
    second = [second[0], second[1], swap(beside, 1)]

    def complete(crossing):
        return [
            piece
            for mine, across in crossing
            for piece in (mine, across, swap(mine, 1), swap(across, 1))
        ]

    relay = complete(relays[0])
    (output,) = run_step(2, (0, 1), second + [prepared[6]] + relay + weights, [whole], {})
    outputs.append(output)
    early = call(
        functools.partial(early_kernel, turns, seq_count, 1, feats),
        "early",
        [shape((turns - 1, rows, cols), kind)] * seq_count + [shape((cols, feats), jnp.float32)],
        [vmem] * (turns + len(second)),
        outputs + second,
        limit=8,
        out_specs=[vmem] * (seq_count + 1),
    )
    early, early_grad = list(early[:-1]), early[-1]
    early = [early[0]] + [swap(early[m], m) for m in range(1, seq_count)]
    tied = tie([piece for pair in relays[1] for piece in pair], [early_grad])
    relay = complete([(tied[0], tied[1]), (tied[2], tied[3])])
    (output,) = run_step(3, (0, 1), second + [prepared[7]] + relay + weights, [whole], {})
    outputs.append(output)

    g_shape = (cols // hops, feats)
    operands = outputs[-2:] + second + early[:-1] + [early_grad]
    settled = call(
        functools.partial(settle_kernel, turns, seq_count, 1, hops, feats),
        "settle",
        [shape((rows, cols), kind)] * seq_count
        + [shape(g_shape, jnp.float32)]
        + [shape(g_shape, kind)] * (hops - 1)
        + [shape((turns, rows, width), kind)],
        [vmem] * len(operands),
        operands,
        [
            pltpu.VMEM((turns - 1, rows, width), kind),
            pltpu.VMEM((cols, feats), jnp.float32),
            pltpu.SemaphoreType.DMA,
        ],
        8,
        out_specs=[vmem] * (seq_count + hops) + [anywhere],
    )
    late, grads, held = settled[:seq_count], settled[seq_count:-1], settled[-1]
    late = [late[0]] + [swap(late[m], m) for m in range(1, seq_count)]
    grads = [grads[0]] + [shifted(grads[k], "dp", k) for k in range(1, hops)]
    section_out, grad_rows = call(
        functools.partial(finish_kernel, seq_count, hops),
        "finish",
        [shape((turns, rows, width), kind), shape(g_shape, jnp.float32)],
        [anywhere] + [vmem] * (seq_count + hops + 1),
        [held, early[-1]] + late + grads,
        [pltpu.VMEM((rows, width), kind), pltpu.SemaphoreType.DMA((2,))],
        out_specs=[anywhere, vmem],
        input_output_aliases={0: 0},
    )
    return (section_out[None, :, None], grad_rows[None])


def body(incoming, contacts, keyframes, timesteps, w_query, *others):
    count = lax.axis_size("seq")
    cols = w_query.shape[2] // count
    paired = (
        lax.axis_size("pipe") == 2
        and lax.axis_size("dp") == 4
        and count == 4
        and cols % 128 == 0
        and w_query.shape[1] % 16 == 0
        and incoming.shape[3] == 128
        and incoming.shape[1] == 3
    )
    chosen = paired_body if paired else general_body
    return chosen(incoming, contacts, keyframes, timesteps, w_query, *others)


def general_body(
    incoming,
    contacts,
    keyframes,
    timesteps,
    w_query,
    w_keyval,
    norm_gain,
    time_freq,
    contact_table,
    key_bias,
    attn_gate,
    head_cotangent,
):
    section_idx = lax.axis_index("pipe")
    seq_idx = lax.axis_index("seq")
    rep_idx = lax.axis_index("dp")
    seq_count = lax.axis_size("seq")
    section_count = lax.axis_size("pipe")
    rep_count = lax.axis_size("dp")
    tok_rows = incoming.shape[3]
    width = incoming.shape[4]
    turns = incoming.shape[1]
    frames = tok_rows * seq_count
    heads_all = key_bias.shape[1]
    head_size = width // heads_all
    heads_local = heads_all // seq_count
    kv_width = w_keyval.shape[2]
    kv_local = kv_width // (2 * head_size * seq_count)
    group_size = heads_local // kv_local
    feat_count = head_cotangent.shape[4]
    score_scale = head_size ** (-0.5)
    q_cols = width // seq_count
    kv_cols = kv_width // seq_count
    w_rows = w_query.shape[1]

    w_parts = jnp.concatenate(
        [
            w_query[0].reshape(w_rows, seq_count, q_cols),
            w_keyval[0].reshape(w_rows, seq_count, kv_cols),
        ],
        axis=2,
    ).transpose(1, 0, 2)
    block = lax.all_to_all(w_parts, "seq", split_axis=0, concat_axis=0, tiled=True)
    weights = jnp.zeros((seq_count, rep_count, w_rows, q_cols + kv_cols), jnp.bfloat16)
    for hop in range(rep_count):
        owner = lax.rem(rep_idx + rep_count - hop, rep_count)
        weights = lax.dynamic_update_slice_in_dim(weights, block[:, None], owner, 1)
        if hop + 1 < rep_count:
            block = ring(block, "dp")
    weights = weights.reshape(width, q_cols + kv_cols)

    gain_row = norm_gain[0]
    freq_row = time_freq[0]
    table = contact_table[0]
    gate_local = lax.dynamic_slice_in_dim(attn_gate[0], seq_idx * q_cols, q_cols)
    table_local = lax.dynamic_slice_in_dim(table, seq_idx * q_cols, q_cols, 1)
    bias_local = lax.dynamic_slice_in_dim(key_bias[0], seq_idx * heads_local, heads_local)
    contact_all = lax.all_gather(contacts[:, 0, :], "seq", axis=1, tiled=True)
    key_all = keyframes[:, 0, :]
    step_all = timesteps[:, 0]
    labels = jnp.arange(table.shape[0], dtype=jnp.int32)
    cot_all = lax.all_gather(head_cotangent[0, :, 0], "seq", axis=1, tiled=True)

    lag = 2 if section_count == 2 else 1
    if lag == 2:
        steps = turns + 1
    else:
        steps = turns

    def turn_at(step):
        if lag == 1:
            return jnp.int32(step)
        return jnp.clip(step - section_idx, 0, turns - 1)

    outputs = []
    handed = {}
    for step in range(steps):
        turn = turn_at(step)
        fresh = lax.dynamic_index_in_dim(incoming[0, :, 0], turn, 0, keepdims=False)
        current = lax.all_gather(fresh, "seq", axis=0, tiled=True)
        if step in handed:
            current = jnp.where((section_idx == 0) | (turn == 0), current, handed[step])
        batch_idx = turn - section_idx + section_count - 1
        contact_rows = lax.dynamic_index_in_dim(contact_all, batch_idx, 0, keepdims=False)
        key_flags = lax.dynamic_index_in_dim(key_all, batch_idx, 0, keepdims=False).astype(
            jnp.float32
        )
        timestep = lax.dynamic_index_in_dim(step_all, batch_idx, 0, keepdims=False).astype(
            jnp.float32
        )
        onehot = (contact_rows[:, None] == labels[None, :]).astype(jnp.bfloat16)
        hidden = current.astype(jnp.float32) + jnp.dot(
            onehot, table, preferred_element_type=jnp.float32
        )
        root_mean = jnp.sqrt(jnp.mean(hidden * hidden, axis=-1, keepdims=True) + epsilon)
        modulation = gain_row * (1.0 + 0.5 * jnp.sin(timestep * freq_row))
        normed = (hidden / root_mean * modulation[None, :]).astype(jnp.bfloat16)
        projected = jnp.dot(normed, weights, preferred_element_type=jnp.float32).astype(
            jnp.bfloat16
        )
        query_heads = projected[:, :q_cols].reshape(frames, heads_local, head_size)
        keyval_heads = projected[:, q_cols:].reshape(frames, kv_local, 2, head_size)
        head_outputs = []
        for head in range(heads_local):
            key_rows = keyval_heads[:, head // group_size, 0]
            value_rows = keyval_heads[:, head // group_size, 1]
            scores = (
                lax.dot_general(
                    query_heads[:, head],
                    key_rows,
                    (((1,), (1,)), ((), ())),
                    preferred_element_type=jnp.float32,
                )
                * score_scale
            )
            scores = scores + bias_local[head] * key_flags[None, :]
            row_max = jnp.max(scores, axis=-1, keepdims=True)
            exponent = jnp.exp(scores - row_max)
            probabilities = (exponent / jnp.sum(exponent, axis=-1, keepdims=True)).astype(
                jnp.bfloat16
            )
            head_outputs.append(
                jnp.dot(probabilities, value_rows, preferred_element_type=jnp.float32).astype(
                    jnp.bfloat16
                )
            )
        attended = jnp.concatenate(head_outputs, axis=1)
        hidden_local = lax.dynamic_slice_in_dim(current, seq_idx * q_cols, q_cols, 1).astype(
            jnp.float32
        ) + jnp.dot(onehot, table_local, preferred_element_type=jnp.float32)
        output = (hidden_local + gate_local[None, :] * attended.astype(jnp.float32)).astype(
            jnp.bfloat16
        )
        outputs.append(output)
        if step + lag < steps:
            piece = passed_along(output, "pipe", 1)
            handed[step + lag] = lax.all_gather(piece, "seq", axis=1, tiled=True)

    factor = float(turns * rep_count * frames) ** (-0.5)
    total = None
    rows_out = []
    for turn in range(turns):
        if lag == 2:
            own = jnp.where(section_idx == 0, outputs[turn], outputs[turn + 1])
        else:
            own = outputs[turn]
        term = lax.dot_general(
            own, cot_all[turn], (((0,), (0,)), ((), ())), preferred_element_type=jnp.float32
        )
        total = term if total is None else total + term
        rows_out.append(lax.all_to_all(own, "seq", split_axis=0, concat_axis=1, tiled=True))
    section_out = jnp.stack(rows_out)[None, :, None]
    grad_parts = lax.all_to_all(
        (total * factor).astype(jnp.bfloat16).reshape(rep_count, q_cols // rep_count, feat_count),
        "dp",
        split_axis=0,
        concat_axis=0,
        tiled=True,
    )
    grad_rows = jnp.sum(grad_parts.astype(jnp.float32), axis=0)
    return (section_out, grad_rows[None])


def solution(mesh):
    in_specs = (
        P("pipe", None, "dp", "seq", None),
        P(None, "dp", "seq"),
        P(None, "dp", None),
        P(None, "dp"),
        P("pipe", ("seq", "dp"), None),
        P("pipe", ("seq", "dp"), None),
        P("pipe", None),
        P("pipe", None),
        P("pipe", None, None),
        P("pipe", None),
        P("pipe", None),
        P("pipe", None, "dp", "seq", None),
    )
    out_specs = (P("pipe", None, "dp", "seq", None), P("pipe", ("seq", "dp"), None))
    return jax.shard_map(body, mesh=mesh, in_specs=in_specs, out_specs=out_specs, check_vma=False)
```

```python
import functools
import math

import jax
import jax.numpy as jnp
from jax import lax
from jax.experimental import pallas as pl
from jax.experimental.pallas import tpu as pltpu
from jax.sharding import PartitionSpec as P

epsilon = 1e-06


def passed_along(value, axis, steps):
    count = lax.axis_size(axis)
    first, last = (max(0, -steps), min(count, count - steps))
    return lax.ppermute(value, axis, [(source, source + steps) for source in range(first, last)])


def ring(value, axis):
    count = lax.axis_size(axis)
    return lax.ppermute(value, axis, [(source, (source + 1) % count) for source in range(count)])


def swap(value, bit):
    count = lax.axis_size("seq")
    return lax.ppermute(value, "seq", [(source, source ^ bit) for source in range(count)])


def handed_over(value):
    return lax.ppermute(value, "pipe", [(0, 1), (1, 0)])


def shifted(value, axis, shift):
    count = lax.axis_size(axis)
    return lax.ppermute(value, axis, [(source, (source + shift) % count) for source in range(count)])


def fold(index):
    return index ^ (index >> 1)


def ring_step(value):
    count = lax.axis_size("dp")
    pairs = [(fold(place), fold((place + 1) % count)) for place in range(count)]
    return lax.ppermute(value, "dp", pairs)


def offsets_of(count):
    offsets = [0]
    bit = count // 2
    while bit:
        offsets = offsets + [offset ^ bit for offset in offsets]
        bit //= 2
    return offsets


def turn_and_batch(step, turns):
    section = lax.axis_index("pipe")
    turn = jnp.clip(step - section, 0, turns - 1)
    return turn, turn - section + 1


def pack_kernel(wq, wkv, *refs):
    outs, (queries, keyvals, sems) = refs[:-3], refs[-3:]
    parts, _, cols = outs[0].shape
    half = cols // 2
    seq = lax.axis_index("seq")
    copies = []
    for m in range(len(outs)):
        start = pl.multiple_of((seq ^ m) * cols, 128)
        for k, (source, held) in enumerate(((wq, queries), (wkv, keyvals))):
            copies.append(
                pltpu.make_async_copy(
                    source.at[0, :, pl.ds(start, cols)], held.at[m], sems.at[2 * m + k]
                )
            )
    for copy in copies:
        copy.start()
    for m, out in enumerate(outs):
        copies[2 * m].wait()
        copies[2 * m + 1].wait()
        for part in range(parts):
            lanes = slice(part * half, (part + 1) * half)
            out[part] = jnp.concatenate([queries[m][:, lanes], keyvals[m][:, lanes]], axis=1)


def pair_kernel(deps, *refs):
    out = refs[-1]
    for at, ref in enumerate(refs[deps:-1]):
        out[at] = ref[...]


def part_kernel(part, near, far, out):
    for at in range(2):
        out[at] = near[at, part]
        out[at + 2] = far[at, part]


def place(hop, hops, blocks, weights):
    seq, rep = lax.axis_index("seq"), lax.axis_index("dp")
    for m, block in enumerate(blocks):
        rows = block.shape[0]
        at = (seq ^ m) * hops + fold(lax.rem(fold(rep) + hops - hop, hops))
        weights[pl.ds(pl.multiple_of(at * rows, 16), rows)] = block[...]


def place_kernel(part, hops, near, far, chunk, weights):
    place(0, hops, [near.at[0, part], near.at[1, part], far.at[0, part], far.at[1, part]], weights)
    place(1, hops, [chunk.at[m] for m in range(4)], weights)


def first_kernel(turns, far, incoming, contacts, out, states):
    rows = incoming.shape[3]
    for turn in range(2):
        out[turn * rows : (turn + 1) * rows] = incoming[0, turn, 0]
    states[...] = jnp.zeros_like(states)
    for step in range(turns + 1):
        _, batch = turn_and_batch(step, turns)
        states[step : step + 1] = contacts[batch].astype(jnp.float32)
    out[2 * rows :, : states.shape[1]] = states[...].astype(jnp.bfloat16)


def second_kernel(dep, incoming, cotangent, out):
    turns, rows, feats = cotangent.shape[1], cotangent.shape[3], cotangent.shape[4]
    out[:rows] = incoming[0, 2, 0]
    for turn in range(turns):
        out[rows:, turn * feats : (turn + 1) * feats] = cotangent[0, turn, 0]


def columns_of(rows_of, pieces, rows):
    labels = lax.broadcasted_iota(jnp.int32, (32, rows), 0)
    columns = []
    for i in range(pieces):
        state, flag = rows_of(i)
        one = jnp.zeros((32, rows), jnp.float32)
        if state is not None:
            one = jnp.where(labels == state, 1.0, 0.0)
        if flag is not None:
            one = jnp.where(labels == 16, flag, one)
        columns.append(one.T)
    return jnp.concatenate(columns, axis=0)


def modulation(step, turns, times, gain, freq):
    _, batch = turn_and_batch(step, turns)
    return gain[...] * (1.0 + 0.5 * jnp.sin(times[0, batch].astype(jnp.float32) * freq[...]))


def norm_kernel(turns, pieces, times, table, gain, freq, *refs):
    sources, refs = refs[:pieces], refs[pieces:]
    scaled, scales, owns, embeds, mod = refs[0:2], refs[2:4], refs[4:6], refs[6:8], refs[8]
    first, sems = refs[9 : 9 + pieces], refs[9 + pieces]
    copies = [
        pltpu.make_async_copy(sources[i], first[i], sems.at[i]) for i in range(pieces)
    ]
    for copy in copies:
        copy.start()
    for copy in copies:
        copy.wait()
    frames, width = scaled[0].shape
    rows, cols = frames // pieces, owns[0].shape[1]
    seq = lax.axis_index("seq")
    offsets = offsets_of(pieces)
    for step in range(turns + 1):

        def state_of(i):
            state = first[i][2 * rows : 2 * rows + 16, :rows][step : step + 1]
            return state.astype(jnp.float32).astype(jnp.int32), None

        onehot = columns_of(state_of, pieces, rows)[:, : table.shape[1]].astype(jnp.bfloat16)
        if step >= 2:
            for at in range(0, width, 256):
                embeds[step - 2][:, at : at + 256] = jnp.dot(
                    onehot, table[0, :, at : at + 256], preferred_element_type=jnp.float32
                ).astype(jnp.bfloat16)
            continue
        turn, _ = turn_and_batch(step, turns)
        at = pl.multiple_of(jnp.minimum(turn, 1) * rows, 128)
        mod[...] = modulation(step, turns, times, gain, freq)
        total = jnp.zeros((frames, 128), jnp.float32)
        for i in range(pieces):
            lanes = pl.ds(pl.multiple_of((seq ^ offsets[i]) * cols, 128), cols)
            current = jnp.concatenate([first[p][pl.ds(at, rows), lanes] for p in range(pieces)])
            hidden = current.astype(jnp.float32) + jnp.dot(
                onehot, table[0, :, lanes], preferred_element_type=jnp.float32
            )
            for lane in range(0, cols, 128):
                piece = hidden[:, lane : lane + 128]
                total = total + piece * piece
            scaled[step][:, lanes] = (hidden * mod[:, lanes]).astype(jnp.bfloat16)
            if i == 0:
                owns[step][...] = hidden
        mean = jnp.sum(total, axis=1, keepdims=True) * (1.0 / width)
        scales[step][...] = jnp.broadcast_to(lax.rsqrt(mean + epsilon), (frames, 128))


def dense(value, lead):
    frames = value.shape[0]
    rest = value[:, :64] if lead else value[:, 128:]
    full = value[:, 64:] if lead else value[:, :128]
    rest = jnp.concatenate([rest[: frames // 2], rest[frames // 2 :]], axis=1)
    return jnp.concatenate([full, rest], axis=0)


def undense(left, right, frames):
    middle = []
    for ref in (left, right):
        rest = ref[frames:]
        middle.append(jnp.concatenate([rest[:, :64], rest[:, 64:]], axis=0))
    return jnp.concatenate([left[:frames], jnp.concatenate(middle, axis=1), right[:frames]], axis=1)


def second_pair_kernel(dep, mine, across, out):
    out[0] = mine[...]
    out[1] = across[...]


def opened(pieces):
    return list(pieces[:2]) + [pieces[2].at[0], pieces[2].at[1]]


def step_kernel(cfg, *refs):
    step, has_relay, parts = cfg["step"], cfg["has_relay"], cfg["parts"]
    pieces, hops, head, turns = cfg["pieces"], cfg["hops"], cfg["head"], cfg["turns"]
    heads, group = cfg["heads"], cfg["group"]
    refs = list(refs)

    def take(count):
        taken, refs[:count] = refs[:count], []
        return taken

    bias, times, gain, freq, gate, flags = take(6)
    if has_relay:
        second, embed, relay = opened(take(3)), take(1)[0], take(2 * pieces)
    else:
        scaled, scales, own_hidden = take(3)
    chunks = take(2) if step == 0 else None
    weights = take(len(parts))
    left = take(1)[0] if parts == (1,) else None
    sends = take(1)[0] if len(parts) == 1 else None
    out = take(1)[0]
    if step == 0:
        weights = take(1)
    proj, att = take(2)
    if has_relay:
        scaled, scales, own_hidden, mod = take(4)
    offsets = offsets_of(pieces)
    frames, width = scaled.shape
    cols = att.shape[0]
    half = cols // 2
    rows = frames // pieces
    seq, section = lax.axis_index("seq"), lax.axis_index("pipe")
    _, batch = turn_and_batch(step, turns)

    if step == 0:
        for hop, chunk in zip((2, 3), chunks):
            place(hop, hops, [chunk.at[m] for m in range(pieces)], weights[0])

    def normalize(relayed):
        total = jnp.zeros((frames, 128), jnp.float32)
        for i in range(pieces):
            lanes = pl.ds(pl.multiple_of((seq ^ offsets[i]) * cols, 128), cols)
            if relayed:
                value = undense(relay[i], relay[pieces + i], frames)
                order = [offsets.index(offsets[i] ^ offsets[p]) for p in range(pieces)]
                blocks = [value[j * rows : (j + 1) * rows] for j in order]
            else:
                blocks = [second[p][:rows, lanes] for p in range(pieces)]
            hidden = jnp.concatenate(blocks, axis=0).astype(jnp.float32)
            hidden = hidden + embed[:, lanes].astype(jnp.float32)
            for lane in range(0, cols, 128):
                piece = hidden[:, lane : lane + 128]
                total = total + piece * piece
            scaled[:, lanes] = (hidden * mod[:, lanes]).astype(jnp.bfloat16)
            if i == 0:
                own_hidden[...] = hidden
        scales[...] = total

    if has_relay:
        mod[...] = modulation(step, turns, times, gain, freq)

        @pl.when(section == 0)
        def _():
            normalize(False)

        @pl.when(section != 0)
        def _():
            normalize(True)

        mean = jnp.sum(scales[...], axis=1, keepdims=True) * (1.0 / width)
        scale = lax.rsqrt(mean + epsilon)
    else:
        scale = scales[:, :1]

    def flag_of(i):
        lanes = pl.ds(pl.multiple_of((seq ^ offsets[i]) * rows, 128), rows)
        return None, flags[batch, :, lanes].astype(jnp.float32)

    flag_column = columns_of(flag_of, pieces, rows)[:, 16:17]
    score_scale = head ** (-0.5) * math.log2(math.e)
    lanes = lax.broadcasted_iota(jnp.int32, (frames, 128), 1)
    row_lanes = lax.broadcasted_iota(jnp.int32, (1, 128), 1)
    flag_lanes = jnp.logical_or(lanes == head, lanes == head + 1)
    pitch = cols + 128

    for k, part in enumerate(parts):
        base = k * pitch
        for at in range(0, cols, 256):
            size = min(256, cols - at)
            lane = at + lax.broadcasted_iota(jnp.int32, (1, size), 1)
            factor = jnp.where(lane < half, score_scale, 1.0)
            projected = jnp.dot(
                scaled[...], weights[k][:, at : at + size], preferred_element_type=jnp.float32
            )
            proj[:, base + at : base + at + size] = (projected * scale * factor).astype(
                jnp.bfloat16
            )
        proj[:, base + cols : base + pitch] = jnp.zeros((frames, 128), jnp.bfloat16)

    def slice_of(at):
        return proj[:, at : at + 128].astype(jnp.float32)

    keys, values = [], []
    for k in range(len(parts)):
        at = k * pitch + half
        key = jnp.where(flag_lanes, flag_column, jnp.where(lanes < head, slice_of(at), 0.0))
        value = jnp.where(
            lanes < head, slice_of(at + head), jnp.where(lanes == head, 1.0, 0.0)
        )
        keys.append(key.astype(jnp.bfloat16))
        values.append(value.T.astype(jnp.bfloat16))

    def scores_of(k, h):
        strength = bias[0, seq * heads + parts[k] * group + h] * math.log2(math.e)
        strength = jnp.zeros((1, 128), jnp.float32) + strength
        coarse = strength.astype(jnp.bfloat16).astype(jnp.float32)
        tail = jnp.where(
            row_lanes == head, coarse, jnp.where(row_lanes == head + 1, strength - coarse, 0.0)
        )
        query = jnp.where(lanes < head, slice_of(k * pitch + h * head), tail).astype(jnp.bfloat16)
        return lax.dot_general(
            keys[k], query, (((1,), (1,)), ((), ())), preferred_element_type=jnp.float32
        )

    tasks = [(k, h) for k in range(len(parts)) for h in range(group)]
    scores = scores_of(*tasks[0])
    for index, (k, h) in enumerate(tasks):
        ahead = scores_of(*tasks[index + 1]) if index + 1 < len(tasks) else None
        top = jnp.max(scores, axis=0, keepdims=True)
        weight = jnp.exp2(scores - top).astype(jnp.bfloat16)
        mixed = jnp.dot(values[k], weight, preferred_element_type=jnp.float32)
        at = (parts[k] * group + h) * head
        att[at : at + head, :] = mixed[:head] * (1.0 / mixed[head : head + 1])
        scores = ahead
    gates = gate[:, pl.ds(pl.multiple_of(seq * cols, 128), cols)]
    first, last = parts[0] * half, (parts[-1] + 1) * half
    attended = att[first:last].T.astype(jnp.bfloat16).astype(jnp.float32)
    output = own_hidden[...][:, first:last] + gates[:, first:last] * attended
    if parts == (0,):
        out[:, :half] = output.astype(jnp.bfloat16)
    elif parts == (1,):
        output_both = jnp.concatenate([left[:, :half].astype(jnp.float32), output], axis=1)
        out[...] = output_both.astype(jnp.bfloat16).reshape(pieces, rows, cols)
    else:
        out[...] = output.astype(jnp.bfloat16).reshape(pieces, rows, cols)
    if sends is not None:
        sends[...] = dense(output, parts == (1,)).astype(jnp.bfloat16)


def tie_kernel(*refs):
    pass


def grad_of(output, second, turn, rows, feats):
    cot = jnp.concatenate(
        [piece[rows : 2 * rows, turn * feats : (turn + 1) * feats] for piece in second], axis=0
    )
    return lax.dot_general(
        output, cot, (((0,), (0,)), ((), ())), preferred_element_type=jnp.float32
    )


def early_kernel(turns, pieces, halves, feats, *refs):
    outs, second = refs[: turns * halves], opened(refs[turns * halves : turns * halves + 3])
    sends, grad = refs[turns * halves + 3 : -1], refs[-1]
    section = lax.axis_index("pipe")
    offsets = offsets_of(pieces)
    part = pieces // halves
    rows = outs[0].shape[1]
    total = None
    for turn in range(turns - 1):
        blocks = []
        for p in range(pieces):
            k, j = p // part, p % part
            block = jnp.where(
                section == 0, outs[turn * halves + k][j], outs[(turn + 1) * halves + k][j]
            )
            sends[offsets[p]][turn] = block
            blocks.append(block)
        share = grad_of(jnp.concatenate(blocks, axis=0), second, turn, rows, feats)
        total = share if total is None else total + share
    grad[...] = total


def settle_kernel(turns, pieces, halves, hops, feats, *refs):
    refs = list(refs)

    def take(count):
        taken, refs[:count] = refs[:count], []
        return taken

    before, now, second, early = take(halves), take(halves), opened(take(3)), take(pieces - 1)
    early_grad = take(1)[0]
    late, own_grad, grads = take(pieces), take(1)[0], take(hops - 1)
    section_out = take(1)[0]
    rows_out, total, sem = take(3)
    section, seq, rep = lax.axis_index("pipe"), lax.axis_index("seq"), lax.axis_index("dp")
    offsets = offsets_of(pieces)
    part = pieces // halves
    rows, cols = early[0].shape[1:]
    for m in range(pieces - 1):
        lanes = pl.ds(pl.multiple_of((seq ^ m) * cols, 128), cols)
        for turn in range(turns - 1):
            rows_out[turn, :, lanes] = early[m][turn]
    copy = pltpu.make_async_copy(rows_out, section_out.at[pl.ds(0, turns - 1)], sem)
    copy.start()
    blocks = []
    for p in range(pieces):
        block = jnp.where(section == 0, before[p // part][p % part], now[p // part][p % part])
        late[offsets[p]][...] = block
        blocks.append(block)
    share = grad_of(jnp.concatenate(blocks, axis=0), second, turns - 1, rows, feats)
    factor = float(turns * hops * rows * pieces) ** (-0.5)
    total[...] = (share + early_grad[...]) * factor
    g_rows = cols // hops
    own_grad[...] = total[pl.ds(pl.multiple_of(rep * g_rows, 8), g_rows)]
    for shift in range(1, hops):
        at = pl.multiple_of(lax.rem(rep + shift, hops) * g_rows, 8)
        grads[shift - 1][...] = total[pl.ds(at, g_rows)].astype(jnp.bfloat16)
    copy.wait()


def finish_kernel(pieces, hops, *refs):
    held, early, late, refs = refs[0], refs[1], refs[2 : pieces + 2], refs[pieces + 2 :]
    own_grad, parts, (section_out, grad, row_out, sems) = refs[0], refs[1:hops], refs[hops:]
    seq = lax.axis_index("seq")
    cols = late[0].shape[1]
    last_lanes = pl.ds(pl.multiple_of((seq ^ (pieces - 1)) * cols, 128), cols)
    early_copy = pltpu.make_async_copy(
        early, section_out.at[pl.ds(0, early.shape[0]), :, last_lanes], sems.at[0]
    )
    early_copy.start()
    for m in range(pieces):
        lanes = pl.ds(pl.multiple_of((seq ^ m) * cols, 128), cols)
        row_out[:, lanes] = late[m][...]
    copy = pltpu.make_async_copy(row_out, section_out.at[section_out.shape[0] - 1], sems.at[1])
    copy.start()
    total = own_grad[...]
    for part in parts:
        total = total + part[...].astype(jnp.float32)
    grad[...] = total
    early_copy.wait()
    copy.wait()


MIB = 1024 * 1024


def paired_body(
    incoming,
    contacts,
    keyframes,
    timesteps,
    w_query,
    w_keyval,
    norm_gain,
    time_freq,
    contact_table,
    key_bias,
    attn_gate,
    head_cotangent,
):
    seq_count = lax.axis_size("seq")
    hops = lax.axis_size("dp")
    rows, width, turns = incoming.shape[3], incoming.shape[4], incoming.shape[1]
    frames = rows * seq_count
    heads_all = key_bias.shape[1]
    head = width // heads_all
    heads = heads_all // seq_count
    kv_heads = w_keyval.shape[2] // (2 * head * seq_count)
    feats = head_cotangent.shape[4]
    cols = width // seq_count
    w_rows = w_query.shape[1]
    kind = jnp.bfloat16
    smem = pl.BlockSpec(memory_space=pltpu.SMEM)
    vmem = pl.BlockSpec(memory_space=pltpu.VMEM)
    anywhere = pl.BlockSpec(memory_space=pl.ANY)
    shape = jax.ShapeDtypeStruct

    def call(kernel, name, out_shape, in_specs, operands, scratch=(), limit=4, flops=0, **options):
        return pl.pallas_call(
            kernel,
            out_shape=out_shape,
            in_specs=in_specs,
            scratch_shapes=list(scratch),
            compiler_params=pltpu.CompilerParams(vmem_limit_bytes=limit * MIB),
            cost_estimate=pl.CostEstimate(
                flops=flops, bytes_accessed=flops // 512, transcendentals=0
            ),
            name=name,
            **options,
        )(*operands)

    timesteps = timesteps.reshape(1, timesteps.shape[0])

    def pin(value, space=pltpu.VMEM):
        return pltpu.with_memory_space_constraint(value, space)

    packed = call(
        pack_kernel,
        "pack",
        [pltpu.VMEM((2, w_rows, cols), kind)] * seq_count,
        [anywhere, anywhere],
        [pin(w_query, pltpu.HBM), pin(w_keyval, pltpu.HBM)],
        [pltpu.VMEM((seq_count, w_rows, cols), kind)] * 2
        + [pltpu.SemaphoreType.DMA((2 * seq_count,))],
        out_specs=[vmem] * seq_count,
    )
    blocks = [packed[0]] + [swap(packed[m], m) for m in range(1, seq_count)]

    def paired(name, deps, values):
        return call(
            functools.partial(pair_kernel, len(deps)),
            name,
            pltpu.VMEM((2, 2, w_rows, cols), kind),
            [anywhere] * len(deps) + [vmem] * 2,
            deps + values,
            out_specs=vmem,
        )

    near = paired("near", [], blocks[:2])
    near_next = ring_step(near)
    far = paired("far", [near_next], blocks[2:])
    far_next = ring_step(far)
    rings, partial = [], []
    for part in range(2):
        chunk = call(
            functools.partial(part_kernel, part),
            "part%d" % part,
            pltpu.VMEM((seq_count, w_rows, cols), kind),
            [vmem, vmem],
            [near_next, far_next],
            out_specs=vmem,
        )
        rings.append([chunk])
        partial.append(
            call(
                functools.partial(place_kernel, part, hops),
                "place%d" % part,
                pltpu.VMEM((width, cols), kind),
                [vmem] * 3,
                [pin(near), pin(far), pin(chunk)],
                out_specs=vmem,
            )
        )
    for hop in range(2):
        for ring in rings:
            ring.append(ring_step(ring[-1]))

    def tie(values, deps):
        return call(
            tie_kernel,
            "tie",
            [shape(value.shape, kind) for value in values],
            [anywhere] * (len(values) + len(deps)),
            list(values) + list(deps),
            out_specs=[anywhere] * len(values),
            input_output_aliases={i: i for i in range(len(values))},
        )

    mine = call(
        functools.partial(first_kernel, turns),
        "first",
        pltpu.VMEM((2 * rows + 16, width), kind),
        [anywhere, vmem, vmem],
        [far, incoming, contacts],
        [pltpu.VMEM((16, 128), jnp.float32)],
        out_specs=vmem,
    )
    across = swap(mine, 2)
    beside = swap(mine, 1)
    (across,) = tie([across], [ring[1] for ring in rings])
    first = [mine, across, beside, swap(across, 1)]
    prepared = call(
        functools.partial(norm_kernel, turns, seq_count),
        "norm",
        [pltpu.VMEM((frames, width), kind)] * 2
        + [pltpu.VMEM((frames, 128), jnp.float32)] * 2
        + [pltpu.VMEM((frames, cols), jnp.float32)] * 2
        + [pltpu.VMEM((frames, width), kind)] * 2,
        [smem] + [vmem] * 3 + [anywhere] * seq_count,
        [timesteps, contact_table, norm_gain, time_freq]
        + first,
        [pltpu.VMEM((1, width), jnp.float32)]
        + [pltpu.VMEM((2 * rows + 16, width), kind)] * seq_count
        + [pltpu.SemaphoreType.DMA((seq_count,))],
        12,
        out_specs=[vmem] * 8,
    )

    mine = call(
        second_kernel,
        "second",
        pltpu.VMEM((2 * rows, width), kind),
        [anywhere, vmem, vmem],
        [across, incoming, head_cotangent],
        out_specs=vmem,
    )
    second = [mine, swap(mine, 2)]

    common = [key_bias, timesteps, norm_gain, time_freq, attn_gate, keyframes]

    def run_step(step, parts, large, out_shape, aliases):
        cfg = {
            "step": step,
            "has_relay": step >= 2,
            "parts": parts,
            "pieces": seq_count,
            "hops": hops,
            "head": head,
            "heads": heads,
            "group": heads // kv_heads,
            "turns": turns,
        }
        scratch = [
            pltpu.VMEM((frames, len(parts) * (cols + 128)), kind),
            pltpu.VMEM((cols, frames), jnp.float32),
        ]
        if step >= 2:
            scratch += [
                pltpu.VMEM((frames, width), kind),
                pltpu.VMEM((frames, 128), jnp.float32),
                pltpu.VMEM((frames, cols), jnp.float32),
                pltpu.VMEM((1, width), jnp.float32),
            ]
        operands = common + [pin(value) for value in large]
        return call(
            functools.partial(step_kernel, cfg),
            "step%d%s" % (step, "".join("ab"[part] for part in parts)),
            out_shape,
            [smem, smem] + [vmem] * (len(operands) - 2),
            operands,
            scratch,
            16,
            len(parts) * frames * (2 * width * cols + 2 * heads * frames * head),
            out_specs=[vmem] * len(out_shape),
            input_output_aliases=aliases,
        )

    whole = pltpu.VMEM((seq_count, rows, cols), kind)
    sent = pltpu.VMEM((frames * 3 // 2, 128), kind)
    weights = list(partial)
    relays, lefts, outputs = ([], []), [], []
    for part in range(2):
        for step in range(2):
            large = [prepared[step], prepared[2 + step], prepared[4 + step]]
            if step == 0:
                chunks = rings[part][1:]
                if part:
                    (last_chunk,) = tie(chunks[1:], [relays[0][0][0], lefts[1]])
                    chunks = [chunks[0], last_chunk]
                large += chunks
            large += [weights[part]]
            aliases = {len(common) + len(large) - 1: 2} if step == 0 else {}
            out_shape = [sent, whole if part else pltpu.VMEM((frames, 256), kind)]
            if step == 0:
                out_shape += [pltpu.VMEM((width, cols), kind)]
            if part:
                large += [lefts[step]]
            results = run_step(step, (part,), large, out_shape, aliases)
            if step == 0:
                weights[part] = results[2]
            (outputs if part else lefts).append(results[1])
            piece = handed_over(results[0])
            relays[step].append([piece, None if part and not step else swap(piece, 2)])
    beside = call(
        second_pair_kernel,
        "beside",
        pltpu.VMEM((2,) + second[0].shape, kind),
        [anywhere, vmem, vmem],
        [outputs[0]] + second,
        limit=8,
        out_specs=vmem,
    )
    second = [second[0], second[1], swap(beside, 1)]

    (piece,) = tie([relays[0][1][0]], [outputs[1], second[2]])
    relays[0][1] = [piece, swap(piece, 2)]
    def complete(crossing):
        return [
            piece
            for mine, across in crossing
            for piece in (mine, across, swap(mine, 1), swap(across, 1))
        ]

    relay = complete(relays[0])
    (output,) = run_step(2, (0, 1), second + [prepared[6]] + relay + weights, [whole], {})
    outputs.append(output)
    early = call(
        functools.partial(early_kernel, turns, seq_count, 1, feats),
        "early",
        [shape((turns - 1, rows, cols), kind)] * seq_count + [shape((cols, feats), jnp.float32)],
        [vmem] * (turns + len(second)),
        outputs + second,
        limit=8,
        out_specs=[vmem] * (seq_count + 1),
    )
    early, early_grad = list(early[:-1]), early[-1]
    early = [early[0]] + [swap(early[m], m) for m in range(1, seq_count)]
    tied = tie([piece for pair in relays[1] for piece in pair], [early_grad])
    relay = complete([(tied[0], tied[1]), (tied[2], tied[3])])
    (output,) = run_step(3, (0, 1), second + [prepared[7]] + relay + weights, [whole], {})
    outputs.append(output)

    g_shape = (cols // hops, feats)
    operands = outputs[-2:] + second + early[:-1] + [early_grad]
    settled = call(
        functools.partial(settle_kernel, turns, seq_count, 1, hops, feats),
        "settle",
        [shape((rows, cols), kind)] * seq_count
        + [shape(g_shape, jnp.float32)]
        + [shape(g_shape, kind)] * (hops - 1)
        + [shape((turns, rows, width), kind)],
        [vmem] * len(operands),
        operands,
        [
            pltpu.VMEM((turns - 1, rows, width), kind),
            pltpu.VMEM((cols, feats), jnp.float32),
            pltpu.SemaphoreType.DMA,
        ],
        8,
        out_specs=[vmem] * (seq_count + hops) + [anywhere],
    )
    late, grads, held = settled[:seq_count], settled[seq_count:-1], settled[-1]
    late = [late[0]] + [swap(late[m], m) for m in range(1, seq_count)]
    grads = [grads[0]] + [shifted(grads[k], "dp", k) for k in range(1, hops)]
    section_out, grad_rows = call(
        functools.partial(finish_kernel, seq_count, hops),
        "finish",
        [shape((turns, rows, width), kind), shape(g_shape, jnp.float32)],
        [anywhere] + [vmem] * (seq_count + hops + 1),
        [held, early[-1]] + late + grads,
        [pltpu.VMEM((rows, width), kind), pltpu.SemaphoreType.DMA((2,))],
        out_specs=[anywhere, vmem],
        input_output_aliases={0: 0},
    )
    return (section_out[None, :, None], grad_rows[None])


def body(incoming, contacts, keyframes, timesteps, w_query, *others):
    count = lax.axis_size("seq")
    cols = w_query.shape[2] // count
    paired = (
        lax.axis_size("pipe") == 2
        and lax.axis_size("dp") == 4
        and count == 4
        and cols % 128 == 0
        and w_query.shape[1] % 16 == 0
        and incoming.shape[3] == 128
        and incoming.shape[1] == 3
    )
    chosen = paired_body if paired else general_body
    return chosen(incoming, contacts, keyframes, timesteps, w_query, *others)


def general_body(
    incoming,
    contacts,
    keyframes,
    timesteps,
    w_query,
    w_keyval,
    norm_gain,
    time_freq,
    contact_table,
    key_bias,
    attn_gate,
    head_cotangent,
):
    section_idx = lax.axis_index("pipe")
    seq_idx = lax.axis_index("seq")
    rep_idx = lax.axis_index("dp")
    seq_count = lax.axis_size("seq")
    section_count = lax.axis_size("pipe")
    rep_count = lax.axis_size("dp")
    tok_rows = incoming.shape[3]
    width = incoming.shape[4]
    turns = incoming.shape[1]
    frames = tok_rows * seq_count
    heads_all = key_bias.shape[1]
    head_size = width // heads_all
    heads_local = heads_all // seq_count
    kv_width = w_keyval.shape[2]
    kv_local = kv_width // (2 * head_size * seq_count)
    group_size = heads_local // kv_local
    feat_count = head_cotangent.shape[4]
    score_scale = head_size ** (-0.5)
    q_cols = width // seq_count
    kv_cols = kv_width // seq_count
    w_rows = w_query.shape[1]

    w_parts = jnp.concatenate(
        [
            w_query[0].reshape(w_rows, seq_count, q_cols),
            w_keyval[0].reshape(w_rows, seq_count, kv_cols),
        ],
        axis=2,
    ).transpose(1, 0, 2)
    block = lax.all_to_all(w_parts, "seq", split_axis=0, concat_axis=0, tiled=True)
    weights = jnp.zeros((seq_count, rep_count, w_rows, q_cols + kv_cols), jnp.bfloat16)
    for hop in range(rep_count):
        owner = lax.rem(rep_idx + rep_count - hop, rep_count)
        weights = lax.dynamic_update_slice_in_dim(weights, block[:, None], owner, 1)
        if hop + 1 < rep_count:
            block = ring(block, "dp")
    weights = weights.reshape(width, q_cols + kv_cols)

    gain_row = norm_gain[0]
    freq_row = time_freq[0]
    table = contact_table[0]
    gate_local = lax.dynamic_slice_in_dim(attn_gate[0], seq_idx * q_cols, q_cols)
    table_local = lax.dynamic_slice_in_dim(table, seq_idx * q_cols, q_cols, 1)
    bias_local = lax.dynamic_slice_in_dim(key_bias[0], seq_idx * heads_local, heads_local)
    contact_all = lax.all_gather(contacts[:, 0, :], "seq", axis=1, tiled=True)
    key_all = keyframes[:, 0, :]
    step_all = timesteps[:, 0]
    labels = jnp.arange(table.shape[0], dtype=jnp.int32)
    cot_all = lax.all_gather(head_cotangent[0, :, 0], "seq", axis=1, tiled=True)

    lag = 2 if section_count == 2 else 1
    if lag == 2:
        steps = turns + 1
    else:
        steps = turns

    def turn_at(step):
        if lag == 1:
            return jnp.int32(step)
        return jnp.clip(step - section_idx, 0, turns - 1)

    outputs = []
    handed = {}
    for step in range(steps):
        turn = turn_at(step)
        fresh = lax.dynamic_index_in_dim(incoming[0, :, 0], turn, 0, keepdims=False)
        current = lax.all_gather(fresh, "seq", axis=0, tiled=True)
        if step in handed:
            current = jnp.where((section_idx == 0) | (turn == 0), current, handed[step])
        batch_idx = turn - section_idx + section_count - 1
        contact_rows = lax.dynamic_index_in_dim(contact_all, batch_idx, 0, keepdims=False)
        key_flags = lax.dynamic_index_in_dim(key_all, batch_idx, 0, keepdims=False).astype(
            jnp.float32
        )
        timestep = lax.dynamic_index_in_dim(step_all, batch_idx, 0, keepdims=False).astype(
            jnp.float32
        )
        onehot = (contact_rows[:, None] == labels[None, :]).astype(jnp.bfloat16)
        hidden = current.astype(jnp.float32) + jnp.dot(
            onehot, table, preferred_element_type=jnp.float32
        )
        root_mean = jnp.sqrt(jnp.mean(hidden * hidden, axis=-1, keepdims=True) + epsilon)
        modulation = gain_row * (1.0 + 0.5 * jnp.sin(timestep * freq_row))
        normed = (hidden / root_mean * modulation[None, :]).astype(jnp.bfloat16)
        projected = jnp.dot(normed, weights, preferred_element_type=jnp.float32).astype(
            jnp.bfloat16
        )
        query_heads = projected[:, :q_cols].reshape(frames, heads_local, head_size)
        keyval_heads = projected[:, q_cols:].reshape(frames, kv_local, 2, head_size)
        head_outputs = []
        for head in range(heads_local):
            key_rows = keyval_heads[:, head // group_size, 0]
            value_rows = keyval_heads[:, head // group_size, 1]
            scores = (
                lax.dot_general(
                    query_heads[:, head],
                    key_rows,
                    (((1,), (1,)), ((), ())),
                    preferred_element_type=jnp.float32,
                )
                * score_scale
            )
            scores = scores + bias_local[head] * key_flags[None, :]
            row_max = jnp.max(scores, axis=-1, keepdims=True)
            exponent = jnp.exp(scores - row_max)
            probabilities = (exponent / jnp.sum(exponent, axis=-1, keepdims=True)).astype(
                jnp.bfloat16
            )
            head_outputs.append(
                jnp.dot(probabilities, value_rows, preferred_element_type=jnp.float32).astype(
                    jnp.bfloat16
                )
            )
        attended = jnp.concatenate(head_outputs, axis=1)
        hidden_local = lax.dynamic_slice_in_dim(current, seq_idx * q_cols, q_cols, 1).astype(
            jnp.float32
        ) + jnp.dot(onehot, table_local, preferred_element_type=jnp.float32)
        output = (hidden_local + gate_local[None, :] * attended.astype(jnp.float32)).astype(
            jnp.bfloat16
        )
        outputs.append(output)
        if step + lag < steps:
            piece = passed_along(output, "pipe", 1)
            handed[step + lag] = lax.all_gather(piece, "seq", axis=1, tiled=True)

    factor = float(turns * rep_count * frames) ** (-0.5)
    total = None
    rows_out = []
    for turn in range(turns):
        if lag == 2:
            own = jnp.where(section_idx == 0, outputs[turn], outputs[turn + 1])
        else:
            own = outputs[turn]
        term = lax.dot_general(
            own, cot_all[turn], (((0,), (0,)), ((), ())), preferred_element_type=jnp.float32
        )
        total = term if total is None else total + term
        rows_out.append(lax.all_to_all(own, "seq", split_axis=0, concat_axis=1, tiled=True))
    section_out = jnp.stack(rows_out)[None, :, None]
    grad_parts = lax.all_to_all(
        (total * factor).astype(jnp.bfloat16).reshape(rep_count, q_cols // rep_count, feat_count),
        "dp",
        split_axis=0,
        concat_axis=0,
        tiled=True,
    )
    grad_rows = jnp.sum(grad_parts.astype(jnp.float32), axis=0)
    return (section_out, grad_rows[None])


def solution(mesh):
    in_specs = (
        P("pipe", None, "dp", "seq", None),
        P(None, "dp", "seq"),
        P(None, "dp", None),
        P(None, "dp"),
        P("pipe", ("seq", "dp"), None),
        P("pipe", ("seq", "dp"), None),
        P("pipe", None),
        P("pipe", None),
        P("pipe", None, None),
        P("pipe", None),
        P("pipe", None),
        P("pipe", None, "dp", "seq", None),
    )
    out_specs = (P("pipe", None, "dp", "seq", None), P("pipe", ("seq", "dp"), None))
    return jax.shard_map(body, mesh=mesh, in_specs=in_specs, out_specs=out_specs, check_vma=False)
```

```python
import functools
import math

import jax
import jax.numpy as jnp
from jax import lax
from jax.experimental import pallas as pl
from jax.experimental.pallas import tpu as pltpu
from jax.sharding import PartitionSpec as P

epsilon = 1e-06


def passed_along(value, axis, steps):
    count = lax.axis_size(axis)
    first, last = (max(0, -steps), min(count, count - steps))
    return lax.ppermute(value, axis, [(source, source + steps) for source in range(first, last)])


def ring(value, axis):
    count = lax.axis_size(axis)
    return lax.ppermute(value, axis, [(source, (source + 1) % count) for source in range(count)])


def swap(value, bit, axis="seq"):
    count = lax.axis_size(axis)
    return lax.ppermute(value, axis, [(source, source ^ bit) for source in range(count)])


def handed_over(value):
    return lax.ppermute(value, "pipe", [(0, 1), (1, 0)])


def fold(index):
    return index ^ (index >> 1)


def ring_step(value):
    count = lax.axis_size("dp")
    pairs = [(fold(place), fold((place + 1) % count)) for place in range(count)]
    return lax.ppermute(value, "dp", pairs)


def offsets_of(count):
    offsets = [0]
    bit = count // 2
    while bit:
        offsets = offsets + [offset ^ bit for offset in offsets]
        bit //= 2
    return offsets


def turn_and_batch(step, turns):
    section = lax.axis_index("pipe")
    turn = jnp.clip(step - section, 0, turns - 1)
    return turn, turn - section + 1


def pack_kernel(wq, wkv, *refs):
    outs, (queries, keyvals, sems) = refs[:-3], refs[-3:]
    parts, _, cols = outs[0].shape
    half = cols // 2
    seq = lax.axis_index("seq")
    copies = []
    for m in range(len(outs)):
        start = pl.multiple_of((seq ^ m) * cols, 128)
        for k, (source, held) in enumerate(((wq, queries), (wkv, keyvals))):
            copies.append(
                pltpu.make_async_copy(
                    source.at[0, :, pl.ds(start, cols)], held.at[m], sems.at[2 * m + k]
                )
            )
    for copy in copies:
        copy.start()
    for m, out in enumerate(outs):
        copies[2 * m].wait()
        copies[2 * m + 1].wait()
        for part in range(parts):
            lanes = slice(part * half, (part + 1) * half)
            out[part] = jnp.concatenate([queries[m][:, lanes], keyvals[m][:, lanes]], axis=1)


def pair_kernel(deps, *refs):
    out = refs[-1]
    for at, ref in enumerate(refs[deps:-1]):
        out[at] = ref[...]


def part_kernel(part, near, far, out):
    for at in range(2):
        out[at] = near[at, part]
        out[at + 2] = far[at, part]


def place(hop, hops, blocks, weights):
    seq, rep = lax.axis_index("seq"), lax.axis_index("dp")
    for m, block in enumerate(blocks):
        rows = block.shape[0]
        at = (seq ^ m) * hops + fold(lax.rem(fold(rep) + hops - hop, hops))
        weights[pl.ds(pl.multiple_of(at * rows, 16), rows)] = block[...]


def place_kernel(part, hops, near, far, chunk, next_chunk, weights):
    place(0, hops, [near.at[0, part], near.at[1, part], far.at[0, part], far.at[1, part]], weights)
    place(1, hops, [chunk.at[m] for m in range(4)], weights)
    place(2, hops, [next_chunk.at[m] for m in range(4)], weights)


def first_kernel(turns, far, incoming, contacts, out, states):
    rows = incoming.shape[3]
    for turn in range(2):
        out[turn * rows : (turn + 1) * rows] = incoming[0, turn, 0]
    states[...] = jnp.zeros_like(states)
    for step in range(turns + 1):
        _, batch = turn_and_batch(step, turns)
        states[step : step + 1] = contacts[batch].astype(jnp.float32)
    out[2 * rows :, : states.shape[1]] = states[...].astype(jnp.bfloat16)


def second_kernel(dep, incoming, cotangent, out):
    turns, rows, feats = cotangent.shape[1], cotangent.shape[3], cotangent.shape[4]
    out[:rows] = incoming[0, 2, 0]
    for turn in range(turns):
        out[rows:, turn * feats : (turn + 1) * feats] = cotangent[0, turn, 0]


def columns_of(rows_of, pieces, rows):
    labels = lax.broadcasted_iota(jnp.int32, (32, rows), 0)
    columns = []
    for i in range(pieces):
        state, flag = rows_of(i)
        one = jnp.zeros((32, rows), jnp.float32)
        if state is not None:
            one = jnp.where(labels == state, 1.0, 0.0)
        if flag is not None:
            one = jnp.where(labels == 16, flag, one)
        columns.append(one.T)
    return jnp.concatenate(columns, axis=0)


def modulation(step, turns, times, gain, freq):
    _, batch = turn_and_batch(step, turns)
    return gain[...] * (1.0 + 0.5 * jnp.sin(times[0, batch].astype(jnp.float32) * freq[...]))


def norm_kernel(turns, pieces, times, table, gain, freq, *refs):
    sources, refs = refs[:pieces], refs[pieces:]
    scaled, scales, owns, embeds, mod = refs[0:2], refs[2:4], refs[4:6], refs[6:8], refs[8]
    first, sems = refs[9 : 9 + pieces], refs[9 + pieces]
    copies = [
        pltpu.make_async_copy(sources[i], first[i], sems.at[i]) for i in range(pieces)
    ]
    for copy in copies:
        copy.start()
    for copy in copies:
        copy.wait()
    frames, width = scaled[0].shape
    rows, cols = frames // pieces, owns[0].shape[1]
    seq = lax.axis_index("seq")
    offsets = offsets_of(pieces)
    for step in range(turns + 1):

        def state_of(i):
            state = first[i][2 * rows : 2 * rows + 16, :rows][step : step + 1]
            return state.astype(jnp.float32).astype(jnp.int32), None

        onehot = columns_of(state_of, pieces, rows)[:, : table.shape[1]].astype(jnp.bfloat16)
        if step >= 2:
            for at in range(0, width, 256):
                embeds[step - 2][:, at : at + 256] = jnp.dot(
                    onehot, table[0, :, at : at + 256], preferred_element_type=jnp.float32
                ).astype(jnp.bfloat16)
            continue
        turn, _ = turn_and_batch(step, turns)
        at = pl.multiple_of(jnp.minimum(turn, 1) * rows, 128)
        mod[...] = modulation(step, turns, times, gain, freq)
        total = jnp.zeros((frames, 128), jnp.float32)
        for i in range(pieces):
            lanes = pl.ds(pl.multiple_of((seq ^ offsets[i]) * cols, 128), cols)
            current = jnp.concatenate([first[p][pl.ds(at, rows), lanes] for p in range(pieces)])
            hidden = current.astype(jnp.float32) + jnp.dot(
                onehot, table[0, :, lanes], preferred_element_type=jnp.float32
            )
            for lane in range(0, cols, 128):
                piece = hidden[:, lane : lane + 128]
                total = total + piece * piece
            scaled[step][:, lanes] = (hidden * mod[:, lanes]).astype(jnp.bfloat16)
            if i == 0:
                owns[step][...] = hidden
        mean = jnp.sum(total, axis=1, keepdims=True) * (1.0 / width)
        scales[step][...] = jnp.broadcast_to(lax.rsqrt(mean + epsilon), (frames, 128))


def dense(value, lead):
    frames = value.shape[0]
    rest = value[:, :64] if lead else value[:, 128:]
    full = value[:, 64:] if lead else value[:, :128]
    rest = jnp.concatenate([rest[: frames // 2], rest[frames // 2 :]], axis=1)
    return jnp.concatenate([full, rest], axis=0)


def undense(left, right, frames):
    middle = []
    for ref in (left, right):
        rest = ref[frames:]
        middle.append(jnp.concatenate([rest[:, :64], rest[:, 64:]], axis=0))
    return jnp.concatenate([left[:frames], jnp.concatenate(middle, axis=1), right[:frames]], axis=1)


def second_pair_kernel(dep, mine, across, out):
    out[0] = mine[...]
    out[1] = across[...]


def opened(pieces):
    return list(pieces[:2]) + [pieces[2].at[0], pieces[2].at[1]]


def step_kernel(cfg, *refs):
    step, has_relay, parts = cfg["step"], cfg["has_relay"], cfg["parts"]
    pieces, hops, head, turns = cfg["pieces"], cfg["hops"], cfg["head"], cfg["turns"]
    heads, group = cfg["heads"], cfg["group"]
    refs = list(refs)

    def take(count):
        taken, refs[:count] = refs[:count], []
        return taken

    bias, times, gain, freq, gate, flags = take(6)
    if has_relay:
        second, embed, relay = opened(take(3)), take(1)[0], take(2 * pieces)
    else:
        scaled, scales, own_hidden = take(3)
    chunks = take(1) if step == 0 else None
    weights = take(len(parts))
    left = take(1)[0] if parts == (1,) else None
    sends = take(1)[0] if len(parts) == 1 else None
    out = take(1)[0]
    if step == 0:
        weights = take(1)
    proj, att = take(2)
    if has_relay:
        scaled, scales, own_hidden, mod = take(4)
    offsets = offsets_of(pieces)
    frames, width = scaled.shape
    cols = att.shape[0]
    half = cols // 2
    rows = frames // pieces
    seq, section = lax.axis_index("seq"), lax.axis_index("pipe")
    _, batch = turn_and_batch(step, turns)

    if step == 0:
        place(hops - 1, hops, [chunks[0].at[m] for m in range(pieces)], weights[0])

    def normalize(relayed):
        total = jnp.zeros((frames, 128), jnp.float32)
        for i in range(pieces):
            lanes = pl.ds(pl.multiple_of((seq ^ offsets[i]) * cols, 128), cols)
            if relayed:
                value = undense(relay[i], relay[pieces + i], frames)
                order = [offsets.index(offsets[i] ^ offsets[p]) for p in range(pieces)]
                blocks = [value[j * rows : (j + 1) * rows] for j in order]
            else:
                blocks = [second[p][:rows, lanes] for p in range(pieces)]
            hidden = jnp.concatenate(blocks, axis=0).astype(jnp.float32)
            hidden = hidden + embed[:, lanes].astype(jnp.float32)
            for lane in range(0, cols, 128):
                piece = hidden[:, lane : lane + 128]
                total = total + piece * piece
            scaled[:, lanes] = (hidden * mod[:, lanes]).astype(jnp.bfloat16)
            if i == 0:
                own_hidden[...] = hidden
        scales[...] = total

    if has_relay:
        mod[...] = modulation(step, turns, times, gain, freq)

        @pl.when(section == 0)
        def _():
            normalize(False)

        @pl.when(section != 0)
        def _():
            normalize(True)

        mean = jnp.sum(scales[...], axis=1, keepdims=True) * (1.0 / width)
        scale = lax.rsqrt(mean + epsilon)
    else:
        scale = scales[:, :1]

    def flag_of(i):
        lanes = pl.ds(pl.multiple_of((seq ^ offsets[i]) * rows, 128), rows)
        return None, flags[batch, :, lanes].astype(jnp.float32)

    flag_column = columns_of(flag_of, pieces, rows)[:, 16:17]
    score_scale = head ** (-0.5) * math.log2(math.e)
    lanes = lax.broadcasted_iota(jnp.int32, (frames, 128), 1)
    row_lanes = lax.broadcasted_iota(jnp.int32, (1, 128), 1)
    flag_lanes = jnp.logical_or(lanes == head, lanes == head + 1)
    pitch = cols + 128

    for k, part in enumerate(parts):
        base = k * pitch
        for at in range(0, cols, 256):
            size = min(256, cols - at)
            lane = at + lax.broadcasted_iota(jnp.int32, (1, size), 1)
            factor = jnp.where(lane < half, score_scale, 1.0)
            projected = jnp.dot(
                scaled[...], weights[k][:, at : at + size], preferred_element_type=jnp.float32
            )
            proj[:, base + at : base + at + size] = (projected * scale * factor).astype(
                jnp.bfloat16
            )
        proj[:, base + cols : base + pitch] = jnp.zeros((frames, 128), jnp.bfloat16)

    def slice_of(at):
        return proj[:, at : at + 128].astype(jnp.float32)

    keys, values = [], []
    for k in range(len(parts)):
        at = k * pitch + half
        key = jnp.where(flag_lanes, flag_column, jnp.where(lanes < head, slice_of(at), 0.0))
        value = jnp.where(
            lanes < head, slice_of(at + head), jnp.where(lanes == head, 1.0, 0.0)
        )
        keys.append(key.astype(jnp.bfloat16))
        values.append(value.T.astype(jnp.bfloat16))

    def scores_of(k, h):
        strength = bias[0, seq * heads + parts[k] * group + h] * math.log2(math.e)
        strength = jnp.zeros((1, 128), jnp.float32) + strength
        coarse = strength.astype(jnp.bfloat16).astype(jnp.float32)
        tail = jnp.where(
            row_lanes == head, coarse, jnp.where(row_lanes == head + 1, strength - coarse, 0.0)
        )
        query = jnp.where(lanes < head, slice_of(k * pitch + h * head), tail).astype(jnp.bfloat16)
        return lax.dot_general(
            keys[k], query, (((1,), (1,)), ((), ())), preferred_element_type=jnp.float32
        )

    tasks = [(k, h) for k in range(len(parts)) for h in range(group)]
    scores = scores_of(*tasks[0])
    for index, (k, h) in enumerate(tasks):
        ahead = scores_of(*tasks[index + 1]) if index + 1 < len(tasks) else None
        top = jnp.max(scores, axis=0, keepdims=True)
        weight = jnp.exp2(scores - top).astype(jnp.bfloat16)
        mixed = jnp.dot(values[k], weight, preferred_element_type=jnp.float32)
        at = (parts[k] * group + h) * head
        att[at : at + head, :] = mixed[:head] * (1.0 / mixed[head : head + 1])
        scores = ahead
    gates = gate[:, pl.ds(pl.multiple_of(seq * cols, 128), cols)]
    first, last = parts[0] * half, (parts[-1] + 1) * half
    attended = att[first:last].T.astype(jnp.bfloat16).astype(jnp.float32)
    output = own_hidden[...][:, first:last] + gates[:, first:last] * attended
    if parts == (0,):
        out[:, :half] = output.astype(jnp.bfloat16)
    elif parts == (1,):
        output_both = jnp.concatenate([left[:, :half].astype(jnp.float32), output], axis=1)
        out[...] = output_both.astype(jnp.bfloat16).reshape(pieces, rows, cols)
    else:
        out[...] = output.astype(jnp.bfloat16).reshape(pieces, rows, cols)
    if sends is not None:
        sends[...] = dense(output, parts == (1,)).astype(jnp.bfloat16)


def tie_kernel(*refs):
    pass


def grad_of(output, second, turn, rows, feats):
    cot = jnp.concatenate(
        [piece[rows : 2 * rows, turn * feats : (turn + 1) * feats] for piece in second], axis=0
    )
    return lax.dot_general(
        output, cot, (((0,), (0,)), ((), ())), preferred_element_type=jnp.float32
    )


def early_kernel(turns, pieces, halves, feats, *refs):
    outs, second = refs[: turns * halves], opened(refs[turns * halves : turns * halves + 3])
    sends, grad = refs[turns * halves + 3 : -1], refs[-1]
    section = lax.axis_index("pipe")
    offsets = offsets_of(pieces)
    part = pieces // halves
    rows = outs[0].shape[1]
    total = None
    for turn in range(turns - 1):
        blocks = []
        for p in range(pieces):
            k, j = p // part, p % part
            block = jnp.where(
                section == 0, outs[turn * halves + k][j], outs[(turn + 1) * halves + k][j]
            )
            sends[offsets[p]][turn] = block
            blocks.append(block)
        share = grad_of(jnp.concatenate(blocks, axis=0), second, turn, rows, feats)
        total = share if total is None else total + share
    grad[...] = total


def settle_kernel(turns, pieces, halves, hops, feats, *refs):
    refs = list(refs)

    def take(count):
        taken, refs[:count] = refs[:count], []
        return taken

    before, now, second, early = take(halves), take(halves), opened(take(3)), take(pieces - 1)
    early_grad = take(1)[0]
    late, own_grad, grads = take(pieces), take(1)[0], take(hops - 1)
    section_out = take(1)[0]
    rows_out, total, sem = take(3)
    section, seq, rep = lax.axis_index("pipe"), lax.axis_index("seq"), lax.axis_index("dp")
    offsets = offsets_of(pieces)
    part = pieces // halves
    rows, cols = early[0].shape[1:]
    for m in range(pieces - 1):
        lanes = pl.ds(pl.multiple_of((seq ^ m) * cols, 128), cols)
        for turn in range(turns - 1):
            rows_out[turn, :, lanes] = early[m][turn]
    copy = pltpu.make_async_copy(rows_out, section_out.at[pl.ds(0, turns - 1)], sem)
    copy.start()
    blocks = []
    for p in range(pieces):
        block = jnp.where(section == 0, before[p // part][p % part], now[p // part][p % part])
        late[offsets[p]][...] = block
        blocks.append(block)
    share = grad_of(jnp.concatenate(blocks, axis=0), second, turns - 1, rows, feats)
    factor = float(turns * hops * rows * pieces) ** (-0.5)
    total[...] = (share + early_grad[...]) * factor
    g_rows = cols // hops
    own_grad[...] = total[pl.ds(pl.multiple_of(rep * g_rows, 8), g_rows)]
    for shift in range(1, hops):
        at = pl.multiple_of((rep ^ shift) * g_rows, 8)
        grads[shift - 1][...] = total[pl.ds(at, g_rows)].astype(jnp.bfloat16)
    copy.wait()


def finish_kernel(pieces, hops, *refs):
    held, early, late, refs = refs[0], refs[1], refs[2 : pieces + 2], refs[pieces + 2 :]
    own_grad, parts, (section_out, grad, row_out, sems) = refs[0], refs[1:hops], refs[hops:]
    seq = lax.axis_index("seq")
    cols = late[0].shape[1]
    last_lanes = pl.ds(pl.multiple_of((seq ^ (pieces - 1)) * cols, 128), cols)
    early_copy = pltpu.make_async_copy(
        early, section_out.at[pl.ds(0, early.shape[0]), :, last_lanes], sems.at[0]
    )
    early_copy.start()
    for m in range(pieces):
        lanes = pl.ds(pl.multiple_of((seq ^ m) * cols, 128), cols)
        row_out[:, lanes] = late[m][...]
    copy = pltpu.make_async_copy(row_out, section_out.at[section_out.shape[0] - 1], sems.at[1])
    copy.start()
    total = own_grad[...]
    for part in parts:
        total = total + part[...].astype(jnp.float32)
    grad[...] = total
    early_copy.wait()
    copy.wait()


MIB = 1024 * 1024


def paired_body(
    incoming,
    contacts,
    keyframes,
    timesteps,
    w_query,
    w_keyval,
    norm_gain,
    time_freq,
    contact_table,
    key_bias,
    attn_gate,
    head_cotangent,
):
    seq_count = lax.axis_size("seq")
    hops = lax.axis_size("dp")
    rows, width, turns = incoming.shape[3], incoming.shape[4], incoming.shape[1]
    frames = rows * seq_count
    heads_all = key_bias.shape[1]
    head = width // heads_all
    heads = heads_all // seq_count
    kv_heads = w_keyval.shape[2] // (2 * head * seq_count)
    feats = head_cotangent.shape[4]
    cols = width // seq_count
    w_rows = w_query.shape[1]
    kind = jnp.bfloat16
    smem = pl.BlockSpec(memory_space=pltpu.SMEM)
    vmem = pl.BlockSpec(memory_space=pltpu.VMEM)
    anywhere = pl.BlockSpec(memory_space=pl.ANY)
    shape = jax.ShapeDtypeStruct

    def call(kernel, name, out_shape, in_specs, operands, scratch=(), limit=4, flops=0, **options):
        return pl.pallas_call(
            kernel,
            out_shape=out_shape,
            in_specs=in_specs,
            scratch_shapes=list(scratch),
            compiler_params=pltpu.CompilerParams(vmem_limit_bytes=limit * MIB),
            cost_estimate=pl.CostEstimate(
                flops=flops, bytes_accessed=flops // 512, transcendentals=0
            ),
            name=name,
            **options,
        )(*operands)

    timesteps = timesteps.reshape(1, timesteps.shape[0])

    def pin(value, space=pltpu.VMEM):
        return pltpu.with_memory_space_constraint(value, space)

    packed = call(
        pack_kernel,
        "pack",
        [pltpu.VMEM((2, w_rows, cols), kind)] * seq_count,
        [anywhere, anywhere],
        [pin(w_query, pltpu.HBM), pin(w_keyval, pltpu.HBM)],
        [pltpu.VMEM((seq_count, w_rows, cols), kind)] * 2
        + [pltpu.SemaphoreType.DMA((2 * seq_count,))],
        out_specs=[vmem] * seq_count,
    )
    blocks = [packed[0]] + [swap(packed[m], m) for m in range(1, seq_count)]

    def paired(name, deps, values):
        return call(
            functools.partial(pair_kernel, len(deps)),
            name,
            pltpu.VMEM((2, 2, w_rows, cols), kind),
            [anywhere] * len(deps) + [vmem] * 2,
            deps + values,
            out_specs=vmem,
        )

    near = paired("near", [], blocks[:2])
    near_next = ring_step(near)
    far = paired("far", [near_next], blocks[2:])
    far_next = ring_step(far)
    rings = []
    for part in range(2):
        chunk = call(
            functools.partial(part_kernel, part),
            "part%d" % part,
            pltpu.VMEM((seq_count, w_rows, cols), kind),
            [vmem, vmem],
            [near_next, far_next],
            out_specs=vmem,
        )
        rings.append([chunk])
    for ring in rings:
        ring.append(ring_step(ring[-1]))
    rings[0].append(ring_step(rings[0][-1]))

    def tie(values, deps):
        return call(
            tie_kernel,
            "tie",
            [shape(value.shape, kind) for value in values],
            [anywhere] * (len(values) + len(deps)),
            list(values) + list(deps),
            out_specs=[anywhere] * len(values),
            input_output_aliases={i: i for i in range(len(values))},
        )

    mine = call(
        functools.partial(first_kernel, turns),
        "first",
        pltpu.VMEM((2 * rows + 16, width), kind),
        [anywhere, vmem, vmem],
        [far, incoming, contacts],
        [pltpu.VMEM((16, 128), jnp.float32)],
        out_specs=vmem,
    )
    across = swap(mine, 2)
    beside = swap(mine, 1)
    (across,) = tie([across], [ring[1] for ring in rings])
    first = [mine, across, beside, swap(across, 1)]
    prepared = call(
        functools.partial(norm_kernel, turns, seq_count),
        "norm",
        [pltpu.VMEM((frames, width), kind)] * 2
        + [pltpu.VMEM((frames, 128), jnp.float32)] * 2
        + [pltpu.VMEM((frames, cols), jnp.float32)] * 2
        + [pltpu.VMEM((frames, width), kind)] * 2,
        [smem] + [vmem] * 3 + [anywhere] * seq_count,
        [timesteps, contact_table, norm_gain, time_freq]
        + first,
        [pltpu.VMEM((1, width), jnp.float32)]
        + [pltpu.VMEM((2 * rows + 16, width), kind)] * seq_count
        + [pltpu.SemaphoreType.DMA((seq_count,))],
        12,
        out_specs=[vmem] * 8,
    )

    mine = call(
        second_kernel,
        "second",
        pltpu.VMEM((2 * rows, width), kind),
        [anywhere, vmem, vmem],
        [across, incoming, head_cotangent],
        out_specs=vmem,
    )
    second = [mine, swap(mine, 2)]

    (rings[1][1],) = tie([rings[1][1]], [prepared[0]])
    rings[1].append(ring_step(rings[1][1]))
    partial = []
    for part, ring in enumerate(rings):
        partial.append(
            call(
                functools.partial(place_kernel, part, hops),
                "place%d" % part,
                pltpu.VMEM((width, cols), kind),
                [vmem] * 4,
                [pin(near), pin(far), pin(ring[0]), pin(ring[1])],
                out_specs=vmem,
            )
        )

    common = [key_bias, timesteps, norm_gain, time_freq, attn_gate, keyframes]

    def run_step(step, parts, large, out_shape, aliases):
        cfg = {
            "step": step,
            "has_relay": step >= 2,
            "parts": parts,
            "pieces": seq_count,
            "hops": hops,
            "head": head,
            "heads": heads,
            "group": heads // kv_heads,
            "turns": turns,
        }
        scratch = [
            pltpu.VMEM((frames, len(parts) * (cols + 128)), kind),
            pltpu.VMEM((cols, frames), jnp.float32),
        ]
        if step >= 2:
            scratch += [
                pltpu.VMEM((frames, width), kind),
                pltpu.VMEM((frames, 128), jnp.float32),
                pltpu.VMEM((frames, cols), jnp.float32),
                pltpu.VMEM((1, width), jnp.float32),
            ]
        operands = common + [pin(value) for value in large]
        return call(
            functools.partial(step_kernel, cfg),
            "step%d%s" % (step, "".join("ab"[part] for part in parts)),
            out_shape,
            [smem, smem] + [vmem] * (len(operands) - 2),
            operands,
            scratch,
            16,
            len(parts) * frames * (2 * width * cols + 2 * heads * frames * head),
            out_specs=[vmem] * len(out_shape),
            input_output_aliases=aliases,
        )

    whole = pltpu.VMEM((seq_count, rows, cols), kind)
    sent = pltpu.VMEM((frames * 3 // 2, 128), kind)
    weights = list(partial)
    relays, lefts, outputs = ([], []), [], []
    for part in range(2):
        for step in range(2):
            large = [prepared[step], prepared[2 + step], prepared[4 + step]]
            if step == 0:
                chunks = rings[part][2:]
                if part:
                    chunks = list(tie(chunks, [relays[0][0][0], lefts[1]]))
                large += chunks
            large += [weights[part]]
            aliases = {len(common) + len(large) - 1: 2} if step == 0 else {}
            out_shape = [sent, whole if part else pltpu.VMEM((frames, 256), kind)]
            if step == 0:
                out_shape += [pltpu.VMEM((width, cols), kind)]
            if part:
                large += [lefts[step]]
            results = run_step(step, (part,), large, out_shape, aliases)
            if step == 0:
                weights[part] = results[2]
            (outputs if part else lefts).append(results[1])
            piece = handed_over(results[0])
            relays[step].append([piece, None if part and not step else swap(piece, 2)])
    beside = call(
        second_pair_kernel,
        "beside",
        pltpu.VMEM((2,) + second[0].shape, kind),
        [anywhere, vmem, vmem],
        [outputs[0]] + second,
        limit=8,
        out_specs=vmem,
    )
    second = [second[0], second[1], swap(beside, 1)]

    (piece,) = tie([relays[0][1][0]], [outputs[1], second[2]])
    relays[0][1] = [piece, swap(piece, 2)]
    def complete(crossing):
        return [
            piece
            for mine, across in crossing
            for piece in (mine, across, swap(mine, 1), swap(across, 1))
        ]

    relay = complete(relays[0])
    (output,) = run_step(2, (0, 1), second + [prepared[6]] + relay + weights, [whole], {})
    outputs.append(output)
    early = call(
        functools.partial(early_kernel, turns, seq_count, 1, feats),
        "early",
        [shape((turns - 1, rows, cols), kind)] * seq_count + [shape((cols, feats), jnp.float32)],
        [vmem] * (turns + len(second)),
        outputs + second,
        limit=8,
        out_specs=[vmem] * (seq_count + 1),
    )
    early, early_grad = list(early[:-1]), early[-1]
    early = [early[0]] + [swap(early[m], m) for m in range(1, seq_count)]
    tied = tie([piece for pair in relays[1] for piece in pair], [early_grad])
    relay = complete([(tied[0], tied[1]), (tied[2], tied[3])])
    (output,) = run_step(3, (0, 1), second + [prepared[7]] + relay + weights, [whole], {})
    outputs.append(output)

    g_shape = (cols // hops, feats)
    operands = outputs[-2:] + second + early[:-1] + [early_grad]
    settled = call(
        functools.partial(settle_kernel, turns, seq_count, 1, hops, feats),
        "settle",
        [shape((rows, cols), kind)] * seq_count
        + [shape(g_shape, jnp.float32)]
        + [shape(g_shape, kind)] * (hops - 1)
        + [shape((turns, rows, width), kind)],
        [vmem] * len(operands),
        operands,
        [
            pltpu.VMEM((turns - 1, rows, width), kind),
            pltpu.VMEM((cols, feats), jnp.float32),
            pltpu.SemaphoreType.DMA,
        ],
        8,
        out_specs=[vmem] * (seq_count + hops) + [anywhere],
    )
    late, grads, held = settled[:seq_count], settled[seq_count:-1], settled[-1]
    late = [late[0]] + [swap(late[m], m) for m in range(1, seq_count)]
    grads = [grads[0]] + [swap(grads[k], k, "dp") for k in range(1, hops)]
    section_out, grad_rows = call(
        functools.partial(finish_kernel, seq_count, hops),
        "finish",
        [shape((turns, rows, width), kind), shape(g_shape, jnp.float32)],
        [anywhere] + [vmem] * (seq_count + hops + 1),
        [held, early[-1]] + late + grads,
        [pltpu.VMEM((rows, width), kind), pltpu.SemaphoreType.DMA((2,))],
        out_specs=[anywhere, vmem],
        input_output_aliases={0: 0},
    )
    return (section_out[None, :, None], grad_rows[None])


def body(incoming, contacts, keyframes, timesteps, w_query, *others):
    count = lax.axis_size("seq")
    cols = w_query.shape[2] // count
    paired = (
        lax.axis_size("pipe") == 2
        and lax.axis_size("dp") == 4
        and count == 4
        and cols % 128 == 0
        and w_query.shape[1] % 16 == 0
        and incoming.shape[3] == 128
        and incoming.shape[1] == 3
    )
    chosen = paired_body if paired else general_body
    return chosen(incoming, contacts, keyframes, timesteps, w_query, *others)


def general_body(
    incoming,
    contacts,
    keyframes,
    timesteps,
    w_query,
    w_keyval,
    norm_gain,
    time_freq,
    contact_table,
    key_bias,
    attn_gate,
    head_cotangent,
):
    section_idx = lax.axis_index("pipe")
    seq_idx = lax.axis_index("seq")
    rep_idx = lax.axis_index("dp")
    seq_count = lax.axis_size("seq")
    section_count = lax.axis_size("pipe")
    rep_count = lax.axis_size("dp")
    tok_rows = incoming.shape[3]
    width = incoming.shape[4]
    turns = incoming.shape[1]
    frames = tok_rows * seq_count
    heads_all = key_bias.shape[1]
    head_size = width // heads_all
    heads_local = heads_all // seq_count
    kv_width = w_keyval.shape[2]
    kv_local = kv_width // (2 * head_size * seq_count)
    group_size = heads_local // kv_local
    feat_count = head_cotangent.shape[4]
    score_scale = head_size ** (-0.5)
    q_cols = width // seq_count
    kv_cols = kv_width // seq_count
    w_rows = w_query.shape[1]

    w_parts = jnp.concatenate(
        [
            w_query[0].reshape(w_rows, seq_count, q_cols),
            w_keyval[0].reshape(w_rows, seq_count, kv_cols),
        ],
        axis=2,
    ).transpose(1, 0, 2)
    block = lax.all_to_all(w_parts, "seq", split_axis=0, concat_axis=0, tiled=True)
    weights = jnp.zeros((seq_count, rep_count, w_rows, q_cols + kv_cols), jnp.bfloat16)
    for hop in range(rep_count):
        owner = lax.rem(rep_idx + rep_count - hop, rep_count)
        weights = lax.dynamic_update_slice_in_dim(weights, block[:, None], owner, 1)
        if hop + 1 < rep_count:
            block = ring(block, "dp")
    weights = weights.reshape(width, q_cols + kv_cols)

    gain_row = norm_gain[0]
    freq_row = time_freq[0]
    table = contact_table[0]
    gate_local = lax.dynamic_slice_in_dim(attn_gate[0], seq_idx * q_cols, q_cols)
    table_local = lax.dynamic_slice_in_dim(table, seq_idx * q_cols, q_cols, 1)
    bias_local = lax.dynamic_slice_in_dim(key_bias[0], seq_idx * heads_local, heads_local)
    contact_all = lax.all_gather(contacts[:, 0, :], "seq", axis=1, tiled=True)
    key_all = keyframes[:, 0, :]
    step_all = timesteps[:, 0]
    labels = jnp.arange(table.shape[0], dtype=jnp.int32)
    cot_all = lax.all_gather(head_cotangent[0, :, 0], "seq", axis=1, tiled=True)

    lag = 2 if section_count == 2 else 1
    if lag == 2:
        steps = turns + 1
    else:
        steps = turns

    def turn_at(step):
        if lag == 1:
            return jnp.int32(step)
        return jnp.clip(step - section_idx, 0, turns - 1)

    outputs = []
    handed = {}
    for step in range(steps):
        turn = turn_at(step)
        fresh = lax.dynamic_index_in_dim(incoming[0, :, 0], turn, 0, keepdims=False)
        current = lax.all_gather(fresh, "seq", axis=0, tiled=True)
        if step in handed:
            current = jnp.where((section_idx == 0) | (turn == 0), current, handed[step])
        batch_idx = turn - section_idx + section_count - 1
        contact_rows = lax.dynamic_index_in_dim(contact_all, batch_idx, 0, keepdims=False)
        key_flags = lax.dynamic_index_in_dim(key_all, batch_idx, 0, keepdims=False).astype(
            jnp.float32
        )
        timestep = lax.dynamic_index_in_dim(step_all, batch_idx, 0, keepdims=False).astype(
            jnp.float32
        )
        onehot = (contact_rows[:, None] == labels[None, :]).astype(jnp.bfloat16)
        hidden = current.astype(jnp.float32) + jnp.dot(
            onehot, table, preferred_element_type=jnp.float32
        )
        root_mean = jnp.sqrt(jnp.mean(hidden * hidden, axis=-1, keepdims=True) + epsilon)
        modulation = gain_row * (1.0 + 0.5 * jnp.sin(timestep * freq_row))
        normed = (hidden / root_mean * modulation[None, :]).astype(jnp.bfloat16)
        projected = jnp.dot(normed, weights, preferred_element_type=jnp.float32).astype(
            jnp.bfloat16
        )
        query_heads = projected[:, :q_cols].reshape(frames, heads_local, head_size)
        keyval_heads = projected[:, q_cols:].reshape(frames, kv_local, 2, head_size)
        head_outputs = []
        for head in range(heads_local):
            key_rows = keyval_heads[:, head // group_size, 0]
            value_rows = keyval_heads[:, head // group_size, 1]
            scores = (
                lax.dot_general(
                    query_heads[:, head],
                    key_rows,
                    (((1,), (1,)), ((), ())),
                    preferred_element_type=jnp.float32,
                )
                * score_scale
            )
            scores = scores + bias_local[head] * key_flags[None, :]
            row_max = jnp.max(scores, axis=-1, keepdims=True)
            exponent = jnp.exp(scores - row_max)
            probabilities = (exponent / jnp.sum(exponent, axis=-1, keepdims=True)).astype(
                jnp.bfloat16
            )
            head_outputs.append(
                jnp.dot(probabilities, value_rows, preferred_element_type=jnp.float32).astype(
                    jnp.bfloat16
                )
            )
        attended = jnp.concatenate(head_outputs, axis=1)
        hidden_local = lax.dynamic_slice_in_dim(current, seq_idx * q_cols, q_cols, 1).astype(
            jnp.float32
        ) + jnp.dot(onehot, table_local, preferred_element_type=jnp.float32)
        output = (hidden_local + gate_local[None, :] * attended.astype(jnp.float32)).astype(
            jnp.bfloat16
        )
        outputs.append(output)
        if step + lag < steps:
            piece = passed_along(output, "pipe", 1)
            handed[step + lag] = lax.all_gather(piece, "seq", axis=1, tiled=True)

    factor = float(turns * rep_count * frames) ** (-0.5)
    total = None
    rows_out = []
    for turn in range(turns):
        if lag == 2:
            own = jnp.where(section_idx == 0, outputs[turn], outputs[turn + 1])
        else:
            own = outputs[turn]
        term = lax.dot_general(
            own, cot_all[turn], (((0,), (0,)), ((), ())), preferred_element_type=jnp.float32
        )
        total = term if total is None else total + term
        rows_out.append(lax.all_to_all(own, "seq", split_axis=0, concat_axis=1, tiled=True))
    section_out = jnp.stack(rows_out)[None, :, None]
    grad_parts = lax.all_to_all(
        (total * factor).astype(jnp.bfloat16).reshape(rep_count, q_cols // rep_count, feat_count),
        "dp",
        split_axis=0,
        concat_axis=0,
        tiled=True,
    )
    grad_rows = jnp.sum(grad_parts.astype(jnp.float32), axis=0)
    return (section_out, grad_rows[None])


def solution(mesh):
    in_specs = (
        P("pipe", None, "dp", "seq", None),
        P(None, "dp", "seq"),
        P(None, "dp", None),
        P(None, "dp"),
        P("pipe", ("seq", "dp"), None),
        P("pipe", ("seq", "dp"), None),
        P("pipe", None),
        P("pipe", None),
        P("pipe", None, None),
        P("pipe", None),
        P("pipe", None),
        P("pipe", None, "dp", "seq", None),
    )
    out_specs = (P("pipe", None, "dp", "seq", None), P("pipe", ("seq", "dp"), None))
    return jax.shard_map(body, mesh=mesh, in_specs=in_specs, out_specs=out_specs, check_vma=False)
```

```python
import functools
import math

import jax
import jax.numpy as jnp
from jax import lax
from jax.experimental import pallas as pl
from jax.experimental.pallas import tpu as pltpu
from jax.sharding import PartitionSpec as P

epsilon = 1e-06


def passed_along(value, axis, steps):
    count = lax.axis_size(axis)
    first, last = (max(0, -steps), min(count, count - steps))
    return lax.ppermute(value, axis, [(source, source + steps) for source in range(first, last)])


def ring(value, axis):
    count = lax.axis_size(axis)
    return lax.ppermute(value, axis, [(source, (source + 1) % count) for source in range(count)])


def swap(value, bit):
    count = lax.axis_size("seq")
    return lax.ppermute(value, "seq", [(source, source ^ bit) for source in range(count)])


def handed_over(value):
    return lax.ppermute(value, "pipe", [(0, 1), (1, 0)])


def shifted(value, axis, shift):
    count = lax.axis_size(axis)
    return lax.ppermute(value, axis, [(source, (source + shift) % count) for source in range(count)])


def fold(index):
    return index ^ (index >> 1)


def ring_step(value):
    count = lax.axis_size("dp")
    pairs = [(fold(place), fold((place + 1) % count)) for place in range(count)]
    return lax.ppermute(value, "dp", pairs)


def offsets_of(count):
    offsets = [0]
    bit = count // 2
    while bit:
        offsets = offsets + [offset ^ bit for offset in offsets]
        bit //= 2
    return offsets


def turn_and_batch(step, turns):
    section = lax.axis_index("pipe")
    turn = jnp.clip(step - section, 0, turns - 1)
    return turn, turn - section + 1


def pack_kernel(wq, wkv, *refs):
    outs, (queries, keyvals, sems) = refs[:-3], refs[-3:]
    parts, _, cols = outs[0].shape
    half = cols // 2
    seq = lax.axis_index("seq")
    copies = []
    for m in range(len(outs)):
        start = pl.multiple_of((seq ^ m) * cols, 128)
        for k, (source, held) in enumerate(((wq, queries), (wkv, keyvals))):
            copies.append(
                pltpu.make_async_copy(
                    source.at[0, :, pl.ds(start, cols)], held.at[m], sems.at[2 * m + k]
                )
            )
    for copy in copies:
        copy.start()
    for m, out in enumerate(outs):
        copies[2 * m].wait()
        copies[2 * m + 1].wait()
        for part in range(parts):
            lanes = slice(part * half, (part + 1) * half)
            out[part] = jnp.concatenate([queries[m][:, lanes], keyvals[m][:, lanes]], axis=1)


def pair_kernel(deps, *refs):
    out = refs[-1]
    for at, ref in enumerate(refs[deps:-1]):
        out[at] = ref[...]


def part_kernel(part, near, far, out):
    for at in range(2):
        out[at] = near[at, part]
        out[at + 2] = far[at, part]


def place(hop, hops, blocks, weights):
    seq, rep = lax.axis_index("seq"), lax.axis_index("dp")
    for m, block in enumerate(blocks):
        rows = block.shape[0]
        at = (seq ^ m) * hops + fold(lax.rem(fold(rep) + hops - hop, hops))
        weights[pl.ds(pl.multiple_of(at * rows, 16), rows)] = block[...]


def place_kernel(part, hops, near, far, chunk, weights):
    place(0, hops, [near.at[0, part], near.at[1, part], far.at[0, part], far.at[1, part]], weights)
    place(1, hops, [chunk.at[m] for m in range(4)], weights)


def first_kernel(turns, far, incoming, contacts, out, states):
    rows = incoming.shape[3]
    for turn in range(2):
        out[turn * rows : (turn + 1) * rows] = incoming[0, turn, 0]
    states[...] = jnp.zeros_like(states)
    for step in range(turns + 1):
        _, batch = turn_and_batch(step, turns)
        states[step : step + 1] = contacts[batch].astype(jnp.float32)
    out[2 * rows :, : states.shape[1]] = states[...].astype(jnp.bfloat16)


def second_kernel(dep, incoming, cotangent, out):
    turns, rows, feats = cotangent.shape[1], cotangent.shape[3], cotangent.shape[4]
    out[:rows] = incoming[0, 2, 0]
    for turn in range(turns):
        out[rows:, turn * feats : (turn + 1) * feats] = cotangent[0, turn, 0]


def columns_of(rows_of, pieces, rows):
    labels = lax.broadcasted_iota(jnp.int32, (32, rows), 0)
    columns = []
    for i in range(pieces):
        state, flag = rows_of(i)
        one = jnp.zeros((32, rows), jnp.float32)
        if state is not None:
            one = jnp.where(labels == state, 1.0, 0.0)
        if flag is not None:
            one = jnp.where(labels == 16, flag, one)
        columns.append(one.T)
    return jnp.concatenate(columns, axis=0)


def modulation(step, turns, times, gain, freq):
    _, batch = turn_and_batch(step, turns)
    return gain[...] * (1.0 + 0.5 * jnp.sin(times[0, batch].astype(jnp.float32) * freq[...]))


def norm_kernel(turns, pieces, times, table, gain, freq, *refs):
    sources, refs = refs[:pieces], refs[pieces:]
    scaled, scales, owns, embeds, mod = refs[0:2], refs[2:4], refs[4:6], refs[6:8], refs[8]
    first, sems = refs[9 : 9 + pieces], refs[9 + pieces]
    copies = [
        pltpu.make_async_copy(sources[i], first[i], sems.at[i]) for i in range(pieces)
    ]
    for copy in copies:
        copy.start()
    for copy in copies:
        copy.wait()
    frames, width = scaled[0].shape
    rows, cols = frames // pieces, owns[0].shape[1]
    seq = lax.axis_index("seq")
    offsets = offsets_of(pieces)
    for step in range(turns + 1):

        def state_of(i):
            state = first[i][2 * rows : 2 * rows + 16, :rows][step : step + 1]
            return state.astype(jnp.float32).astype(jnp.int32), None

        onehot = columns_of(state_of, pieces, rows)[:, : table.shape[1]].astype(jnp.bfloat16)
        if step >= 2:
            for at in range(0, width, 256):
                embeds[step - 2][:, at : at + 256] = jnp.dot(
                    onehot, table[0, :, at : at + 256], preferred_element_type=jnp.float32
                ).astype(jnp.bfloat16)
            continue
        turn, _ = turn_and_batch(step, turns)
        at = pl.multiple_of(jnp.minimum(turn, 1) * rows, 128)
        mod[...] = modulation(step, turns, times, gain, freq)
        total = jnp.zeros((frames, 128), jnp.float32)
        for i in range(pieces):
            lanes = pl.ds(pl.multiple_of((seq ^ offsets[i]) * cols, 128), cols)
            current = jnp.concatenate([first[p][pl.ds(at, rows), lanes] for p in range(pieces)])
            hidden = current.astype(jnp.float32) + jnp.dot(
                onehot, table[0, :, lanes], preferred_element_type=jnp.float32
            )
            for lane in range(0, cols, 128):
                piece = hidden[:, lane : lane + 128]
                total = total + piece * piece
            scaled[step][:, lanes] = (hidden * mod[:, lanes]).astype(jnp.bfloat16)
            if i == 0:
                owns[step][...] = hidden
        mean = jnp.sum(total, axis=1, keepdims=True) * (1.0 / width)
        scales[step][...] = jnp.broadcast_to(lax.rsqrt(mean + epsilon), (frames, 128))


def dense(value, lead):
    frames = value.shape[0]
    rest = value[:, :64] if lead else value[:, 128:]
    full = value[:, 64:] if lead else value[:, :128]
    rest = jnp.concatenate([rest[: frames // 2], rest[frames // 2 :]], axis=1)
    return jnp.concatenate([full, rest], axis=0)


def undense(left, right, frames):
    middle = []
    for ref in (left, right):
        rest = ref[frames:]
        middle.append(jnp.concatenate([rest[:, :64], rest[:, 64:]], axis=0))
    return jnp.concatenate([left[:frames], jnp.concatenate(middle, axis=1), right[:frames]], axis=1)


def second_pair_kernel(dep, mine, across, out):
    out[0] = mine[...]
    out[1] = across[...]


def opened(pieces):
    return list(pieces[:2]) + [pieces[2].at[0], pieces[2].at[1]]


def step_kernel(cfg, *refs):
    step, has_relay, parts = cfg["step"], cfg["has_relay"], cfg["parts"]
    pieces, hops, head, turns = cfg["pieces"], cfg["hops"], cfg["head"], cfg["turns"]
    heads, group = cfg["heads"], cfg["group"]
    refs = list(refs)

    def take(count):
        taken, refs[:count] = refs[:count], []
        return taken

    bias, times, gain, freq, gate, flags = take(6)
    if has_relay:
        second, embed, relay = opened(take(3)), take(1)[0], take(2 * pieces)
    else:
        scaled, scales, own_hidden = take(3)
    chunks = take(2) if step == 0 else None
    weights = take(len(parts))
    left = take(1)[0] if parts == (1,) else None
    sends = take(1)[0] if len(parts) == 1 else None
    out = take(1)[0]
    if step == 0:
        weights = take(1)
    proj, att = take(2)
    if has_relay:
        scaled, scales, own_hidden, mod = take(4)
    offsets = offsets_of(pieces)
    frames, width = scaled.shape
    cols = att.shape[0]
    half = cols // 2
    rows = frames // pieces
    seq, section = lax.axis_index("seq"), lax.axis_index("pipe")
    _, batch = turn_and_batch(step, turns)

    if step == 0:
        for hop, chunk in zip((2, 3), chunks):
            place(hop, hops, [chunk.at[m] for m in range(pieces)], weights[0])

    def normalize(relayed):
        total = jnp.zeros((frames, 128), jnp.float32)
        for i in range(pieces):
            lanes = pl.ds(pl.multiple_of((seq ^ offsets[i]) * cols, 128), cols)
            if relayed:
                value = undense(relay[i], relay[pieces + i], frames)
                order = [offsets.index(offsets[i] ^ offsets[p]) for p in range(pieces)]
                blocks = [value[j * rows : (j + 1) * rows] for j in order]
            else:
                blocks = [second[p][:rows, lanes] for p in range(pieces)]
            hidden = jnp.concatenate(blocks, axis=0).astype(jnp.float32)
            hidden = hidden + embed[:, lanes].astype(jnp.float32)
            for lane in range(0, cols, 128):
                piece = hidden[:, lane : lane + 128]
                total = total + piece * piece
            scaled[:, lanes] = (hidden * mod[:, lanes]).astype(jnp.bfloat16)
            if i == 0:
                own_hidden[...] = hidden
        scales[...] = total

    if has_relay:
        mod[...] = modulation(step, turns, times, gain, freq)

        @pl.when(section == 0)
        def _():
            normalize(False)

        @pl.when(section != 0)
        def _():
            normalize(True)

        mean = jnp.sum(scales[...], axis=1, keepdims=True) * (1.0 / width)
        scale = lax.rsqrt(mean + epsilon)
    else:
        scale = scales[:, :1]

    def flag_of(i):
        lanes = pl.ds(pl.multiple_of((seq ^ offsets[i]) * rows, 128), rows)
        return None, flags[batch, :, lanes].astype(jnp.float32)

    flag_column = columns_of(flag_of, pieces, rows)[:, 16:17]
    score_scale = head ** (-0.5) * math.log2(math.e)
    lanes = lax.broadcasted_iota(jnp.int32, (frames, 128), 1)
    row_lanes = lax.broadcasted_iota(jnp.int32, (1, 128), 1)
    flag_lanes = jnp.logical_or(lanes == head, lanes == head + 1)
    pitch = cols + 128

    for k, part in enumerate(parts):
        base = k * pitch
        for at in range(0, cols, 256):
            size = min(256, cols - at)
            lane = at + lax.broadcasted_iota(jnp.int32, (1, size), 1)
            factor = jnp.where(lane < half, score_scale, 1.0)
            projected = jnp.dot(
                scaled[...], weights[k][:, at : at + size], preferred_element_type=jnp.float32
            )
            proj[:, base + at : base + at + size] = (projected * scale * factor).astype(
                jnp.bfloat16
            )
        proj[:, base + cols : base + pitch] = jnp.zeros((frames, 128), jnp.bfloat16)

    def slice_of(at):
        return proj[:, at : at + 128].astype(jnp.float32)

    keys, values = [], []
    for k in range(len(parts)):
        at = k * pitch + half
        key = jnp.where(flag_lanes, flag_column, jnp.where(lanes < head, slice_of(at), 0.0))
        value = jnp.where(
            lanes < head, slice_of(at + head), jnp.where(lanes == head, 1.0, 0.0)
        )
        keys.append(key.astype(jnp.bfloat16))
        values.append(value.T.astype(jnp.bfloat16))

    def scores_of(k, h):
        strength = bias[0, seq * heads + parts[k] * group + h] * math.log2(math.e)
        strength = jnp.zeros((1, 128), jnp.float32) + strength
        coarse = strength.astype(jnp.bfloat16).astype(jnp.float32)
        tail = jnp.where(
            row_lanes == head, coarse, jnp.where(row_lanes == head + 1, strength - coarse, 0.0)
        )
        query = jnp.where(lanes < head, slice_of(k * pitch + h * head), tail).astype(jnp.bfloat16)
        return lax.dot_general(
            keys[k], query, (((1,), (1,)), ((), ())), preferred_element_type=jnp.float32
        )

    tasks = [(k, h) for k in range(len(parts)) for h in range(group)]
    scores = scores_of(*tasks[0])
    for index, (k, h) in enumerate(tasks):
        ahead = scores_of(*tasks[index + 1]) if index + 1 < len(tasks) else None
        top = jnp.max(scores, axis=0, keepdims=True)
        weight = jnp.exp2(scores - top).astype(jnp.bfloat16)
        mixed = jnp.dot(values[k], weight, preferred_element_type=jnp.float32)
        at = (parts[k] * group + h) * head
        att[at : at + head, :] = mixed[:head] * (1.0 / mixed[head : head + 1])
        scores = ahead
    gates = gate[:, pl.ds(pl.multiple_of(seq * cols, 128), cols)]
    first, last = parts[0] * half, (parts[-1] + 1) * half
    attended = att[first:last].T.astype(jnp.bfloat16).astype(jnp.float32)
    output = own_hidden[...][:, first:last] + gates[:, first:last] * attended
    if parts == (0,):
        out[:, :half] = output.astype(jnp.bfloat16)
    elif parts == (1,):
        output_both = jnp.concatenate([left[:, :half].astype(jnp.float32), output], axis=1)
        out[...] = output_both.astype(jnp.bfloat16).reshape(pieces, rows, cols)
    else:
        out[...] = output.astype(jnp.bfloat16).reshape(pieces, rows, cols)
    if sends is not None:
        sends[...] = dense(output, parts == (1,)).astype(jnp.bfloat16)


def tie_kernel(*refs):
    pass


def grad_of(output, second, turn, rows, feats):
    cot = jnp.concatenate(
        [piece[rows : 2 * rows, turn * feats : (turn + 1) * feats] for piece in second], axis=0
    )
    return lax.dot_general(
        output, cot, (((0,), (0,)), ((), ())), preferred_element_type=jnp.float32
    )


def early_kernel(turns, pieces, halves, feats, *refs):
    outs, second = refs[: turns * halves], opened(refs[turns * halves : turns * halves + 3])
    sends, grad = refs[turns * halves + 3 : -1], refs[-1]
    section = lax.axis_index("pipe")
    offsets = offsets_of(pieces)
    part = pieces // halves
    rows = outs[0].shape[1]
    total = None
    for turn in range(turns - 1):
        blocks = []
        for p in range(pieces):
            k, j = p // part, p % part
            block = jnp.where(
                section == 0, outs[turn * halves + k][j], outs[(turn + 1) * halves + k][j]
            )
            sends[offsets[p]][turn] = block
            blocks.append(block)
        share = grad_of(jnp.concatenate(blocks, axis=0), second, turn, rows, feats)
        total = share if total is None else total + share
    grad[...] = total


def share_kernel(turns, pieces, hops, feats, *refs):
    before, now, second, early_grad = refs[0], refs[1], opened(refs[2:5]), refs[5]
    own_grad, grads, total = refs[6], refs[7:-1], refs[-1]
    section, rep = lax.axis_index("pipe"), lax.axis_index("dp")
    rows, cols = before.shape[1:]
    output = jnp.where(section == 0, before[...], now[...]).reshape(pieces * rows, cols)
    share = grad_of(output, second, turns - 1, rows, feats)
    total[...] = (share + early_grad[...]) * float(turns * hops * rows * pieces) ** (-0.5)
    g_rows = cols // hops
    own_grad[...] = total[pl.ds(pl.multiple_of(rep * g_rows, 8), g_rows)]
    for shift in range(1, hops):
        at = pl.multiple_of(lax.rem(rep + shift, hops) * g_rows, 8)
        grads[shift - 1][...] = total[pl.ds(at, g_rows)].astype(jnp.bfloat16)


def settle_kernel(turns, pieces, *refs):
    before, now, early = refs[0], refs[1], refs[2 : pieces + 1]
    late, (section_out, rows_out, sem) = refs[pieces + 1 : -3], refs[-3:]
    section, seq = lax.axis_index("pipe"), lax.axis_index("seq")
    offsets = offsets_of(pieces)
    rows, cols = early[0].shape[1:]
    for p in range(pieces):
        late[offsets[p]][...] = jnp.where(section == 0, before[p], now[p])
    for m in range(pieces - 1):
        lanes = pl.ds(pl.multiple_of((seq ^ m) * cols, 128), cols)
        for turn in range(turns - 1):
            rows_out[turn, :, lanes] = early[m][turn]
    copy = pltpu.make_async_copy(rows_out, section_out.at[pl.ds(0, turns - 1)], sem)
    copy.start()
    copy.wait()


def finish_kernel(pieces, hops, *refs):
    held, early, late, refs = refs[0], refs[1], refs[2 : pieces + 2], refs[pieces + 2 :]
    own_grad, parts, (section_out, grad, row_out, sems) = refs[0], refs[1:hops], refs[hops:]
    seq = lax.axis_index("seq")
    cols = late[0].shape[1]
    last_lanes = pl.ds(pl.multiple_of((seq ^ (pieces - 1)) * cols, 128), cols)
    early_copy = pltpu.make_async_copy(
        early, section_out.at[pl.ds(0, early.shape[0]), :, last_lanes], sems.at[0]
    )
    early_copy.start()
    for m in range(pieces):
        lanes = pl.ds(pl.multiple_of((seq ^ m) * cols, 128), cols)
        row_out[:, lanes] = late[m][...]
    copy = pltpu.make_async_copy(row_out, section_out.at[section_out.shape[0] - 1], sems.at[1])
    copy.start()
    total = own_grad[...]
    for part in parts:
        total = total + part[...].astype(jnp.float32)
    grad[...] = total
    early_copy.wait()
    copy.wait()


MIB = 1024 * 1024


def paired_body(
    incoming,
    contacts,
    keyframes,
    timesteps,
    w_query,
    w_keyval,
    norm_gain,
    time_freq,
    contact_table,
    key_bias,
    attn_gate,
    head_cotangent,
):
    seq_count = lax.axis_size("seq")
    hops = lax.axis_size("dp")
    rows, width, turns = incoming.shape[3], incoming.shape[4], incoming.shape[1]
    frames = rows * seq_count
    heads_all = key_bias.shape[1]
    head = width // heads_all
    heads = heads_all // seq_count
    kv_heads = w_keyval.shape[2] // (2 * head * seq_count)
    feats = head_cotangent.shape[4]
    cols = width // seq_count
    w_rows = w_query.shape[1]
    kind = jnp.bfloat16
    smem = pl.BlockSpec(memory_space=pltpu.SMEM)
    vmem = pl.BlockSpec(memory_space=pltpu.VMEM)
    anywhere = pl.BlockSpec(memory_space=pl.ANY)
    shape = jax.ShapeDtypeStruct

    def call(kernel, name, out_shape, in_specs, operands, scratch=(), limit=4, flops=0, **options):
        return pl.pallas_call(
            kernel,
            out_shape=out_shape,
            in_specs=in_specs,
            scratch_shapes=list(scratch),
            compiler_params=pltpu.CompilerParams(vmem_limit_bytes=limit * MIB),
            cost_estimate=pl.CostEstimate(
                flops=flops, bytes_accessed=flops // 512, transcendentals=0
            ),
            name=name,
            **options,
        )(*operands)

    timesteps = timesteps.reshape(1, timesteps.shape[0])

    def pin(value, space=pltpu.VMEM):
        return pltpu.with_memory_space_constraint(value, space)

    packed = call(
        pack_kernel,
        "pack",
        [pltpu.VMEM((2, w_rows, cols), kind)] * seq_count,
        [anywhere, anywhere],
        [pin(w_query, pltpu.HBM), pin(w_keyval, pltpu.HBM)],
        [pltpu.VMEM((seq_count, w_rows, cols), kind)] * 2
        + [pltpu.SemaphoreType.DMA((2 * seq_count,))],
        out_specs=[vmem] * seq_count,
    )
    blocks = [packed[0]] + [swap(packed[m], m) for m in range(1, seq_count)]

    def paired(name, deps, values):
        return call(
            functools.partial(pair_kernel, len(deps)),
            name,
            pltpu.VMEM((2, 2, w_rows, cols), kind),
            [anywhere] * len(deps) + [vmem] * 2,
            deps + values,
            out_specs=vmem,
        )

    near = paired("near", [], blocks[:2])
    near_next = ring_step(near)
    far = paired("far", [near_next], blocks[2:])
    far_next = ring_step(far)
    rings, partial = [], []
    for part in range(2):
        chunk = call(
            functools.partial(part_kernel, part),
            "part%d" % part,
            pltpu.VMEM((seq_count, w_rows, cols), kind),
            [vmem, vmem],
            [near_next, far_next],
            out_specs=vmem,
        )
        rings.append([chunk])
        partial.append(
            call(
                functools.partial(place_kernel, part, hops),
                "place%d" % part,
                pltpu.VMEM((width, cols), kind),
                [vmem] * 3,
                [pin(near), pin(far), pin(chunk)],
                out_specs=vmem,
            )
        )
    for hop in range(2):
        for ring in rings:
            ring.append(ring_step(ring[-1]))

    def tie(values, deps):
        return call(
            tie_kernel,
            "tie",
            [shape(value.shape, kind) for value in values],
            [anywhere] * (len(values) + len(deps)),
            list(values) + list(deps),
            out_specs=[anywhere] * len(values),
            input_output_aliases={i: i for i in range(len(values))},
        )

    mine = call(
        functools.partial(first_kernel, turns),
        "first",
        pltpu.VMEM((2 * rows + 16, width), kind),
        [anywhere, vmem, vmem],
        [far, incoming, contacts],
        [pltpu.VMEM((16, 128), jnp.float32)],
        out_specs=vmem,
    )
    across = swap(mine, 2)
    beside = swap(mine, 1)
    (across,) = tie([across], [ring[1] for ring in rings])
    first = [mine, across, beside, swap(across, 1)]
    prepared = call(
        functools.partial(norm_kernel, turns, seq_count),
        "norm",
        [pltpu.VMEM((frames, width), kind)] * 2
        + [pltpu.VMEM((frames, 128), jnp.float32)] * 2
        + [pltpu.VMEM((frames, cols), jnp.float32)] * 2
        + [pltpu.VMEM((frames, width), kind)] * 2,
        [smem] + [vmem] * 3 + [anywhere] * seq_count,
        [timesteps, contact_table, norm_gain, time_freq]
        + first,
        [pltpu.VMEM((1, width), jnp.float32)]
        + [pltpu.VMEM((2 * rows + 16, width), kind)] * seq_count
        + [pltpu.SemaphoreType.DMA((seq_count,))],
        12,
        out_specs=[vmem] * 8,
    )

    mine = call(
        second_kernel,
        "second",
        pltpu.VMEM((2 * rows, width), kind),
        [anywhere, vmem, vmem],
        [across, incoming, head_cotangent],
        out_specs=vmem,
    )
    second = [mine, swap(mine, 2)]

    common = [key_bias, timesteps, norm_gain, time_freq, attn_gate, keyframes]

    def run_step(step, parts, large, out_shape, aliases):
        cfg = {
            "step": step,
            "has_relay": step >= 2,
            "parts": parts,
            "pieces": seq_count,
            "hops": hops,
            "head": head,
            "heads": heads,
            "group": heads // kv_heads,
            "turns": turns,
        }
        scratch = [
            pltpu.VMEM((frames, len(parts) * (cols + 128)), kind),
            pltpu.VMEM((cols, frames), jnp.float32),
        ]
        if step >= 2:
            scratch += [
                pltpu.VMEM((frames, width), kind),
                pltpu.VMEM((frames, 128), jnp.float32),
                pltpu.VMEM((frames, cols), jnp.float32),
                pltpu.VMEM((1, width), jnp.float32),
            ]
        operands = common + [pin(value) for value in large]
        return call(
            functools.partial(step_kernel, cfg),
            "step%d%s" % (step, "".join("ab"[part] for part in parts)),
            out_shape,
            [smem, smem] + [vmem] * (len(operands) - 2),
            operands,
            scratch,
            16,
            len(parts) * frames * (2 * width * cols + 2 * heads * frames * head),
            out_specs=[vmem] * len(out_shape),
            input_output_aliases=aliases,
        )

    whole = pltpu.VMEM((seq_count, rows, cols), kind)
    sent = pltpu.VMEM((frames * 3 // 2, 128), kind)
    weights = list(partial)
    relays, lefts, outputs = ([], []), [], []
    for part in range(2):
        for step in range(2):
            large = [prepared[step], prepared[2 + step], prepared[4 + step]]
            if step == 0:
                chunks = rings[part][1:]
                if part:
                    (last_chunk,) = tie(chunks[1:], [relays[0][0][0], lefts[1]])
                    chunks = [chunks[0], last_chunk]
                large += chunks
            large += [weights[part]]
            aliases = {len(common) + len(large) - 1: 2} if step == 0 else {}
            out_shape = [sent, whole if part else pltpu.VMEM((frames, 256), kind)]
            if step == 0:
                out_shape += [pltpu.VMEM((width, cols), kind)]
            if part:
                large += [lefts[step]]
            results = run_step(step, (part,), large, out_shape, aliases)
            if step == 0:
                weights[part] = results[2]
            (outputs if part else lefts).append(results[1])
            piece = handed_over(results[0])
            relays[step].append([piece, None if part and not step else swap(piece, 2)])
    beside = call(
        second_pair_kernel,
        "beside",
        pltpu.VMEM((2,) + second[0].shape, kind),
        [anywhere, vmem, vmem],
        [outputs[0]] + second,
        limit=8,
        out_specs=vmem,
    )
    second = [second[0], second[1], swap(beside, 1)]

    (piece,) = tie([relays[0][1][0]], [outputs[1], second[2]])
    relays[0][1] = [piece, swap(piece, 2)]
    def complete(crossing):
        return [
            piece
            for mine, across in crossing
            for piece in (mine, across, swap(mine, 1), swap(across, 1))
        ]

    relay = complete(relays[0])
    (output,) = run_step(2, (0, 1), second + [prepared[6]] + relay + weights, [whole], {})
    outputs.append(output)
    early = call(
        functools.partial(early_kernel, turns, seq_count, 1, feats),
        "early",
        [shape((turns - 1, rows, cols), kind)] * seq_count + [shape((cols, feats), jnp.float32)],
        [vmem] * (turns + len(second)),
        outputs + second,
        limit=8,
        out_specs=[vmem] * (seq_count + 1),
    )
    early, early_grad = list(early[:-1]), early[-1]
    early = [early[0]] + [swap(early[m], m) for m in range(1, seq_count)]
    tied = tie([piece for pair in relays[1] for piece in pair], [early_grad])
    relay = complete([(tied[0], tied[1]), (tied[2], tied[3])])
    (output,) = run_step(3, (0, 1), second + [prepared[7]] + relay + weights, [whole], {})
    outputs.append(output)

    g_shape = (cols // hops, feats)
    operands = outputs[-2:] + second + [early_grad]
    grads = call(
        functools.partial(share_kernel, turns, seq_count, hops, feats),
        "share",
        [shape(g_shape, jnp.float32)] + [shape(g_shape, kind)] * (hops - 1),
        [vmem] * len(operands),
        operands,
        [pltpu.VMEM((cols, feats), jnp.float32)],
        8,
        out_specs=[vmem] * hops,
    )
    operands = outputs[-2:] + early[:-1]
    settled = call(
        functools.partial(settle_kernel, turns, seq_count),
        "settle",
        [shape((rows, cols), kind)] * seq_count + [shape((turns, rows, width), kind)],
        [vmem] * len(operands),
        operands,
        [pltpu.VMEM((turns - 1, rows, width), kind), pltpu.SemaphoreType.DMA],
        8,
        out_specs=[vmem] * seq_count + [anywhere],
    )
    late, held = settled[:seq_count], settled[-1]
    late = [late[0]] + [swap(late[m], m) for m in range(1, seq_count)]
    grads = [grads[0]] + [shifted(grads[k], "dp", k) for k in range(1, hops)]
    section_out, grad_rows = call(
        functools.partial(finish_kernel, seq_count, hops),
        "finish",
        [shape((turns, rows, width), kind), shape(g_shape, jnp.float32)],
        [anywhere] + [vmem] * (seq_count + hops + 1),
        [held, early[-1]] + late + grads,
        [pltpu.VMEM((rows, width), kind), pltpu.SemaphoreType.DMA((2,))],
        out_specs=[anywhere, vmem],
        input_output_aliases={0: 0},
    )
    return (section_out[None, :, None], grad_rows[None])


def body(incoming, contacts, keyframes, timesteps, w_query, *others):
    count = lax.axis_size("seq")
    cols = w_query.shape[2] // count
    paired = (
        lax.axis_size("pipe") == 2
        and lax.axis_size("dp") == 4
        and count == 4
        and cols % 128 == 0
        and w_query.shape[1] % 16 == 0
        and incoming.shape[3] == 128
        and incoming.shape[1] == 3
    )
    chosen = paired_body if paired else general_body
    return chosen(incoming, contacts, keyframes, timesteps, w_query, *others)


def general_body(
    incoming,
    contacts,
    keyframes,
    timesteps,
    w_query,
    w_keyval,
    norm_gain,
    time_freq,
    contact_table,
    key_bias,
    attn_gate,
    head_cotangent,
):
    section_idx = lax.axis_index("pipe")
    seq_idx = lax.axis_index("seq")
    rep_idx = lax.axis_index("dp")
    seq_count = lax.axis_size("seq")
    section_count = lax.axis_size("pipe")
    rep_count = lax.axis_size("dp")
    tok_rows = incoming.shape[3]
    width = incoming.shape[4]
    turns = incoming.shape[1]
    frames = tok_rows * seq_count
    heads_all = key_bias.shape[1]
    head_size = width // heads_all
    heads_local = heads_all // seq_count
    kv_width = w_keyval.shape[2]
    kv_local = kv_width // (2 * head_size * seq_count)
    group_size = heads_local // kv_local
    feat_count = head_cotangent.shape[4]
    score_scale = head_size ** (-0.5)
    q_cols = width // seq_count
    kv_cols = kv_width // seq_count
    w_rows = w_query.shape[1]

    w_parts = jnp.concatenate(
        [
            w_query[0].reshape(w_rows, seq_count, q_cols),
            w_keyval[0].reshape(w_rows, seq_count, kv_cols),
        ],
        axis=2,
    ).transpose(1, 0, 2)
    block = lax.all_to_all(w_parts, "seq", split_axis=0, concat_axis=0, tiled=True)
    weights = jnp.zeros((seq_count, rep_count, w_rows, q_cols + kv_cols), jnp.bfloat16)
    for hop in range(rep_count):
        owner = lax.rem(rep_idx + rep_count - hop, rep_count)
        weights = lax.dynamic_update_slice_in_dim(weights, block[:, None], owner, 1)
        if hop + 1 < rep_count:
            block = ring(block, "dp")
    weights = weights.reshape(width, q_cols + kv_cols)

    gain_row = norm_gain[0]
    freq_row = time_freq[0]
    table = contact_table[0]
    gate_local = lax.dynamic_slice_in_dim(attn_gate[0], seq_idx * q_cols, q_cols)
    table_local = lax.dynamic_slice_in_dim(table, seq_idx * q_cols, q_cols, 1)
    bias_local = lax.dynamic_slice_in_dim(key_bias[0], seq_idx * heads_local, heads_local)
    contact_all = lax.all_gather(contacts[:, 0, :], "seq", axis=1, tiled=True)
    key_all = keyframes[:, 0, :]
    step_all = timesteps[:, 0]
    labels = jnp.arange(table.shape[0], dtype=jnp.int32)
    cot_all = lax.all_gather(head_cotangent[0, :, 0], "seq", axis=1, tiled=True)

    lag = 2 if section_count == 2 else 1
    if lag == 2:
        steps = turns + 1
    else:
        steps = turns

    def turn_at(step):
        if lag == 1:
            return jnp.int32(step)
        return jnp.clip(step - section_idx, 0, turns - 1)

    outputs = []
    handed = {}
    for step in range(steps):
        turn = turn_at(step)
        fresh = lax.dynamic_index_in_dim(incoming[0, :, 0], turn, 0, keepdims=False)
        current = lax.all_gather(fresh, "seq", axis=0, tiled=True)
        if step in handed:
            current = jnp.where((section_idx == 0) | (turn == 0), current, handed[step])
        batch_idx = turn - section_idx + section_count - 1
        contact_rows = lax.dynamic_index_in_dim(contact_all, batch_idx, 0, keepdims=False)
        key_flags = lax.dynamic_index_in_dim(key_all, batch_idx, 0, keepdims=False).astype(
            jnp.float32
        )
        timestep = lax.dynamic_index_in_dim(step_all, batch_idx, 0, keepdims=False).astype(
            jnp.float32
        )
        onehot = (contact_rows[:, None] == labels[None, :]).astype(jnp.bfloat16)
        hidden = current.astype(jnp.float32) + jnp.dot(
            onehot, table, preferred_element_type=jnp.float32
        )
        root_mean = jnp.sqrt(jnp.mean(hidden * hidden, axis=-1, keepdims=True) + epsilon)
        modulation = gain_row * (1.0 + 0.5 * jnp.sin(timestep * freq_row))
        normed = (hidden / root_mean * modulation[None, :]).astype(jnp.bfloat16)
        projected = jnp.dot(normed, weights, preferred_element_type=jnp.float32).astype(
            jnp.bfloat16
        )
        query_heads = projected[:, :q_cols].reshape(frames, heads_local, head_size)
        keyval_heads = projected[:, q_cols:].reshape(frames, kv_local, 2, head_size)
        head_outputs = []
        for head in range(heads_local):
            key_rows = keyval_heads[:, head // group_size, 0]
            value_rows = keyval_heads[:, head // group_size, 1]
            scores = (
                lax.dot_general(
                    query_heads[:, head],
                    key_rows,
                    (((1,), (1,)), ((), ())),
                    preferred_element_type=jnp.float32,
                )
                * score_scale
            )
            scores = scores + bias_local[head] * key_flags[None, :]
            row_max = jnp.max(scores, axis=-1, keepdims=True)
            exponent = jnp.exp(scores - row_max)
            probabilities = (exponent / jnp.sum(exponent, axis=-1, keepdims=True)).astype(
                jnp.bfloat16
            )
            head_outputs.append(
                jnp.dot(probabilities, value_rows, preferred_element_type=jnp.float32).astype(
                    jnp.bfloat16
                )
            )
        attended = jnp.concatenate(head_outputs, axis=1)
        hidden_local = lax.dynamic_slice_in_dim(current, seq_idx * q_cols, q_cols, 1).astype(
            jnp.float32
        ) + jnp.dot(onehot, table_local, preferred_element_type=jnp.float32)
        output = (hidden_local + gate_local[None, :] * attended.astype(jnp.float32)).astype(
            jnp.bfloat16
        )
        outputs.append(output)
        if step + lag < steps:
            piece = passed_along(output, "pipe", 1)
            handed[step + lag] = lax.all_gather(piece, "seq", axis=1, tiled=True)

    factor = float(turns * rep_count * frames) ** (-0.5)
    total = None
    rows_out = []
    for turn in range(turns):
        if lag == 2:
            own = jnp.where(section_idx == 0, outputs[turn], outputs[turn + 1])
        else:
            own = outputs[turn]
        term = lax.dot_general(
            own, cot_all[turn], (((0,), (0,)), ((), ())), preferred_element_type=jnp.float32
        )
        total = term if total is None else total + term
        rows_out.append(lax.all_to_all(own, "seq", split_axis=0, concat_axis=1, tiled=True))
    section_out = jnp.stack(rows_out)[None, :, None]
    grad_parts = lax.all_to_all(
        (total * factor).astype(jnp.bfloat16).reshape(rep_count, q_cols // rep_count, feat_count),
        "dp",
        split_axis=0,
        concat_axis=0,
        tiled=True,
    )
    grad_rows = jnp.sum(grad_parts.astype(jnp.float32), axis=0)
    return (section_out, grad_rows[None])


def solution(mesh):
    in_specs = (
        P("pipe", None, "dp", "seq", None),
        P(None, "dp", "seq"),
        P(None, "dp", None),
        P(None, "dp"),
        P("pipe", ("seq", "dp"), None),
        P("pipe", ("seq", "dp"), None),
        P("pipe", None),
        P("pipe", None),
        P("pipe", None, None),
        P("pipe", None),
        P("pipe", None),
        P("pipe", None, "dp", "seq", None),
    )
    out_specs = (P("pipe", None, "dp", "seq", None), P("pipe", ("seq", "dp"), None))
    return jax.shard_map(body, mesh=mesh, in_specs=in_specs, out_specs=out_specs, check_vma=False)
```

```python
import functools
import math

import jax
import jax.numpy as jnp
from jax import lax
from jax.experimental import pallas as pl
from jax.experimental.pallas import tpu as pltpu
from jax.sharding import PartitionSpec as P

epsilon = 1e-06


def passed_along(value, axis, steps):
    count = lax.axis_size(axis)
    first, last = (max(0, -steps), min(count, count - steps))
    return lax.ppermute(value, axis, [(source, source + steps) for source in range(first, last)])


def ring(value, axis):
    count = lax.axis_size(axis)
    return lax.ppermute(value, axis, [(source, (source + 1) % count) for source in range(count)])


def swap(value, bit):
    count = lax.axis_size("seq")
    return lax.ppermute(value, "seq", [(source, source ^ bit) for source in range(count)])


def handed_over(value):
    return lax.ppermute(value, "pipe", [(0, 1), (1, 0)])


def shifted(value, axis, shift):
    count = lax.axis_size(axis)
    return lax.ppermute(value, axis, [(source, (source + shift) % count) for source in range(count)])


def fold(index):
    return index ^ (index >> 1)


def ring_step(value):
    count = lax.axis_size("dp")
    pairs = [(fold(place), fold((place + 1) % count)) for place in range(count)]
    return lax.ppermute(value, "dp", pairs)


def offsets_of(count):
    offsets = [0]
    bit = count // 2
    while bit:
        offsets = offsets + [offset ^ bit for offset in offsets]
        bit //= 2
    return offsets


def turn_and_batch(step, turns):
    section = lax.axis_index("pipe")
    turn = jnp.clip(step - section, 0, turns - 1)
    return turn, turn - section + 1


def pack_kernel(wq, wkv, *refs):
    outs, (queries, keyvals, sems) = refs[:-3], refs[-3:]
    parts, _, cols = outs[0].shape
    half = cols // 2
    seq = lax.axis_index("seq")
    copies = []
    for m in range(len(outs)):
        start = pl.multiple_of((seq ^ m) * cols, 128)
        for k, (source, held) in enumerate(((wq, queries), (wkv, keyvals))):
            copies.append(
                pltpu.make_async_copy(
                    source.at[0, :, pl.ds(start, cols)], held.at[m], sems.at[2 * m + k]
                )
            )
    for copy in copies:
        copy.start()
    for m, out in enumerate(outs):
        copies[2 * m].wait()
        copies[2 * m + 1].wait()
        for part in range(parts):
            lanes = slice(part * half, (part + 1) * half)
            out[part] = jnp.concatenate([queries[m][:, lanes], keyvals[m][:, lanes]], axis=1)


def pair_kernel(deps, *refs):
    out = refs[-1]
    for at, ref in enumerate(refs[deps:-1]):
        out[at] = ref[...]


def part_kernel(part, near, far, *outs):
    for at in range(2):
        outs[0][at] = near[at, part]
        if len(outs) == 1:
            outs[0][at + 2] = far[at, part]
        else:
            outs[1][at] = far[at, part]


def place(hop, hops, blocks, weights):
    seq, rep = lax.axis_index("seq"), lax.axis_index("dp")
    for m, block in enumerate(blocks):
        rows = block.shape[0]
        at = (seq ^ m) * hops + fold(lax.rem(fold(rep) + hops - hop, hops))
        weights[pl.ds(pl.multiple_of(at * rows, 16), rows)] = block[...]


def blocks_in(chunk):
    return [ref.at[m] for ref in chunk for m in range(ref.shape[0])]


def place_kernel(part, hops, near, far, *refs):
    chunk, weights = refs[:-1], refs[-1]
    place(0, hops, [near.at[0, part], near.at[1, part], far.at[0, part], far.at[1, part]], weights)
    place(1, hops, blocks_in(chunk), weights)


def first_kernel(turns, far, incoming, contacts, out, states):
    rows = incoming.shape[3]
    for turn in range(2):
        out[turn * rows : (turn + 1) * rows] = incoming[0, turn, 0]
    states[...] = jnp.zeros_like(states)
    for step in range(turns + 1):
        _, batch = turn_and_batch(step, turns)
        states[step : step + 1] = contacts[batch].astype(jnp.float32)
    out[2 * rows :, : states.shape[1]] = states[...].astype(jnp.bfloat16)


def second_kernel(dep, incoming, cotangent, out):
    turns, rows, feats = cotangent.shape[1], cotangent.shape[3], cotangent.shape[4]
    out[:rows] = incoming[0, 2, 0]
    for turn in range(turns):
        out[rows:, turn * feats : (turn + 1) * feats] = cotangent[0, turn, 0]


def columns_of(rows_of, pieces, rows):
    labels = lax.broadcasted_iota(jnp.int32, (32, rows), 0)
    columns = []
    for i in range(pieces):
        state, flag = rows_of(i)
        one = jnp.zeros((32, rows), jnp.float32)
        if state is not None:
            one = jnp.where(labels == state, 1.0, 0.0)
        if flag is not None:
            one = jnp.where(labels == 16, flag, one)
        columns.append(one.T)
    return jnp.concatenate(columns, axis=0)


def modulation(step, turns, times, gain, freq):
    _, batch = turn_and_batch(step, turns)
    return gain[...] * (1.0 + 0.5 * jnp.sin(times[0, batch].astype(jnp.float32) * freq[...]))


def norm_kernel(turns, pieces, times, table, gain, freq, *refs):
    sources, refs = refs[:pieces], refs[pieces:]
    scaled, scales, owns, embeds, mod = refs[0:2], refs[2:4], refs[4:6], refs[6:8], refs[8]
    first, sems = refs[9 : 9 + pieces], refs[9 + pieces]
    copies = [
        pltpu.make_async_copy(sources[i], first[i], sems.at[i]) for i in range(pieces)
    ]
    for copy in copies:
        copy.start()
    for copy in copies:
        copy.wait()
    frames, width = scaled[0].shape
    rows, cols = frames // pieces, owns[0].shape[1]
    seq = lax.axis_index("seq")
    offsets = offsets_of(pieces)
    for step in range(turns + 1):

        def state_of(i):
            state = first[i][2 * rows : 2 * rows + 16, :rows][step : step + 1]
            return state.astype(jnp.float32).astype(jnp.int32), None

        onehot = columns_of(state_of, pieces, rows)[:, : table.shape[1]].astype(jnp.bfloat16)
        if step >= 2:
            for at in range(0, width, 256):
                embeds[step - 2][:, at : at + 256] = jnp.dot(
                    onehot, table[0, :, at : at + 256], preferred_element_type=jnp.float32
                ).astype(jnp.bfloat16)
            continue
        turn, _ = turn_and_batch(step, turns)
        at = pl.multiple_of(jnp.minimum(turn, 1) * rows, 128)
        mod[...] = modulation(step, turns, times, gain, freq)
        total = jnp.zeros((frames, 128), jnp.float32)
        for i in range(pieces):
            lanes = pl.ds(pl.multiple_of((seq ^ offsets[i]) * cols, 128), cols)
            current = jnp.concatenate([first[p][pl.ds(at, rows), lanes] for p in range(pieces)])
            hidden = current.astype(jnp.float32) + jnp.dot(
                onehot, table[0, :, lanes], preferred_element_type=jnp.float32
            )
            for lane in range(0, cols, 128):
                piece = hidden[:, lane : lane + 128]
                total = total + piece * piece
            scaled[step][:, lanes] = (hidden * mod[:, lanes]).astype(jnp.bfloat16)
            if i == 0:
                owns[step][...] = hidden
        mean = jnp.sum(total, axis=1, keepdims=True) * (1.0 / width)
        scales[step][...] = jnp.broadcast_to(lax.rsqrt(mean + epsilon), (frames, 128))


def dense(value, lead):
    frames = value.shape[0]
    rest = value[:, :64] if lead else value[:, 128:]
    full = value[:, 64:] if lead else value[:, :128]
    rest = jnp.concatenate([rest[: frames // 2], rest[frames // 2 :]], axis=1)
    return jnp.concatenate([full, rest], axis=0)


def undense(left, right, frames):
    middle = []
    for ref in (left, right):
        rest = ref[frames:]
        middle.append(jnp.concatenate([rest[:, :64], rest[:, 64:]], axis=0))
    return jnp.concatenate([left[:frames], jnp.concatenate(middle, axis=1), right[:frames]], axis=1)


def second_pair_kernel(dep, mine, across, out):
    out[0] = mine[...]
    out[1] = across[...]


def opened(pieces):
    return list(pieces[:2]) + [pieces[2].at[0], pieces[2].at[1]]


def step_kernel(cfg, *refs):
    step, has_relay, parts = cfg["step"], cfg["has_relay"], cfg["parts"]
    pieces, hops, head, turns = cfg["pieces"], cfg["hops"], cfg["head"], cfg["turns"]
    heads, group = cfg["heads"], cfg["group"]
    refs = list(refs)

    def take(count):
        taken, refs[:count] = refs[:count], []
        return taken

    bias, times, gain, freq, gate, flags = take(6)
    if has_relay:
        second, embed, relay = opened(take(3)), take(1)[0], take(2 * pieces)
    else:
        scaled, scales, own_hidden = take(3)
    streams = cfg["streams"]
    chunks = [take(streams), take(streams)] if step == 0 else None
    weights = take(len(parts))
    left = take(1)[0] if parts == (1,) else None
    sends = take(1)[0] if len(parts) == 1 else None
    out = take(1)[0]
    if step == 0:
        weights = take(1)
    proj, att = take(2)
    if has_relay:
        scaled, scales, own_hidden, mod = take(4)
    offsets = offsets_of(pieces)
    frames, width = scaled.shape
    cols = att.shape[0]
    half = cols // 2
    rows = frames // pieces
    seq, section = lax.axis_index("seq"), lax.axis_index("pipe")
    _, batch = turn_and_batch(step, turns)

    if step == 0:
        for hop, chunk in zip((2, 3), chunks):
            place(hop, hops, blocks_in(chunk), weights[0])

    def normalize(relayed):
        total = jnp.zeros((frames, 128), jnp.float32)
        for i in range(pieces):
            lanes = pl.ds(pl.multiple_of((seq ^ offsets[i]) * cols, 128), cols)
            if relayed:
                value = undense(relay[i], relay[pieces + i], frames)
                order = [offsets.index(offsets[i] ^ offsets[p]) for p in range(pieces)]
                blocks = [value[j * rows : (j + 1) * rows] for j in order]
            else:
                blocks = [second[p][:rows, lanes] for p in range(pieces)]
            hidden = jnp.concatenate(blocks, axis=0).astype(jnp.float32)
            hidden = hidden + embed[:, lanes].astype(jnp.float32)
            for lane in range(0, cols, 128):
                piece = hidden[:, lane : lane + 128]
                total = total + piece * piece
            scaled[:, lanes] = (hidden * mod[:, lanes]).astype(jnp.bfloat16)
            if i == 0:
                own_hidden[...] = hidden
        scales[...] = total

    if has_relay:
        mod[...] = modulation(step, turns, times, gain, freq)

        @pl.when(section == 0)
        def _():
            normalize(False)

        @pl.when(section != 0)
        def _():
            normalize(True)

        mean = jnp.sum(scales[...], axis=1, keepdims=True) * (1.0 / width)
        scale = lax.rsqrt(mean + epsilon)
    else:
        scale = scales[:, :1]

    def flag_of(i):
        lanes = pl.ds(pl.multiple_of((seq ^ offsets[i]) * rows, 128), rows)
        return None, flags[batch, :, lanes].astype(jnp.float32)

    flag_column = columns_of(flag_of, pieces, rows)[:, 16:17]
    score_scale = head ** (-0.5) * math.log2(math.e)
    lanes = lax.broadcasted_iota(jnp.int32, (frames, 128), 1)
    row_lanes = lax.broadcasted_iota(jnp.int32, (1, 128), 1)
    flag_lanes = jnp.logical_or(lanes == head, lanes == head + 1)
    pitch = cols + 128

    for k, part in enumerate(parts):
        base = k * pitch
        for at in range(0, cols, 256):
            size = min(256, cols - at)
            lane = at + lax.broadcasted_iota(jnp.int32, (1, size), 1)
            factor = jnp.where(lane < half, score_scale, 1.0)
            projected = jnp.dot(
                scaled[...], weights[k][:, at : at + size], preferred_element_type=jnp.float32
            )
            proj[:, base + at : base + at + size] = (projected * scale * factor).astype(
                jnp.bfloat16
            )
        proj[:, base + cols : base + pitch] = jnp.zeros((frames, 128), jnp.bfloat16)

    def slice_of(at):
        return proj[:, at : at + 128].astype(jnp.float32)

    keys, values = [], []
    for k in range(len(parts)):
        at = k * pitch + half
        key = jnp.where(flag_lanes, flag_column, jnp.where(lanes < head, slice_of(at), 0.0))
        value = jnp.where(
            lanes < head, slice_of(at + head), jnp.where(lanes == head, 1.0, 0.0)
        )
        keys.append(key.astype(jnp.bfloat16))
        values.append(value.T.astype(jnp.bfloat16))

    def scores_of(k, h):
        strength = bias[0, seq * heads + parts[k] * group + h] * math.log2(math.e)
        strength = jnp.zeros((1, 128), jnp.float32) + strength
        coarse = strength.astype(jnp.bfloat16).astype(jnp.float32)
        tail = jnp.where(
            row_lanes == head, coarse, jnp.where(row_lanes == head + 1, strength - coarse, 0.0)
        )
        query = jnp.where(lanes < head, slice_of(k * pitch + h * head), tail).astype(jnp.bfloat16)
        return lax.dot_general(
            keys[k], query, (((1,), (1,)), ((), ())), preferred_element_type=jnp.float32
        )

    tasks = [(k, h) for k in range(len(parts)) for h in range(group)]
    scores = scores_of(*tasks[0])
    for index, (k, h) in enumerate(tasks):
        ahead = scores_of(*tasks[index + 1]) if index + 1 < len(tasks) else None
        top = jnp.max(scores, axis=0, keepdims=True)
        weight = jnp.exp2(scores - top).astype(jnp.bfloat16)
        mixed = jnp.dot(values[k], weight, preferred_element_type=jnp.float32)
        at = (parts[k] * group + h) * head
        att[at : at + head, :] = mixed[:head] * (1.0 / mixed[head : head + 1])
        scores = ahead
    gates = gate[:, pl.ds(pl.multiple_of(seq * cols, 128), cols)]
    first, last = parts[0] * half, (parts[-1] + 1) * half
    attended = att[first:last].T.astype(jnp.bfloat16).astype(jnp.float32)
    output = own_hidden[...][:, first:last] + gates[:, first:last] * attended
    if parts == (0,):
        out[:, :half] = output.astype(jnp.bfloat16)
    elif parts == (1,):
        output_both = jnp.concatenate([left[:, :half].astype(jnp.float32), output], axis=1)
        out[...] = output_both.astype(jnp.bfloat16).reshape(pieces, rows, cols)
    else:
        out[...] = output.astype(jnp.bfloat16).reshape(pieces, rows, cols)
    if sends is not None:
        sends[...] = dense(output, parts == (1,)).astype(jnp.bfloat16)


def tie_kernel(*refs):
    pass


def grad_of(output, second, turn, rows, feats):
    cot = jnp.concatenate(
        [piece[rows : 2 * rows, turn * feats : (turn + 1) * feats] for piece in second], axis=0
    )
    return lax.dot_general(
        output, cot, (((0,), (0,)), ((), ())), preferred_element_type=jnp.float32
    )


def early_kernel(turns, pieces, halves, feats, *refs):
    outs, second = refs[: turns * halves], opened(refs[turns * halves : turns * halves + 3])
    sends, grad = refs[turns * halves + 3 : -1], refs[-1]
    section = lax.axis_index("pipe")
    offsets = offsets_of(pieces)
    part = pieces // halves
    rows = outs[0].shape[1]
    total = None
    for turn in range(turns - 1):
        blocks = []
        for p in range(pieces):
            k, j = p // part, p % part
            block = jnp.where(
                section == 0, outs[turn * halves + k][j], outs[(turn + 1) * halves + k][j]
            )
            sends[offsets[p]][turn] = block
            blocks.append(block)
        share = grad_of(jnp.concatenate(blocks, axis=0), second, turn, rows, feats)
        total = share if total is None else total + share
    grad[...] = total


def share_kernel(turns, pieces, hops, feats, *refs):
    before, now, second, early_grad = refs[0], refs[1], opened(refs[2:5]), refs[5]
    own_grad, grads, total = refs[6], refs[7:-1], refs[-1]
    section, rep = lax.axis_index("pipe"), lax.axis_index("dp")
    rows, cols = before.shape[1:]
    output = jnp.where(section == 0, before[...], now[...]).reshape(pieces * rows, cols)
    share = grad_of(output, second, turns - 1, rows, feats)
    total[...] = (share + early_grad[...]) * float(turns * hops * rows * pieces) ** (-0.5)
    g_rows = cols // hops
    own_grad[...] = total[pl.ds(pl.multiple_of(rep * g_rows, 8), g_rows)]
    for shift in range(1, hops):
        at = pl.multiple_of(lax.rem(rep + shift, hops) * g_rows, 8)
        grads[shift - 1][...] = total[pl.ds(at, g_rows)].astype(jnp.bfloat16)


def settle_kernel(turns, pieces, *refs):
    before, now, early = refs[0], refs[1], refs[2 : pieces + 1]
    late, (section_out, rows_out, sem) = refs[pieces + 1 : -3], refs[-3:]
    section, seq = lax.axis_index("pipe"), lax.axis_index("seq")
    offsets = offsets_of(pieces)
    rows, cols = early[0].shape[1:]
    for p in range(pieces):
        late[offsets[p]][...] = jnp.where(section == 0, before[p], now[p])
    for m in range(pieces - 1):
        lanes = pl.ds(pl.multiple_of((seq ^ m) * cols, 128), cols)
        for turn in range(turns - 1):
            rows_out[turn, :, lanes] = early[m][turn]
    copy = pltpu.make_async_copy(rows_out, section_out.at[pl.ds(0, turns - 1)], sem)
    copy.start()
    copy.wait()


def finish_kernel(pieces, hops, *refs):
    held, early, late, refs = refs[0], refs[1], refs[2 : pieces + 2], refs[pieces + 2 :]
    own_grad, parts, (section_out, grad, row_out, sems) = refs[0], refs[1:hops], refs[hops:]
    seq = lax.axis_index("seq")
    cols = late[0].shape[1]
    last_lanes = pl.ds(pl.multiple_of((seq ^ (pieces - 1)) * cols, 128), cols)
    early_copy = pltpu.make_async_copy(
        early, section_out.at[pl.ds(0, early.shape[0]), :, last_lanes], sems.at[0]
    )
    early_copy.start()
    for m in range(pieces):
        lanes = pl.ds(pl.multiple_of((seq ^ m) * cols, 128), cols)
        row_out[:, lanes] = late[m][...]
    copy = pltpu.make_async_copy(row_out, section_out.at[section_out.shape[0] - 1], sems.at[1])
    copy.start()
    total = own_grad[...]
    for part in parts:
        total = total + part[...].astype(jnp.float32)
    grad[...] = total
    early_copy.wait()
    copy.wait()


MIB = 1024 * 1024


def paired_body(
    incoming,
    contacts,
    keyframes,
    timesteps,
    w_query,
    w_keyval,
    norm_gain,
    time_freq,
    contact_table,
    key_bias,
    attn_gate,
    head_cotangent,
):
    seq_count = lax.axis_size("seq")
    hops = lax.axis_size("dp")
    rows, width, turns = incoming.shape[3], incoming.shape[4], incoming.shape[1]
    frames = rows * seq_count
    heads_all = key_bias.shape[1]
    head = width // heads_all
    heads = heads_all // seq_count
    kv_heads = w_keyval.shape[2] // (2 * head * seq_count)
    feats = head_cotangent.shape[4]
    cols = width // seq_count
    w_rows = w_query.shape[1]
    kind = jnp.bfloat16
    smem = pl.BlockSpec(memory_space=pltpu.SMEM)
    vmem = pl.BlockSpec(memory_space=pltpu.VMEM)
    anywhere = pl.BlockSpec(memory_space=pl.ANY)
    shape = jax.ShapeDtypeStruct

    def call(kernel, name, out_shape, in_specs, operands, scratch=(), limit=4, flops=0, **options):
        return pl.pallas_call(
            kernel,
            out_shape=out_shape,
            in_specs=in_specs,
            scratch_shapes=list(scratch),
            compiler_params=pltpu.CompilerParams(vmem_limit_bytes=limit * MIB),
            cost_estimate=pl.CostEstimate(
                flops=flops, bytes_accessed=flops // 512, transcendentals=0
            ),
            name=name,
            **options,
        )(*operands)

    timesteps = timesteps.reshape(1, timesteps.shape[0])

    def pin(value, space=pltpu.VMEM):
        return pltpu.with_memory_space_constraint(value, space)

    packed = call(
        pack_kernel,
        "pack",
        [pltpu.VMEM((2, w_rows, cols), kind)] * seq_count,
        [anywhere, anywhere],
        [pin(w_query, pltpu.HBM), pin(w_keyval, pltpu.HBM)],
        [pltpu.VMEM((seq_count, w_rows, cols), kind)] * 2
        + [pltpu.SemaphoreType.DMA((2 * seq_count,))],
        out_specs=[vmem] * seq_count,
    )
    blocks = [packed[0]] + [swap(packed[m], m) for m in range(1, seq_count)]

    def paired(name, deps, values):
        return call(
            functools.partial(pair_kernel, len(deps)),
            name,
            pltpu.VMEM((2, 2, w_rows, cols), kind),
            [anywhere] * len(deps) + [vmem] * 2,
            deps + values,
            out_specs=vmem,
        )

    near = paired("near", [], blocks[:2])
    near_next = ring_step(near)
    far = paired("far", [near_next], blocks[2:])
    far_next = ring_step(far)
    streams = (2, 1)
    rings, partial = [], []
    for part in range(2):
        count = streams[part]
        chunk = call(
            functools.partial(part_kernel, part),
            "part%d" % part,
            [pltpu.VMEM((seq_count // count, w_rows, cols), kind)] * count,
            [vmem, vmem],
            [near_next, far_next],
            out_specs=[vmem] * count,
        )
        rings.append([list(chunk)])
        partial.append(
            call(
                functools.partial(place_kernel, part, hops),
                "place%d" % part,
                pltpu.VMEM((width, cols), kind),
                [vmem] * (2 + count),
                [pin(near), pin(far)] + [pin(value) for value in chunk],
                out_specs=vmem,
            )
        )
    for ring in rings:
        ring.append([ring_step(value) for value in ring[-1]])
    rings[0].append([ring_step(value) for value in rings[0][-1]])

    def tie(values, deps):
        return call(
            tie_kernel,
            "tie",
            [shape(value.shape, kind) for value in values],
            [anywhere] * (len(values) + len(deps)),
            list(values) + list(deps),
            out_specs=[anywhere] * len(values),
            input_output_aliases={i: i for i in range(len(values))},
        )

    mine = call(
        functools.partial(first_kernel, turns),
        "first",
        pltpu.VMEM((2 * rows + 16, width), kind),
        [anywhere, vmem, vmem],
        [far, incoming, contacts],
        [pltpu.VMEM((16, 128), jnp.float32)],
        out_specs=vmem,
    )
    across = swap(mine, 2)
    beside = swap(mine, 1)
    (across,) = tie([across], rings[0][1] + rings[1][1])
    first = [mine, across, beside, swap(across, 1)]
    prepared = call(
        functools.partial(norm_kernel, turns, seq_count),
        "norm",
        [pltpu.VMEM((frames, width), kind)] * 2
        + [pltpu.VMEM((frames, 128), jnp.float32)] * 2
        + [pltpu.VMEM((frames, cols), jnp.float32)] * 2
        + [pltpu.VMEM((frames, width), kind)] * 2,
        [smem] + [vmem] * 3 + [anywhere] * seq_count,
        [timesteps, contact_table, norm_gain, time_freq]
        + first,
        [pltpu.VMEM((1, width), jnp.float32)]
        + [pltpu.VMEM((2 * rows + 16, width), kind)] * seq_count
        + [pltpu.SemaphoreType.DMA((seq_count,))],
        12,
        out_specs=[vmem] * 8,
    )

    mine = call(
        second_kernel,
        "second",
        pltpu.VMEM((2 * rows, width), kind),
        [anywhere, vmem, vmem],
        [across, incoming, head_cotangent],
        out_specs=vmem,
    )
    second = [mine, swap(mine, 2)]

    rings[1][1] = list(tie(rings[1][1], [prepared[0]]))
    rings[1].append([ring_step(value) for value in rings[1][1]])

    common = [key_bias, timesteps, norm_gain, time_freq, attn_gate, keyframes]

    def run_step(step, parts, large, out_shape, aliases):
        cfg = {
            "step": step,
            "has_relay": step >= 2,
            "parts": parts,
            "pieces": seq_count,
            "hops": hops,
            "head": head,
            "heads": heads,
            "group": heads // kv_heads,
            "turns": turns,
            "streams": streams[parts[0]],
        }
        scratch = [
            pltpu.VMEM((frames, len(parts) * (cols + 128)), kind),
            pltpu.VMEM((cols, frames), jnp.float32),
        ]
        if step >= 2:
            scratch += [
                pltpu.VMEM((frames, width), kind),
                pltpu.VMEM((frames, 128), jnp.float32),
                pltpu.VMEM((frames, cols), jnp.float32),
                pltpu.VMEM((1, width), jnp.float32),
            ]
        operands = common + [pin(value) for value in large]
        return call(
            functools.partial(step_kernel, cfg),
            "step%d%s" % (step, "".join("ab"[part] for part in parts)),
            out_shape,
            [smem, smem] + [vmem] * (len(operands) - 2),
            operands,
            scratch,
            16,
            len(parts) * frames * (2 * width * cols + 2 * heads * frames * head),
            out_specs=[vmem] * len(out_shape),
            input_output_aliases=aliases,
        )

    whole = pltpu.VMEM((seq_count, rows, cols), kind)
    sent = pltpu.VMEM((frames * 3 // 2, 128), kind)
    weights = list(partial)
    relays, lefts, outputs = ([], []), [], []
    for part in range(2):
        for step in range(2):
            large = [prepared[step], prepared[2 + step], prepared[4 + step]]
            if step == 0:
                chunks = rings[part][1] + rings[part][2]
                if part:
                    last = tie(rings[part][2], [relays[0][0][0], lefts[1]])
                    chunks = rings[part][1] + list(last)
                large += chunks
            large += [weights[part]]
            aliases = {len(common) + len(large) - 1: 2} if step == 0 else {}
            out_shape = [sent, whole if part else pltpu.VMEM((frames, 256), kind)]
            if step == 0:
                out_shape += [pltpu.VMEM((width, cols), kind)]
            if part:
                large += [lefts[step]]
            results = run_step(step, (part,), large, out_shape, aliases)
            if step == 0:
                weights[part] = results[2]
            (outputs if part else lefts).append(results[1])
            piece = handed_over(results[0])
            relays[step].append([piece, None if part and not step else swap(piece, 2)])
    beside = call(
        second_pair_kernel,
        "beside",
        pltpu.VMEM((2,) + second[0].shape, kind),
        [anywhere, vmem, vmem],
        [outputs[0]] + second,
        limit=8,
        out_specs=vmem,
    )
    second = [second[0], second[1], swap(beside, 1)]

    (piece,) = tie([relays[0][1][0]], [outputs[1], second[2]])
    relays[0][1] = [piece, swap(piece, 2)]
    def complete(crossing):
        return [
            piece
            for mine, across in crossing
            for piece in (mine, across, swap(mine, 1), swap(across, 1))
        ]

    relay = complete(relays[0])
    (output,) = run_step(2, (0, 1), second + [prepared[6]] + relay + weights, [whole], {})
    outputs.append(output)
    early = call(
        functools.partial(early_kernel, turns, seq_count, 1, feats),
        "early",
        [shape((turns - 1, rows, cols), kind)] * seq_count + [shape((cols, feats), jnp.float32)],
        [vmem] * (turns + len(second)),
        outputs + second,
        limit=8,
        out_specs=[vmem] * (seq_count + 1),
    )
    early, early_grad = list(early[:-1]), early[-1]
    early = [early[0]] + [swap(early[m], m) for m in range(1, seq_count)]
    tied = tie([piece for pair in relays[1] for piece in pair], [early_grad])
    relay = complete([(tied[0], tied[1]), (tied[2], tied[3])])
    (output,) = run_step(3, (0, 1), second + [prepared[7]] + relay + weights, [whole], {})
    outputs.append(output)

    g_shape = (cols // hops, feats)
    operands = outputs[-2:] + second + [early_grad]
    grads = call(
        functools.partial(share_kernel, turns, seq_count, hops, feats),
        "share",
        [shape(g_shape, jnp.float32)] + [shape(g_shape, kind)] * (hops - 1),
        [vmem] * len(operands),
        operands,
        [pltpu.VMEM((cols, feats), jnp.float32)],
        8,
        out_specs=[vmem] * hops,
    )
    operands = outputs[-2:] + early[:-1]
    settled = call(
        functools.partial(settle_kernel, turns, seq_count),
        "settle",
        [shape((rows, cols), kind)] * seq_count + [shape((turns, rows, width), kind)],
        [vmem] * len(operands),
        operands,
        [pltpu.VMEM((turns - 1, rows, width), kind), pltpu.SemaphoreType.DMA],
        8,
        out_specs=[vmem] * seq_count + [anywhere],
    )
    late, held = settled[:seq_count], settled[-1]
    late = [late[0]] + [swap(late[m], m) for m in range(1, seq_count)]
    grads = [grads[0]] + [shifted(grads[k], "dp", k) for k in range(1, hops)]
    section_out, grad_rows = call(
        functools.partial(finish_kernel, seq_count, hops),
        "finish",
        [shape((turns, rows, width), kind), shape(g_shape, jnp.float32)],
        [anywhere] + [vmem] * (seq_count + hops + 1),
        [held, early[-1]] + late + grads,
        [pltpu.VMEM((rows, width), kind), pltpu.SemaphoreType.DMA((2,))],
        out_specs=[anywhere, vmem],
        input_output_aliases={0: 0},
    )
    return (section_out[None, :, None], grad_rows[None])


def body(incoming, contacts, keyframes, timesteps, w_query, *others):
    count = lax.axis_size("seq")
    cols = w_query.shape[2] // count
    paired = (
        lax.axis_size("pipe") == 2
        and lax.axis_size("dp") == 4
        and count == 4
        and cols % 128 == 0
        and w_query.shape[1] % 16 == 0
        and incoming.shape[3] == 128
        and incoming.shape[1] == 3
    )
    chosen = paired_body if paired else general_body
    return chosen(incoming, contacts, keyframes, timesteps, w_query, *others)


def general_body(
    incoming,
    contacts,
    keyframes,
    timesteps,
    w_query,
    w_keyval,
    norm_gain,
    time_freq,
    contact_table,
    key_bias,
    attn_gate,
    head_cotangent,
):
    section_idx = lax.axis_index("pipe")
    seq_idx = lax.axis_index("seq")
    rep_idx = lax.axis_index("dp")
    seq_count = lax.axis_size("seq")
    section_count = lax.axis_size("pipe")
    rep_count = lax.axis_size("dp")
    tok_rows = incoming.shape[3]
    width = incoming.shape[4]
    turns = incoming.shape[1]
    frames = tok_rows * seq_count
    heads_all = key_bias.shape[1]
    head_size = width // heads_all
    heads_local = heads_all // seq_count
    kv_width = w_keyval.shape[2]
    kv_local = kv_width // (2 * head_size * seq_count)
    group_size = heads_local // kv_local
    feat_count = head_cotangent.shape[4]
    score_scale = head_size ** (-0.5)
    q_cols = width // seq_count
    kv_cols = kv_width // seq_count
    w_rows = w_query.shape[1]

    w_parts = jnp.concatenate(
        [
            w_query[0].reshape(w_rows, seq_count, q_cols),
            w_keyval[0].reshape(w_rows, seq_count, kv_cols),
        ],
        axis=2,
    ).transpose(1, 0, 2)
    block = lax.all_to_all(w_parts, "seq", split_axis=0, concat_axis=0, tiled=True)
    weights = jnp.zeros((seq_count, rep_count, w_rows, q_cols + kv_cols), jnp.bfloat16)
    for hop in range(rep_count):
        owner = lax.rem(rep_idx + rep_count - hop, rep_count)
        weights = lax.dynamic_update_slice_in_dim(weights, block[:, None], owner, 1)
        if hop + 1 < rep_count:
            block = ring(block, "dp")
    weights = weights.reshape(width, q_cols + kv_cols)

    gain_row = norm_gain[0]
    freq_row = time_freq[0]
    table = contact_table[0]
    gate_local = lax.dynamic_slice_in_dim(attn_gate[0], seq_idx * q_cols, q_cols)
    table_local = lax.dynamic_slice_in_dim(table, seq_idx * q_cols, q_cols, 1)
    bias_local = lax.dynamic_slice_in_dim(key_bias[0], seq_idx * heads_local, heads_local)
    contact_all = lax.all_gather(contacts[:, 0, :], "seq", axis=1, tiled=True)
    key_all = keyframes[:, 0, :]
    step_all = timesteps[:, 0]
    labels = jnp.arange(table.shape[0], dtype=jnp.int32)
    cot_all = lax.all_gather(head_cotangent[0, :, 0], "seq", axis=1, tiled=True)

    lag = 2 if section_count == 2 else 1
    if lag == 2:
        steps = turns + 1
    else:
        steps = turns

    def turn_at(step):
        if lag == 1:
            return jnp.int32(step)
        return jnp.clip(step - section_idx, 0, turns - 1)

    outputs = []
    handed = {}
    for step in range(steps):
        turn = turn_at(step)
        fresh = lax.dynamic_index_in_dim(incoming[0, :, 0], turn, 0, keepdims=False)
        current = lax.all_gather(fresh, "seq", axis=0, tiled=True)
        if step in handed:
            current = jnp.where((section_idx == 0) | (turn == 0), current, handed[step])
        batch_idx = turn - section_idx + section_count - 1
        contact_rows = lax.dynamic_index_in_dim(contact_all, batch_idx, 0, keepdims=False)
        key_flags = lax.dynamic_index_in_dim(key_all, batch_idx, 0, keepdims=False).astype(
            jnp.float32
        )
        timestep = lax.dynamic_index_in_dim(step_all, batch_idx, 0, keepdims=False).astype(
            jnp.float32
        )
        onehot = (contact_rows[:, None] == labels[None, :]).astype(jnp.bfloat16)
        hidden = current.astype(jnp.float32) + jnp.dot(
            onehot, table, preferred_element_type=jnp.float32
        )
        root_mean = jnp.sqrt(jnp.mean(hidden * hidden, axis=-1, keepdims=True) + epsilon)
        modulation = gain_row * (1.0 + 0.5 * jnp.sin(timestep * freq_row))
        normed = (hidden / root_mean * modulation[None, :]).astype(jnp.bfloat16)
        projected = jnp.dot(normed, weights, preferred_element_type=jnp.float32).astype(
            jnp.bfloat16
        )
        query_heads = projected[:, :q_cols].reshape(frames, heads_local, head_size)
        keyval_heads = projected[:, q_cols:].reshape(frames, kv_local, 2, head_size)
        head_outputs = []
        for head in range(heads_local):
            key_rows = keyval_heads[:, head // group_size, 0]
            value_rows = keyval_heads[:, head // group_size, 1]
            scores = (
                lax.dot_general(
                    query_heads[:, head],
                    key_rows,
                    (((1,), (1,)), ((), ())),
                    preferred_element_type=jnp.float32,
                )
                * score_scale
            )
            scores = scores + bias_local[head] * key_flags[None, :]
            row_max = jnp.max(scores, axis=-1, keepdims=True)
            exponent = jnp.exp(scores - row_max)
            probabilities = (exponent / jnp.sum(exponent, axis=-1, keepdims=True)).astype(
                jnp.bfloat16
            )
            head_outputs.append(
                jnp.dot(probabilities, value_rows, preferred_element_type=jnp.float32).astype(
                    jnp.bfloat16
                )
            )
        attended = jnp.concatenate(head_outputs, axis=1)
        hidden_local = lax.dynamic_slice_in_dim(current, seq_idx * q_cols, q_cols, 1).astype(
            jnp.float32
        ) + jnp.dot(onehot, table_local, preferred_element_type=jnp.float32)
        output = (hidden_local + gate_local[None, :] * attended.astype(jnp.float32)).astype(
            jnp.bfloat16
        )
        outputs.append(output)
        if step + lag < steps:
            piece = passed_along(output, "pipe", 1)
            handed[step + lag] = lax.all_gather(piece, "seq", axis=1, tiled=True)

    factor = float(turns * rep_count * frames) ** (-0.5)
    total = None
    rows_out = []
    for turn in range(turns):
        if lag == 2:
            own = jnp.where(section_idx == 0, outputs[turn], outputs[turn + 1])
        else:
            own = outputs[turn]
        term = lax.dot_general(
            own, cot_all[turn], (((0,), (0,)), ((), ())), preferred_element_type=jnp.float32
        )
        total = term if total is None else total + term
        rows_out.append(lax.all_to_all(own, "seq", split_axis=0, concat_axis=1, tiled=True))
    section_out = jnp.stack(rows_out)[None, :, None]
    grad_parts = lax.all_to_all(
        (total * factor).astype(jnp.bfloat16).reshape(rep_count, q_cols // rep_count, feat_count),
        "dp",
        split_axis=0,
        concat_axis=0,
        tiled=True,
    )
    grad_rows = jnp.sum(grad_parts.astype(jnp.float32), axis=0)
    return (section_out, grad_rows[None])


def solution(mesh):
    in_specs = (
        P("pipe", None, "dp", "seq", None),
        P(None, "dp", "seq"),
        P(None, "dp", None),
        P(None, "dp"),
        P("pipe", ("seq", "dp"), None),
        P("pipe", ("seq", "dp"), None),
        P("pipe", None),
        P("pipe", None),
        P("pipe", None, None),
        P("pipe", None),
        P("pipe", None),
        P("pipe", None, "dp", "seq", None),
    )
    out_specs = (P("pipe", None, "dp", "seq", None), P("pipe", ("seq", "dp"), None))
    return jax.shard_map(body, mesh=mesh, in_specs=in_specs, out_specs=out_specs, check_vma=False)
```

```python
import functools
import math

import jax
import jax.numpy as jnp
from jax import lax
from jax.experimental import pallas as pl
from jax.experimental.pallas import tpu as pltpu
from jax.sharding import PartitionSpec as P

epsilon = 1e-06


def passed_along(value, axis, steps):
    count = lax.axis_size(axis)
    first, last = (max(0, -steps), min(count, count - steps))
    return lax.ppermute(value, axis, [(source, source + steps) for source in range(first, last)])


def ring(value, axis):
    count = lax.axis_size(axis)
    return lax.ppermute(value, axis, [(source, (source + 1) % count) for source in range(count)])


def swap(value, bit):
    count = lax.axis_size("seq")
    return lax.ppermute(value, "seq", [(source, source ^ bit) for source in range(count)])


def handed_over(value):
    return lax.ppermute(value, "pipe", [(0, 1), (1, 0)])


def shifted(value, axis, shift):
    count = lax.axis_size(axis)
    return lax.ppermute(value, axis, [(source, (source + shift) % count) for source in range(count)])


def fold(index):
    return index ^ (index >> 1)


def ring_step(value):
    count = lax.axis_size("dp")
    pairs = [(fold(place), fold((place + 1) % count)) for place in range(count)]
    return lax.ppermute(value, "dp", pairs)


def offsets_of(count):
    offsets = [0]
    bit = count // 2
    while bit:
        offsets = offsets + [offset ^ bit for offset in offsets]
        bit //= 2
    return offsets


def turn_and_batch(step, turns):
    section = lax.axis_index("pipe")
    turn = jnp.clip(step - section, 0, turns - 1)
    return turn, turn - section + 1


def pack_kernel(wq, wkv, *refs):
    outs, (queries, keyvals, sems) = refs[:-3], refs[-3:]
    parts, _, cols = outs[0].shape
    half = cols // 2
    seq = lax.axis_index("seq")
    copies = []
    for m in range(len(outs)):
        start = pl.multiple_of((seq ^ m) * cols, 128)
        for k, (source, held) in enumerate(((wq, queries), (wkv, keyvals))):
            copies.append(
                pltpu.make_async_copy(
                    source.at[0, :, pl.ds(start, cols)], held.at[m], sems.at[2 * m + k]
                )
            )
    for copy in copies:
        copy.start()
    for m, out in enumerate(outs):
        copies[2 * m].wait()
        copies[2 * m + 1].wait()
        for part in range(parts):
            lanes = slice(part * half, (part + 1) * half)
            out[part] = jnp.concatenate([queries[m][:, lanes], keyvals[m][:, lanes]], axis=1)


def pair_kernel(deps, *refs):
    out = refs[-1]
    for at, ref in enumerate(refs[deps:-1]):
        out[at] = ref[...]


def far_kernel(dep, first, second, *outs):
    for part, out in enumerate(outs):
        out[0] = first[part]
        out[1] = second[part]


def part_kernel(part, near, far, *outs):
    for at in range(2):
        outs[0][at] = near[at, part]
        if len(outs) == 1:
            outs[0][at + 2] = far[at]
        else:
            outs[1][at] = far[at]


def place(hop, hops, blocks, weights):
    seq, rep = lax.axis_index("seq"), lax.axis_index("dp")
    for m, block in enumerate(blocks):
        rows = block.shape[0]
        at = (seq ^ m) * hops + fold(lax.rem(fold(rep) + hops - hop, hops))
        weights[pl.ds(pl.multiple_of(at * rows, 16), rows)] = block[...]


def blocks_in(chunk):
    return [ref.at[m] for ref in chunk for m in range(ref.shape[0])]


def place_kernel(part, hops, near, far, *refs):
    chunk, weights = refs[:-1], refs[-1]
    place(0, hops, [near.at[0, part], near.at[1, part], far.at[0], far.at[1]], weights)
    place(1, hops, blocks_in(chunk), weights)


def first_kernel(turns, far, incoming, contacts, out, states):
    rows = incoming.shape[3]
    for turn in range(2):
        out[turn * rows : (turn + 1) * rows] = incoming[0, turn, 0]
    states[...] = jnp.zeros_like(states)
    for step in range(turns + 1):
        _, batch = turn_and_batch(step, turns)
        states[step : step + 1] = contacts[batch].astype(jnp.float32)
    out[2 * rows :, : states.shape[1]] = states[...].astype(jnp.bfloat16)


def second_kernel(dep, incoming, cotangent, out):
    turns, rows, feats = cotangent.shape[1], cotangent.shape[3], cotangent.shape[4]
    out[:rows] = incoming[0, 2, 0]
    for turn in range(turns):
        out[rows:, turn * feats : (turn + 1) * feats] = cotangent[0, turn, 0]


def columns_of(rows_of, pieces, rows):
    labels = lax.broadcasted_iota(jnp.int32, (32, rows), 0)
    columns = []
    for i in range(pieces):
        state, flag = rows_of(i)
        one = jnp.zeros((32, rows), jnp.float32)
        if state is not None:
            one = jnp.where(labels == state, 1.0, 0.0)
        if flag is not None:
            one = jnp.where(labels == 16, flag, one)
        columns.append(one.T)
    return jnp.concatenate(columns, axis=0)


def modulation(step, turns, times, gain, freq):
    _, batch = turn_and_batch(step, turns)
    return gain[...] * (1.0 + 0.5 * jnp.sin(times[0, batch].astype(jnp.float32) * freq[...]))


def norm_kernel(turns, pieces, times, table, gain, freq, *refs):
    sources, refs = refs[:pieces], refs[pieces:]
    scaled, scales, owns, embeds, mod = refs[0:2], refs[2:4], refs[4:6], refs[6:8], refs[8]
    first, sems = refs[9 : 9 + pieces], refs[9 + pieces]
    copies = [
        pltpu.make_async_copy(sources[i], first[i], sems.at[i]) for i in range(pieces)
    ]
    for copy in copies:
        copy.start()
    for copy in copies:
        copy.wait()
    frames, width = scaled[0].shape
    rows, cols = frames // pieces, owns[0].shape[1]
    seq = lax.axis_index("seq")
    offsets = offsets_of(pieces)
    for step in range(turns + 1):

        def state_of(i):
            state = first[i][2 * rows : 2 * rows + 16, :rows][step : step + 1]
            return state.astype(jnp.float32).astype(jnp.int32), None

        onehot = columns_of(state_of, pieces, rows)[:, : table.shape[1]].astype(jnp.bfloat16)
        if step >= 2:
            for at in range(0, width, 256):
                embeds[step - 2][:, at : at + 256] = jnp.dot(
                    onehot, table[0, :, at : at + 256], preferred_element_type=jnp.float32
                ).astype(jnp.bfloat16)
            continue
        turn, _ = turn_and_batch(step, turns)
        at = pl.multiple_of(jnp.minimum(turn, 1) * rows, 128)
        mod[...] = modulation(step, turns, times, gain, freq)
        total = jnp.zeros((frames, 128), jnp.float32)
        for i in range(pieces):
            lanes = pl.ds(pl.multiple_of((seq ^ offsets[i]) * cols, 128), cols)
            current = jnp.concatenate([first[p][pl.ds(at, rows), lanes] for p in range(pieces)])
            hidden = current.astype(jnp.float32) + jnp.dot(
                onehot, table[0, :, lanes], preferred_element_type=jnp.float32
            )
            for lane in range(0, cols, 128):
                piece = hidden[:, lane : lane + 128]
                total = total + piece * piece
            scaled[step][:, lanes] = (hidden * mod[:, lanes]).astype(jnp.bfloat16)
            if i == 0:
                owns[step][...] = hidden
        mean = jnp.sum(total, axis=1, keepdims=True) * (1.0 / width)
        scales[step][...] = jnp.broadcast_to(lax.rsqrt(mean + epsilon), (frames, 128))


def dense(value, lead):
    frames = value.shape[0]
    rest = value[:, :64] if lead else value[:, 128:]
    full = value[:, 64:] if lead else value[:, :128]
    rest = jnp.concatenate([rest[: frames // 2], rest[frames // 2 :]], axis=1)
    return jnp.concatenate([full, rest], axis=0)


def undense(left, right, frames):
    middle = []
    for ref in (left, right):
        rest = ref[frames:]
        middle.append(jnp.concatenate([rest[:, :64], rest[:, 64:]], axis=0))
    return jnp.concatenate([left[:frames], jnp.concatenate(middle, axis=1), right[:frames]], axis=1)


def second_pair_kernel(dep, mine, across, out):
    out[0] = mine[...]
    out[1] = across[...]


def opened(pieces):
    return list(pieces[:2]) + [pieces[2].at[0], pieces[2].at[1]]


def step_kernel(cfg, *refs):
    step, has_relay, parts = cfg["step"], cfg["has_relay"], cfg["parts"]
    pieces, hops, head, turns = cfg["pieces"], cfg["hops"], cfg["head"], cfg["turns"]
    heads, group = cfg["heads"], cfg["group"]
    refs = list(refs)

    def take(count):
        taken, refs[:count] = refs[:count], []
        return taken

    bias, times, gain, freq, gate, flags = take(6)
    if has_relay:
        second, embed, relay = opened(take(3)), take(1)[0], take(2 * pieces)
    else:
        scaled, scales, own_hidden = take(3)
    streams = cfg["streams"]
    chunks = [take(streams), take(streams)] if step == 0 else None
    weights = take(len(parts))
    left = take(1)[0] if parts == (1,) else None
    sends = take(1)[0] if len(parts) == 1 else None
    out = take(1)[0]
    if step == 0:
        weights = take(1)
    proj, att = take(2)
    if has_relay:
        scaled, scales, own_hidden, mod = take(4)
    offsets = offsets_of(pieces)
    frames, width = scaled.shape
    cols = att.shape[0]
    half = cols // 2
    rows = frames // pieces
    seq, section = lax.axis_index("seq"), lax.axis_index("pipe")
    _, batch = turn_and_batch(step, turns)

    if step == 0:
        for hop, chunk in zip((2, 3), chunks):
            place(hop, hops, blocks_in(chunk), weights[0])

    def normalize(relayed):
        total = jnp.zeros((frames, 128), jnp.float32)
        for i in range(pieces):
            lanes = pl.ds(pl.multiple_of((seq ^ offsets[i]) * cols, 128), cols)
            if relayed:
                value = undense(relay[i], relay[pieces + i], frames)
                order = [offsets.index(offsets[i] ^ offsets[p]) for p in range(pieces)]
                blocks = [value[j * rows : (j + 1) * rows] for j in order]
            else:
                blocks = [second[p][:rows, lanes] for p in range(pieces)]
            hidden = jnp.concatenate(blocks, axis=0).astype(jnp.float32)
            hidden = hidden + embed[:, lanes].astype(jnp.float32)
            for lane in range(0, cols, 128):
                piece = hidden[:, lane : lane + 128]
                total = total + piece * piece
            scaled[:, lanes] = (hidden * mod[:, lanes]).astype(jnp.bfloat16)
            if i == 0:
                own_hidden[...] = hidden
        scales[...] = total

    if has_relay:
        mod[...] = modulation(step, turns, times, gain, freq)

        @pl.when(section == 0)
        def _():
            normalize(False)

        @pl.when(section != 0)
        def _():
            normalize(True)

        mean = jnp.sum(scales[...], axis=1, keepdims=True) * (1.0 / width)
        scale = lax.rsqrt(mean + epsilon)
    else:
        scale = scales[:, :1]

    def flag_of(i):
        lanes = pl.ds(pl.multiple_of((seq ^ offsets[i]) * rows, 128), rows)
        return None, flags[batch, :, lanes].astype(jnp.float32)

    flag_column = columns_of(flag_of, pieces, rows)[:, 16:17]
    score_scale = head ** (-0.5) * math.log2(math.e)
    lanes = lax.broadcasted_iota(jnp.int32, (frames, 128), 1)
    row_lanes = lax.broadcasted_iota(jnp.int32, (1, 128), 1)
    flag_lanes = jnp.logical_or(lanes == head, lanes == head + 1)
    pitch = cols + 128

    for k, part in enumerate(parts):
        base = k * pitch
        for at in range(0, cols, 256):
            size = min(256, cols - at)
            lane = at + lax.broadcasted_iota(jnp.int32, (1, size), 1)
            factor = jnp.where(lane < half, score_scale, 1.0)
            projected = jnp.dot(
                scaled[...], weights[k][:, at : at + size], preferred_element_type=jnp.float32
            )
            proj[:, base + at : base + at + size] = (projected * scale * factor).astype(
                jnp.bfloat16
            )
        proj[:, base + cols : base + pitch] = jnp.zeros((frames, 128), jnp.bfloat16)

    def slice_of(at):
        return proj[:, at : at + 128].astype(jnp.float32)

    keys, values = [], []
    for k in range(len(parts)):
        at = k * pitch + half
        key = jnp.where(flag_lanes, flag_column, jnp.where(lanes < head, slice_of(at), 0.0))
        value = jnp.where(
            lanes < head, slice_of(at + head), jnp.where(lanes == head, 1.0, 0.0)
        )
        keys.append(key.astype(jnp.bfloat16))
        values.append(value.T.astype(jnp.bfloat16))

    def scores_of(k, h):
        strength = bias[0, seq * heads + parts[k] * group + h] * math.log2(math.e)
        strength = jnp.zeros((1, 128), jnp.float32) + strength
        coarse = strength.astype(jnp.bfloat16).astype(jnp.float32)
        tail = jnp.where(
            row_lanes == head, coarse, jnp.where(row_lanes == head + 1, strength - coarse, 0.0)
        )
        query = jnp.where(lanes < head, slice_of(k * pitch + h * head), tail).astype(jnp.bfloat16)
        return lax.dot_general(
            keys[k], query, (((1,), (1,)), ((), ())), preferred_element_type=jnp.float32
        )

    tasks = [(k, h) for k in range(len(parts)) for h in range(group)]
    scores = scores_of(*tasks[0])
    for index, (k, h) in enumerate(tasks):
        ahead = scores_of(*tasks[index + 1]) if index + 1 < len(tasks) else None
        top = jnp.max(scores, axis=0, keepdims=True)
        weight = jnp.exp2(scores - top).astype(jnp.bfloat16)
        mixed = jnp.dot(values[k], weight, preferred_element_type=jnp.float32)
        at = (parts[k] * group + h) * head
        att[at : at + head, :] = mixed[:head] * (1.0 / mixed[head : head + 1])
        scores = ahead
    gates = gate[:, pl.ds(pl.multiple_of(seq * cols, 128), cols)]
    first, last = parts[0] * half, (parts[-1] + 1) * half
    attended = att[first:last].T.astype(jnp.bfloat16).astype(jnp.float32)
    output = own_hidden[...][:, first:last] + gates[:, first:last] * attended
    if parts == (0,):
        out[:, :half] = output.astype(jnp.bfloat16)
    elif parts == (1,):
        output_both = jnp.concatenate([left[:, :half].astype(jnp.float32), output], axis=1)
        out[...] = output_both.astype(jnp.bfloat16).reshape(pieces, rows, cols)
    else:
        out[...] = output.astype(jnp.bfloat16).reshape(pieces, rows, cols)
    if sends is not None:
        sends[...] = dense(output, parts == (1,)).astype(jnp.bfloat16)


def tie_kernel(*refs):
    pass


def grad_of(output, second, turn, rows, feats):
    cot = jnp.concatenate(
        [piece[rows : 2 * rows, turn * feats : (turn + 1) * feats] for piece in second], axis=0
    )
    return lax.dot_general(
        output, cot, (((0,), (0,)), ((), ())), preferred_element_type=jnp.float32
    )


def early_kernel(turns, pieces, halves, feats, *refs):
    outs, second = refs[: turns * halves], opened(refs[turns * halves : turns * halves + 3])
    sends, grad = refs[turns * halves + 3 : -1], refs[-1]
    section = lax.axis_index("pipe")
    offsets = offsets_of(pieces)
    part = pieces // halves
    rows = outs[0].shape[1]
    total = None
    for turn in range(turns - 1):
        blocks = []
        for p in range(pieces):
            k, j = p // part, p % part
            block = jnp.where(
                section == 0, outs[turn * halves + k][j], outs[(turn + 1) * halves + k][j]
            )
            sends[offsets[p]][turn] = block
            blocks.append(block)
        share = grad_of(jnp.concatenate(blocks, axis=0), second, turn, rows, feats)
        total = share if total is None else total + share
    grad[...] = total


def share_kernel(turns, pieces, hops, feats, *refs):
    before, now, second, early_grad = refs[0], refs[1], opened(refs[2:5]), refs[5]
    own_grad, grads, total = refs[6], refs[7:-1], refs[-1]
    section, rep = lax.axis_index("pipe"), lax.axis_index("dp")
    rows, cols = before.shape[1:]
    output = jnp.where(section == 0, before[...], now[...]).reshape(pieces * rows, cols)
    share = grad_of(output, second, turns - 1, rows, feats)
    total[...] = (share + early_grad[...]) * float(turns * hops * rows * pieces) ** (-0.5)
    g_rows = cols // hops
    own_grad[...] = total[pl.ds(pl.multiple_of(rep * g_rows, 8), g_rows)]
    for shift in range(1, hops):
        at = pl.multiple_of(lax.rem(rep + shift, hops) * g_rows, 8)
        grads[shift - 1][...] = total[pl.ds(at, g_rows)].astype(jnp.bfloat16)


def settle_kernel(turns, pieces, *refs):
    before, now, early = refs[0], refs[1], refs[2 : pieces + 1]
    late, (section_out, rows_out, sem) = refs[pieces + 1 : -3], refs[-3:]
    section, seq = lax.axis_index("pipe"), lax.axis_index("seq")
    offsets = offsets_of(pieces)
    rows, cols = early[0].shape[1:]
    for p in range(pieces):
        late[offsets[p]][...] = jnp.where(section == 0, before[p], now[p])
    for m in range(pieces - 1):
        lanes = pl.ds(pl.multiple_of((seq ^ m) * cols, 128), cols)
        for turn in range(turns - 1):
            rows_out[turn, :, lanes] = early[m][turn]
    copy = pltpu.make_async_copy(rows_out, section_out.at[pl.ds(0, turns - 1)], sem)
    copy.start()
    copy.wait()


def finish_kernel(pieces, hops, *refs):
    held, early, late, refs = refs[0], refs[1], refs[2 : pieces + 2], refs[pieces + 2 :]
    own_grad, parts, (section_out, grad, row_out, sems) = refs[0], refs[1:hops], refs[hops:]
    seq = lax.axis_index("seq")
    cols = late[0].shape[1]
    last_lanes = pl.ds(pl.multiple_of((seq ^ (pieces - 1)) * cols, 128), cols)
    early_copy = pltpu.make_async_copy(
        early, section_out.at[pl.ds(0, early.shape[0]), :, last_lanes], sems.at[0]
    )
    early_copy.start()
    for m in range(pieces):
        lanes = pl.ds(pl.multiple_of((seq ^ m) * cols, 128), cols)
        row_out[:, lanes] = late[m][...]
    copy = pltpu.make_async_copy(row_out, section_out.at[section_out.shape[0] - 1], sems.at[1])
    copy.start()
    total = own_grad[...]
    for part in parts:
        total = total + part[...].astype(jnp.float32)
    grad[...] = total
    early_copy.wait()
    copy.wait()


MIB = 1024 * 1024


def paired_body(
    incoming,
    contacts,
    keyframes,
    timesteps,
    w_query,
    w_keyval,
    norm_gain,
    time_freq,
    contact_table,
    key_bias,
    attn_gate,
    head_cotangent,
):
    seq_count = lax.axis_size("seq")
    hops = lax.axis_size("dp")
    rows, width, turns = incoming.shape[3], incoming.shape[4], incoming.shape[1]
    frames = rows * seq_count
    heads_all = key_bias.shape[1]
    head = width // heads_all
    heads = heads_all // seq_count
    kv_heads = w_keyval.shape[2] // (2 * head * seq_count)
    feats = head_cotangent.shape[4]
    cols = width // seq_count
    w_rows = w_query.shape[1]
    kind = jnp.bfloat16
    smem = pl.BlockSpec(memory_space=pltpu.SMEM)
    vmem = pl.BlockSpec(memory_space=pltpu.VMEM)
    anywhere = pl.BlockSpec(memory_space=pl.ANY)
    shape = jax.ShapeDtypeStruct

    def call(kernel, name, out_shape, in_specs, operands, scratch=(), limit=4, flops=0, **options):
        return pl.pallas_call(
            kernel,
            out_shape=out_shape,
            in_specs=in_specs,
            scratch_shapes=list(scratch),
            compiler_params=pltpu.CompilerParams(vmem_limit_bytes=limit * MIB),
            cost_estimate=pl.CostEstimate(
                flops=flops, bytes_accessed=flops // 512, transcendentals=0
            ),
            name=name,
            **options,
        )(*operands)

    timesteps = timesteps.reshape(1, timesteps.shape[0])

    def pin(value, space=pltpu.VMEM):
        return pltpu.with_memory_space_constraint(value, space)

    packed = call(
        pack_kernel,
        "pack",
        [pltpu.VMEM((2, w_rows, cols), kind)] * seq_count,
        [anywhere, anywhere],
        [pin(w_query, pltpu.HBM), pin(w_keyval, pltpu.HBM)],
        [pltpu.VMEM((seq_count, w_rows, cols), kind)] * 2
        + [pltpu.SemaphoreType.DMA((2 * seq_count,))],
        out_specs=[vmem] * seq_count,
    )
    blocks = [packed[0]] + [swap(packed[m], m) for m in range(1, seq_count)]

    def paired(name, deps, values):
        return call(
            functools.partial(pair_kernel, len(deps)),
            name,
            pltpu.VMEM((2, 2, w_rows, cols), kind),
            [anywhere] * len(deps) + [vmem] * 2,
            deps + values,
            out_specs=vmem,
        )

    near = paired("near", [], blocks[:2])
    near_next = ring_step(near)
    far = call(
        far_kernel,
        "far",
        [pltpu.VMEM((2, w_rows, cols), kind)] * 2,
        [anywhere, vmem, vmem],
        [near_next] + blocks[2:],
        out_specs=[vmem] * 2,
    )
    far_next = [ring_step(value) for value in far]
    streams = (2, 1)
    rings, partial = [], []
    for part in range(2):
        count = streams[part]
        chunk = call(
            functools.partial(part_kernel, part),
            "part%d" % part,
            [pltpu.VMEM((seq_count // count, w_rows, cols), kind)] * count,
            [vmem, vmem],
            [near_next, far_next[part]],
            out_specs=[vmem] * count,
        )
        rings.append([list(chunk)])
        partial.append(
            call(
                functools.partial(place_kernel, part, hops),
                "place%d" % part,
                pltpu.VMEM((width, cols), kind),
                [vmem] * (2 + count),
                [pin(near), pin(far[part])] + [pin(value) for value in chunk],
                out_specs=vmem,
            )
        )
    for ring in rings:
        ring.append([ring_step(value) for value in ring[-1]])
    rings[0].append([ring_step(value) for value in rings[0][-1]])

    def tie(values, deps):
        return call(
            tie_kernel,
            "tie",
            [shape(value.shape, kind) for value in values],
            [anywhere] * (len(values) + len(deps)),
            list(values) + list(deps),
            out_specs=[anywhere] * len(values),
            input_output_aliases={i: i for i in range(len(values))},
        )

    mine = call(
        functools.partial(first_kernel, turns),
        "first",
        pltpu.VMEM((2 * rows + 16, width), kind),
        [anywhere, vmem, vmem],
        [far[0], incoming, contacts],
        [pltpu.VMEM((16, 128), jnp.float32)],
        out_specs=vmem,
    )
    across = swap(mine, 2)
    beside = swap(mine, 1)
    (across,) = tie([across], rings[0][1] + rings[1][1])
    first = [mine, across, beside, swap(across, 1)]
    prepared = call(
        functools.partial(norm_kernel, turns, seq_count),
        "norm",
        [pltpu.VMEM((frames, width), kind)] * 2
        + [pltpu.VMEM((frames, 128), jnp.float32)] * 2
        + [pltpu.VMEM((frames, cols), jnp.float32)] * 2
        + [pltpu.VMEM((frames, width), kind)] * 2,
        [smem] + [vmem] * 3 + [anywhere] * seq_count,
        [timesteps, contact_table, norm_gain, time_freq]
        + first,
        [pltpu.VMEM((1, width), jnp.float32)]
        + [pltpu.VMEM((2 * rows + 16, width), kind)] * seq_count
        + [pltpu.SemaphoreType.DMA((seq_count,))],
        12,
        out_specs=[vmem] * 8,
    )

    mine = call(
        second_kernel,
        "second",
        pltpu.VMEM((2 * rows, width), kind),
        [anywhere, vmem, vmem],
        [across, incoming, head_cotangent],
        out_specs=vmem,
    )
    second = [mine, swap(mine, 2)]

    rings[1][1] = list(tie(rings[1][1], [prepared[0]]))
    rings[1].append([ring_step(value) for value in rings[1][1]])

    common = [key_bias, timesteps, norm_gain, time_freq, attn_gate, keyframes]

    def run_step(step, parts, large, out_shape, aliases):
        cfg = {
            "step": step,
            "has_relay": step >= 2,
            "parts": parts,
            "pieces": seq_count,
            "hops": hops,
            "head": head,
            "heads": heads,
            "group": heads // kv_heads,
            "turns": turns,
            "streams": streams[parts[0]],
        }
        scratch = [
            pltpu.VMEM((frames, len(parts) * (cols + 128)), kind),
            pltpu.VMEM((cols, frames), jnp.float32),
        ]
        if step >= 2:
            scratch += [
                pltpu.VMEM((frames, width), kind),
                pltpu.VMEM((frames, 128), jnp.float32),
                pltpu.VMEM((frames, cols), jnp.float32),
                pltpu.VMEM((1, width), jnp.float32),
            ]
        operands = common + [pin(value) for value in large]
        return call(
            functools.partial(step_kernel, cfg),
            "step%d%s" % (step, "".join("ab"[part] for part in parts)),
            out_shape,
            [smem, smem] + [vmem] * (len(operands) - 2),
            operands,
            scratch,
            16,
            len(parts) * frames * (2 * width * cols + 2 * heads * frames * head),
            out_specs=[vmem] * len(out_shape),
            input_output_aliases=aliases,
        )

    whole = pltpu.VMEM((seq_count, rows, cols), kind)
    sent = pltpu.VMEM((frames * 3 // 2, 128), kind)
    weights = list(partial)
    relays, lefts, outputs = ([], []), [], []
    for part in range(2):
        for step in range(2):
            large = [prepared[step], prepared[2 + step], prepared[4 + step]]
            if step == 0:
                chunks = rings[part][1] + rings[part][2]
                if part:
                    last = tie(rings[part][2], [relays[0][0][0], lefts[1]])
                    chunks = rings[part][1] + list(last)
                large += chunks
            large += [weights[part]]
            aliases = {len(common) + len(large) - 1: 2} if step == 0 else {}
            out_shape = [sent, whole if part else pltpu.VMEM((frames, 256), kind)]
            if step == 0:
                out_shape += [pltpu.VMEM((width, cols), kind)]
            if part:
                large += [lefts[step]]
            results = run_step(step, (part,), large, out_shape, aliases)
            if step == 0:
                weights[part] = results[2]
            (outputs if part else lefts).append(results[1])
            piece = handed_over(results[0])
            relays[step].append([piece, None if part and not step else swap(piece, 2)])
    beside = call(
        second_pair_kernel,
        "beside",
        pltpu.VMEM((2,) + second[0].shape, kind),
        [anywhere, vmem, vmem],
        [outputs[0]] + second,
        limit=8,
        out_specs=vmem,
    )
    second = [second[0], second[1], swap(beside, 1)]

    (piece,) = tie([relays[0][1][0]], [outputs[1], second[2]])
    relays[0][1] = [piece, swap(piece, 2)]
    def complete(crossing):
        return [
            piece
            for mine, across in crossing
            for piece in (mine, across, swap(mine, 1), swap(across, 1))
        ]

    relay = complete(relays[0])
    (output,) = run_step(2, (0, 1), second + [prepared[6]] + relay + weights, [whole], {})
    outputs.append(output)
    early = call(
        functools.partial(early_kernel, turns, seq_count, 1, feats),
        "early",
        [shape((turns - 1, rows, cols), kind)] * seq_count + [shape((cols, feats), jnp.float32)],
        [vmem] * (turns + len(second)),
        outputs + second,
        limit=8,
        out_specs=[vmem] * (seq_count + 1),
    )
    early, early_grad = list(early[:-1]), early[-1]
    early = [early[0]] + [swap(early[m], m) for m in range(1, seq_count)]
    tied = tie([piece for pair in relays[1] for piece in pair], [early_grad])
    relay = complete([(tied[0], tied[1]), (tied[2], tied[3])])
    (output,) = run_step(3, (0, 1), second + [prepared[7]] + relay + weights, [whole], {})
    outputs.append(output)

    g_shape = (cols // hops, feats)
    operands = outputs[-2:] + second + [early_grad]
    grads = call(
        functools.partial(share_kernel, turns, seq_count, hops, feats),
        "share",
        [shape(g_shape, jnp.float32)] + [shape(g_shape, kind)] * (hops - 1),
        [vmem] * len(operands),
        operands,
        [pltpu.VMEM((cols, feats), jnp.float32)],
        8,
        out_specs=[vmem] * hops,
    )
    operands = outputs[-2:] + early[:-1]
    settled = call(
        functools.partial(settle_kernel, turns, seq_count),
        "settle",
        [shape((rows, cols), kind)] * seq_count + [shape((turns, rows, width), kind)],
        [vmem] * len(operands),
        operands,
        [pltpu.VMEM((turns - 1, rows, width), kind), pltpu.SemaphoreType.DMA],
        8,
        out_specs=[vmem] * seq_count + [anywhere],
    )
    late, held = settled[:seq_count], settled[-1]
    late = [late[0]] + [swap(late[m], m) for m in range(1, seq_count)]
    grads = [grads[0]] + [shifted(grads[k], "dp", k) for k in range(1, hops)]
    section_out, grad_rows = call(
        functools.partial(finish_kernel, seq_count, hops),
        "finish",
        [shape((turns, rows, width), kind), shape(g_shape, jnp.float32)],
        [anywhere] + [vmem] * (seq_count + hops + 1),
        [held, early[-1]] + late + grads,
        [pltpu.VMEM((rows, width), kind), pltpu.SemaphoreType.DMA((2,))],
        out_specs=[anywhere, vmem],
        input_output_aliases={0: 0},
    )
    return (section_out[None, :, None], grad_rows[None])


def body(incoming, contacts, keyframes, timesteps, w_query, *others):
    count = lax.axis_size("seq")
    cols = w_query.shape[2] // count
    paired = (
        lax.axis_size("pipe") == 2
        and lax.axis_size("dp") == 4
        and count == 4
        and cols % 128 == 0
        and w_query.shape[1] % 16 == 0
        and incoming.shape[3] == 128
        and incoming.shape[1] == 3
    )
    chosen = paired_body if paired else general_body
    return chosen(incoming, contacts, keyframes, timesteps, w_query, *others)


def general_body(
    incoming,
    contacts,
    keyframes,
    timesteps,
    w_query,
    w_keyval,
    norm_gain,
    time_freq,
    contact_table,
    key_bias,
    attn_gate,
    head_cotangent,
):
    section_idx = lax.axis_index("pipe")
    seq_idx = lax.axis_index("seq")
    rep_idx = lax.axis_index("dp")
    seq_count = lax.axis_size("seq")
    section_count = lax.axis_size("pipe")
    rep_count = lax.axis_size("dp")
    tok_rows = incoming.shape[3]
    width = incoming.shape[4]
    turns = incoming.shape[1]
    frames = tok_rows * seq_count
    heads_all = key_bias.shape[1]
    head_size = width // heads_all
    heads_local = heads_all // seq_count
    kv_width = w_keyval.shape[2]
    kv_local = kv_width // (2 * head_size * seq_count)
    group_size = heads_local // kv_local
    feat_count = head_cotangent.shape[4]
    score_scale = head_size ** (-0.5)
    q_cols = width // seq_count
    kv_cols = kv_width // seq_count
    w_rows = w_query.shape[1]

    w_parts = jnp.concatenate(
        [
            w_query[0].reshape(w_rows, seq_count, q_cols),
            w_keyval[0].reshape(w_rows, seq_count, kv_cols),
        ],
        axis=2,
    ).transpose(1, 0, 2)
    block = lax.all_to_all(w_parts, "seq", split_axis=0, concat_axis=0, tiled=True)
    weights = jnp.zeros((seq_count, rep_count, w_rows, q_cols + kv_cols), jnp.bfloat16)
    for hop in range(rep_count):
        owner = lax.rem(rep_idx + rep_count - hop, rep_count)
        weights = lax.dynamic_update_slice_in_dim(weights, block[:, None], owner, 1)
        if hop + 1 < rep_count:
            block = ring(block, "dp")
    weights = weights.reshape(width, q_cols + kv_cols)

    gain_row = norm_gain[0]
    freq_row = time_freq[0]
    table = contact_table[0]
    gate_local = lax.dynamic_slice_in_dim(attn_gate[0], seq_idx * q_cols, q_cols)
    table_local = lax.dynamic_slice_in_dim(table, seq_idx * q_cols, q_cols, 1)
    bias_local = lax.dynamic_slice_in_dim(key_bias[0], seq_idx * heads_local, heads_local)
    contact_all = lax.all_gather(contacts[:, 0, :], "seq", axis=1, tiled=True)
    key_all = keyframes[:, 0, :]
    step_all = timesteps[:, 0]
    labels = jnp.arange(table.shape[0], dtype=jnp.int32)
    cot_all = lax.all_gather(head_cotangent[0, :, 0], "seq", axis=1, tiled=True)

    lag = 2 if section_count == 2 else 1
    if lag == 2:
        steps = turns + 1
    else:
        steps = turns

    def turn_at(step):
        if lag == 1:
            return jnp.int32(step)
        return jnp.clip(step - section_idx, 0, turns - 1)

    outputs = []
    handed = {}
    for step in range(steps):
        turn = turn_at(step)
        fresh = lax.dynamic_index_in_dim(incoming[0, :, 0], turn, 0, keepdims=False)
        current = lax.all_gather(fresh, "seq", axis=0, tiled=True)
        if step in handed:
            current = jnp.where((section_idx == 0) | (turn == 0), current, handed[step])
        batch_idx = turn - section_idx + section_count - 1
        contact_rows = lax.dynamic_index_in_dim(contact_all, batch_idx, 0, keepdims=False)
        key_flags = lax.dynamic_index_in_dim(key_all, batch_idx, 0, keepdims=False).astype(
            jnp.float32
        )
        timestep = lax.dynamic_index_in_dim(step_all, batch_idx, 0, keepdims=False).astype(
            jnp.float32
        )
        onehot = (contact_rows[:, None] == labels[None, :]).astype(jnp.bfloat16)
        hidden = current.astype(jnp.float32) + jnp.dot(
            onehot, table, preferred_element_type=jnp.float32
        )
        root_mean = jnp.sqrt(jnp.mean(hidden * hidden, axis=-1, keepdims=True) + epsilon)
        modulation = gain_row * (1.0 + 0.5 * jnp.sin(timestep * freq_row))
        normed = (hidden / root_mean * modulation[None, :]).astype(jnp.bfloat16)
        projected = jnp.dot(normed, weights, preferred_element_type=jnp.float32).astype(
            jnp.bfloat16
        )
        query_heads = projected[:, :q_cols].reshape(frames, heads_local, head_size)
        keyval_heads = projected[:, q_cols:].reshape(frames, kv_local, 2, head_size)
        head_outputs = []
        for head in range(heads_local):
            key_rows = keyval_heads[:, head // group_size, 0]
            value_rows = keyval_heads[:, head // group_size, 1]
            scores = (
                lax.dot_general(
                    query_heads[:, head],
                    key_rows,
                    (((1,), (1,)), ((), ())),
                    preferred_element_type=jnp.float32,
                )
                * score_scale
            )
            scores = scores + bias_local[head] * key_flags[None, :]
            row_max = jnp.max(scores, axis=-1, keepdims=True)
            exponent = jnp.exp(scores - row_max)
            probabilities = (exponent / jnp.sum(exponent, axis=-1, keepdims=True)).astype(
                jnp.bfloat16
            )
            head_outputs.append(
                jnp.dot(probabilities, value_rows, preferred_element_type=jnp.float32).astype(
                    jnp.bfloat16
                )
            )
        attended = jnp.concatenate(head_outputs, axis=1)
        hidden_local = lax.dynamic_slice_in_dim(current, seq_idx * q_cols, q_cols, 1).astype(
            jnp.float32
        ) + jnp.dot(onehot, table_local, preferred_element_type=jnp.float32)
        output = (hidden_local + gate_local[None, :] * attended.astype(jnp.float32)).astype(
            jnp.bfloat16
        )
        outputs.append(output)
        if step + lag < steps:
            piece = passed_along(output, "pipe", 1)
            handed[step + lag] = lax.all_gather(piece, "seq", axis=1, tiled=True)

    factor = float(turns * rep_count * frames) ** (-0.5)
    total = None
    rows_out = []
    for turn in range(turns):
        if lag == 2:
            own = jnp.where(section_idx == 0, outputs[turn], outputs[turn + 1])
        else:
            own = outputs[turn]
        term = lax.dot_general(
            own, cot_all[turn], (((0,), (0,)), ((), ())), preferred_element_type=jnp.float32
        )
        total = term if total is None else total + term
        rows_out.append(lax.all_to_all(own, "seq", split_axis=0, concat_axis=1, tiled=True))
    section_out = jnp.stack(rows_out)[None, :, None]
    grad_parts = lax.all_to_all(
        (total * factor).astype(jnp.bfloat16).reshape(rep_count, q_cols // rep_count, feat_count),
        "dp",
        split_axis=0,
        concat_axis=0,
        tiled=True,
    )
    grad_rows = jnp.sum(grad_parts.astype(jnp.float32), axis=0)
    return (section_out, grad_rows[None])


def solution(mesh):
    in_specs = (
        P("pipe", None, "dp", "seq", None),
        P(None, "dp", "seq"),
        P(None, "dp", None),
        P(None, "dp"),
        P("pipe", ("seq", "dp"), None),
        P("pipe", ("seq", "dp"), None),
        P("pipe", None),
        P("pipe", None),
        P("pipe", None, None),
        P("pipe", None),
        P("pipe", None),
        P("pipe", None, "dp", "seq", None),
    )
    out_specs = (P("pipe", None, "dp", "seq", None), P("pipe", ("seq", "dp"), None))
    return jax.shard_map(body, mesh=mesh, in_specs=in_specs, out_specs=out_specs, check_vma=False)
```

```python
import functools
import math

import jax
import jax.numpy as jnp
from jax import lax
from jax.experimental import pallas as pl
from jax.experimental.pallas import tpu as pltpu
from jax.sharding import PartitionSpec as P

epsilon = 1e-06


def passed_along(value, axis, steps):
    count = lax.axis_size(axis)
    first, last = (max(0, -steps), min(count, count - steps))
    return lax.ppermute(value, axis, [(source, source + steps) for source in range(first, last)])


def ring(value, axis):
    count = lax.axis_size(axis)
    return lax.ppermute(value, axis, [(source, (source + 1) % count) for source in range(count)])


def swap(value, bit):
    count = lax.axis_size("seq")
    return lax.ppermute(value, "seq", [(source, source ^ bit) for source in range(count)])


def handed_over(value):
    return lax.ppermute(value, "pipe", [(0, 1), (1, 0)])


def shifted(value, axis, shift):
    count = lax.axis_size(axis)
    return lax.ppermute(value, axis, [(source, (source + shift) % count) for source in range(count)])


def fold(index):
    return index ^ (index >> 1)


def ring_step(value):
    count = lax.axis_size("dp")
    pairs = [(fold(place), fold((place + 1) % count)) for place in range(count)]
    return lax.ppermute(value, "dp", pairs)


def offsets_of(count):
    offsets = [0]
    bit = count // 2
    while bit:
        offsets = offsets + [offset ^ bit for offset in offsets]
        bit //= 2
    return offsets


def turn_and_batch(step, turns):
    section = lax.axis_index("pipe")
    turn = jnp.clip(step - section, 0, turns - 1)
    return turn, turn - section + 1


def pack_kernel(wq, wkv, *refs):
    outs, (queries, keyvals, sems) = refs[:-3], refs[-3:]
    parts, _, cols = outs[0].shape
    half = cols // 2
    seq = lax.axis_index("seq")
    copies = []
    for m in range(len(outs)):
        start = pl.multiple_of((seq ^ m) * cols, 128)
        for k, (source, held) in enumerate(((wq, queries), (wkv, keyvals))):
            copies.append(
                pltpu.make_async_copy(
                    source.at[0, :, pl.ds(start, cols)], held.at[m], sems.at[2 * m + k]
                )
            )
    for copy in copies:
        copy.start()
    for m, out in enumerate(outs):
        copies[2 * m].wait()
        copies[2 * m + 1].wait()
        for part in range(parts):
            lanes = slice(part * half, (part + 1) * half)
            out[part] = jnp.concatenate([queries[m][:, lanes], keyvals[m][:, lanes]], axis=1)


def pair_kernel(deps, *refs):
    out = refs[-1]
    for at, ref in enumerate(refs[deps:-1]):
        out[at] = ref[...]


def far_kernel(dep, first, second, *outs):
    for part, out in enumerate(outs):
        out[0] = first[part]
        out[1] = second[part]


def part_kernel(part, near, far, *outs):
    for at in range(2):
        outs[0][at] = near[at, part]
        if len(outs) == 1:
            outs[0][at + 2] = far[at]
        else:
            outs[1][at] = far[at]


def place(hop, hops, blocks, weights):
    seq, rep = lax.axis_index("seq"), lax.axis_index("dp")
    for m, block in enumerate(blocks):
        rows = block.shape[0]
        at = (seq ^ m) * hops + fold(lax.rem(fold(rep) + hops - hop, hops))
        weights[pl.ds(pl.multiple_of(at * rows, 16), rows)] = block[...]


def blocks_in(chunk):
    return [ref.at[m] for ref in chunk for m in range(ref.shape[0])]


def place_kernel(part, hops, near, far, *refs):
    chunk, weights = refs[:-1], refs[-1]
    place(0, hops, [near.at[0, part], near.at[1, part], far.at[0], far.at[1]], weights)
    place(1, hops, blocks_in(chunk), weights)


def first_kernel(turns, far, incoming, contacts, out, states):
    rows = incoming.shape[3]
    for turn in range(2):
        out[turn * rows : (turn + 1) * rows] = incoming[0, turn, 0]
    states[...] = jnp.zeros_like(states)
    for step in range(turns + 1):
        _, batch = turn_and_batch(step, turns)
        states[step : step + 1] = contacts[batch].astype(jnp.float32)
    out[2 * rows :, : states.shape[1]] = states[...].astype(jnp.bfloat16)


def second_kernel(dep, incoming, cotangent, out):
    turns, rows, feats = cotangent.shape[1], cotangent.shape[3], cotangent.shape[4]
    out[:rows] = incoming[0, 2, 0]
    for turn in range(turns):
        out[rows:, turn * feats : (turn + 1) * feats] = cotangent[0, turn, 0]


def columns_of(rows_of, pieces, rows):
    labels = lax.broadcasted_iota(jnp.int32, (32, rows), 0)
    columns = []
    for i in range(pieces):
        state, flag = rows_of(i)
        one = jnp.zeros((32, rows), jnp.float32)
        if state is not None:
            one = jnp.where(labels == state, 1.0, 0.0)
        if flag is not None:
            one = jnp.where(labels == 16, flag, one)
        columns.append(one.T)
    return jnp.concatenate(columns, axis=0)


def modulation(step, turns, times, gain, freq):
    _, batch = turn_and_batch(step, turns)
    return gain[...] * (1.0 + 0.5 * jnp.sin(times[0, batch].astype(jnp.float32) * freq[...]))


def norm_kernel(turns, pieces, times, table, gain, freq, *refs):
    sources, refs = refs[:pieces], refs[pieces:]
    scaled, scales, owns, embeds, mod = refs[0:2], refs[2:4], refs[4:6], refs[6:8], refs[8]
    first, sems = refs[9 : 9 + pieces], refs[9 + pieces]
    copies = [
        pltpu.make_async_copy(sources[i], first[i], sems.at[i]) for i in range(pieces)
    ]
    for copy in copies:
        copy.start()
    for copy in copies:
        copy.wait()
    frames, width = scaled[0].shape
    rows, cols = frames // pieces, owns[0].shape[1]
    seq = lax.axis_index("seq")
    offsets = offsets_of(pieces)
    for step in range(turns + 1):

        def state_of(i):
            state = first[i][2 * rows : 2 * rows + 16, :rows][step : step + 1]
            return state.astype(jnp.float32).astype(jnp.int32), None

        onehot = columns_of(state_of, pieces, rows)[:, : table.shape[1]].astype(jnp.bfloat16)
        if step >= 2:
            for at in range(0, width, 256):
                embeds[step - 2][:, at : at + 256] = jnp.dot(
                    onehot, table[0, :, at : at + 256], preferred_element_type=jnp.float32
                ).astype(jnp.bfloat16)
            continue
        turn, _ = turn_and_batch(step, turns)
        at = pl.multiple_of(jnp.minimum(turn, 1) * rows, 128)
        mod[...] = modulation(step, turns, times, gain, freq)
        total = jnp.zeros((frames, 128), jnp.float32)
        for i in range(pieces):
            lanes = pl.ds(pl.multiple_of((seq ^ offsets[i]) * cols, 128), cols)
            current = jnp.concatenate([first[p][pl.ds(at, rows), lanes] for p in range(pieces)])
            hidden = current.astype(jnp.float32) + jnp.dot(
                onehot, table[0, :, lanes], preferred_element_type=jnp.float32
            )
            for lane in range(0, cols, 128):
                piece = hidden[:, lane : lane + 128]
                total = total + piece * piece
            scaled[step][:, lanes] = (hidden * mod[:, lanes]).astype(jnp.bfloat16)
            if i == 0:
                owns[step][...] = hidden
        mean = jnp.sum(total, axis=1, keepdims=True) * (1.0 / width)
        scales[step][...] = jnp.broadcast_to(lax.rsqrt(mean + epsilon), (frames, 128))


def dense(value, lead):
    frames = value.shape[0]
    rest = value[:, :64] if lead else value[:, 128:]
    full = value[:, 64:] if lead else value[:, :128]
    rest = jnp.concatenate([rest[: frames // 2], rest[frames // 2 :]], axis=1)
    return jnp.concatenate([full, rest], axis=0)


def undense(left, right, frames):
    middle = []
    for ref in (left, right):
        rest = ref[frames:]
        middle.append(jnp.concatenate([rest[:, :64], rest[:, 64:]], axis=0))
    return jnp.concatenate([left[:frames], jnp.concatenate(middle, axis=1), right[:frames]], axis=1)


def second_pair_kernel(dep, mine, across, out):
    out[0] = mine[...]
    out[1] = across[...]


def opened(pieces):
    return list(pieces[:2]) + [pieces[2].at[0], pieces[2].at[1]]


def step_kernel(cfg, *refs):
    step, has_relay, parts = cfg["step"], cfg["has_relay"], cfg["parts"]
    pieces, hops, head, turns = cfg["pieces"], cfg["hops"], cfg["head"], cfg["turns"]
    heads, group = cfg["heads"], cfg["group"]
    refs = list(refs)

    def take(count):
        taken, refs[:count] = refs[:count], []
        return taken

    bias, times, gain, freq, gate, flags = take(6)
    if has_relay:
        second, embed, relay = opened(take(3)), take(1)[0], take(2 * pieces)
    else:
        scaled, scales, own_hidden = take(3)
    streams = cfg["streams"]
    chunks = [take(streams), take(streams)] if step == 0 else None
    weights = take(len(parts))
    left = take(1)[0] if parts == (1,) else None
    sends = take(1)[0] if len(parts) == 1 else None
    out = take(1)[0]
    if step == 0:
        weights = take(1)
    proj, att = take(2)
    if has_relay:
        scaled, scales, own_hidden, mod = take(4)
    offsets = offsets_of(pieces)
    frames, width = scaled.shape
    cols = att.shape[0]
    half = cols // 2
    rows = frames // pieces
    seq, section = lax.axis_index("seq"), lax.axis_index("pipe")
    _, batch = turn_and_batch(step, turns)

    if step == 0:
        for hop, chunk in zip((2, 3), chunks):
            place(hop, hops, blocks_in(chunk), weights[0])

    def normalize(relayed):
        total = jnp.zeros((frames, 128), jnp.float32)
        for i in range(pieces):
            lanes = pl.ds(pl.multiple_of((seq ^ offsets[i]) * cols, 128), cols)
            if relayed:
                value = undense(relay[i], relay[pieces + i], frames)
                order = [offsets.index(offsets[i] ^ offsets[p]) for p in range(pieces)]
                blocks = [value[j * rows : (j + 1) * rows] for j in order]
            else:
                blocks = [second[p][:rows, lanes] for p in range(pieces)]
            hidden = jnp.concatenate(blocks, axis=0).astype(jnp.float32)
            hidden = hidden + embed[:, lanes].astype(jnp.float32)
            for lane in range(0, cols, 128):
                piece = hidden[:, lane : lane + 128]
                total = total + piece * piece
            scaled[:, lanes] = (hidden * mod[:, lanes]).astype(jnp.bfloat16)
            if i == 0:
                own_hidden[...] = hidden
        scales[...] = total

    if has_relay:
        mod[...] = modulation(step, turns, times, gain, freq)

        @pl.when(section == 0)
        def _():
            normalize(False)

        @pl.when(section != 0)
        def _():
            normalize(True)

        mean = jnp.sum(scales[...], axis=1, keepdims=True) * (1.0 / width)
        scale = lax.rsqrt(mean + epsilon)
    else:
        scale = scales[:, :1]

    def flag_of(i):
        lanes = pl.ds(pl.multiple_of((seq ^ offsets[i]) * rows, 128), rows)
        return None, flags[batch, :, lanes].astype(jnp.float32)

    flag_column = columns_of(flag_of, pieces, rows)[:, 16:17]
    score_scale = head ** (-0.5) * math.log2(math.e)
    lanes = lax.broadcasted_iota(jnp.int32, (frames, 128), 1)
    row_lanes = lax.broadcasted_iota(jnp.int32, (1, 128), 1)
    flag_lanes = jnp.logical_or(lanes == head, lanes == head + 1)
    pitch = cols + 128

    for k, part in enumerate(parts):
        base = k * pitch
        for at in range(0, cols, 256):
            size = min(256, cols - at)
            lane = at + lax.broadcasted_iota(jnp.int32, (1, size), 1)
            factor = jnp.where(lane < half, score_scale, 1.0)
            projected = jnp.dot(
                scaled[...], weights[k][:, at : at + size], preferred_element_type=jnp.float32
            )
            proj[:, base + at : base + at + size] = (projected * scale * factor).astype(
                jnp.bfloat16
            )
        proj[:, base + cols : base + pitch] = jnp.zeros((frames, 128), jnp.bfloat16)

    def slice_of(at):
        return proj[:, at : at + 128].astype(jnp.float32)

    keys, values = [], []
    for k in range(len(parts)):
        at = k * pitch + half
        key = jnp.where(flag_lanes, flag_column, jnp.where(lanes < head, slice_of(at), 0.0))
        value = jnp.where(
            lanes < head, slice_of(at + head), jnp.where(lanes == head, 1.0, 0.0)
        )
        keys.append(key.astype(jnp.bfloat16))
        values.append(value.T.astype(jnp.bfloat16))

    def scores_of(k, h):
        strength = bias[0, seq * heads + parts[k] * group + h] * math.log2(math.e)
        strength = jnp.zeros((1, 128), jnp.float32) + strength
        coarse = strength.astype(jnp.bfloat16).astype(jnp.float32)
        tail = jnp.where(
            row_lanes == head, coarse, jnp.where(row_lanes == head + 1, strength - coarse, 0.0)
        )
        query = jnp.where(lanes < head, slice_of(k * pitch + h * head), tail).astype(jnp.bfloat16)
        return lax.dot_general(
            keys[k], query, (((1,), (1,)), ((), ())), preferred_element_type=jnp.float32
        )

    tasks = [(k, h) for k in range(len(parts)) for h in range(group)]
    scores = scores_of(*tasks[0])
    for index, (k, h) in enumerate(tasks):
        ahead = scores_of(*tasks[index + 1]) if index + 1 < len(tasks) else None
        top = jnp.max(scores, axis=0, keepdims=True)
        weight = jnp.exp2(scores - top).astype(jnp.bfloat16)
        mixed = jnp.dot(values[k], weight, preferred_element_type=jnp.float32)
        at = (parts[k] * group + h) * head
        att[at : at + head, :] = mixed[:head] * (1.0 / mixed[head : head + 1])
        scores = ahead
    gates = gate[:, pl.ds(pl.multiple_of(seq * cols, 128), cols)]
    first, last = parts[0] * half, (parts[-1] + 1) * half
    attended = att[first:last].T.astype(jnp.bfloat16).astype(jnp.float32)
    output = own_hidden[...][:, first:last] + gates[:, first:last] * attended
    if parts == (0,):
        out[:, :half] = output.astype(jnp.bfloat16)
    elif parts == (1,):
        output_both = jnp.concatenate([left[:, :half].astype(jnp.float32), output], axis=1)
        out[...] = output_both.astype(jnp.bfloat16).reshape(pieces, rows, cols)
    else:
        out[...] = output.astype(jnp.bfloat16).reshape(pieces, rows, cols)
    if sends is not None:
        sends[...] = dense(output, parts == (1,)).astype(jnp.bfloat16)


def tie_kernel(*refs):
    pass


def grad_of(output, second, turn, rows, feats):
    cot = jnp.concatenate(
        [piece[rows : 2 * rows, turn * feats : (turn + 1) * feats] for piece in second], axis=0
    )
    return lax.dot_general(
        output, cot, (((0,), (0,)), ((), ())), preferred_element_type=jnp.float32
    )


def early_kernel(turns, pieces, halves, feats, *refs):
    outs, second = refs[: turns * halves], opened(refs[turns * halves : turns * halves + 3])
    sends, grad = refs[turns * halves + 3 : -1], refs[-1]
    section = lax.axis_index("pipe")
    offsets = offsets_of(pieces)
    part = pieces // halves
    rows = outs[0].shape[1]
    total = None
    for turn in range(turns - 1):
        blocks = []
        for p in range(pieces):
            k, j = p // part, p % part
            block = jnp.where(
                section == 0, outs[turn * halves + k][j], outs[(turn + 1) * halves + k][j]
            )
            sends[offsets[p]][turn] = block
            blocks.append(block)
        share = grad_of(jnp.concatenate(blocks, axis=0), second, turn, rows, feats)
        total = share if total is None else total + share
    grad[...] = total


def share_kernel(turns, pieces, hops, feats, *refs):
    before, now, second, early_grad = refs[0], refs[1], opened(refs[2:5]), refs[5]
    own_grad, grads, total = refs[6], refs[7:-1], refs[-1]
    section, rep = lax.axis_index("pipe"), lax.axis_index("dp")
    rows, cols = before.shape[1:]
    output = jnp.where(section == 0, before[...], now[...]).reshape(pieces * rows, cols)
    share = grad_of(output, second, turns - 1, rows, feats)
    total[...] = (share + early_grad[...]) * float(turns * hops * rows * pieces) ** (-0.5)
    g_rows = cols // hops
    own_grad[...] = total[pl.ds(pl.multiple_of(rep * g_rows, 8), g_rows)]
    for shift in range(1, hops):
        at = pl.multiple_of(lax.rem(rep + shift, hops) * g_rows, 8)
        grads[shift - 1][...] = total[pl.ds(at, g_rows)].astype(jnp.bfloat16)


def settle_kernel(turns, pieces, *refs):
    before, now, early = refs[0], refs[1], refs[2 : pieces + 1]
    late, (section_out, rows_out, sem) = refs[pieces + 1 : -3], refs[-3:]
    section, seq = lax.axis_index("pipe"), lax.axis_index("seq")
    offsets = offsets_of(pieces)
    rows, cols = early[0].shape[1:]
    for p in range(pieces):
        late[offsets[p]][...] = jnp.where(section == 0, before[p], now[p])
    for m in range(pieces - 1):
        lanes = pl.ds(pl.multiple_of((seq ^ m) * cols, 128), cols)
        for turn in range(turns - 1):
            rows_out[turn, :, lanes] = early[m][turn]
    copy = pltpu.make_async_copy(rows_out, section_out.at[pl.ds(0, turns - 1)], sem)
    copy.start()
    copy.wait()


def finish_kernel(pieces, hops, *refs):
    held, early, late, refs = refs[0], refs[1], refs[2 : pieces + 2], refs[pieces + 2 :]
    own_grad, parts, (section_out, grad, row_out, sems) = refs[0], refs[1:hops], refs[hops:]
    seq = lax.axis_index("seq")
    cols = late[0].shape[1]
    last_lanes = pl.ds(pl.multiple_of((seq ^ (pieces - 1)) * cols, 128), cols)
    early_copy = pltpu.make_async_copy(
        early, section_out.at[pl.ds(0, early.shape[0]), :, last_lanes], sems.at[0]
    )
    early_copy.start()
    for m in range(pieces):
        lanes = pl.ds(pl.multiple_of((seq ^ m) * cols, 128), cols)
        row_out[:, lanes] = late[m][...]
    copy = pltpu.make_async_copy(row_out, section_out.at[section_out.shape[0] - 1], sems.at[1])
    copy.start()
    total = own_grad[...]
    for part in parts:
        total = total + part[...].astype(jnp.float32)
    grad[...] = total
    early_copy.wait()
    copy.wait()


MIB = 1024 * 1024


def paired_body(
    incoming,
    contacts,
    keyframes,
    timesteps,
    w_query,
    w_keyval,
    norm_gain,
    time_freq,
    contact_table,
    key_bias,
    attn_gate,
    head_cotangent,
):
    seq_count = lax.axis_size("seq")
    hops = lax.axis_size("dp")
    rows, width, turns = incoming.shape[3], incoming.shape[4], incoming.shape[1]
    frames = rows * seq_count
    heads_all = key_bias.shape[1]
    head = width // heads_all
    heads = heads_all // seq_count
    kv_heads = w_keyval.shape[2] // (2 * head * seq_count)
    feats = head_cotangent.shape[4]
    cols = width // seq_count
    w_rows = w_query.shape[1]
    kind = jnp.bfloat16
    smem = pl.BlockSpec(memory_space=pltpu.SMEM)
    vmem = pl.BlockSpec(memory_space=pltpu.VMEM)
    anywhere = pl.BlockSpec(memory_space=pl.ANY)
    shape = jax.ShapeDtypeStruct

    def call(kernel, name, out_shape, in_specs, operands, scratch=(), limit=4, flops=0, **options):
        return pl.pallas_call(
            kernel,
            out_shape=out_shape,
            in_specs=in_specs,
            scratch_shapes=list(scratch),
            compiler_params=pltpu.CompilerParams(vmem_limit_bytes=limit * MIB),
            cost_estimate=pl.CostEstimate(
                flops=flops, bytes_accessed=flops // 512, transcendentals=0
            ),
            name=name,
            **options,
        )(*operands)

    timesteps = timesteps.reshape(1, timesteps.shape[0])

    def pin(value, space=pltpu.VMEM):
        return pltpu.with_memory_space_constraint(value, space)

    packed = call(
        pack_kernel,
        "pack",
        [pltpu.VMEM((2, w_rows, cols), kind)] * seq_count,
        [anywhere, anywhere],
        [pin(w_query, pltpu.HBM), pin(w_keyval, pltpu.HBM)],
        [pltpu.VMEM((seq_count, w_rows, cols), kind)] * 2
        + [pltpu.SemaphoreType.DMA((2 * seq_count,))],
        out_specs=[vmem] * seq_count,
    )
    blocks = [packed[0]] + [swap(packed[m], m) for m in range(1, seq_count)]

    def paired(name, deps, values):
        return call(
            functools.partial(pair_kernel, len(deps)),
            name,
            pltpu.VMEM((2, 2, w_rows, cols), kind),
            [anywhere] * len(deps) + [vmem] * 2,
            deps + values,
            out_specs=vmem,
        )

    def tie(values, deps):
        return call(
            tie_kernel,
            "tie",
            [shape(value.shape, kind) for value in values],
            [anywhere] * (len(values) + len(deps)),
            list(values) + list(deps),
            out_specs=[anywhere] * len(values),
            input_output_aliases={i: i for i in range(len(values))},
        )

    near = paired("near", [], blocks[:2])
    near_next = ring_step(near)
    far = call(
        far_kernel,
        "far",
        [pltpu.VMEM((2, w_rows, cols), kind)] * 2,
        [anywhere, vmem, vmem],
        [near_next] + blocks[2:],
        out_specs=[vmem] * 2,
    )
    far_next = [ring_step(value) for value in far]
    (far_next[1],) = tie([far_next[1]], [far_next[0]])
    streams = (2, 1)
    rings, partial = [], []
    for part in range(2):
        count = streams[part]
        chunk = call(
            functools.partial(part_kernel, part),
            "part%d" % part,
            [pltpu.VMEM((seq_count // count, w_rows, cols), kind)] * count,
            [vmem, vmem],
            [near_next, far_next[part]],
            out_specs=[vmem] * count,
        )
        rings.append([list(chunk)])
        partial.append(
            call(
                functools.partial(place_kernel, part, hops),
                "place%d" % part,
                pltpu.VMEM((width, cols), kind),
                [vmem] * (2 + count),
                [pin(near), pin(far[part])] + [pin(value) for value in chunk],
                out_specs=vmem,
            )
        )
    for ring in rings:
        ring.append([ring_step(value) for value in ring[-1]])
    rings[0].append([ring_step(value) for value in rings[0][-1]])

    mine = call(
        functools.partial(first_kernel, turns),
        "first",
        pltpu.VMEM((2 * rows + 16, width), kind),
        [anywhere, vmem, vmem],
        [far[0], incoming, contacts],
        [pltpu.VMEM((16, 128), jnp.float32)],
        out_specs=vmem,
    )
    across = swap(mine, 2)
    beside = swap(mine, 1)
    (across,) = tie([across], rings[0][1] + rings[1][1])
    first = [mine, across, beside, swap(across, 1)]
    prepared = call(
        functools.partial(norm_kernel, turns, seq_count),
        "norm",
        [pltpu.VMEM((frames, width), kind)] * 2
        + [pltpu.VMEM((frames, 128), jnp.float32)] * 2
        + [pltpu.VMEM((frames, cols), jnp.float32)] * 2
        + [pltpu.VMEM((frames, width), kind)] * 2,
        [smem] + [vmem] * 3 + [anywhere] * seq_count,
        [timesteps, contact_table, norm_gain, time_freq]
        + first,
        [pltpu.VMEM((1, width), jnp.float32)]
        + [pltpu.VMEM((2 * rows + 16, width), kind)] * seq_count
        + [pltpu.SemaphoreType.DMA((seq_count,))],
        12,
        out_specs=[vmem] * 8,
    )

    mine = call(
        second_kernel,
        "second",
        pltpu.VMEM((2 * rows, width), kind),
        [anywhere, vmem, vmem],
        [across, incoming, head_cotangent],
        out_specs=vmem,
    )
    second = [mine, swap(mine, 2)]

    rings[1][1] = list(tie(rings[1][1], [prepared[0]]))
    rings[1].append([ring_step(value) for value in rings[1][1]])

    common = [key_bias, timesteps, norm_gain, time_freq, attn_gate, keyframes]

    def run_step(step, parts, large, out_shape, aliases):
        cfg = {
            "step": step,
            "has_relay": step >= 2,
            "parts": parts,
            "pieces": seq_count,
            "hops": hops,
            "head": head,
            "heads": heads,
            "group": heads // kv_heads,
            "turns": turns,
            "streams": streams[parts[0]],
        }
        scratch = [
            pltpu.VMEM((frames, len(parts) * (cols + 128)), kind),
            pltpu.VMEM((cols, frames), jnp.float32),
        ]
        if step >= 2:
            scratch += [
                pltpu.VMEM((frames, width), kind),
                pltpu.VMEM((frames, 128), jnp.float32),
                pltpu.VMEM((frames, cols), jnp.float32),
                pltpu.VMEM((1, width), jnp.float32),
            ]
        operands = common + [pin(value) for value in large]
        return call(
            functools.partial(step_kernel, cfg),
            "step%d%s" % (step, "".join("ab"[part] for part in parts)),
            out_shape,
            [smem, smem] + [vmem] * (len(operands) - 2),
            operands,
            scratch,
            16,
            len(parts) * frames * (2 * width * cols + 2 * heads * frames * head),
            out_specs=[vmem] * len(out_shape),
            input_output_aliases=aliases,
        )

    whole = pltpu.VMEM((seq_count, rows, cols), kind)
    sent = pltpu.VMEM((frames * 3 // 2, 128), kind)
    weights = list(partial)
    relays, lefts, outputs = ([], []), [], []
    for part in range(2):
        for step in range(2):
            large = [prepared[step], prepared[2 + step], prepared[4 + step]]
            if step == 0:
                chunks = rings[part][1] + rings[part][2]
                if part:
                    last = tie(rings[part][2], [relays[0][0][0], lefts[1]])
                    chunks = rings[part][1] + list(last)
                large += chunks
            large += [weights[part]]
            aliases = {len(common) + len(large) - 1: 2} if step == 0 else {}
            out_shape = [sent, whole if part else pltpu.VMEM((frames, 256), kind)]
            if step == 0:
                out_shape += [pltpu.VMEM((width, cols), kind)]
            if part:
                large += [lefts[step]]
            results = run_step(step, (part,), large, out_shape, aliases)
            if step == 0:
                weights[part] = results[2]
            (outputs if part else lefts).append(results[1])
            piece = handed_over(results[0])
            relays[step].append([piece, None if part and not step else swap(piece, 2)])
    beside = call(
        second_pair_kernel,
        "beside",
        pltpu.VMEM((2,) + second[0].shape, kind),
        [anywhere, vmem, vmem],
        [outputs[0]] + second,
        limit=8,
        out_specs=vmem,
    )
    second = [second[0], second[1], swap(beside, 1)]

    (piece,) = tie([relays[0][1][0]], [outputs[1], second[2]])
    relays[0][1] = [piece, swap(piece, 2)]
    def complete(crossing):
        return [
            piece
            for mine, across in crossing
            for piece in (mine, across, swap(mine, 1), swap(across, 1))
        ]

    relay = complete(relays[0])
    (output,) = run_step(2, (0, 1), second + [prepared[6]] + relay + weights, [whole], {})
    outputs.append(output)
    early = call(
        functools.partial(early_kernel, turns, seq_count, 1, feats),
        "early",
        [shape((turns - 1, rows, cols), kind)] * seq_count + [shape((cols, feats), jnp.float32)],
        [vmem] * (turns + len(second)),
        outputs + second,
        limit=8,
        out_specs=[vmem] * (seq_count + 1),
    )
    early, early_grad = list(early[:-1]), early[-1]
    early = [early[0]] + [swap(early[m], m) for m in range(1, seq_count)]
    tied = tie([piece for pair in relays[1] for piece in pair], [early_grad])
    relay = complete([(tied[0], tied[1]), (tied[2], tied[3])])
    (output,) = run_step(3, (0, 1), second + [prepared[7]] + relay + weights, [whole], {})
    outputs.append(output)

    g_shape = (cols // hops, feats)
    operands = outputs[-2:] + second + [early_grad]
    grads = call(
        functools.partial(share_kernel, turns, seq_count, hops, feats),
        "share",
        [shape(g_shape, jnp.float32)] + [shape(g_shape, kind)] * (hops - 1),
        [vmem] * len(operands),
        operands,
        [pltpu.VMEM((cols, feats), jnp.float32)],
        8,
        out_specs=[vmem] * hops,
    )
    operands = outputs[-2:] + early[:-1]
    settled = call(
        functools.partial(settle_kernel, turns, seq_count),
        "settle",
        [shape((rows, cols), kind)] * seq_count + [shape((turns, rows, width), kind)],
        [vmem] * len(operands),
        operands,
        [pltpu.VMEM((turns - 1, rows, width), kind), pltpu.SemaphoreType.DMA],
        8,
        out_specs=[vmem] * seq_count + [anywhere],
    )
    late, held = settled[:seq_count], settled[-1]
    late = [late[0]] + [swap(late[m], m) for m in range(1, seq_count)]
    grads = [grads[0]] + [shifted(grads[k], "dp", k) for k in range(1, hops)]
    section_out, grad_rows = call(
        functools.partial(finish_kernel, seq_count, hops),
        "finish",
        [shape((turns, rows, width), kind), shape(g_shape, jnp.float32)],
        [anywhere] + [vmem] * (seq_count + hops + 1),
        [held, early[-1]] + late + grads,
        [pltpu.VMEM((rows, width), kind), pltpu.SemaphoreType.DMA((2,))],
        out_specs=[anywhere, vmem],
        input_output_aliases={0: 0},
    )
    return (section_out[None, :, None], grad_rows[None])


def body(incoming, contacts, keyframes, timesteps, w_query, *others):
    count = lax.axis_size("seq")
    cols = w_query.shape[2] // count
    paired = (
        lax.axis_size("pipe") == 2
        and lax.axis_size("dp") == 4
        and count == 4
        and cols % 128 == 0
        and w_query.shape[1] % 16 == 0
        and incoming.shape[3] == 128
        and incoming.shape[1] == 3
    )
    chosen = paired_body if paired else general_body
    return chosen(incoming, contacts, keyframes, timesteps, w_query, *others)


def general_body(
    incoming,
    contacts,
    keyframes,
    timesteps,
    w_query,
    w_keyval,
    norm_gain,
    time_freq,
    contact_table,
    key_bias,
    attn_gate,
    head_cotangent,
):
    section_idx = lax.axis_index("pipe")
    seq_idx = lax.axis_index("seq")
    rep_idx = lax.axis_index("dp")
    seq_count = lax.axis_size("seq")
    section_count = lax.axis_size("pipe")
    rep_count = lax.axis_size("dp")
    tok_rows = incoming.shape[3]
    width = incoming.shape[4]
    turns = incoming.shape[1]
    frames = tok_rows * seq_count
    heads_all = key_bias.shape[1]
    head_size = width // heads_all
    heads_local = heads_all // seq_count
    kv_width = w_keyval.shape[2]
    kv_local = kv_width // (2 * head_size * seq_count)
    group_size = heads_local // kv_local
    feat_count = head_cotangent.shape[4]
    score_scale = head_size ** (-0.5)
    q_cols = width // seq_count
    kv_cols = kv_width // seq_count
    w_rows = w_query.shape[1]

    w_parts = jnp.concatenate(
        [
            w_query[0].reshape(w_rows, seq_count, q_cols),
            w_keyval[0].reshape(w_rows, seq_count, kv_cols),
        ],
        axis=2,
    ).transpose(1, 0, 2)
    block = lax.all_to_all(w_parts, "seq", split_axis=0, concat_axis=0, tiled=True)
    weights = jnp.zeros((seq_count, rep_count, w_rows, q_cols + kv_cols), jnp.bfloat16)
    for hop in range(rep_count):
        owner = lax.rem(rep_idx + rep_count - hop, rep_count)
        weights = lax.dynamic_update_slice_in_dim(weights, block[:, None], owner, 1)
        if hop + 1 < rep_count:
            block = ring(block, "dp")
    weights = weights.reshape(width, q_cols + kv_cols)

    gain_row = norm_gain[0]
    freq_row = time_freq[0]
    table = contact_table[0]
    gate_local = lax.dynamic_slice_in_dim(attn_gate[0], seq_idx * q_cols, q_cols)
    table_local = lax.dynamic_slice_in_dim(table, seq_idx * q_cols, q_cols, 1)
    bias_local = lax.dynamic_slice_in_dim(key_bias[0], seq_idx * heads_local, heads_local)
    contact_all = lax.all_gather(contacts[:, 0, :], "seq", axis=1, tiled=True)
    key_all = keyframes[:, 0, :]
    step_all = timesteps[:, 0]
    labels = jnp.arange(table.shape[0], dtype=jnp.int32)
    cot_all = lax.all_gather(head_cotangent[0, :, 0], "seq", axis=1, tiled=True)

    lag = 2 if section_count == 2 else 1
    if lag == 2:
        steps = turns + 1
    else:
        steps = turns

    def turn_at(step):
        if lag == 1:
            return jnp.int32(step)
        return jnp.clip(step - section_idx, 0, turns - 1)

    outputs = []
    handed = {}
    for step in range(steps):
        turn = turn_at(step)
        fresh = lax.dynamic_index_in_dim(incoming[0, :, 0], turn, 0, keepdims=False)
        current = lax.all_gather(fresh, "seq", axis=0, tiled=True)
        if step in handed:
            current = jnp.where((section_idx == 0) | (turn == 0), current, handed[step])
        batch_idx = turn - section_idx + section_count - 1
        contact_rows = lax.dynamic_index_in_dim(contact_all, batch_idx, 0, keepdims=False)
        key_flags = lax.dynamic_index_in_dim(key_all, batch_idx, 0, keepdims=False).astype(
            jnp.float32
        )
        timestep = lax.dynamic_index_in_dim(step_all, batch_idx, 0, keepdims=False).astype(
            jnp.float32
        )
        onehot = (contact_rows[:, None] == labels[None, :]).astype(jnp.bfloat16)
        hidden = current.astype(jnp.float32) + jnp.dot(
            onehot, table, preferred_element_type=jnp.float32
        )
        root_mean = jnp.sqrt(jnp.mean(hidden * hidden, axis=-1, keepdims=True) + epsilon)
        modulation = gain_row * (1.0 + 0.5 * jnp.sin(timestep * freq_row))
        normed = (hidden / root_mean * modulation[None, :]).astype(jnp.bfloat16)
        projected = jnp.dot(normed, weights, preferred_element_type=jnp.float32).astype(
            jnp.bfloat16
        )
        query_heads = projected[:, :q_cols].reshape(frames, heads_local, head_size)
        keyval_heads = projected[:, q_cols:].reshape(frames, kv_local, 2, head_size)
        head_outputs = []
        for head in range(heads_local):
            key_rows = keyval_heads[:, head // group_size, 0]
            value_rows = keyval_heads[:, head // group_size, 1]
            scores = (
                lax.dot_general(
                    query_heads[:, head],
                    key_rows,
                    (((1,), (1,)), ((), ())),
                    preferred_element_type=jnp.float32,
                )
                * score_scale
            )
            scores = scores + bias_local[head] * key_flags[None, :]
            row_max = jnp.max(scores, axis=-1, keepdims=True)
            exponent = jnp.exp(scores - row_max)
            probabilities = (exponent / jnp.sum(exponent, axis=-1, keepdims=True)).astype(
                jnp.bfloat16
            )
            head_outputs.append(
                jnp.dot(probabilities, value_rows, preferred_element_type=jnp.float32).astype(
                    jnp.bfloat16
                )
            )
        attended = jnp.concatenate(head_outputs, axis=1)
        hidden_local = lax.dynamic_slice_in_dim(current, seq_idx * q_cols, q_cols, 1).astype(
            jnp.float32
        ) + jnp.dot(onehot, table_local, preferred_element_type=jnp.float32)
        output = (hidden_local + gate_local[None, :] * attended.astype(jnp.float32)).astype(
            jnp.bfloat16
        )
        outputs.append(output)
        if step + lag < steps:
            piece = passed_along(output, "pipe", 1)
            handed[step + lag] = lax.all_gather(piece, "seq", axis=1, tiled=True)

    factor = float(turns * rep_count * frames) ** (-0.5)
    total = None
    rows_out = []
    for turn in range(turns):
        if lag == 2:
            own = jnp.where(section_idx == 0, outputs[turn], outputs[turn + 1])
        else:
            own = outputs[turn]
        term = lax.dot_general(
            own, cot_all[turn], (((0,), (0,)), ((), ())), preferred_element_type=jnp.float32
        )
        total = term if total is None else total + term
        rows_out.append(lax.all_to_all(own, "seq", split_axis=0, concat_axis=1, tiled=True))
    section_out = jnp.stack(rows_out)[None, :, None]
    grad_parts = lax.all_to_all(
        (total * factor).astype(jnp.bfloat16).reshape(rep_count, q_cols // rep_count, feat_count),
        "dp",
        split_axis=0,
        concat_axis=0,
        tiled=True,
    )
    grad_rows = jnp.sum(grad_parts.astype(jnp.float32), axis=0)
    return (section_out, grad_rows[None])


def solution(mesh):
    in_specs = (
        P("pipe", None, "dp", "seq", None),
        P(None, "dp", "seq"),
        P(None, "dp", None),
        P(None, "dp"),
        P("pipe", ("seq", "dp"), None),
        P("pipe", ("seq", "dp"), None),
        P("pipe", None),
        P("pipe", None),
        P("pipe", None, None),
        P("pipe", None),
        P("pipe", None),
        P("pipe", None, "dp", "seq", None),
    )
    out_specs = (P("pipe", None, "dp", "seq", None), P("pipe", ("seq", "dp"), None))
    return jax.shard_map(body, mesh=mesh, in_specs=in_specs, out_specs=out_specs, check_vma=False)
```
